32 devices in a mesh: rep: 8 (over y, x, core), shard: 4 (over z).
Axes of the slice: x: 2, y: 2, z: 4, core: 2. Of those that a mesh axis runs over, the one named last changes fastest.
Arguments:
- latents: bfloat16 [64, 4096], P(('rep', 'shard')), may hold values from -6 to 6
- noise: bfloat16 [64, 4096], P(('rep', 'shard')), may hold values from -6 to 6
- labels: int32 [64], P(('rep', 'shard')), may hold values from 0 to 999
- t_index: int32 [64], P(('rep', 'shard')), may hold values from 0 to 999, as said below
- owner: int32 [234], replicated, may hold values from 0 to 479, as said below
- master: float32 [768, 480, 128], P(None, ('rep', 'shard'))
- first_moment: float32 [768, 480, 128], P(None, ('rep', 'shard'))
- second_moment: float32 [768, 480, 128], P(None, ('rep', 'shard'))
- small: float32 [1288, 768], replicated
- small_first: float32 [1288, 768], replicated
- small_second: float32 [1288, 768], replicated
Outputs:
- loss_sum: float32 [], replicated
- weight_total: float32 [], replicated
- new_master: float32 [768, 480, 128], P(None, ('rep', 'shard'))
- new_first: float32 [768, 480, 128], P(None, ('rep', 'shard'))
- new_second: float32 [768, 480, 128], P(None, ('rep', 'shard'))
- new_small: float32 [1288, 768], replicated
- new_small_first: float32 [1288, 768], replicated
- new_small_second: float32 [1288, 768], replicated
The draws below stay inside these ranges and needn't reach their ends.
Inputs may be any that keep to these rules, and one draw needn't show every extreme that they name: `t_index`: image b's index lies between b * 1000 // 64 and ((b + 1) * 1000 - 1) // 64. `owner`: distinct slots; slot s belongs to device s // 15, devices in the order rep then shard; some device holds 15 blocks.
All inputs are finite; a program needn't handle non-finite values.
Results may differ from the reference program's by a relative error of at most 0.022.
Values may be sent and summed in bfloat16 or wider, within the bound.
A program may use at most 320 MiB of HBM per device.

```python
import math
import jax
import jax.numpy as jnp
from jax import lax

D = 768
HEADS = 12
HEAD_DIM = 64
FF = 3072
FREQ = 256
CLASSES = 1000
CHANNELS = 16
GRID = 16
PATCHES = 256
LAYERS = 2
TSTEPS = 1000
STEP = 10
BLOCK = 128
IMAGES = 64
TOKENS = 16384
LAYER_COLS = 13824
LAYER_UNITS = 108
UNITS = 234
SLOT_DEV = 15
SLOTS = 480
SMALL_ROWS = 1288
DEVICES = 32


def unit_scale_drawn(unit_ids):
    column = unit_ids % LAYER_UNITS * BLOCK
    in_layer = unit_ids < LAYERS * LAYER_UNITS
    is_output = in_layer & (column >= 9 * D) & (column < 10 * D)
    is_down = in_layer & (column >= 10 * D + FF)
    factor = jnp.where(is_output, 4.0, jnp.where(is_down, 1.5 * (D / FF) ** 0.5, 1.0))
    return factor / D ** 0.5


def table_scale_drawn(row_ids):
    return jnp.where(row_ids < CHANNELS, CHANNELS ** (-0.5), jnp.where(row_ids < CHANNELS + FREQ, FREQ ** (-0.5), jnp.where(row_ids < CHANNELS + FREQ + CLASSES, 0.5, D ** (-0.5))))


def small_grad_size(row_ids):
    token_root = math.sqrt(TOKENS)
    return jnp.where(row_ids < CHANNELS, 0.07 * token_root, jnp.where(row_ids < CHANNELS + FREQ, 0.04 * token_root, jnp.where(row_ids < CHANNELS + FREQ + CLASSES, 2.0, 0.5 * token_root)))


def owner_slots(key):
    chosen = jax.random.randint(jax.random.fold_in(key, 11), (), 0, DEVICES)
    shuffled = jax.random.permutation(jax.random.fold_in(key, 12), SLOTS)
    position = jnp.zeros((SLOTS,), jnp.int32).at[shuffled].set(jnp.arange(SLOTS, dtype=jnp.int32))
    device_of = jnp.arange(SLOTS, dtype=jnp.int32) // SLOT_DEV
    priority = jnp.where(device_of == chosen, position - SLOTS, position)
    return jnp.argsort(priority, stable=True)[:UNITS].astype(jnp.int32)


def draw_owner(key, part):
    return owner_slots(key)


def draw_t_index(key, part):
    key = jax.random.fold_in(key, 2)
    offset = jax.random.randint(key, (IMAGES,), 0, TSTEPS)
    image_ids = jnp.arange(IMAGES, dtype=jnp.int32)
    return ((image_ids * TSTEPS + offset) // IMAGES).astype(jnp.int32)


def draw_master(key, part):
    owner = owner_slots(key)
    key = jax.random.fold_in(key, 3)
    unit_of_slot = jnp.zeros((SLOTS,), jnp.int32).at[owner].set(jnp.arange(UNITS, dtype=jnp.int32))
    scale = unit_scale_drawn(unit_of_slot)[None, :, None]
    base = jnp.clip(jax.random.normal(key, (D, SLOTS, BLOCK), jnp.float32), -4.0, 4.0)
    return base * scale


def draw_first_moment(key, part):
    key = jax.random.fold_in(key, 4)
    size = 0.03 * math.sqrt(TOKENS)
    return jax.random.uniform(key, (D, SLOTS, BLOCK), jnp.float32, -1.0, 1.0) * size


def draw_second_moment(key, part):
    key = jax.random.fold_in(key, 5)
    size = 0.1 * math.sqrt(TOKENS)
    factor = jnp.exp(jax.random.uniform(key, (D, SLOTS, BLOCK), jnp.float32, 0.0, math.log(4.0)))
    return factor * size * size


def draw_small(key, part):
    key = jax.random.fold_in(key, 6)
    scale = table_scale_drawn(jnp.arange(SMALL_ROWS, dtype=jnp.int32))[:, None]
    base = jnp.clip(jax.random.normal(key, (SMALL_ROWS, D), jnp.float32), -4.0, 4.0)
    return base * scale


def draw_small_first(key, part):
    key = jax.random.fold_in(key, 7)
    size = small_grad_size(jnp.arange(SMALL_ROWS, dtype=jnp.int32))[:, None]
    return jax.random.uniform(key, (SMALL_ROWS, D), jnp.float32, -1.0, 1.0) * size


def draw_small_second(key, part):
    key = jax.random.fold_in(key, 8)
    size = small_grad_size(jnp.arange(SMALL_ROWS, dtype=jnp.int32))[:, None]
    factor = jnp.exp(jax.random.uniform(key, (SMALL_ROWS, D), jnp.float32, 0.0, math.log(4.0)))
    return factor * size * size


def touch_ends(array, rng, low, high):
    place = [jax.random.randint(jax.random.fold_in(rng, axis), (), 0, length) for axis, length in enumerate(array.shape)]
    main_axis = array.shape.index(max(array.shape))
    neighbour = place[:main_axis] + [(place[main_axis] + 1) % array.shape[main_axis]] + place[main_axis + 1:]
    return array.at[tuple(place)].set(low).at[tuple(neighbour)].set(high)


def block_scale(own_key, dims, pieces, smallest, largest):
    def one(dim, blocks):
        heights = jax.random.uniform(jax.random.fold_in(jax.random.fold_in(own_key, 6), dim), (blocks,), jnp.float32, smallest / len(pieces), largest / len(pieces))
        return jnp.repeat(jnp.exp(heights), dims[dim] // blocks).reshape((-1,) + (1,) * (len(dims) - dim - 1))

    loudness = one(*pieces[0])
    for cut in pieces[1:]:
        loudness = loudness * one(*cut)
    return loudness


def bell_draw(stream_key, extent, width, limit, pieces=(), kind=jnp.bfloat16):
    factor_of = block_scale(stream_key, extent, pieces, -0.22, 0.18) if pieces else 1.0
    result = jax.random.normal(stream_key, extent, jnp.float32) * width * factor_of
    return jnp.minimum(jnp.maximum(result, -limit), limit).astype(kind)


def setup_inputs(seed: int = 0) -> dict:
    seeds = jax.random.split(jax.random.key(seed), 12)
    return {
        "latents": bell_draw(seeds[0], (IMAGES, PATCHES * CHANNELS), 1.0, 6.0, ((0, 32),)),
        "noise": bell_draw(seeds[1], (IMAGES, PATCHES * CHANNELS), 1.0, 6.0, ((0, 32),)),
        "labels": touch_ends(jax.random.randint(seeds[2], (IMAGES,), 0, CLASSES), jax.random.fold_in(seeds[2], 1), 0, CLASSES - 1).astype(jnp.int32),
        "t_index": draw_t_index(jax.random.fold_in(seeds[11], 71), 0),
        "owner": draw_owner(jax.random.fold_in(seeds[11], 71), 0),
        "master": draw_master(jax.random.fold_in(seeds[11], 71), 0),
        "first_moment": draw_first_moment(jax.random.fold_in(seeds[11], 71), 0),
        "second_moment": draw_second_moment(jax.random.fold_in(seeds[11], 71), 0),
        "small": draw_small(jax.random.fold_in(seeds[11], 71), 0),
        "small_first": draw_small_first(jax.random.fold_in(seeds[11], 71), 0),
        "small_second": draw_small_second(jax.random.fold_in(seeds[11], 71), 0),
    }


@jax.custom_vjp
def low(v):
    return lax.optimization_barrier(v.astype(jnp.bfloat16)).astype(jnp.float32)

@jax.custom_vjp
def low_back(v):
    return v

def low_keep(v):
    return (low(v), None)

def low_pass(kept, grad):
    return (grad,)

def back_keep(v):
    return (v, None)

def back_low(kept, grad):
    return (low(grad),)
low.defvjp(low_keep, low_pass)
low_back.defvjp(back_keep, back_low)
beta_one = 0.5
beta_two = 0.5
adam_eps = 1e-08
decay_rate = 0.1
rate_factor = 0.5

def matmul_high(left_side, right_side):
    return jnp.matmul(left_side, right_side, precision=lax.Precision.HIGHEST)

def einsum_high(pattern, left_side, right_side):
    return jnp.einsum(pattern, left_side, right_side, precision=lax.Precision.HIGHEST)

def gelu_tanh(values):
    return jax.nn.gelu(values, approximate=True)

def norm_rows(hidden):
    centered = hidden - lax.optimization_barrier(jnp.mean(hidden, -1, keepdims=True))
    return centered * lax.rsqrt(lax.optimization_barrier(jnp.mean(centered * centered, -1, keepdims=True)) + 1e-06)

def positions():
    quarter = D // 4
    angular = jnp.exp(-jnp.log(10000.0) * jnp.arange(quarter, dtype=jnp.float32) / quarter)
    patch_idx = jnp.arange(PATCHES, dtype=jnp.int32)
    row_pos = (patch_idx // GRID).astype(jnp.float32)[:, None] * angular
    col_pos = (patch_idx % GRID).astype(jnp.float32)[:, None] * angular
    return jnp.concatenate([jnp.sin(col_pos), jnp.cos(col_pos), jnp.sin(row_pos), jnp.cos(row_pos)], -1)

def frequencies(times):
    half_size = FREQ // 2
    spacing = jnp.exp(-jnp.log(10000.0) * jnp.arange(half_size, dtype=jnp.float32) / half_size)
    angles = 1000.0 * times[:, None] * spacing
    return jnp.concatenate([jnp.cos(angles), jnp.sin(angles)], -1)

def unit_scale(unit_ids):
    column = unit_ids % LAYER_UNITS * BLOCK
    in_layer = unit_ids < LAYERS * LAYER_UNITS
    is_output = in_layer & (column >= 9 * D) & (column < 10 * D)
    is_down = in_layer & (column >= 10 * D + FF)
    factor = jnp.where(is_output, 4.0, jnp.where(is_down, 1.5 * (D / FF) ** 0.5, 1.0))
    return factor / D ** 0.5

def table_scale(row_ids):
    return jnp.where(row_ids < CHANNELS, CHANNELS ** (-0.5), jnp.where(row_ids < CHANNELS + FREQ, FREQ ** (-0.5), jnp.where(row_ids < CHANNELS + FREQ + CLASSES, 0.5, D ** (-0.5))))

def adam_update(weight, first_mom, second, gradient, rate):
    first_new = beta_one * first_mom + (1.0 - beta_one) * gradient
    second_new = beta_two * second + (1.0 - beta_two) * gradient * gradient
    ratio = first_new / (1.0 - beta_one ** STEP) / (jnp.sqrt(second_new / (1.0 - beta_two ** STEP)) + adam_eps)
    return (weight - rate * (ratio + decay_rate * weight), first_new, second_new)

def layer_ref(hidden, cond_act, weights):
    w_ada = weights[:, :6 * D]
    w_qkv = weights[:, 6 * D:9 * D]
    w_out = weights[:, 9 * D:10 * D]
    w_up = weights[:, 10 * D:10 * D + FF]
    w_down = weights[:, 10 * D + FF:]
    groups = hidden.shape[0]
    modul = low_back(matmul_high(cond_act, w_ada))
    shift_a, scale_a, gate_a, shift_b, scale_b, gate_b = jnp.split(modul[:, None, :], 6, -1)
    attn_in = low(norm_rows(hidden) * (1.0 + scale_a) + shift_a)
    qkv_all = low_back(low(matmul_high(attn_in, w_qkv)))
    queries = qkv_all[..., :D].reshape(groups, PATCHES, HEADS, HEAD_DIM)
    keys_all = qkv_all[..., D:2 * D].reshape(groups, PATCHES, HEADS, HEAD_DIM)
    values = qkv_all[..., 2 * D:].reshape(groups, PATCHES, HEADS, HEAD_DIM)
    scores = low_back(einsum_high('gqhe,gkhe->ghqk', queries, keys_all)) * HEAD_DIM ** (-0.5)
    attn_prob = low(jax.nn.softmax(scores, -1))
    heads_out = low_back(low(einsum_high('ghqk,gkhe->gqhe', attn_prob, values))).reshape(groups, PATCHES, D)
    branch_a = low_back(matmul_high(heads_out, w_out))
    middle = hidden + gate_a * branch_a
    mlp_in = low(norm_rows(middle) * (1.0 + scale_b) + shift_b)
    pre_act = low_back(matmul_high(mlp_in, w_up))
    post_act = low(gelu_tanh(pre_act))
    branch_b = low_back(einsum_high('gpf,df->gpd', post_act, w_down))
    return middle + gate_b * branch_b

def group_loss(units, small, noisy, target, times, loss_weight, labels):
    weights_low = low(units)
    patch_w = low(small[:CHANNELS])
    time_w = low(small[CHANNELS:CHANNELS + FREQ])
    table = small[CHANNELS + FREQ:CHANNELS + FREQ + CLASSES]
    head_w = low(small[CHANNELS + FREQ + CLASSES:])
    hidden = low_back(matmul_high(low(noisy), patch_w)) + positions()
    time_pre = low_back(matmul_high(low(frequencies(times)), time_w))
    time_act = low(jax.nn.silu(time_pre))
    tail_start = LAYERS * LAYER_COLS
    cond = low_back(matmul_high(time_act, weights_low[:, tail_start:tail_start + D])) + jnp.take(table, labels, axis=0)
    cond_act = low(jax.nn.silu(cond))
    for layer_idx in range(LAYERS):
        hidden = layer_ref(hidden, cond_act, weights_low[:, layer_idx * LAYER_COLS:(layer_idx + 1) * LAYER_COLS])
    modul_f = low_back(matmul_high(cond_act, weights_low[:, tail_start + D:tail_start + 3 * D]))
    shift_f, scale_f = jnp.split(modul_f[:, None, :], 2, -1)
    final_in = low(norm_rows(hidden) * (1.0 + scale_f) + shift_f)
    predict = low_back(einsum_high('gpd,cd->gpc', final_in, head_w))
    error = predict - target
    return jnp.sum(loss_weight[:, None, None] * error * error) / CHANNELS

def reference(latents, noise, labels, t_index, owner, master, first_moment, second_moment, small, small_first, small_second):
    units = master[:, owner, :].reshape(D, UNITS * BLOCK)
    x_start = latents.astype(jnp.float32).reshape(IMAGES, PATCHES, CHANNELS)
    noise_f = noise.astype(jnp.float32).reshape(IMAGES, PATCHES, CHANNELS)
    times = (t_index.astype(jnp.float32) + 0.5) / TSTEPS
    noisy = (1.0 - times)[:, None, None] * x_start + times[:, None, None] * noise_f
    target = noise_f - x_start
    loss_weight = 1.0 + 3.0 * times
    group_size = 16 if IMAGES % 16 == 0 else 1
    group_count = IMAGES // group_size

    def shape_group(member):
        return member.reshape((group_count, group_size) + member.shape[1:])

    def accumulate(running, group_data):
        unit_sum, small_sum, loss_total = running
        noisy_g, target_g, times_g, weight_g, labels_g = group_data
        group_value, pullback = jax.vjp(lambda unit_arg, small_arg: group_loss(unit_arg, small_arg, noisy_g, target_g, times_g, weight_g, labels_g), units, small)
        unit_grad, small_grad = pullback(jnp.ones_like(group_value))
        return ((unit_sum + unit_grad, small_sum + small_grad, loss_total + group_value), None)
    start_state = (jnp.zeros_like(units), jnp.zeros_like(small), jnp.zeros((), jnp.float32))
    data = tuple((shape_group(member) for member in (noisy, target, times, loss_weight, labels)))
    (unit_grad, small_grad, loss_sum), unused = lax.scan(accumulate, start_state, data)
    weight_total = jnp.sum(loss_weight) * PATCHES
    unit_ids = jnp.arange(UNITS, dtype=jnp.int32)
    slot_grad = jnp.zeros((D, SLOTS, BLOCK), jnp.float32).at[:, owner, :].set(unit_grad.reshape(D, UNITS, BLOCK))
    unit_of_slot = jnp.zeros((SLOTS,), jnp.int32).at[owner].set(unit_ids)
    used_slot = (jnp.zeros((SLOTS,), jnp.int32).at[owner].set(1) > 0)[None, :, None]
    rate = rate_factor * unit_scale(unit_of_slot)[None, :, None]
    new_w, new_first, new_second = adam_update(master, first_moment, second_moment, slot_grad, rate)
    new_master = jnp.where(used_slot, new_w, master)
    new_first = jnp.where(used_slot, new_first, first_moment)
    new_second = jnp.where(used_slot, new_second, second_moment)
    small_rate = rate_factor * table_scale(jnp.arange(SMALL_ROWS, dtype=jnp.int32))[:, None]
    new_small, new_small_first, new_small_second = adam_update(small, small_first, small_second, small_grad, small_rate)
    return (loss_sum, weight_total, new_master, new_first, new_second, new_small, new_small_first, new_small_second)
```

```python
import jax
import jax.numpy as jnp
import numpy as np
from jax import lax
from jax.sharding import PartitionSpec as P

D = 768
HEADS = 12
HEAD_DIM = 64
FF = 3072
FREQ = 256
CLASSES = 1000
CHANNELS = 16
GRID = 16
PATCHES = 256
LAYERS = 2
TSTEPS = 1000
STEP = 10
BLOCK = 128
LAYER_COLS = 13824
LAYER_UNITS = 108
UNITS = 234

ADA_UNITS = 6 * D // BLOCK
DENSE_UNITS = LAYER_UNITS - ADA_UNITS
DENSE_COLS = DENSE_UNITS * BLOCK
TIME_UNITS = D // BLOCK
TAIL_FIRST = LAYERS * LAYER_UNITS
AXES = ("rep", "shard")


beta_one = 0.5
beta_two = 0.5
adam_eps = 1e-08
decay_rate = 0.1
rate_factor = 0.5


def gelu_tanh(values):
    return jax.nn.gelu(values, approximate=True)


def norm_rows(hidden):
    centered = hidden - jnp.mean(hidden, -1, keepdims=True)
    return centered * lax.rsqrt(jnp.mean(centered * centered, -1, keepdims=True) + 1e-06)


def local_back(function, primal, upstream):
    return jax.vjp(function, primal)[1](upstream)[0]


def dot_low(pattern, left_side, right_side):
    return jnp.einsum(pattern, left_side, right_side, preferred_element_type=jnp.float32)


def positions():
    quarter = D // 4
    angular = jnp.exp(-jnp.log(10000.0) * jnp.arange(quarter, dtype=jnp.float32) / quarter)
    patch_idx = jnp.arange(PATCHES, dtype=jnp.int32)
    row_pos = (patch_idx // GRID).astype(jnp.float32)[:, None] * angular
    col_pos = (patch_idx % GRID).astype(jnp.float32)[:, None] * angular
    return jnp.concatenate(
        [jnp.sin(col_pos), jnp.cos(col_pos), jnp.sin(row_pos), jnp.cos(row_pos)], -1
    )


def frequencies(times):
    half_size = FREQ // 2
    spacing = jnp.exp(-jnp.log(10000.0) * jnp.arange(half_size, dtype=jnp.float32) / half_size)
    angles = 1000.0 * times[:, None] * spacing
    return jnp.concatenate([jnp.cos(angles), jnp.sin(angles)], -1)


def unit_scale(unit_ids):
    column = unit_ids % LAYER_UNITS * BLOCK
    in_layer = unit_ids < LAYERS * LAYER_UNITS
    is_output = in_layer & (column >= 9 * D) & (column < 10 * D)
    is_down = in_layer & (column >= 10 * D + FF)
    factor = jnp.where(is_output, 4.0, jnp.where(is_down, 1.5 * (D / FF) ** 0.5, 1.0))
    return factor / D**0.5


def table_scale(row_ids):
    return jnp.where(
        row_ids < CHANNELS,
        CHANNELS ** (-0.5),
        jnp.where(
            row_ids < CHANNELS + FREQ,
            FREQ ** (-0.5),
            jnp.where(row_ids < CHANNELS + FREQ + CLASSES, 0.5, D ** (-0.5)),
        ),
    )


def adam_update(weight, first_mom, second, gradient, rate):
    first_new = beta_one * first_mom + (1.0 - beta_one) * gradient
    second_new = beta_two * second + (1.0 - beta_two) * gradient * gradient
    ratio = (
        first_new
        / (1.0 - beta_one**STEP)
        / (jnp.sqrt(second_new / (1.0 - beta_two**STEP)) + adam_eps)
    )
    return (weight - rate * (ratio + decay_rate * weight), first_new, second_new)


def split_dense(weights):
    return (
        weights[:, : 3 * D],
        weights[:, 3 * D : 4 * D],
        weights[:, 4 * D : 4 * D + FF],
        weights[:, 4 * D + FF :],
    )


def split_heads(qkv_all):
    groups, length = (qkv_all.shape[0], qkv_all.shape[1])
    return tuple(
        (
            qkv_all[..., part_idx * D : (part_idx + 1) * D].reshape(groups, length, HEADS, HEAD_DIM)
            for part_idx in range(3)
        )
    )


def modulate(normed, shift, scale):
    return normed * (1.0 + scale[:, None, :]) + shift[:, None, :]


def layer_forward(hidden, modul, weights):
    w_qkv, w_out, w_up, w_down = split_dense(weights)
    groups = hidden.shape[0]
    shift_a, scale_a, gate_a, shift_b, scale_b, gate_b = jnp.split(modul, 6, -1)
    attn_in = modulate(norm_rows(hidden), shift_a, scale_a).astype(jnp.bfloat16)
    qkv_all = dot_low("gpd,de->gpe", attn_in, w_qkv).astype(jnp.bfloat16)
    queries, keys_all, values = split_heads(qkv_all)
    scores = dot_low("gqhe,gkhe->ghqk", queries, keys_all) * HEAD_DIM ** (-0.5)
    top_score = jnp.max(scores, -1, keepdims=True)
    log_total = top_score + jnp.log(jnp.sum(jnp.exp(scores - top_score), -1, keepdims=True))
    attn_prob = jnp.exp(scores - log_total).astype(jnp.bfloat16)
    heads_out = (
        dot_low("ghqk,gkhe->gqhe", attn_prob, values).astype(jnp.bfloat16).reshape(groups, -1, D)
    )
    branch_a = dot_low("gpd,de->gpe", heads_out, w_out)
    middle = hidden + gate_a[:, None, :] * branch_a
    mlp_in = modulate(norm_rows(middle), shift_b, scale_b).astype(jnp.bfloat16)
    pre_act = dot_low("gpd,df->gpf", mlp_in, w_up)
    post_act = gelu_tanh(pre_act).astype(jnp.bfloat16)
    branch_b = dot_low("gpf,df->gpd", post_act, w_down)
    output = middle + gate_b[:, None, :] * branch_b
    return (
        output,
        (
            hidden,
            modul,
            attn_in,
            qkv_all,
            log_total,
            heads_out,
            branch_a,
            middle,
            mlp_in,
            pre_act,
            post_act,
            branch_b,
        ),
    )


def layer_backward(grad_out, weights, saved):
    w_qkv, w_out, w_up, w_down = split_dense(weights)
    (
        hidden,
        modul,
        attn_in,
        qkv_all,
        log_total,
        heads_out,
        branch_a,
        middle,
        mlp_in,
        pre_act,
        post_act,
        branch_b,
    ) = saved
    groups = hidden.shape[0]
    shift_a, scale_a, gate_a, shift_b, scale_b, gate_b = jnp.split(modul, 6, -1)
    grad_gate_b = jnp.sum(grad_out * branch_b, 1)
    grad_branch_b = (gate_b[:, None, :] * grad_out).astype(jnp.bfloat16)
    grad_down = dot_low("gpd,gpf->df", grad_branch_b, post_act)
    grad_post = dot_low("gpd,df->gpf", grad_branch_b, w_down)
    grad_pre = local_back(gelu_tanh, pre_act, grad_post).astype(jnp.bfloat16)
    grad_up = dot_low("gpd,gpf->df", mlp_in, grad_pre)
    grad_mlp_in = dot_low("gpf,df->gpd", grad_pre, w_up)
    normed_b = norm_rows(middle)
    grad_scale_b = jnp.sum(grad_mlp_in * normed_b, 1)
    grad_shift_b = jnp.sum(grad_mlp_in, 1)
    grad_middle = grad_out + local_back(
        norm_rows, middle, grad_mlp_in * (1.0 + scale_b[:, None, :])
    )
    grad_gate_a = jnp.sum(grad_middle * branch_a, 1)
    grad_branch_a = (gate_a[:, None, :] * grad_middle).astype(jnp.bfloat16)
    grad_out_w = dot_low("gpd,gpe->de", heads_out, grad_branch_a)
    grad_heads = (
        dot_low("gpe,de->gpd", grad_branch_a, w_out)
        .astype(jnp.bfloat16)
        .reshape(groups, -1, HEADS, HEAD_DIM)
    )
    queries, keys_all, values = split_heads(qkv_all)
    scores = dot_low("gqhe,gkhe->ghqk", queries, keys_all) * HEAD_DIM ** (-0.5)
    attn_prob = jnp.exp(scores - log_total)
    grad_prob = dot_low("gqhe,gkhe->ghqk", grad_heads, values)
    grad_values = dot_low("ghqk,gqhe->gkhe", attn_prob.astype(jnp.bfloat16), grad_heads)
    inner_sum = jnp.sum(attn_prob * grad_prob, -1, keepdims=True)
    grad_scores = (HEAD_DIM ** (-0.5) * attn_prob * (grad_prob - inner_sum)).astype(jnp.bfloat16)
    grad_queries = dot_low("ghqk,gkhe->gqhe", grad_scores, keys_all)
    grad_keys = dot_low("ghqk,gqhe->gkhe", grad_scores, queries)
    grad_qkv = jnp.concatenate(
        [
            grad_queries.reshape(groups, -1, D),
            grad_keys.reshape(groups, -1, D),
            grad_values.reshape(groups, -1, D),
        ],
        -1,
    ).astype(jnp.bfloat16)
    grad_qkv_w = dot_low("gpd,gpe->de", attn_in, grad_qkv)
    grad_attn_in = dot_low("gpe,de->gpd", grad_qkv, w_qkv)
    normed_a = norm_rows(hidden)
    grad_scale_a = jnp.sum(grad_attn_in * normed_a, 1)
    grad_shift_a = jnp.sum(grad_attn_in, 1)
    grad_in = grad_middle + local_back(
        norm_rows, hidden, grad_attn_in * (1.0 + scale_a[:, None, :])
    )
    grad_modul = jnp.concatenate(
        [grad_shift_a, grad_scale_a, grad_gate_a, grad_shift_b, grad_scale_b, grad_gate_b], -1
    ).astype(jnp.bfloat16)
    weight_grad = jnp.concatenate([grad_qkv_w, grad_out_w, grad_up, grad_down], 1)
    return (grad_in, grad_modul, weight_grad)


def unit_lists():
    dense = np.concatenate(
        [np.arange(l * LAYER_UNITS + ADA_UNITS, (l + 1) * LAYER_UNITS) for l in range(LAYERS)]
    )
    time_units = np.arange(TAIL_FIRST, TAIL_FIRST + TIME_UNITS)
    image_units = np.concatenate(
        [np.arange(l * LAYER_UNITS, l * LAYER_UNITS + ADA_UNITS) for l in range(LAYERS)]
        + [np.arange(TAIL_FIRST + TIME_UNITS, UNITS)]
    )
    return dense, time_units, image_units


def on_device(
    latents,
    noise,
    labels,
    t_index,
    owner,
    master,
    first_moment,
    second_moment,
    small,
    small_first,
    small_second,
):
    count = lax.axis_size("rep") * lax.axis_size("shard")
    me = lax.axis_index(AXES)
    slot_dev = master.shape[1]
    slot_total = count * slot_dev
    rows = D // count
    images = latents.shape[0]
    dense_units, time_units, image_units = unit_lists()

    unit_of_slot = (
        jnp.full((slot_total,), -1, jnp.int32).at[owner].set(jnp.arange(UNITS, dtype=jnp.int32))
    )
    my_unit = lax.dynamic_slice_in_dim(unit_of_slot, me * slot_dev, slot_dev)
    low_slots = master.astype(jnp.bfloat16)

    spread = lax.all_to_all(low_slots, AXES, split_axis=0, concat_axis=1, tiled=True)
    moved = np.concatenate([dense_units, time_units])
    unit_rows = jnp.take(spread, owner[moved], axis=1)
    time_two = lax.all_gather(
        unit_rows[:, len(dense_units) :].reshape(rows, D), AXES, axis=0, tiled=True
    )
    weights_all = [
        lax.all_gather(
            unit_rows[:, l * DENSE_UNITS : (l + 1) * DENSE_UNITS].reshape(rows, DENSE_COLS),
            AXES,
            axis=0,
            tiled=True,
        )
        for l in range(LAYERS)
    ]

    every_t = lax.all_gather(t_index, AXES, axis=0, tiled=True)
    every_label = lax.all_gather(labels, AXES, axis=0, tiled=True)
    all_images = every_t.shape[0]

    x_start = latents.astype(jnp.float32).reshape(-1, PATCHES, CHANNELS)
    noise_f = noise.astype(jnp.float32).reshape(-1, PATCHES, CHANNELS)
    times = (t_index.astype(jnp.float32) + 0.5) / TSTEPS
    noisy = (1.0 - times)[:, None, None] * x_start + times[:, None, None] * noise_f
    target = noise_f - x_start
    loss_weight = 1.0 + 3.0 * times
    small_low = small.astype(jnp.bfloat16)
    patch_w = small_low[:CHANNELS]
    time_w = small_low[CHANNELS : CHANNELS + FREQ]
    table = small[CHANNELS + FREQ : CHANNELS + FREQ + CLASSES]
    head_w = small_low[CHANNELS + FREQ + CLASSES :]
    noisy_low = noisy.astype(jnp.bfloat16)
    hidden = dot_low("gpc,cd->gpd", noisy_low, patch_w) + positions()

    every_time = (every_t.astype(jnp.float32) + 0.5) / TSTEPS
    weight_total = jnp.sum(1.0 + 3.0 * every_time) * PATCHES
    freq_low = frequencies(every_time).astype(jnp.bfloat16)
    time_pre = jnp.dot(freq_low, time_w, preferred_element_type=jnp.float32)
    time_act = jax.nn.silu(time_pre).astype(jnp.bfloat16)
    cond = jnp.dot(time_act, time_two, preferred_element_type=jnp.float32) + jnp.take(
        table, every_label, axis=0
    )
    cond_act = jax.nn.silu(cond).astype(jnp.bfloat16)

    slot_modul = dot_low("gd,dsc->gsc", cond_act, low_slots)
    slot_modul = lax.all_to_all(slot_modul, AXES, split_axis=0, concat_axis=1, tiled=True)
    modul_all = jnp.take(slot_modul, owner[image_units], axis=1).reshape(images, -1)

    saved_all = []
    for l in range(LAYERS):
        hidden, saved = layer_forward(
            hidden, modul_all[:, l * 6 * D : (l + 1) * 6 * D], weights_all[l]
        )
        saved_all.append(saved)
    shift_f, scale_f = jnp.split(modul_all[:, LAYERS * 6 * D :], 2, -1)
    normed_f = norm_rows(hidden)
    final_in = modulate(normed_f, shift_f, scale_f).astype(jnp.bfloat16)
    predict = dot_low("gpd,cd->gpc", final_in, head_w)
    error = predict - target
    loss_part = jnp.sum(loss_weight[:, None, None] * error * error) / CHANNELS
    grad_pred = (loss_weight[:, None, None] * 2.0 * error / CHANNELS).astype(jnp.bfloat16)
    grad_head = dot_low("gpc,gpd->cd", grad_pred, final_in)
    grad_final_in = dot_low("gpc,cd->gpd", grad_pred, head_w)
    grad_modul_f = jnp.concatenate(
        [jnp.sum(grad_final_in, 1), jnp.sum(grad_final_in * normed_f, 1)], -1
    ).astype(jnp.bfloat16)
    grad_hidden = local_back(norm_rows, hidden, grad_final_in * (1.0 + scale_f[:, None, :]))
    grad_rows = [None] * LAYERS
    grad_moduls = [None] * LAYERS
    for l in reversed(range(LAYERS)):
        grad_hidden, grad_moduls[l], weight_grad = layer_backward(
            grad_hidden, weights_all[l], saved_all[l]
        )
        grad_rows[l] = lax.psum_scatter(
            weight_grad.astype(jnp.bfloat16), AXES, scatter_dimension=0, tiled=True
        )
    grad_embed = grad_hidden.astype(jnp.bfloat16)
    grad_patch = dot_low("gpc,gpd->cd", noisy_low, grad_embed)

    every_modul = lax.all_gather(
        jnp.concatenate(grad_moduls + [grad_modul_f], -1), AXES, axis=0, tiled=True
    ).reshape(all_images, len(image_units), BLOCK)
    image_place = np.full((UNITS + 1,), -1, np.int32)
    image_place[image_units] = np.arange(len(image_units))
    my_place = jnp.asarray(image_place)[my_unit]
    slot_grad_out = jnp.where(
        (my_place >= 0)[None, :, None],
        jnp.take(every_modul, jnp.maximum(my_place, 0), axis=1),
        jnp.zeros((), jnp.bfloat16),
    )
    cond_part = dot_low("gsc,dsc->gd", slot_grad_out, low_slots)
    small_part = jnp.concatenate([cond_part, grad_patch, grad_head], 0)
    small_sum, loss_sum = lax.psum((small_part, loss_part), AXES)
    grad_cond_act = small_sum[:all_images]
    grad_patch = small_sum[all_images : all_images + CHANNELS]
    grad_head = small_sum[all_images + CHANNELS :]
    grad_cond = local_back(jax.nn.silu, cond, grad_cond_act)
    grad_time_out = grad_cond.astype(jnp.bfloat16)
    grad_time_act = dot_low("ge,de->gd", grad_time_out, time_two)
    grad_time_pre = local_back(jax.nn.silu, time_pre, grad_time_act).astype(jnp.bfloat16)
    grad_time_w = dot_low("gf,gd->fd", freq_low, grad_time_pre)
    grad_table = jnp.zeros((CLASSES, D), jnp.float32).at[every_label].add(grad_cond)
    small_grad = jnp.concatenate([grad_patch, grad_time_w, grad_table, grad_head], 0)

    my_time = jnp.clip(my_unit - TAIL_FIRST, 0, TIME_UNITS - 1)
    is_time = (my_unit >= TAIL_FIRST) & (my_unit < TAIL_FIRST + TIME_UNITS)
    time_cols = jnp.take(grad_time_out.reshape(all_images, TIME_UNITS, BLOCK), my_time, axis=1)
    is_image = my_place >= 0
    image_grad = dot_low("gd,gsc->dsc", cond_act, slot_grad_out)
    time_grad = dot_low("gd,gsc->dsc", time_act, time_cols)

    dense_place = np.full((UNITS + 1,), 0, np.int32)
    dense_place[dense_units] = np.arange(len(dense_units))
    slot_place = jnp.asarray(dense_place)[unit_of_slot]
    all_rows = jnp.concatenate(
        [rows_l.reshape(rows, DENSE_UNITS, BLOCK) for rows_l in grad_rows], 1
    )
    slot_rows = jnp.take(all_rows, slot_place, axis=1)
    dense_grad = lax.all_to_all(
        slot_rows, AXES, split_axis=1, concat_axis=0, tiled=True
    ).astype(jnp.float32)

    owned_grad = jnp.where(
        is_image[None, :, None],
        image_grad,
        jnp.where(is_time[None, :, None], time_grad, dense_grad),
    )
    used = (my_unit >= 0)[None, :, None]
    rate = rate_factor * unit_scale(jnp.maximum(my_unit, 0))[None, :, None]
    new_w, new_first, new_second = adam_update(
        master, first_moment, second_moment, owned_grad, rate
    )
    new_master = jnp.where(used, new_w, master)
    new_first = jnp.where(used, new_first, first_moment)
    new_second = jnp.where(used, new_second, second_moment)
    small_rate = rate_factor * table_scale(jnp.arange(small.shape[0], dtype=jnp.int32))[:, None]
    new_small, new_small_first, new_small_second = adam_update(
        small, small_first, small_second, small_grad, small_rate
    )
    return (
        loss_sum,
        weight_total,
        new_master,
        new_first,
        new_second,
        new_small,
        new_small_first,
        new_small_second,
    )


def solution(mesh):
    return jax.shard_map(
        on_device,
        mesh=mesh,
        in_specs=(
            P(("rep", "shard"), None),
            P(("rep", "shard"), None),
            P(("rep", "shard")),
            P(("rep", "shard")),
            P(),
            P(None, ("rep", "shard"), None),
            P(None, ("rep", "shard"), None),
            P(None, ("rep", "shard"), None),
            P(),
            P(),
            P(),
        ),
        out_specs=(
            P(),
            P(),
            P(None, ("rep", "shard"), None),
            P(None, ("rep", "shard"), None),
            P(None, ("rep", "shard"), None),
            P(),
            P(),
            P(),
        ),
        check_vma=False,
    )
```

```python
import jax
import jax.numpy as jnp
import numpy as np
from jax import lax
from jax.experimental import pallas as pl
from jax.experimental.pallas import tpu as pltpu
from jax.sharding import PartitionSpec as P

D = 768
HEADS = 12
HEAD_DIM = 64
FF = 3072
FREQ = 256
CLASSES = 1000
CHANNELS = 16
GRID = 16
PATCHES = 256
LAYERS = 2
TSTEPS = 1000
STEP = 10
BLOCK = 128
LAYER_COLS = 13824
LAYER_UNITS = 108
UNITS = 234

ADA_UNITS = 6 * D // BLOCK
DENSE_UNITS = LAYER_UNITS - ADA_UNITS
DENSE_COLS = DENSE_UNITS * BLOCK
TIME_UNITS = D // BLOCK
TAIL_FIRST = LAYERS * LAYER_UNITS
AXES = ("rep", "shard")


beta_one = 0.5
beta_two = 0.5
adam_eps = 1e-08
decay_rate = 0.1
rate_factor = 0.5


def gelu_tanh(values):
    return jax.nn.gelu(values, approximate=True)


def norm_rows(hidden):
    centered = hidden - jnp.mean(hidden, -1, keepdims=True)
    return centered * lax.rsqrt(jnp.mean(centered * centered, -1, keepdims=True) + 1e-06)


def local_back(function, primal, upstream):
    return jax.vjp(function, primal)[1](upstream)[0]


def dot_low(pattern, left_side, right_side):
    return jnp.einsum(pattern, left_side, right_side, preferred_element_type=jnp.float32)


def positions():
    quarter = D // 4
    angular = jnp.exp(-jnp.log(10000.0) * jnp.arange(quarter, dtype=jnp.float32) / quarter)
    patch_idx = jnp.arange(PATCHES, dtype=jnp.int32)
    row_pos = (patch_idx // GRID).astype(jnp.float32)[:, None] * angular
    col_pos = (patch_idx % GRID).astype(jnp.float32)[:, None] * angular
    return jnp.concatenate(
        [jnp.sin(col_pos), jnp.cos(col_pos), jnp.sin(row_pos), jnp.cos(row_pos)], -1
    )


def frequencies(times):
    half_size = FREQ // 2
    spacing = jnp.exp(-jnp.log(10000.0) * jnp.arange(half_size, dtype=jnp.float32) / half_size)
    angles = 1000.0 * times[:, None] * spacing
    return jnp.concatenate([jnp.cos(angles), jnp.sin(angles)], -1)


def unit_scale(unit_ids):
    column = unit_ids % LAYER_UNITS * BLOCK
    in_layer = unit_ids < LAYERS * LAYER_UNITS
    is_output = in_layer & (column >= 9 * D) & (column < 10 * D)
    is_down = in_layer & (column >= 10 * D + FF)
    factor = jnp.where(is_output, 4.0, jnp.where(is_down, 1.5 * (D / FF) ** 0.5, 1.0))
    return factor / D**0.5


def table_scale(row_ids):
    return jnp.where(
        row_ids < CHANNELS,
        CHANNELS ** (-0.5),
        jnp.where(
            row_ids < CHANNELS + FREQ,
            FREQ ** (-0.5),
            jnp.where(row_ids < CHANNELS + FREQ + CLASSES, 0.5, D ** (-0.5)),
        ),
    )


def adam_update(weight, first_mom, second, gradient, rate):
    first_new = beta_one * first_mom + (1.0 - beta_one) * gradient
    second_new = beta_two * second + (1.0 - beta_two) * gradient * gradient
    ratio = (
        first_new
        / (1.0 - beta_one**STEP)
        / (jnp.sqrt(second_new / (1.0 - beta_two**STEP)) + adam_eps)
    )
    return (weight - rate * (ratio + decay_rate * weight), first_new, second_new)


def split_heads(qkv_all):
    groups, length = (qkv_all.shape[0], qkv_all.shape[1])
    return tuple(
        (
            qkv_all[..., part_idx * D : (part_idx + 1) * D].reshape(groups, length, HEADS, HEAD_DIM)
            for part_idx in range(3)
        )
    )


def modulate(normed, shift, scale):
    return normed * (1.0 + scale[:, None, :]) + shift[:, None, :]


def layer_forward(hidden, modul, weights):
    w_qkv, w_out, w_up, w_down = weights
    groups = hidden.shape[0]
    shift_a, scale_a, gate_a, shift_b, scale_b, gate_b = jnp.split(modul, 6, -1)
    attn_in = modulate(norm_rows(hidden), shift_a, scale_a).astype(jnp.bfloat16)
    qkv_all = dot_low("gpd,de->gpe", attn_in, w_qkv).astype(jnp.bfloat16)
    queries, keys_all, values = split_heads(qkv_all)
    scores = dot_low("gqhe,gkhe->ghqk", queries, keys_all) * HEAD_DIM ** (-0.5)
    top_score = jnp.max(scores, -1, keepdims=True)
    log_total = top_score + jnp.log(jnp.sum(jnp.exp(scores - top_score), -1, keepdims=True))
    attn_prob = jnp.exp(scores - log_total).astype(jnp.bfloat16)
    heads_out = (
        dot_low("ghqk,gkhe->gqhe", attn_prob, values).astype(jnp.bfloat16).reshape(groups, -1, D)
    )
    branch_a = dot_low("gpd,de->gpe", heads_out, w_out)
    middle = hidden + gate_a[:, None, :] * branch_a
    mlp_in = modulate(norm_rows(middle), shift_b, scale_b).astype(jnp.bfloat16)
    pre_act = dot_low("gpd,df->gpf", mlp_in, w_up)
    post_act = gelu_tanh(pre_act).astype(jnp.bfloat16)
    branch_b = dot_low("gpf,df->gpd", post_act, w_down)
    output = middle + gate_b[:, None, :] * branch_b
    return (
        output,
        (
            hidden,
            modul,
            attn_in,
            qkv_all,
            log_total,
            heads_out,
            branch_a,
            middle,
            mlp_in,
            pre_act,
            post_act,
            branch_b,
        ),
    )


def layer_backward(grad_out, weights, saved):
    w_qkv, w_out, w_up, w_down = weights
    (
        hidden,
        modul,
        attn_in,
        qkv_all,
        log_total,
        heads_out,
        branch_a,
        middle,
        mlp_in,
        pre_act,
        post_act,
        branch_b,
    ) = saved
    groups = hidden.shape[0]
    shift_a, scale_a, gate_a, shift_b, scale_b, gate_b = jnp.split(modul, 6, -1)
    grad_gate_b = jnp.sum(grad_out * branch_b, 1)
    grad_branch_b = (gate_b[:, None, :] * grad_out).astype(jnp.bfloat16)
    grad_down = row_product(grad_branch_b, post_act)
    grad_post = dot_low("gpd,df->gpf", grad_branch_b, w_down)
    grad_pre = local_back(gelu_tanh, pre_act, grad_post).astype(jnp.bfloat16)
    grad_up = row_product(mlp_in, grad_pre)
    grad_mlp_in = dot_low("gpf,df->gpd", grad_pre, w_up)
    normed_b = norm_rows(middle)
    grad_scale_b = jnp.sum(grad_mlp_in * normed_b, 1)
    grad_shift_b = jnp.sum(grad_mlp_in, 1)
    grad_middle = grad_out + local_back(
        norm_rows, middle, grad_mlp_in * (1.0 + scale_b[:, None, :])
    )
    grad_gate_a = jnp.sum(grad_middle * branch_a, 1)
    grad_branch_a = (gate_a[:, None, :] * grad_middle).astype(jnp.bfloat16)
    grad_out_w = row_product(heads_out, grad_branch_a)
    grad_heads = (
        dot_low("gpe,de->gpd", grad_branch_a, w_out)
        .astype(jnp.bfloat16)
        .reshape(groups, -1, HEADS, HEAD_DIM)
    )
    queries, keys_all, values = split_heads(qkv_all)
    scores = dot_low("gqhe,gkhe->ghqk", queries, keys_all) * HEAD_DIM ** (-0.5)
    attn_prob = jnp.exp(scores - log_total)
    grad_prob = dot_low("gqhe,gkhe->ghqk", grad_heads, values)
    grad_values = dot_low("ghqk,gqhe->gkhe", attn_prob.astype(jnp.bfloat16), grad_heads)
    inner_sum = jnp.sum(attn_prob * grad_prob, -1, keepdims=True)
    grad_scores = (HEAD_DIM ** (-0.5) * attn_prob * (grad_prob - inner_sum)).astype(jnp.bfloat16)
    grad_queries = dot_low("ghqk,gkhe->gqhe", grad_scores, keys_all)
    grad_keys = dot_low("ghqk,gqhe->gkhe", grad_scores, queries)
    grad_qkv = jnp.concatenate(
        [
            grad_queries.reshape(groups, -1, D),
            grad_keys.reshape(groups, -1, D),
            grad_values.reshape(groups, -1, D),
        ],
        -1,
    ).astype(jnp.bfloat16)
    grad_qkv_w = row_product(attn_in, grad_qkv)
    grad_attn_in = dot_low("gpe,de->gpd", grad_qkv, w_qkv)
    normed_a = norm_rows(hidden)
    grad_scale_a = jnp.sum(grad_attn_in * normed_a, 1)
    grad_shift_a = jnp.sum(grad_attn_in, 1)
    grad_in = grad_middle + local_back(
        norm_rows, hidden, grad_attn_in * (1.0 + scale_a[:, None, :])
    )
    grad_modul = jnp.concatenate(
        [grad_shift_a, grad_scale_a, grad_gate_a, grad_shift_b, grad_scale_b, grad_gate_b], -1
    ).astype(jnp.bfloat16)
    return (grad_in, grad_modul, [jnp.concatenate([grad_qkv_w, grad_out_w], 1), grad_up, grad_down])


def swap_bit(values, bit, count):
    return lax.ppermute(values, AXES, [(i, i ^ bit) for i in range(count)])


def gather_small(values, count):
    if count & (count - 1):
        return lax.all_gather(values, AXES, axis=0, tiled=True)
    me = lax.axis_index(AXES)
    bit = 1
    while bit < count:
        other = swap_bit(values, bit, count)
        upper = (me & bit) > 0
        values = jnp.concatenate(
            [jnp.where(upper, other, values), jnp.where(upper, values, other)], 0
        )
        bit *= 2
    return values


def scatter_small(values, count):
    if count & (count - 1):
        return lax.psum_scatter(values, AXES, scatter_dimension=0, tiled=False)
    me = lax.axis_index(AXES)
    bit = count // 2
    while bit:
        half = values.shape[0] // 2
        upper = (me & bit) > 0
        low, high = values[:half], values[half:]
        other = swap_bit(jnp.where(upper, low, high), bit, count)
        values = jnp.where(upper, high, low) + other
        bit //= 2
    return values[0]


MESH = pl.DeviceIdType.MESH
SCATTER_VMEM = 56 * 2**20


def dot_rows(left_side, right_side):
    return lax.dot_general(
        left_side, right_side, (((0,), (0,)), ((), ())), preferred_element_type=jnp.float32
    )


def row_product(left_side, right_side):
    left_side = left_side.reshape(-1, left_side.shape[-1])
    right_side = right_side.reshape(-1, right_side.shape[-1])
    return dot_rows(left_side, right_side).astype(jnp.bfloat16)


def place_of():
    rep = lax.axis_index("rep")
    return rep // 4, (rep // 2) % 2, rep % 2, lax.axis_index("shard")


def rep_of(y, x, c):
    return (y * 2 + x) * 2 + c


def meet(targets):
    barrier = pltpu.get_barrier_semaphore()
    for target in targets:
        pl.semaphore_signal(barrier, inc=1, device_id=target, device_id_type=MESH)
    pl.semaphore_wait(barrier, len(targets))


def neighbours():
    y, x, c, z = place_of()
    to_x = (rep_of(y, 1 - x, c), z)
    to_y = (rep_of(1 - y, x, c), z)
    to_core = (rep_of(y, x, 1 - c), z)
    to_z = [(rep_of(y, x, c), lax.rem(z + step, 4)) for step in (1, 2, 3)]
    return to_x, to_y, to_core, to_z


def gather_kernel(widths, *refs):
    count = len(widths)
    pieces, outs = refs[:count], refs[count : 2 * count]
    own_sem, send_sem, recv_sem = refs[2 * count :]
    y, x, c, z = place_of()
    to_x, to_y, to_core, to_z = neighbours()
    meet([to_x, to_y, to_core] + to_z)

    def remote(k, number, source, dest, target):
        return pltpu.make_async_remote_copy(
            src_ref=source,
            dst_ref=dest,
            send_sem=send_sem.at[k, number],
            recv_sem=recv_sem.at[k, number],
            device_id=target,
            device_id_type=MESH,
        )

    def own_copy(k):
        return pltpu.make_async_copy(pieces[k], outs[k].at[c, y, x, z], own_sem.at[k])

    def line_copies(k, arriving):
        copies = []
        for step in (1, 2, 3):
            at_z = lax.rem(z + 4 - step, 4) if arriving else z
            copies.append(
                remote(k, step - 1, pieces[k], outs[k].at[c, y, x, at_z], to_z[step - 1])
            )
        return copies

    def first_copies(k, arriving):
        half = widths[k] // 2
        left, right = pl.ds(0, half), pl.ds(half, half)
        at_x = 1 - x if arriving else x
        at_y = 1 - y if arriving else y
        a_block = outs[k].at[c, y, at_x, :, :, left]
        b_block = outs[k].at[c, at_y, x, :, :, right]
        return [remote(k, 3, a_block, a_block, to_x), remote(k, 4, b_block, b_block, to_y)]

    def second_copies(k, arriving):
        half = widths[k] // 2
        left, right = pl.ds(0, half), pl.ds(half, half)
        at_x = 1 - x if arriving else x
        at_y = 1 - y if arriving else y
        a_block = outs[k].at[c, at_y, :, :, :, left]
        b_block = outs[k].at[c, :, at_x, :, :, right]
        return [remote(k, 5, a_block, a_block, to_y), remote(k, 6, b_block, b_block, to_x)]

    def core_copies(k, arriving):
        block = outs[k].at[1 - c if arriving else c]
        return [remote(k, 7, block, block, to_core)]

    def start(copies):
        for copy in copies:
            copy.start()

    def arrived(copies):
        for copy in copies:
            copy.wait_recv()

    for k in range(count):
        own_copy(k).start()
    start(line_copies(0, False))
    for t in range(count + 2):
        if t + 1 < count:
            start(line_copies(t + 1, False))
        if t < count:
            own_copy(t).wait()
            arrived(line_copies(t, True))
            start(first_copies(t, False))
        if 0 <= t - 1 < count:
            arrived(first_copies(t - 1, True))
            start(second_copies(t - 1, False))
        if 0 <= t - 2 < count:
            arrived(second_copies(t - 2, True))
            start(core_copies(t - 2, False))
    for k in range(count):
        arrived(core_copies(k, True))
    for k in range(count):
        for copies in (line_copies, first_copies, second_copies, core_copies):
            for copy in copies(k, False):
                copy.wait_send()


def scatter_kernel(widths, *refs):
    count = len(widths)
    grads, outs = refs[:count], refs[count : 2 * count]
    scratch = refs[2 * count :]
    own, core_in, first_in, second_in, line_in = (
        scratch[i * count : (i + 1) * count] for i in range(5)
    )
    own_sem, send_sem, recv_sem = scratch[5 * count :]
    y, x, c, z = place_of()
    to_x, to_y, to_core, to_z = neighbours()
    meet([to_x, to_y, to_core] + to_z)

    def remote(k, number, source, dest, target):
        return pltpu.make_async_remote_copy(
            src_ref=source,
            dst_ref=dest,
            send_sem=send_sem.at[k, number],
            recv_sem=recv_sem.at[k, number],
            device_id=target,
            device_id_type=MESH,
        )

    def own_copy(k):
        return pltpu.make_async_copy(grads[k].at[c], own[k], own_sem.at[k])

    def core_copies(k):
        return [remote(k, 0, grads[k].at[1 - c], core_in[k], to_core)]

    def first_copies(k):
        half = widths[k] // 2
        return [
            remote(k, 1, own[k].at[:, 1 - x, :, :, pl.ds(0, half)], first_in[k].at[0], to_x),
            remote(k, 2, own[k].at[1 - y, :, :, :, pl.ds(half, half)], first_in[k].at[1], to_y),
        ]

    def second_copies(k):
        half = widths[k] // 2
        return [
            remote(k, 3, own[k].at[1 - y, x, :, :, pl.ds(0, half)], second_in[k].at[0], to_y),
            remote(k, 4, own[k].at[y, 1 - x, :, :, pl.ds(half, half)], second_in[k].at[1], to_x),
        ]

    def line_copies(k):
        return [
            remote(
                k,
                4 + step,
                own[k].at[y, x, lax.rem(z + step, 4)],
                line_in[k].at[step - 1],
                to_z[step - 1],
            )
            for step in (1, 2, 3)
        ]

    def start(copies):
        for copy in copies:
            copy.start()

    def arrived(copies):
        for copy in copies:
            copy.wait_recv()

    def core_sum(k):
        @pl.loop(0, 16)
        def _(i):
            at = (i // 8, (i // 4) % 2, i % 4)
            own[k][at] = own[k][at] + core_in[k][at]

    def first_sum(k):
        half = widths[k] // 2

        @pl.loop(0, 8)
        def _(i):
            two, at_z = i // 4, i % 4
            a_at = (two, x, at_z, slice(None), pl.ds(0, half))
            b_at = (y, two, at_z, slice(None), pl.ds(half, half))
            own[k][a_at] = own[k][a_at] + first_in[k][0, two, at_z]
            own[k][b_at] = own[k][b_at] + first_in[k][1, two, at_z]

    def second_sum(k):
        half = widths[k] // 2

        @pl.loop(0, 4)
        def _(at_z):
            a_at = (y, x, at_z, slice(None), pl.ds(0, half))
            b_at = (y, x, at_z, slice(None), pl.ds(half, half))
            own[k][a_at] = own[k][a_at] + second_in[k][0, at_z]
            own[k][b_at] = own[k][b_at] + second_in[k][1, at_z]

    for k in range(count):
        start(core_copies(k))
        own_copy(k).start()
    for t in range(count + 3):
        if t < count:
            own_copy(t).wait()
            arrived(core_copies(t))
            core_sum(t)
            start(first_copies(t))
        if 0 <= t - 1 < count:
            arrived(first_copies(t - 1))
            first_sum(t - 1)
            start(second_copies(t - 1))
        if 0 <= t - 2 < count:
            arrived(second_copies(t - 2))
            second_sum(t - 2)
            start(line_copies(t - 2))
        if 0 <= t - 3 < count:
            k = t - 3
            arrived(line_copies(k))
            total = own[k][y, x, z].astype(jnp.float32)
            for step in (1, 2, 3):
                total = total + line_in[k][step - 1].astype(jnp.float32)
            outs[k][...] = total.astype(jnp.bfloat16)
    for k in range(count):
        for copies in (core_copies, first_copies, second_copies, line_copies):
            for copy in copies(k):
                copy.wait_send()


def share_kernel(finish, parts, extra, out, landed, send_sem, recv_sem):
    devices = parts.shape[0]
    shards = lax.axis_size("shard")
    me = lax.axis_index("rep") * shards + lax.axis_index("shard")

    def target(j):
        peer = lax.rem(me + j, devices)
        return peer, (peer // shards, lax.rem(peer, shards))

    barrier = pltpu.get_barrier_semaphore()

    @pl.loop(1, devices)
    def _(j):
        pl.semaphore_signal(barrier, inc=1, device_id=target(j)[1], device_id_type=MESH)

    pl.semaphore_wait(barrier, devices - 1)

    def copy_part(j):
        peer, where = target(j)
        return pltpu.make_async_remote_copy(
            src_ref=parts.at[peer],
            dst_ref=landed.at[j],
            send_sem=send_sem.at[0, j],
            recv_sem=recv_sem.at[0, j],
            device_id=where,
            device_id_type=MESH,
        )

    def copy_sum(j, arriving):
        owner = lax.rem(me + devices - j, devices) if arriving else me
        return pltpu.make_async_remote_copy(
            src_ref=out.at[owner],
            dst_ref=out.at[owner],
            send_sem=send_sem.at[1, j],
            recv_sem=recv_sem.at[1, j],
            device_id=target(j)[1],
            device_id_type=MESH,
        )

    @pl.loop(1, devices)
    def _(j):
        copy_part(j).start()

    landed[0] = parts[me]

    @pl.loop(1, devices)
    def _(j):
        copy_part(j).wait_recv()

    out[me] = finish(jnp.sum(landed[...], 0), extra[...])

    @pl.loop(1, devices)
    def _(j):
        copy_sum(j, False).start()

    @pl.loop(1, devices)
    def _(j):
        copy_sum(j, True).wait_recv()

    @pl.loop(1, devices)
    def _(j):
        copy_part(j).wait_send()
        copy_sum(j, False).wait_send()


def share(finish, parts, extra, number):
    devices = parts.shape[0]
    return pl.pallas_call(
        lambda *refs: share_kernel(finish, *refs),
        out_shape=jax.ShapeDtypeStruct(parts.shape, jnp.float32),
        in_specs=[pl.BlockSpec(memory_space=pltpu.VMEM)] * 2,
        out_specs=pl.BlockSpec(memory_space=pltpu.VMEM),
        scratch_shapes=[
            pltpu.VMEM(parts.shape, jnp.float32),
            pltpu.SemaphoreType.DMA((2, devices)),
            pltpu.SemaphoreType.DMA((2, devices)),
        ],
        compiler_params=pltpu.CompilerParams(collective_id=number, has_side_effects=True),
        cost_estimate=pl.CostEstimate(flops=0, bytes_accessed=20_000_000, transcendentals=0),
    )(parts, extra)


class RingPlan:
    def order_rows(self, values):
        shape = values.shape
        split = values.reshape((2, 2, 2, 4, D // 32) + shape[1:])
        return jnp.moveaxis(split, 0, 2).reshape(shape)

    def restore_rows(self, values):
        shape = values.shape
        split = values.reshape((2, 2, 2, 4, D // 32) + shape[1:])
        return jnp.moveaxis(split, 2, 0).reshape(shape)

    def gather(self, pieces):
        widths = tuple(piece.shape[1] for piece in pieces)
        count, rows = len(pieces), D // 32
        size = sum(4 * D * width for width in widths)
        whole = pl.pallas_call(
            lambda *refs: gather_kernel(widths, *refs),
            out_shape=[
                jax.ShapeDtypeStruct((2, 2, 2, 4, rows, width), jnp.bfloat16) for width in widths
            ],
            in_specs=[pl.BlockSpec(memory_space=pltpu.VMEM)] * count,
            out_specs=[pl.BlockSpec(memory_space=pl.ANY)] * count,
            scratch_shapes=[
                pltpu.SemaphoreType.DMA((count,)),
                pltpu.SemaphoreType.DMA((count, 8)),
                pltpu.SemaphoreType.DMA((count, 8)),
            ],
            compiler_params=pltpu.CompilerParams(collective_id=0, has_side_effects=True),
            cost_estimate=pl.CostEstimate(flops=0, bytes_accessed=size, transcendentals=0),
        )(*pieces)
        return [part.reshape(D, -1) for part in whole]

    def scatter(self, grads):
        widths = tuple(grad.shape[1] for grad in grads)
        count, rows = len(grads), D // 32
        size = sum(4 * D * width for width in widths)
        scratch = [pltpu.VMEM((2, 2, 4, rows, width), jnp.bfloat16) for width in widths] * 2
        scratch += [pltpu.VMEM((2, 2, 4, rows, width // 2), jnp.bfloat16) for width in widths]
        scratch += [pltpu.VMEM((2, 4, rows, width // 2), jnp.bfloat16) for width in widths]
        scratch += [pltpu.VMEM((3, rows, width), jnp.bfloat16) for width in widths]
        return pl.pallas_call(
            lambda *refs: scatter_kernel(widths, *refs),
            out_shape=[jax.ShapeDtypeStruct((rows, width), jnp.bfloat16) for width in widths],
            in_specs=[pl.BlockSpec(memory_space=pl.ANY)] * count,
            out_specs=[pl.BlockSpec(memory_space=pltpu.VMEM)] * count,
            scratch_shapes=scratch
            + [
                pltpu.SemaphoreType.DMA((count,)),
                pltpu.SemaphoreType.DMA((count, 8)),
                pltpu.SemaphoreType.DMA((count, 8)),
            ],
            compiler_params=pltpu.CompilerParams(
                collective_id=1, has_side_effects=True, vmem_limit_bytes=SCATTER_VMEM
            ),
            cost_estimate=pl.CostEstimate(flops=0, bytes_accessed=size, transcendentals=0),
        )(*[grad.reshape(2, 2, 2, 4, rows, -1) for grad in grads])

    def share(self, finish, parts, extra, number):
        return share(finish, parts, extra, number)


class PlainPlan:
    def order_rows(self, values):
        return values

    def restore_rows(self, values):
        return values

    def gather(self, pieces):
        return [lax.all_gather(piece, AXES, axis=0, tiled=True) for piece in pieces]

    def scatter(self, grads):
        return [
            lax.psum_scatter(grad, AXES, scatter_dimension=0, tiled=True) for grad in grads
        ]

    def share(self, finish, parts, extra, number):
        own = finish(scatter_small(parts, parts.shape[0]), extra)
        return gather_small(own[None], parts.shape[0])


def unit_lists():
    dense = np.concatenate(
        [np.arange(l * LAYER_UNITS + ADA_UNITS, (l + 1) * LAYER_UNITS) for l in range(LAYERS)]
    )
    time_units = np.arange(TAIL_FIRST, TAIL_FIRST + TIME_UNITS)
    image_units = np.concatenate(
        [np.arange(l * LAYER_UNITS, l * LAYER_UNITS + ADA_UNITS) for l in range(LAYERS)]
        + [np.arange(TAIL_FIRST + TIME_UNITS, UNITS)]
    )
    return dense, time_units, image_units


def on_device(
    latents,
    noise,
    labels,
    t_index,
    owner,
    master,
    first_moment,
    second_moment,
    small,
    small_first,
    small_second,
):
    count = lax.axis_size("rep") * lax.axis_size("shard")
    me = lax.axis_index(AXES)
    slot_dev = master.shape[1]
    slot_total = count * slot_dev
    rows = D // count
    images = latents.shape[0]
    dense_units, time_units, image_units = unit_lists()

    unit_of_slot = (
        jnp.full((slot_total,), -1, jnp.int32).at[owner].set(jnp.arange(UNITS, dtype=jnp.int32))
    )
    my_unit = lax.dynamic_slice_in_dim(unit_of_slot, me * slot_dev, slot_dev)
    low_slots = master.astype(jnp.bfloat16)

    plan = RingPlan() if (lax.axis_size("rep"), lax.axis_size("shard")) == (8, 4) else PlainPlan()
    every_int = gather_small(jnp.stack([t_index, labels], 1), count)
    every_t, every_label = every_int[:, 0], every_int[:, 1]
    all_images = every_t.shape[0]

    spread = lax.all_to_all(
        plan.order_rows(low_slots), AXES, split_axis=0, concat_axis=1, tiled=True
    )
    moved = np.concatenate([dense_units, time_units])
    unit_rows = jnp.take(spread, owner[moved], axis=1).reshape(rows, -1)
    pieces = []
    for l in range(LAYERS):
        base = l * DENSE_COLS
        cuts = (base, base + 4 * D, base + 4 * D + FF, base + DENSE_COLS)
        pieces += [unit_rows[:, cuts[i] : cuts[i + 1]] for i in range(3)]
    whole = plan.gather(pieces)
    weights_all = [
        (whole[3 * l][:, : 3 * D], whole[3 * l][:, 3 * D :], whole[3 * l + 1], whole[3 * l + 2])
        for l in range(LAYERS)
    ]
    time_two = plan.restore_rows(gather_small(unit_rows[:, LAYERS * DENSE_COLS :], count))

    x_start = latents.astype(jnp.float32).reshape(-1, PATCHES, CHANNELS)
    noise_f = noise.astype(jnp.float32).reshape(-1, PATCHES, CHANNELS)
    times = (t_index.astype(jnp.float32) + 0.5) / TSTEPS
    noisy = (1.0 - times)[:, None, None] * x_start + times[:, None, None] * noise_f
    target = noise_f - x_start
    loss_weight = 1.0 + 3.0 * times
    small_low = small.astype(jnp.bfloat16)
    patch_w = small_low[:CHANNELS]
    time_w = small_low[CHANNELS : CHANNELS + FREQ]
    table = small[CHANNELS + FREQ : CHANNELS + FREQ + CLASSES]
    head_w = small_low[CHANNELS + FREQ + CLASSES :]
    noisy_low = noisy.astype(jnp.bfloat16)
    hidden = dot_low("gpc,cd->gpd", noisy_low, patch_w) + positions()

    every_time = (every_t.astype(jnp.float32) + 0.5) / TSTEPS
    weight_total = jnp.sum(1.0 + 3.0 * every_time) * PATCHES
    freq_low = frequencies(every_time).astype(jnp.bfloat16)
    time_pre = jnp.dot(freq_low, time_w, preferred_element_type=jnp.float32)
    time_act = jax.nn.silu(time_pre).astype(jnp.bfloat16)
    slot_cond = dot_low("gd,dsc->gsc", time_act, low_slots)
    time_place = owner[time_units] - me * slot_dev
    is_here = (time_place >= 0) & (time_place < slot_dev)
    cond_part = jnp.where(
        is_here[None, :, None],
        jnp.take(slot_cond, jnp.clip(time_place, 0, slot_dev - 1), axis=1),
        0.0,
    ).reshape(count, images, D)
    cond_all = plan.share(lambda a, b: a + b, cond_part, jnp.take(table, labels, axis=0), 2)
    cond = lax.dynamic_index_in_dim(cond_all, me, 0, False)
    cond_act = jax.nn.silu(cond_all.reshape(all_images, D)).astype(jnp.bfloat16)

    slot_modul = dot_low("gd,dsc->gsc", cond_act, low_slots)
    slot_modul = lax.all_to_all(slot_modul, AXES, split_axis=0, concat_axis=1, tiled=True)
    modul_all = jnp.take(slot_modul, owner[image_units], axis=1).reshape(images, -1)

    saved_all = []
    for l in range(LAYERS):
        hidden, saved = layer_forward(
            hidden, modul_all[:, l * 6 * D : (l + 1) * 6 * D], weights_all[l]
        )
        saved_all.append(saved)
    shift_f, scale_f = jnp.split(modul_all[:, LAYERS * 6 * D :], 2, -1)
    normed_f = norm_rows(hidden)
    final_in = modulate(normed_f, shift_f, scale_f).astype(jnp.bfloat16)
    predict = dot_low("gpd,cd->gpc", final_in, head_w)
    error = predict - target
    loss_part = jnp.sum(loss_weight[:, None, None] * error * error) / CHANNELS
    grad_pred = (loss_weight[:, None, None] * 2.0 * error / CHANNELS).astype(jnp.bfloat16)
    grad_head = dot_low("gpc,gpd->cd", grad_pred, final_in)
    grad_final_in = dot_low("gpc,cd->gpd", grad_pred, head_w)
    grad_modul_f = jnp.concatenate(
        [jnp.sum(grad_final_in, 1), jnp.sum(grad_final_in * normed_f, 1)], -1
    ).astype(jnp.bfloat16)
    grad_hidden = local_back(norm_rows, hidden, grad_final_in * (1.0 + scale_f[:, None, :]))
    layer_grads = [None] * LAYERS
    grad_moduls = [None] * LAYERS
    for l in reversed(range(LAYERS)):
        grad_hidden, grad_moduls[l], layer_grads[l] = layer_backward(
            grad_hidden, weights_all[l], saved_all[l]
        )
    order = list(reversed(range(LAYERS)))
    scattered = plan.scatter([grad for l in order for grad in reversed(layer_grads[l])])
    grad_rows = {
        (l, 2 - i): scattered[3 * n + i] for n, l in enumerate(order) for i in range(3)
    }
    grad_embed = grad_hidden.astype(jnp.bfloat16)
    grad_patch = dot_low("gpc,gpd->cd", noisy_low, grad_embed)

    every_modul = gather_small(
        jnp.concatenate(grad_moduls + [grad_modul_f], -1), count
    ).reshape(all_images, len(image_units), BLOCK)
    image_place = np.full((UNITS + 1,), -1, np.int32)
    image_place[image_units] = np.arange(len(image_units))
    my_place = jnp.asarray(image_place)[my_unit]
    slot_grad_out = jnp.where(
        (my_place >= 0)[None, :, None],
        jnp.take(every_modul, jnp.maximum(my_place, 0), axis=1),
        jnp.zeros((), jnp.bfloat16),
    )
    cond_part = dot_low("gsc,dsc->gd", slot_grad_out, low_slots)
    edge_rows = max(1, 2 * CHANNELS // count)
    edge = jnp.concatenate([grad_patch, grad_head], 0)
    edge = jnp.concatenate(
        [edge, jnp.zeros((edge_rows * count - 2 * CHANNELS, D), jnp.float32)], 0
    )
    small_part = jnp.concatenate(
        [
            cond_part.reshape(count, images, D),
            edge.reshape(count, edge_rows, D),
            jnp.broadcast_to(loss_part, (count, 1, D)),
        ],
        1,
    )
    factor = local_back(jax.nn.silu, cond, jnp.ones_like(cond))
    factor = jnp.concatenate([factor, jnp.ones((edge_rows + 1, D), jnp.float32)], 0)
    small_sum = plan.share(lambda a, b: a * b, small_part, factor, 3)
    grad_cond = small_sum[:, :images].reshape(all_images, D)
    edge = small_sum[:, images : images + edge_rows].reshape(-1, D)
    grad_patch, grad_head = edge[:CHANNELS], edge[CHANNELS : 2 * CHANNELS]
    loss_sum = small_sum[0, images + edge_rows, 0]
    grad_time_out = grad_cond.astype(jnp.bfloat16)
    grad_time_act = dot_low("ge,de->gd", grad_time_out, time_two)
    grad_time_pre = local_back(jax.nn.silu, time_pre, grad_time_act).astype(jnp.bfloat16)
    grad_time_w = dot_low("gf,gd->fd", freq_low, grad_time_pre)
    grad_table = jnp.zeros((CLASSES, D), jnp.float32).at[every_label].add(grad_cond)
    small_grad = jnp.concatenate([grad_patch, grad_time_w, grad_table, grad_head], 0)

    my_time = jnp.clip(my_unit - TAIL_FIRST, 0, TIME_UNITS - 1)
    is_time = (my_unit >= TAIL_FIRST) & (my_unit < TAIL_FIRST + TIME_UNITS)
    time_cols = jnp.take(grad_time_out.reshape(all_images, TIME_UNITS, BLOCK), my_time, axis=1)
    is_image = my_place >= 0
    image_grad = dot_low("gd,gsc->dsc", cond_act, slot_grad_out)
    time_grad = dot_low("gd,gsc->dsc", time_act, time_cols)

    dense_place = np.full((UNITS + 1,), 0, np.int32)
    dense_place[dense_units] = np.arange(len(dense_units))
    slot_place = jnp.asarray(dense_place)[unit_of_slot]
    all_rows = jnp.concatenate(
        [
            grad_rows[l, i].reshape(rows, -1, BLOCK)
            for l in range(LAYERS)
            for i in range(3)
        ],
        1,
    )
    slot_rows = jnp.take(all_rows, slot_place, axis=1)
    dense_grad = plan.restore_rows(
        lax.all_to_all(slot_rows, AXES, split_axis=1, concat_axis=0, tiled=True)
    ).astype(jnp.float32)

    owned_grad = jnp.where(
        is_image[None, :, None],
        image_grad,
        jnp.where(is_time[None, :, None], time_grad, dense_grad),
    )
    used = (my_unit >= 0)[None, :, None]
    rate = rate_factor * unit_scale(jnp.maximum(my_unit, 0))[None, :, None]
    new_w, new_first, new_second = adam_update(
        master, first_moment, second_moment, owned_grad, rate
    )
    new_master = jnp.where(used, new_w, master)
    new_first = jnp.where(used, new_first, first_moment)
    new_second = jnp.where(used, new_second, second_moment)
    small_rate = rate_factor * table_scale(jnp.arange(small.shape[0], dtype=jnp.int32))[:, None]
    new_small, new_small_first, new_small_second = adam_update(
        small, small_first, small_second, small_grad, small_rate
    )
    return (
        loss_sum,
        weight_total,
        new_master,
        new_first,
        new_second,
        new_small,
        new_small_first,
        new_small_second,
    )


def solution(mesh):
    return jax.shard_map(
        on_device,
        mesh=mesh,
        in_specs=(
            P(("rep", "shard"), None),
            P(("rep", "shard"), None),
            P(("rep", "shard")),
            P(("rep", "shard")),
            P(),
            P(None, ("rep", "shard"), None),
            P(None, ("rep", "shard"), None),
            P(None, ("rep", "shard"), None),
            P(),
            P(),
            P(),
        ),
        out_specs=(
            P(),
            P(),
            P(None, ("rep", "shard"), None),
            P(None, ("rep", "shard"), None),
            P(None, ("rep", "shard"), None),
            P(),
            P(),
            P(),
        ),
        check_vma=False,
    )
```

```python
import jax
import jax.numpy as jnp
import numpy as np
from jax import lax
from jax.experimental import pallas as pl
from jax.experimental.pallas import tpu as pltpu
from jax.sharding import PartitionSpec as P

D = 768
HEADS = 12
HEAD_DIM = 64
FF = 3072
FREQ = 256
CLASSES = 1000
CHANNELS = 16
GRID = 16
PATCHES = 256
LAYERS = 2
TSTEPS = 1000
STEP = 10
BLOCK = 128
LAYER_COLS = 13824
LAYER_UNITS = 108
UNITS = 234

ADA_UNITS = 6 * D // BLOCK
DENSE_UNITS = LAYER_UNITS - ADA_UNITS
DENSE_COLS = DENSE_UNITS * BLOCK
TIME_UNITS = D // BLOCK
TAIL_FIRST = LAYERS * LAYER_UNITS
AXES = ("rep", "shard")


beta_one = 0.5
beta_two = 0.5
adam_eps = 1e-08
decay_rate = 0.1
rate_factor = 0.5


def gelu_tanh(values):
    return jax.nn.gelu(values, approximate=True)


def norm_rows(hidden):
    centered = hidden - jnp.mean(hidden, -1, keepdims=True)
    return centered * lax.rsqrt(jnp.mean(centered * centered, -1, keepdims=True) + 1e-06)


def local_back(function, primal, upstream):
    return jax.vjp(function, primal)[1](upstream)[0]


def dot_low(pattern, left_side, right_side):
    return jnp.einsum(pattern, left_side, right_side, preferred_element_type=jnp.float32)


def positions():
    quarter = D // 4
    angular = jnp.exp(-jnp.log(10000.0) * jnp.arange(quarter, dtype=jnp.float32) / quarter)
    patch_idx = jnp.arange(PATCHES, dtype=jnp.int32)
    row_pos = (patch_idx // GRID).astype(jnp.float32)[:, None] * angular
    col_pos = (patch_idx % GRID).astype(jnp.float32)[:, None] * angular
    return jnp.concatenate(
        [jnp.sin(col_pos), jnp.cos(col_pos), jnp.sin(row_pos), jnp.cos(row_pos)], -1
    )


def frequencies(times):
    half_size = FREQ // 2
    spacing = jnp.exp(-jnp.log(10000.0) * jnp.arange(half_size, dtype=jnp.float32) / half_size)
    angles = 1000.0 * times[:, None] * spacing
    return jnp.concatenate([jnp.cos(angles), jnp.sin(angles)], -1)


def unit_scale(unit_ids):
    column = unit_ids % LAYER_UNITS * BLOCK
    in_layer = unit_ids < LAYERS * LAYER_UNITS
    is_output = in_layer & (column >= 9 * D) & (column < 10 * D)
    is_down = in_layer & (column >= 10 * D + FF)
    factor = jnp.where(is_output, 4.0, jnp.where(is_down, 1.5 * (D / FF) ** 0.5, 1.0))
    return factor / D**0.5


def table_scale(row_ids):
    return jnp.where(
        row_ids < CHANNELS,
        CHANNELS ** (-0.5),
        jnp.where(
            row_ids < CHANNELS + FREQ,
            FREQ ** (-0.5),
            jnp.where(row_ids < CHANNELS + FREQ + CLASSES, 0.5, D ** (-0.5)),
        ),
    )


def adam_update(weight, first_mom, second, gradient, rate):
    first_new = beta_one * first_mom + (1.0 - beta_one) * gradient
    second_new = beta_two * second + (1.0 - beta_two) * gradient * gradient
    ratio = (
        first_new
        / (1.0 - beta_one**STEP)
        / (jnp.sqrt(second_new / (1.0 - beta_two**STEP)) + adam_eps)
    )
    return (weight - rate * (ratio + decay_rate * weight), first_new, second_new)


def split_heads(qkv_all):
    groups, length = (qkv_all.shape[0], qkv_all.shape[1])
    return tuple(
        (
            qkv_all[..., part_idx * D : (part_idx + 1) * D].reshape(groups, length, HEADS, HEAD_DIM)
            for part_idx in range(3)
        )
    )


def modulate(normed, shift, scale):
    return normed * (1.0 + scale[:, None, :]) + shift[:, None, :]


def layer_forward(hidden, modul, weights):
    w_qkv, w_out, w_up, w_down = weights
    groups = hidden.shape[0]
    shift_a, scale_a, gate_a, shift_b, scale_b, gate_b = jnp.split(modul, 6, -1)
    attn_in = modulate(norm_rows(hidden), shift_a, scale_a).astype(jnp.bfloat16)
    qkv_all = dot_low("gpd,de->gpe", attn_in, w_qkv).astype(jnp.bfloat16)
    queries, keys_all, values = split_heads(qkv_all)
    scores = dot_low("gqhe,gkhe->ghqk", queries, keys_all) * HEAD_DIM ** (-0.5)
    top_score = jnp.max(scores, -1, keepdims=True)
    log_total = top_score + jnp.log(jnp.sum(jnp.exp(scores - top_score), -1, keepdims=True))
    attn_prob = jnp.exp(scores - log_total).astype(jnp.bfloat16)
    heads_out = (
        dot_low("ghqk,gkhe->gqhe", attn_prob, values).astype(jnp.bfloat16).reshape(groups, -1, D)
    )
    branch_a = dot_low("gpd,de->gpe", heads_out, w_out)
    middle = hidden + gate_a[:, None, :] * branch_a
    mlp_in = modulate(norm_rows(middle), shift_b, scale_b).astype(jnp.bfloat16)
    pre_act = dot_low("gpd,df->gpf", mlp_in, w_up)
    post_act = gelu_tanh(pre_act).astype(jnp.bfloat16)
    branch_b = dot_low("gpf,df->gpd", post_act, w_down)
    output = middle + gate_b[:, None, :] * branch_b
    return (
        output,
        (
            hidden,
            modul,
            attn_in,
            qkv_all,
            log_total,
            heads_out,
            branch_a,
            middle,
            mlp_in,
            pre_act,
            post_act,
            branch_b,
        ),
    )


def layer_backward(grad_out, weights, saved):
    w_qkv, w_out, w_up, w_down = weights
    (
        hidden,
        modul,
        attn_in,
        qkv_all,
        log_total,
        heads_out,
        branch_a,
        middle,
        mlp_in,
        pre_act,
        post_act,
        branch_b,
    ) = saved
    groups = hidden.shape[0]
    shift_a, scale_a, gate_a, shift_b, scale_b, gate_b = jnp.split(modul, 6, -1)
    grad_gate_b = jnp.sum(grad_out * branch_b, 1)
    grad_branch_b = (gate_b[:, None, :] * grad_out).astype(jnp.bfloat16)
    grad_down = row_product(grad_branch_b, post_act)
    grad_post = dot_low("gpd,df->gpf", grad_branch_b, w_down)
    grad_pre = local_back(gelu_tanh, pre_act, grad_post).astype(jnp.bfloat16)
    grad_up = row_product(mlp_in, grad_pre)
    grad_mlp_in = dot_low("gpf,df->gpd", grad_pre, w_up)
    normed_b = norm_rows(middle)
    grad_scale_b = jnp.sum(grad_mlp_in * normed_b, 1)
    grad_shift_b = jnp.sum(grad_mlp_in, 1)
    grad_middle = grad_out + local_back(
        norm_rows, middle, grad_mlp_in * (1.0 + scale_b[:, None, :])
    )
    grad_gate_a = jnp.sum(grad_middle * branch_a, 1)
    grad_branch_a = (gate_a[:, None, :] * grad_middle).astype(jnp.bfloat16)
    grad_out_w = row_product(heads_out, grad_branch_a)
    grad_heads = (
        dot_low("gpe,de->gpd", grad_branch_a, w_out)
        .astype(jnp.bfloat16)
        .reshape(groups, -1, HEADS, HEAD_DIM)
    )
    queries, keys_all, values = split_heads(qkv_all)
    scores = dot_low("gqhe,gkhe->ghqk", queries, keys_all) * HEAD_DIM ** (-0.5)
    attn_prob = jnp.exp(scores - log_total)
    grad_prob = dot_low("gqhe,gkhe->ghqk", grad_heads, values)
    grad_values = dot_low("ghqk,gqhe->gkhe", attn_prob.astype(jnp.bfloat16), grad_heads)
    inner_sum = jnp.sum(attn_prob * grad_prob, -1, keepdims=True)
    grad_scores = (HEAD_DIM ** (-0.5) * attn_prob * (grad_prob - inner_sum)).astype(jnp.bfloat16)
    grad_queries = dot_low("ghqk,gkhe->gqhe", grad_scores, keys_all)
    grad_keys = dot_low("ghqk,gqhe->gkhe", grad_scores, queries)
    grad_qkv = jnp.concatenate(
        [
            grad_queries.reshape(groups, -1, D),
            grad_keys.reshape(groups, -1, D),
            grad_values.reshape(groups, -1, D),
        ],
        -1,
    ).astype(jnp.bfloat16)
    grad_qkv_w = row_product(attn_in, grad_qkv)
    grad_attn_in = dot_low("gpe,de->gpd", grad_qkv, w_qkv)
    normed_a = norm_rows(hidden)
    grad_scale_a = jnp.sum(grad_attn_in * normed_a, 1)
    grad_shift_a = jnp.sum(grad_attn_in, 1)
    grad_in = grad_middle + local_back(
        norm_rows, hidden, grad_attn_in * (1.0 + scale_a[:, None, :])
    )
    grad_modul = jnp.concatenate(
        [grad_shift_a, grad_scale_a, grad_gate_a, grad_shift_b, grad_scale_b, grad_gate_b], -1
    ).astype(jnp.bfloat16)
    return (grad_in, grad_modul, [jnp.concatenate([grad_qkv_w, grad_out_w], 1), grad_up, grad_down])


def swap_bit(values, bit, count):
    return lax.ppermute(values, AXES, [(i, i ^ bit) for i in range(count)])


def gather_small(values, count):
    if count & (count - 1):
        return lax.all_gather(values, AXES, axis=0, tiled=True)
    me = lax.axis_index(AXES)
    bit = 1
    while bit < count:
        other = swap_bit(values, bit, count)
        upper = (me & bit) > 0
        values = jnp.concatenate(
            [jnp.where(upper, other, values), jnp.where(upper, values, other)], 0
        )
        bit *= 2
    return values


def scatter_small(values, count):
    if count & (count - 1):
        return lax.psum_scatter(values, AXES, scatter_dimension=0, tiled=False)
    me = lax.axis_index(AXES)
    bit = count // 2
    while bit:
        half = values.shape[0] // 2
        upper = (me & bit) > 0
        low, high = values[:half], values[half:]
        other = swap_bit(jnp.where(upper, low, high), bit, count)
        values = jnp.where(upper, high, low) + other
        bit //= 2
    return values[0]


MESH = pl.DeviceIdType.MESH
GATHER_VMEM = 40 * 2**20
SCATTER_VMEM = 56 * 2**20


def dot_rows(left_side, right_side):
    return lax.dot_general(
        left_side, right_side, (((0,), (0,)), ((), ())), preferred_element_type=jnp.float32
    )


def row_product(left_side, right_side):
    left_side = left_side.reshape(-1, left_side.shape[-1])
    right_side = right_side.reshape(-1, right_side.shape[-1])
    return dot_rows(left_side, right_side).astype(jnp.bfloat16)


def place_of():
    rep = lax.axis_index("rep")
    return rep // 4, (rep // 2) % 2, rep % 2, lax.axis_index("shard")


def rep_of(y, x, c):
    return (y * 2 + x) * 2 + c


def device_at(j):
    shards = lax.axis_size("shard")
    devices = lax.axis_size("rep") * shards
    me = lax.axis_index("rep") * shards + lax.axis_index("shard")
    peer = lax.rem(me + j, devices)
    return peer, (peer // shards, lax.rem(peer, shards))


def meet_all(devices):
    barrier = pltpu.get_barrier_semaphore()

    @pl.loop(1, devices)
    def _(j):
        pl.semaphore_signal(barrier, inc=1, device_id=device_at(j)[1], device_id_type=MESH)

    pl.semaphore_wait(barrier, devices - 1)


def neighbours():
    y, x, c, z = place_of()
    to_x = (rep_of(y, 1 - x, c), z)
    to_y = (rep_of(1 - y, x, c), z)
    to_core = (rep_of(y, x, 1 - c), z)
    to_z = [(rep_of(y, x, c), lax.rem(z + step, 4)) for step in (1, 2, 3)]
    return to_x, to_y, to_core, to_z


def gather_kernel(widths, *refs):
    count = len(widths)
    pieces = refs[:count]
    time_act, label_rows, low_slots = refs[count : count + 3]
    outs = refs[count + 3 : 2 * count + 3]
    cond_out, modul_out = refs[2 * count + 3 : 2 * count + 5]
    time_two, parts, own_sem, send_sem, recv_sem, time_sem, modul_sem = refs[2 * count + 5 :]
    devices, images = modul_out.shape[:2]
    slots = low_slots.shape[0]
    y, x, c, z = place_of()
    to_x, to_y, to_core, to_z = neighbours()
    me = rep_of(y, x, c) * 4 + z
    meet_all(devices)

    def remote(k, number, source, dest, target):
        return pltpu.make_async_remote_copy(
            src_ref=source,
            dst_ref=dest,
            send_sem=send_sem.at[k, number],
            recv_sem=recv_sem.at[k, number],
            device_id=target,
            device_id_type=MESH,
        )

    def own_copy(k):
        return pltpu.make_async_copy(pieces[k], outs[k].at[c, y, x, z], own_sem.at[k])

    def line_copies(k, arriving):
        copies = []
        for step in (1, 2, 3):
            at_z = lax.rem(z + 4 - step, 4) if arriving else z
            copies.append(
                remote(k, step - 1, pieces[k], outs[k].at[c, y, x, at_z], to_z[step - 1])
            )
        return copies

    def first_copies(k, arriving):
        half = widths[k] // 2
        left, right = pl.ds(0, half), pl.ds(half, half)
        at_x = 1 - x if arriving else x
        at_y = 1 - y if arriving else y
        a_block = outs[k].at[c, y, at_x, :, :, left]
        b_block = outs[k].at[c, at_y, x, :, :, right]
        return [remote(k, 3, a_block, a_block, to_x), remote(k, 4, b_block, b_block, to_y)]

    def second_copies(k, arriving):
        half = widths[k] // 2
        left, right = pl.ds(0, half), pl.ds(half, half)
        at_x = 1 - x if arriving else x
        at_y = 1 - y if arriving else y
        a_block = outs[k].at[c, at_y, :, :, :, left]
        b_block = outs[k].at[c, :, at_x, :, :, right]
        return [remote(k, 5, a_block, a_block, to_y), remote(k, 6, b_block, b_block, to_x)]

    def core_copies(k, arriving):
        block = outs[k].at[1 - c if arriving else c]
        return [remote(k, 7, block, block, to_core)]

    def start(copies):
        for copy in copies:
            copy.start()

    def arrived(copies):
        for copy in copies:
            copy.wait_recv()

    def modul_copy(j, arriving):
        peer, where = device_at(devices - j if arriving else j)
        return pltpu.make_async_remote_copy(
            src_ref=parts.at[pl.ds(peer * images, images)],
            dst_ref=modul_out.at[peer if arriving else me],
            send_sem=modul_sem.at[0, j],
            recv_sem=modul_sem.at[1, j],
            device_id=where,
            device_id_type=MESH,
        )

    def image_products():
        copy = pltpu.make_async_copy(outs[0], time_two, time_sem)
        copy.start()
        copy.wait()
        weight = time_two[...].reshape(D, D).astype(jnp.bfloat16)
        cond = jnp.dot(time_act[...], weight, preferred_element_type=jnp.float32)
        cond = cond + label_rows[...]
        cond_out[...] = cond
        act = (cond * jax.nn.sigmoid(cond)).astype(jnp.bfloat16)
        for s in range(slots):
            parts[:, s, :] = jnp.dot(act, low_slots[s], preferred_element_type=jnp.float32)
        for i in range(images):
            modul_out[me, i] = parts[me * images + i]

        @pl.loop(1, devices)
        def _(j):
            modul_copy(j, False).start()

    for k in range(count):
        own_copy(k).start()
    start(line_copies(0, False))
    for t in range(count + 2):
        if t + 1 < count:
            start(line_copies(t + 1, False))
        if t < count:
            own_copy(t).wait()
            arrived(line_copies(t, True))
            start(first_copies(t, False))
        if 0 <= t - 1 < count:
            arrived(first_copies(t - 1, True))
            start(second_copies(t - 1, False))
        if 0 <= t - 2 < count:
            arrived(second_copies(t - 2, True))
            start(core_copies(t - 2, False))
        if t == 3:
            arrived(core_copies(0, True))
            image_products()
    for k in range(1, count):
        arrived(core_copies(k, True))

    @pl.loop(1, devices)
    def _(j):
        modul_copy(j, True).wait_recv()
        modul_copy(j, False).wait_send()

    for k in range(count):
        for copies in (line_copies, first_copies, second_copies, core_copies):
            for copy in copies(k, False):
                copy.wait_send()


def scatter_kernel(widths, *refs):
    count = len(widths)
    grads, modul = refs[:count], refs[count]
    outs, every_modul = refs[count + 1 : 2 * count + 1], refs[2 * count + 1]
    scratch = refs[2 * count + 2 :]
    devices = every_modul.shape[0]
    own, core_in, first_in, second_in, line_in = (
        scratch[i * count : (i + 1) * count] for i in range(5)
    )
    own_sem, send_sem, recv_sem, modul_sem = scratch[5 * count :]
    y, x, c, z = place_of()
    to_x, to_y, to_core, to_z = neighbours()
    me = rep_of(y, x, c) * 4 + z
    meet_all(devices)

    def modul_copy(j, arriving):
        peer, where = device_at(devices - j if arriving else j)
        return pltpu.make_async_remote_copy(
            src_ref=modul,
            dst_ref=every_modul.at[peer if arriving else me],
            send_sem=modul_sem.at[0, j],
            recv_sem=modul_sem.at[1, j],
            device_id=where,
            device_id_type=MESH,
        )

    def remote(k, number, source, dest, target):
        return pltpu.make_async_remote_copy(
            src_ref=source,
            dst_ref=dest,
            send_sem=send_sem.at[k, number],
            recv_sem=recv_sem.at[k, number],
            device_id=target,
            device_id_type=MESH,
        )

    def own_copy(k):
        return pltpu.make_async_copy(grads[k].at[c], own[k], own_sem.at[k])

    def core_copies(k):
        return [remote(k, 0, grads[k].at[1 - c], core_in[k], to_core)]

    def first_copies(k):
        half = widths[k] // 2
        return [
            remote(k, 1, own[k].at[:, 1 - x, :, :, pl.ds(0, half)], first_in[k].at[0], to_x),
            remote(k, 2, own[k].at[1 - y, :, :, :, pl.ds(half, half)], first_in[k].at[1], to_y),
        ]

    def second_copies(k):
        half = widths[k] // 2
        return [
            remote(k, 3, own[k].at[1 - y, x, :, :, pl.ds(0, half)], second_in[k].at[0], to_y),
            remote(k, 4, own[k].at[y, 1 - x, :, :, pl.ds(half, half)], second_in[k].at[1], to_x),
        ]

    def line_copies(k):
        return [
            remote(
                k,
                4 + step,
                own[k].at[y, x, lax.rem(z + step, 4)],
                line_in[k].at[step - 1],
                to_z[step - 1],
            )
            for step in (1, 2, 3)
        ]

    def start(copies):
        for copy in copies:
            copy.start()

    def arrived(copies):
        for copy in copies:
            copy.wait_recv()

    def core_sum(k):
        @pl.loop(0, 16)
        def _(i):
            at = (i // 8, (i // 4) % 2, i % 4)
            own[k][at] = own[k][at] + core_in[k][at]

    def first_sum(k):
        half = widths[k] // 2

        @pl.loop(0, 8)
        def _(i):
            two, at_z = i // 4, i % 4
            a_at = (two, x, at_z, slice(None), pl.ds(0, half))
            b_at = (y, two, at_z, slice(None), pl.ds(half, half))
            own[k][a_at] = own[k][a_at] + first_in[k][0, two, at_z]
            own[k][b_at] = own[k][b_at] + first_in[k][1, two, at_z]

    def second_sum(k):
        half = widths[k] // 2

        @pl.loop(0, 4)
        def _(at_z):
            a_at = (y, x, at_z, slice(None), pl.ds(0, half))
            b_at = (y, x, at_z, slice(None), pl.ds(half, half))
            own[k][a_at] = own[k][a_at] + second_in[k][0, at_z]
            own[k][b_at] = own[k][b_at] + second_in[k][1, at_z]

    for k in range(count):
        start(core_copies(k))
        own_copy(k).start()
    every_modul[me] = modul[...]

    @pl.loop(1, devices)
    def _(j):
        modul_copy(j, False).start()

    for t in range(count + 3):
        if t < count:
            own_copy(t).wait()
            arrived(core_copies(t))
            core_sum(t)
            start(first_copies(t))
        if 0 <= t - 1 < count:
            arrived(first_copies(t - 1))
            first_sum(t - 1)
            start(second_copies(t - 1))
        if 0 <= t - 2 < count:
            arrived(second_copies(t - 2))
            second_sum(t - 2)
            start(line_copies(t - 2))
        if 0 <= t - 3 < count:
            k = t - 3
            arrived(line_copies(k))
            total = own[k][y, x, z].astype(jnp.float32)
            for step in (1, 2, 3):
                total = total + line_in[k][step - 1].astype(jnp.float32)
            outs[k][...] = total.astype(jnp.bfloat16)
    for k in range(count):
        for copies in (core_copies, first_copies, second_copies, line_copies):
            for copy in copies(k):
                copy.wait_send()

    @pl.loop(1, devices)
    def _(j):
        modul_copy(j, True).wait_recv()
        modul_copy(j, False).wait_send()


def share_kernel(finish, parts, extra, out, landed, send_sem, recv_sem):
    devices = parts.shape[0]
    shards = lax.axis_size("shard")
    me = lax.axis_index("rep") * shards + lax.axis_index("shard")

    def target(j):
        peer = lax.rem(me + j, devices)
        return peer, (peer // shards, lax.rem(peer, shards))

    barrier = pltpu.get_barrier_semaphore()

    @pl.loop(1, devices)
    def _(j):
        pl.semaphore_signal(barrier, inc=1, device_id=target(j)[1], device_id_type=MESH)

    pl.semaphore_wait(barrier, devices - 1)

    def copy_part(j):
        peer, where = target(j)
        return pltpu.make_async_remote_copy(
            src_ref=parts.at[peer],
            dst_ref=landed.at[j],
            send_sem=send_sem.at[0, j],
            recv_sem=recv_sem.at[0, j],
            device_id=where,
            device_id_type=MESH,
        )

    def copy_sum(j, arriving):
        owner = lax.rem(me + devices - j, devices) if arriving else me
        return pltpu.make_async_remote_copy(
            src_ref=out.at[owner],
            dst_ref=out.at[owner],
            send_sem=send_sem.at[1, j],
            recv_sem=recv_sem.at[1, j],
            device_id=target(j)[1],
            device_id_type=MESH,
        )

    @pl.loop(1, devices)
    def _(j):
        copy_part(j).start()

    landed[0] = parts[me]

    @pl.loop(1, devices)
    def _(j):
        copy_part(j).wait_recv()

    out[me] = finish(jnp.sum(landed[...], 0), extra[...])

    @pl.loop(1, devices)
    def _(j):
        copy_sum(j, False).start()

    @pl.loop(1, devices)
    def _(j):
        copy_sum(j, True).wait_recv()

    @pl.loop(1, devices)
    def _(j):
        copy_part(j).wait_send()
        copy_sum(j, False).wait_send()


def share(finish, parts, extra, number):
    devices = parts.shape[0]
    return pl.pallas_call(
        lambda *refs: share_kernel(finish, *refs),
        out_shape=jax.ShapeDtypeStruct(parts.shape, jnp.float32),
        in_specs=[pl.BlockSpec(memory_space=pltpu.VMEM)] * 2,
        out_specs=pl.BlockSpec(memory_space=pltpu.VMEM),
        scratch_shapes=[
            pltpu.VMEM(parts.shape, jnp.float32),
            pltpu.SemaphoreType.DMA((2, devices)),
            pltpu.SemaphoreType.DMA((2, devices)),
        ],
        compiler_params=pltpu.CompilerParams(collective_id=number, has_side_effects=True),
        cost_estimate=pl.CostEstimate(flops=0, bytes_accessed=20_000_000, transcendentals=0),
    )(parts, extra)


class RingPlan:
    def order_rows(self, values):
        shape = values.shape
        split = values.reshape((2, 2, 2, 4, D // 32) + shape[1:])
        return jnp.moveaxis(split, 0, 2).reshape(shape)

    def restore_rows(self, values):
        shape = values.shape
        split = values.reshape((2, 2, 2, 4, D // 32) + shape[1:])
        return jnp.moveaxis(split, 2, 0).reshape(shape)

    def gather(self, pieces, time_piece, time_act, label_rows, low_slots):
        pieces = [time_piece.astype(jnp.float32)] + list(pieces)
        widths = tuple(piece.shape[1] for piece in pieces)
        count, rows = len(pieces), D // 32
        all_images = time_act.shape[0]
        slots = low_slots.shape[1]
        room = -(-slots // 8) * 8
        size = sum(4 * D * width for width in widths)
        whole_shape = [(2, 2, 2, 4, rows, width) for width in widths]
        *whole, cond, modul = pl.pallas_call(
            lambda *refs: gather_kernel(widths, *refs),
            out_shape=[
                jax.ShapeDtypeStruct(shape, piece.dtype)
                for shape, piece in zip(whole_shape, pieces)
            ]
            + [
                jax.ShapeDtypeStruct((all_images, D), jnp.float32),
                jax.ShapeDtypeStruct((32, all_images // 32, room, BLOCK), jnp.float32),
            ],
            in_specs=[pl.BlockSpec(memory_space=pltpu.VMEM)] * (count + 3),
            out_specs=[pl.BlockSpec(memory_space=pl.ANY)] * count
            + [pl.BlockSpec(memory_space=pltpu.VMEM)] * 2,
            scratch_shapes=[
                pltpu.VMEM(whole_shape[0], jnp.float32),
                pltpu.VMEM((all_images, room, BLOCK), jnp.float32),
                pltpu.SemaphoreType.DMA((count,)),
                pltpu.SemaphoreType.DMA((count, 8)),
                pltpu.SemaphoreType.DMA((count, 8)),
                pltpu.SemaphoreType.DMA,
                pltpu.SemaphoreType.DMA((2, 32)),
            ],
            compiler_params=pltpu.CompilerParams(
                collective_id=0, has_side_effects=True, vmem_limit_bytes=GATHER_VMEM
            ),
            cost_estimate=pl.CostEstimate(flops=0, bytes_accessed=size, transcendentals=0),
        )(*pieces, time_act, label_rows, jnp.swapaxes(low_slots, 0, 1))
        whole = [part.reshape(D, -1) for part in whole]
        modul = jnp.swapaxes(modul[:, :, :slots], 0, 1).reshape(-1, 32 * slots, BLOCK)
        return whole[1:], whole[0].astype(jnp.bfloat16), cond, modul

    def scatter(self, grads, modul):
        widths = tuple(grad.shape[1] for grad in grads)
        count, rows = len(grads), D // 32
        size = sum(4 * D * width for width in widths)
        scratch = [pltpu.VMEM((2, 2, 4, rows, width), jnp.bfloat16) for width in widths] * 2
        scratch += [pltpu.VMEM((2, 2, 4, rows, width // 2), jnp.bfloat16) for width in widths]
        scratch += [pltpu.VMEM((2, 4, rows, width // 2), jnp.bfloat16) for width in widths]
        scratch += [pltpu.VMEM((3, rows, width), jnp.bfloat16) for width in widths]
        piece = modul.reshape(-1, BLOCK)
        *scattered, every_modul = pl.pallas_call(
            lambda *refs: scatter_kernel(widths, *refs),
            out_shape=[jax.ShapeDtypeStruct((rows, width), jnp.bfloat16) for width in widths]
            + [jax.ShapeDtypeStruct((32,) + piece.shape, jnp.bfloat16)],
            in_specs=[pl.BlockSpec(memory_space=pl.ANY)] * count
            + [pl.BlockSpec(memory_space=pltpu.VMEM)],
            out_specs=[pl.BlockSpec(memory_space=pltpu.VMEM)] * (count + 1),
            scratch_shapes=scratch
            + [
                pltpu.SemaphoreType.DMA((count,)),
                pltpu.SemaphoreType.DMA((count, 8)),
                pltpu.SemaphoreType.DMA((count, 8)),
                pltpu.SemaphoreType.DMA((2, 32)),
            ],
            compiler_params=pltpu.CompilerParams(
                collective_id=1, has_side_effects=True, vmem_limit_bytes=SCATTER_VMEM
            ),
            cost_estimate=pl.CostEstimate(flops=0, bytes_accessed=size, transcendentals=0),
        )(*[grad.reshape(2, 2, 2, 4, rows, -1) for grad in grads], piece)
        return scattered, every_modul.reshape(32 * modul.shape[0], -1)

    def share(self, finish, parts, extra, number):
        return share(finish, parts, extra, number)


class PlainPlan:
    def order_rows(self, values):
        return values

    def restore_rows(self, values):
        return values

    def gather(self, pieces, time_piece, time_act, label_rows, low_slots):
        whole = [lax.all_gather(piece, AXES, axis=0, tiled=True) for piece in pieces]
        time_two = lax.all_gather(time_piece, AXES, axis=0, tiled=True)
        cond = jnp.dot(time_act, time_two, preferred_element_type=jnp.float32) + label_rows
        modul = dot_low("gd,dsc->gsc", jax.nn.silu(cond).astype(jnp.bfloat16), low_slots)
        modul = lax.all_to_all(modul, AXES, split_axis=0, concat_axis=1, tiled=True)
        return whole, time_two, cond, modul

    def scatter(self, grads, modul):
        scattered = [
            lax.psum_scatter(grad, AXES, scatter_dimension=0, tiled=True) for grad in grads
        ]
        return scattered, lax.all_gather(modul, AXES, axis=0, tiled=True)

    def share(self, finish, parts, extra, number):
        own = finish(scatter_small(parts, parts.shape[0]), extra)
        return gather_small(own[None], parts.shape[0])


def unit_lists():
    dense = np.concatenate(
        [np.arange(l * LAYER_UNITS + ADA_UNITS, (l + 1) * LAYER_UNITS) for l in range(LAYERS)]
    )
    time_units = np.arange(TAIL_FIRST, TAIL_FIRST + TIME_UNITS)
    image_units = np.concatenate(
        [np.arange(l * LAYER_UNITS, l * LAYER_UNITS + ADA_UNITS) for l in range(LAYERS)]
        + [np.arange(TAIL_FIRST + TIME_UNITS, UNITS)]
    )
    return dense, time_units, image_units


def on_device(
    latents,
    noise,
    labels,
    t_index,
    owner,
    master,
    first_moment,
    second_moment,
    small,
    small_first,
    small_second,
):
    count = lax.axis_size("rep") * lax.axis_size("shard")
    me = lax.axis_index(AXES)
    slot_dev = master.shape[1]
    slot_total = count * slot_dev
    rows = D // count
    images = latents.shape[0]
    dense_units, time_units, image_units = unit_lists()

    unit_of_slot = (
        jnp.full((slot_total,), -1, jnp.int32).at[owner].set(jnp.arange(UNITS, dtype=jnp.int32))
    )
    my_unit = lax.dynamic_slice_in_dim(unit_of_slot, me * slot_dev, slot_dev)
    low_slots = master.astype(jnp.bfloat16)

    plan = RingPlan() if (lax.axis_size("rep"), lax.axis_size("shard")) == (8, 4) else PlainPlan()
    every_int = gather_small(jnp.stack([t_index, labels], 1), count)
    every_t, every_label = every_int[:, 0], every_int[:, 1]
    all_images = every_t.shape[0]

    spread = lax.all_to_all(
        plan.order_rows(low_slots), AXES, split_axis=0, concat_axis=1, tiled=True
    )
    moved = np.concatenate([dense_units, time_units])
    unit_rows = jnp.take(spread, owner[moved], axis=1).reshape(rows, -1)
    pieces = []
    for l in range(LAYERS):
        base = l * DENSE_COLS
        cuts = (base, base + 4 * D, base + 4 * D + FF, base + DENSE_COLS)
        pieces += [unit_rows[:, cuts[i] : cuts[i + 1]] for i in range(3)]
    x_start = latents.astype(jnp.float32).reshape(-1, PATCHES, CHANNELS)
    noise_f = noise.astype(jnp.float32).reshape(-1, PATCHES, CHANNELS)
    times = (t_index.astype(jnp.float32) + 0.5) / TSTEPS
    noisy = (1.0 - times)[:, None, None] * x_start + times[:, None, None] * noise_f
    target = noise_f - x_start
    loss_weight = 1.0 + 3.0 * times
    small_low = small.astype(jnp.bfloat16)
    patch_w = small_low[:CHANNELS]
    time_w = small_low[CHANNELS : CHANNELS + FREQ]
    table = small[CHANNELS + FREQ : CHANNELS + FREQ + CLASSES]
    head_w = small_low[CHANNELS + FREQ + CLASSES :]
    noisy_low = noisy.astype(jnp.bfloat16)
    hidden = dot_low("gpc,cd->gpd", noisy_low, patch_w) + positions()

    every_time = (every_t.astype(jnp.float32) + 0.5) / TSTEPS
    weight_total = jnp.sum(1.0 + 3.0 * every_time) * PATCHES
    freq_low = frequencies(every_time).astype(jnp.bfloat16)
    time_pre = jnp.dot(freq_low, time_w, preferred_element_type=jnp.float32)
    time_act = jax.nn.silu(time_pre).astype(jnp.bfloat16)
    label_rows = jnp.take(table, every_label, axis=0)
    whole, time_two, cond_all, slot_modul = plan.gather(
        pieces, unit_rows[:, LAYERS * DENSE_COLS :], time_act, label_rows, low_slots
    )
    weights_all = [
        (whole[3 * l][:, : 3 * D], whole[3 * l][:, 3 * D :], whole[3 * l + 1], whole[3 * l + 2])
        for l in range(LAYERS)
    ]
    cond = lax.dynamic_slice_in_dim(cond_all, me * images, images)
    cond_act = jax.nn.silu(cond_all).astype(jnp.bfloat16)
    modul_all = jnp.take(slot_modul, owner[image_units], axis=1).reshape(images, -1)

    saved_all = []
    for l in range(LAYERS):
        hidden, saved = layer_forward(
            hidden, modul_all[:, l * 6 * D : (l + 1) * 6 * D], weights_all[l]
        )
        saved_all.append(saved)
    shift_f, scale_f = jnp.split(modul_all[:, LAYERS * 6 * D :], 2, -1)
    normed_f = norm_rows(hidden)
    final_in = modulate(normed_f, shift_f, scale_f).astype(jnp.bfloat16)
    predict = dot_low("gpd,cd->gpc", final_in, head_w)
    error = predict - target
    loss_part = jnp.sum(loss_weight[:, None, None] * error * error) / CHANNELS
    grad_pred = (loss_weight[:, None, None] * 2.0 * error / CHANNELS).astype(jnp.bfloat16)
    grad_head = dot_low("gpc,gpd->cd", grad_pred, final_in)
    grad_final_in = dot_low("gpc,cd->gpd", grad_pred, head_w)
    grad_modul_f = jnp.concatenate(
        [jnp.sum(grad_final_in, 1), jnp.sum(grad_final_in * normed_f, 1)], -1
    ).astype(jnp.bfloat16)
    grad_hidden = local_back(norm_rows, hidden, grad_final_in * (1.0 + scale_f[:, None, :]))
    layer_grads = [None] * LAYERS
    grad_moduls = [None] * LAYERS
    for l in reversed(range(LAYERS)):
        grad_hidden, grad_moduls[l], layer_grads[l] = layer_backward(
            grad_hidden, weights_all[l], saved_all[l]
        )
    order = list(reversed(range(LAYERS)))
    scattered, every_modul = plan.scatter(
        [grad for l in order for grad in reversed(layer_grads[l])],
        jnp.concatenate(grad_moduls + [grad_modul_f], -1),
    )
    every_modul = every_modul.reshape(all_images, len(image_units), BLOCK)
    grad_rows = {
        (l, 2 - i): scattered[3 * n + i] for n, l in enumerate(order) for i in range(3)
    }
    grad_embed = grad_hidden.astype(jnp.bfloat16)
    grad_patch = dot_low("gpc,gpd->cd", noisy_low, grad_embed)

    image_place = np.full((UNITS + 1,), -1, np.int32)
    image_place[image_units] = np.arange(len(image_units))
    my_place = jnp.asarray(image_place)[my_unit]
    slot_grad_out = jnp.where(
        (my_place >= 0)[None, :, None],
        jnp.take(every_modul, jnp.maximum(my_place, 0), axis=1),
        jnp.zeros((), jnp.bfloat16),
    )
    cond_part = dot_low("gsc,dsc->gd", slot_grad_out, low_slots)
    edge_rows = max(1, 2 * CHANNELS // count)
    edge = jnp.concatenate([grad_patch, grad_head], 0)
    edge = jnp.concatenate(
        [edge, jnp.zeros((edge_rows * count - 2 * CHANNELS, D), jnp.float32)], 0
    )
    small_part = jnp.concatenate(
        [
            cond_part.reshape(count, images, D),
            edge.reshape(count, edge_rows, D),
            jnp.broadcast_to(loss_part, (count, 1, D)),
        ],
        1,
    )
    factor = local_back(jax.nn.silu, cond, jnp.ones_like(cond))
    factor = jnp.concatenate([factor, jnp.ones((edge_rows + 1, D), jnp.float32)], 0)
    small_sum = plan.share(lambda a, b: a * b, small_part, factor, 3)
    grad_cond = small_sum[:, :images].reshape(all_images, D)
    edge = small_sum[:, images : images + edge_rows].reshape(-1, D)
    grad_patch, grad_head = edge[:CHANNELS], edge[CHANNELS : 2 * CHANNELS]
    loss_sum = small_sum[0, images + edge_rows, 0]
    grad_time_out = grad_cond.astype(jnp.bfloat16)
    grad_time_act = dot_low("ge,de->gd", grad_time_out, time_two)
    grad_time_pre = local_back(jax.nn.silu, time_pre, grad_time_act).astype(jnp.bfloat16)
    grad_time_w = dot_low("gf,gd->fd", freq_low, grad_time_pre)
    grad_table = jnp.zeros((CLASSES, D), jnp.float32).at[every_label].add(grad_cond)
    small_grad = jnp.concatenate([grad_patch, grad_time_w, grad_table, grad_head], 0)

    my_time = jnp.clip(my_unit - TAIL_FIRST, 0, TIME_UNITS - 1)
    is_time = (my_unit >= TAIL_FIRST) & (my_unit < TAIL_FIRST + TIME_UNITS)
    time_cols = jnp.take(grad_time_out.reshape(all_images, TIME_UNITS, BLOCK), my_time, axis=1)
    is_image = my_place >= 0
    image_grad = dot_low("gd,gsc->dsc", cond_act, slot_grad_out)
    time_grad = dot_low("gd,gsc->dsc", time_act, time_cols)

    dense_place = np.full((UNITS + 1,), 0, np.int32)
    dense_place[dense_units] = np.arange(len(dense_units))
    slot_place = jnp.asarray(dense_place)[unit_of_slot]
    all_rows = jnp.concatenate(
        [
            grad_rows[l, i].reshape(rows, -1, BLOCK)
            for l in range(LAYERS)
            for i in range(3)
        ],
        1,
    )
    slot_rows = jnp.take(all_rows, slot_place, axis=1)
    dense_grad = plan.restore_rows(
        lax.all_to_all(slot_rows, AXES, split_axis=1, concat_axis=0, tiled=True)
    ).astype(jnp.float32)

    owned_grad = jnp.where(
        is_image[None, :, None],
        image_grad,
        jnp.where(is_time[None, :, None], time_grad, dense_grad),
    )
    used = (my_unit >= 0)[None, :, None]
    rate = rate_factor * unit_scale(jnp.maximum(my_unit, 0))[None, :, None]
    new_w, new_first, new_second = adam_update(
        master, first_moment, second_moment, owned_grad, rate
    )
    new_master = jnp.where(used, new_w, master)
    new_first = jnp.where(used, new_first, first_moment)
    new_second = jnp.where(used, new_second, second_moment)
    small_rate = rate_factor * table_scale(jnp.arange(small.shape[0], dtype=jnp.int32))[:, None]
    new_small, new_small_first, new_small_second = adam_update(
        small, small_first, small_second, small_grad, small_rate
    )
    return (
        loss_sum,
        weight_total,
        new_master,
        new_first,
        new_second,
        new_small,
        new_small_first,
        new_small_second,
    )


def solution(mesh):
    return jax.shard_map(
        on_device,
        mesh=mesh,
        in_specs=(
            P(("rep", "shard"), None),
            P(("rep", "shard"), None),
            P(("rep", "shard")),
            P(("rep", "shard")),
            P(),
            P(None, ("rep", "shard"), None),
            P(None, ("rep", "shard"), None),
            P(None, ("rep", "shard"), None),
            P(),
            P(),
            P(),
        ),
        out_specs=(
            P(),
            P(),
            P(None, ("rep", "shard"), None),
            P(None, ("rep", "shard"), None),
            P(None, ("rep", "shard"), None),
            P(),
            P(),
            P(),
        ),
        check_vma=False,
    )
```

```python
import jax
import jax.numpy as jnp
import numpy as np
from jax import lax
from jax.experimental import pallas as pl
from jax.experimental.pallas import tpu as pltpu
from jax.sharding import PartitionSpec as P

D = 768
HEADS = 12
HEAD_DIM = 64
FF = 3072
FREQ = 256
CLASSES = 1000
CHANNELS = 16
GRID = 16
PATCHES = 256
LAYERS = 2
TSTEPS = 1000
STEP = 10
BLOCK = 128
LAYER_COLS = 13824
LAYER_UNITS = 108
UNITS = 234

ADA_UNITS = 6 * D // BLOCK
DENSE_UNITS = LAYER_UNITS - ADA_UNITS
DENSE_COLS = DENSE_UNITS * BLOCK
TIME_UNITS = D // BLOCK
TAIL_FIRST = LAYERS * LAYER_UNITS
AXES = ("rep", "shard")


beta_one = 0.5
beta_two = 0.5
adam_eps = 1e-08
decay_rate = 0.1
rate_factor = 0.5


def gelu_tanh(values):
    return jax.nn.gelu(values, approximate=True)


def norm_rows(hidden):
    centered = hidden - jnp.mean(hidden, -1, keepdims=True)
    return centered * lax.rsqrt(jnp.mean(centered * centered, -1, keepdims=True) + 1e-06)


def local_back(function, primal, upstream):
    return jax.vjp(function, primal)[1](upstream)[0]


def dot_low(pattern, left_side, right_side):
    return jnp.einsum(pattern, left_side, right_side, preferred_element_type=jnp.float32)


def positions():
    quarter = D // 4
    angular = jnp.exp(-jnp.log(10000.0) * jnp.arange(quarter, dtype=jnp.float32) / quarter)
    patch_idx = jnp.arange(PATCHES, dtype=jnp.int32)
    row_pos = (patch_idx // GRID).astype(jnp.float32)[:, None] * angular
    col_pos = (patch_idx % GRID).astype(jnp.float32)[:, None] * angular
    return jnp.concatenate(
        [jnp.sin(col_pos), jnp.cos(col_pos), jnp.sin(row_pos), jnp.cos(row_pos)], -1
    )


def frequencies(times):
    half_size = FREQ // 2
    spacing = jnp.exp(-jnp.log(10000.0) * jnp.arange(half_size, dtype=jnp.float32) / half_size)
    angles = 1000.0 * times[:, None] * spacing
    return jnp.concatenate([jnp.cos(angles), jnp.sin(angles)], -1)


def unit_scale(unit_ids):
    column = unit_ids % LAYER_UNITS * BLOCK
    in_layer = unit_ids < LAYERS * LAYER_UNITS
    is_output = in_layer & (column >= 9 * D) & (column < 10 * D)
    is_down = in_layer & (column >= 10 * D + FF)
    factor = jnp.where(is_output, 4.0, jnp.where(is_down, 1.5 * (D / FF) ** 0.5, 1.0))
    return factor / D**0.5


def table_scale(row_ids):
    return jnp.where(
        row_ids < CHANNELS,
        CHANNELS ** (-0.5),
        jnp.where(
            row_ids < CHANNELS + FREQ,
            FREQ ** (-0.5),
            jnp.where(row_ids < CHANNELS + FREQ + CLASSES, 0.5, D ** (-0.5)),
        ),
    )


def adam_update(weight, first_mom, second, gradient, rate):
    first_new = beta_one * first_mom + (1.0 - beta_one) * gradient
    second_new = beta_two * second + (1.0 - beta_two) * gradient * gradient
    ratio = (
        first_new
        / (1.0 - beta_one**STEP)
        / (jnp.sqrt(second_new / (1.0 - beta_two**STEP)) + adam_eps)
    )
    return (weight - rate * (ratio + decay_rate * weight), first_new, second_new)


def split_heads(qkv_all):
    groups, length = (qkv_all.shape[0], qkv_all.shape[1])
    return tuple(
        (
            qkv_all[..., part_idx * D : (part_idx + 1) * D].reshape(groups, length, HEADS, HEAD_DIM)
            for part_idx in range(3)
        )
    )


def modulate(normed, shift, scale):
    return normed * (1.0 + scale[:, None, :]) + shift[:, None, :]


def layer_forward(hidden, modul, weights):
    w_qkv, w_out, w_up, w_down = weights
    groups = hidden.shape[0]
    shift_a, scale_a, gate_a, shift_b, scale_b, gate_b = jnp.split(modul, 6, -1)
    attn_in = modulate(norm_rows(hidden), shift_a, scale_a).astype(jnp.bfloat16)
    qkv_all = dot_low("gpd,de->gpe", attn_in, w_qkv).astype(jnp.bfloat16)
    queries, keys_all, values = split_heads(qkv_all)
    scores = dot_low("gqhe,gkhe->ghqk", queries, keys_all) * HEAD_DIM ** (-0.5)
    top_score = jnp.max(scores, -1, keepdims=True)
    log_total = top_score + jnp.log(jnp.sum(jnp.exp(scores - top_score), -1, keepdims=True))
    attn_prob = jnp.exp(scores - log_total).astype(jnp.bfloat16)
    heads_out = (
        dot_low("ghqk,gkhe->gqhe", attn_prob, values).astype(jnp.bfloat16).reshape(groups, -1, D)
    )
    branch_a = dot_low("gpd,de->gpe", heads_out, w_out)
    middle = hidden + gate_a[:, None, :] * branch_a
    mlp_in = modulate(norm_rows(middle), shift_b, scale_b).astype(jnp.bfloat16)
    pre_act = dot_low("gpd,df->gpf", mlp_in, w_up)
    post_act = gelu_tanh(pre_act).astype(jnp.bfloat16)
    branch_b = dot_low("gpf,df->gpd", post_act, w_down)
    output = middle + gate_b[:, None, :] * branch_b
    return (
        output,
        (
            hidden,
            modul,
            attn_in,
            qkv_all,
            log_total,
            heads_out,
            branch_a,
            middle,
            mlp_in,
            pre_act,
            post_act,
            branch_b,
        ),
    )


def layer_backward(grad_out, weights, saved):
    w_qkv, w_out, w_up, w_down = weights
    (
        hidden,
        modul,
        attn_in,
        qkv_all,
        log_total,
        heads_out,
        branch_a,
        middle,
        mlp_in,
        pre_act,
        post_act,
        branch_b,
    ) = saved
    groups = hidden.shape[0]
    shift_a, scale_a, gate_a, shift_b, scale_b, gate_b = jnp.split(modul, 6, -1)
    grad_gate_b = jnp.sum(grad_out * branch_b, 1)
    grad_branch_b = (gate_b[:, None, :] * grad_out).astype(jnp.bfloat16)
    grad_down = (grad_branch_b, post_act)
    grad_post = dot_low("gpd,df->gpf", grad_branch_b, w_down)
    grad_pre = local_back(gelu_tanh, pre_act, grad_post).astype(jnp.bfloat16)
    grad_up = (mlp_in, grad_pre)
    grad_mlp_in = dot_low("gpf,df->gpd", grad_pre, w_up)
    normed_b = norm_rows(middle)
    grad_scale_b = jnp.sum(grad_mlp_in * normed_b, 1)
    grad_shift_b = jnp.sum(grad_mlp_in, 1)
    grad_middle = grad_out + local_back(
        norm_rows, middle, grad_mlp_in * (1.0 + scale_b[:, None, :])
    )
    grad_gate_a = jnp.sum(grad_middle * branch_a, 1)
    grad_branch_a = (gate_a[:, None, :] * grad_middle).astype(jnp.bfloat16)
    grad_out_w = (heads_out, grad_branch_a)
    grad_heads = (
        dot_low("gpe,de->gpd", grad_branch_a, w_out)
        .astype(jnp.bfloat16)
        .reshape(groups, -1, HEADS, HEAD_DIM)
    )
    queries, keys_all, values = split_heads(qkv_all)
    scores = dot_low("gqhe,gkhe->ghqk", queries, keys_all) * HEAD_DIM ** (-0.5)
    attn_prob = jnp.exp(scores - log_total)
    grad_prob = dot_low("gqhe,gkhe->ghqk", grad_heads, values)
    grad_values = dot_low("ghqk,gqhe->gkhe", attn_prob.astype(jnp.bfloat16), grad_heads)
    inner_sum = jnp.sum(attn_prob * grad_prob, -1, keepdims=True)
    grad_scores = (HEAD_DIM ** (-0.5) * attn_prob * (grad_prob - inner_sum)).astype(jnp.bfloat16)
    grad_queries = dot_low("ghqk,gkhe->gqhe", grad_scores, keys_all)
    grad_keys = dot_low("ghqk,gqhe->gkhe", grad_scores, queries)
    grad_qkv = jnp.concatenate(
        [
            grad_queries.reshape(groups, -1, D),
            grad_keys.reshape(groups, -1, D),
            grad_values.reshape(groups, -1, D),
        ],
        -1,
    ).astype(jnp.bfloat16)
    grad_qkv_w = (attn_in, grad_qkv)
    grad_attn_in = dot_low("gpe,de->gpd", grad_qkv, w_qkv)
    normed_a = norm_rows(hidden)
    grad_scale_a = jnp.sum(grad_attn_in * normed_a, 1)
    grad_shift_a = jnp.sum(grad_attn_in, 1)
    grad_in = grad_middle + local_back(
        norm_rows, hidden, grad_attn_in * (1.0 + scale_a[:, None, :])
    )
    grad_modul = jnp.concatenate(
        [grad_shift_a, grad_scale_a, grad_gate_a, grad_shift_b, grad_scale_b, grad_gate_b], -1
    ).astype(jnp.bfloat16)
    return (grad_in, grad_modul, [grad_qkv_w, grad_out_w, grad_up, grad_down])


MESH = pl.DeviceIdType.MESH
GATHER_VMEM = 40 * 2**20
SCATTER_VMEM = 56 * 2**20


def dot_rows(left_side, right_side):
    return lax.dot_general(
        left_side, right_side, (((0,), (0,)), ((), ())), preferred_element_type=jnp.float32
    )


def row_product(left_side, right_side):
    left_side = left_side.reshape(-1, left_side.shape[-1])
    right_side = right_side.reshape(-1, right_side.shape[-1])
    return dot_rows(left_side, right_side).astype(jnp.bfloat16)


def place_of():
    rep = lax.axis_index("rep")
    return rep // 4, (rep // 2) % 2, rep % 2, lax.axis_index("shard")


def rep_of(y, x, c):
    return (y * 2 + x) * 2 + c


def device_at(j):
    shards = lax.axis_size("shard")
    devices = lax.axis_size("rep") * shards
    me = lax.axis_index("rep") * shards + lax.axis_index("shard")
    peer = lax.rem(me + j, devices)
    return peer, (peer // shards, lax.rem(peer, shards))


def meet_all(devices):
    barrier = pltpu.get_barrier_semaphore()

    @pl.loop(1, devices)
    def _(j):
        pl.semaphore_signal(barrier, inc=1, device_id=device_at(j)[1], device_id_type=MESH)

    pl.semaphore_wait(barrier, devices - 1)


def neighbours():
    y, x, c, z = place_of()
    to_x = (rep_of(y, 1 - x, c), z)
    to_y = (rep_of(1 - y, x, c), z)
    to_core = (rep_of(y, x, 1 - c), z)
    to_z = [(rep_of(y, x, c), lax.rem(z + step, 4)) for step in (1, 2, 3)]
    return to_x, to_y, to_core, to_z


def gather_kernel(widths, *refs):
    count = len(widths)
    pieces = refs[:count]
    info, low_slots = refs[count : count + 2]
    outs = refs[count + 2 : 2 * count + 2]
    every_info, cond_out, modul_out = refs[2 * count + 2 : 2 * count + 5]
    time_two, parts, own_sem, send_sem, recv_sem, time_sem, modul_sem, info_sem = refs[
        2 * count + 5 :
    ]
    devices, images = modul_out.shape[:2]
    slots = low_slots.shape[0]
    y, x, c, z = place_of()
    to_x, to_y, to_core, to_z = neighbours()
    me = rep_of(y, x, c) * 4 + z
    meet_all(devices)

    def remote(k, number, source, dest, target):
        return pltpu.make_async_remote_copy(
            src_ref=source,
            dst_ref=dest,
            send_sem=send_sem.at[k, number],
            recv_sem=recv_sem.at[k, number],
            device_id=target,
            device_id_type=MESH,
        )

    def own_copy(k):
        return pltpu.make_async_copy(pieces[k], outs[k].at[c, y, x, z], own_sem.at[k])

    def line_copies(k, arriving):
        copies = []
        for step in (1, 2, 3):
            at_z = lax.rem(z + 4 - step, 4) if arriving else z
            copies.append(
                remote(k, step - 1, pieces[k], outs[k].at[c, y, x, at_z], to_z[step - 1])
            )
        return copies

    def first_copies(k, arriving):
        half = widths[k] // 2
        left, right = pl.ds(0, half), pl.ds(half, half)
        at_x = 1 - x if arriving else x
        at_y = 1 - y if arriving else y
        a_block = outs[k].at[c, y, at_x, :, :, left]
        b_block = outs[k].at[c, at_y, x, :, :, right]
        return [remote(k, 3, a_block, a_block, to_x), remote(k, 4, b_block, b_block, to_y)]

    def second_copies(k, arriving):
        half = widths[k] // 2
        left, right = pl.ds(0, half), pl.ds(half, half)
        at_x = 1 - x if arriving else x
        at_y = 1 - y if arriving else y
        a_block = outs[k].at[c, at_y, :, :, :, left]
        b_block = outs[k].at[c, :, at_x, :, :, right]
        return [remote(k, 5, a_block, a_block, to_y), remote(k, 6, b_block, b_block, to_x)]

    def core_copies(k, arriving):
        block = outs[k].at[1 - c if arriving else c]
        return [remote(k, 7, block, block, to_core)]

    def start(copies):
        for copy in copies:
            copy.start()

    def arrived(copies):
        for copy in copies:
            copy.wait_recv()

    def modul_copy(j, arriving):
        peer, where = device_at(devices - j if arriving else j)
        return pltpu.make_async_remote_copy(
            src_ref=parts.at[pl.ds(peer * images, images)],
            dst_ref=modul_out.at[peer if arriving else me],
            send_sem=modul_sem.at[0, j],
            recv_sem=modul_sem.at[1, j],
            device_id=where,
            device_id_type=MESH,
        )

    def info_copy(j, arriving):
        peer, where = device_at(devices - j if arriving else j)
        return pltpu.make_async_remote_copy(
            src_ref=info,
            dst_ref=every_info.at[pl.ds((peer if arriving else me) * images, images)],
            send_sem=info_sem.at[0, j],
            recv_sem=info_sem.at[1, j],
            device_id=where,
            device_id_type=MESH,
        )

    def info_rows(first):
        return jnp.concatenate([every_info[:, first + j, :] for j in range(D // BLOCK)], -1)

    def image_products():
        copy = pltpu.make_async_copy(outs[0], time_two, time_sem)
        copy.start()

        @pl.loop(1, devices)
        def _(j):
            info_copy(j, True).wait_recv()
            info_copy(j, False).wait_send()

        copy.wait()
        weight = time_two[...].astype(jnp.float32).reshape(D, D).astype(jnp.bfloat16)
        cond = jnp.dot(
            info_rows(0).astype(jnp.bfloat16), weight, preferred_element_type=jnp.float32
        )
        cond = cond + info_rows(8)
        cond_out[...] = cond
        act = (cond * jax.nn.sigmoid(cond)).astype(jnp.bfloat16)
        for s in range(slots):
            parts[:, s, :] = jnp.dot(act, low_slots[s], preferred_element_type=jnp.float32)
        for i in range(images):
            modul_out[me, i] = parts[me * images + i]

        @pl.loop(1, devices)
        def _(j):
            modul_copy(j, False).start()

    @pl.loop(1, devices)
    def _(j):
        info_copy(j, False).start()

    for i in range(images):
        every_info[me * images + i] = info[i]
    for k in range(count):
        own_copy(k).start()
    start(line_copies(0, False))
    for t in range(count + 2):
        if t + 1 < count:
            start(line_copies(t + 1, False))
        if t < count:
            own_copy(t).wait()
            arrived(line_copies(t, True))
            start(first_copies(t, False))
        if 0 <= t - 1 < count:
            arrived(first_copies(t - 1, True))
            start(second_copies(t - 1, False))
        if 0 <= t - 2 < count:
            arrived(second_copies(t - 2, True))
            start(core_copies(t - 2, False))
        if t == 3:
            arrived(core_copies(0, True))
            image_products()
    for k in range(1, count):
        arrived(core_copies(k, True))

    @pl.loop(1, devices)
    def _(j):
        modul_copy(j, True).wait_recv()
        modul_copy(j, False).wait_send()

    for k in range(count):
        for copies in (line_copies, first_copies, second_copies, core_copies):
            for copy in copies(k, False):
                copy.wait_send()


def scatter_kernel(widths, slots, *refs):
    count = len(widths)
    lefts, rights = refs[:count], refs[count : 2 * count]
    modul, pick, low_slots, edge, factor = refs[2 * count : 2 * count + 5]
    outs = refs[2 * count + 5 : 3 * count + 5]
    chosen, shared = refs[3 * count + 5 : 3 * count + 7]
    scratch = refs[3 * count + 7 :]
    own, first_in, second_in, line_in = (scratch[i * count : (i + 1) * count] for i in range(4))
    (
        left_in, right_in, away, every_modul, parts, landed,
        load_sem, send_sem, recv_sem, modul_sem, part_sem, sum_sem,
    ) = scratch[4 * count :]
    devices, images = shared.shape[:2]
    y, x, c, z = place_of()
    to_x, to_y, to_core, to_z = neighbours()
    me = rep_of(y, x, c) * 4 + z
    rows = D // 32
    half_rows = D // 2
    meet_all(devices)

    def exchange(source, dest, sem, j, arriving):
        peer, where = device_at(devices - j if arriving else j)
        return pltpu.make_async_remote_copy(
            src_ref=source(peer, me),
            dst_ref=dest(peer if arriving else me),
            send_sem=sem.at[0, j],
            recv_sem=sem.at[1, j],
            device_id=where,
            device_id_type=MESH,
        )

    def modul_copy(j, arriving):
        return exchange(
            lambda peer, mine: modul,
            lambda owner: every_modul.at[pl.ds(owner * images, images)],
            modul_sem, j, arriving,
        )

    def part_copy(j, arriving):
        return exchange(
            lambda peer, mine: parts.at[pl.ds(peer * images, images)],
            lambda owner: landed.at[owner],
            part_sem, j, arriving,
        )

    def sum_copy(j, arriving):
        return exchange(
            lambda peer, mine: shared.at[mine], lambda owner: shared.at[owner], sum_sem, j, arriving
        )

    def all_start(copy):
        @pl.loop(1, devices)
        def _(j):
            copy(j, False).start()

    def all_arrived(copy):
        @pl.loop(1, devices)
        def _(j):
            copy(j, True).wait_recv()

    def all_sent(copy):
        @pl.loop(1, devices)
        def _(j):
            copy(j, False).wait_send()

    def image_parts():
        all_arrived(modul_copy)

        @pl.loop(0, devices * images)
        def _(i):
            chosen[i] = jnp.dot(pick[...], every_modul[i], preferred_element_type=jnp.float32)

        total = jnp.zeros((devices * images, D), jnp.float32)
        for s in range(slots):
            total = total + lax.dot_general(
                chosen[:, s, :].astype(jnp.bfloat16),
                low_slots[s],
                (((1,), (1,)), ((), ())),
                preferred_element_type=jnp.float32,
            )
        parts[...] = edge[...]
        for j in range(D // BLOCK):
            parts[:, j, :] = total[:, j * BLOCK : (j + 1) * BLOCK]
        all_start(part_copy)
        for i in range(images):
            landed[me, i] = parts[me * images + i]

    def image_sums():
        all_arrived(part_copy)
        shared[me] = jnp.sum(landed[...], 0) * factor[...]
        all_start(sum_copy)

    def remote(k, number, source, dest, target):
        return pltpu.make_async_remote_copy(
            src_ref=source,
            dst_ref=dest,
            send_sem=send_sem.at[k, number],
            recv_sem=recv_sem.at[k, number],
            device_id=target,
            device_id_type=MESH,
        )

    def loads(k):
        slot = k % 3
        return [
            pltpu.make_async_copy(lefts[k], left_in.at[slot], load_sem.at[0, slot]),
            pltpu.make_async_copy(
                rights[k], right_in.at[slot, :, pl.ds(0, widths[k])], load_sem.at[1, slot]
            ),
        ]

    def core_copies(k):
        source = away.at[k % 3, :, :, :, :, pl.ds(0, widths[k])]
        return [remote(k, 0, source, own[k], to_core)]

    def first_copies(k):
        half = widths[k] // 2
        return [
            remote(k, 1, own[k].at[:, 1 - x, :, :, pl.ds(0, half)], first_in[k].at[0], to_x),
            remote(k, 2, own[k].at[1 - y, :, :, :, pl.ds(half, half)], first_in[k].at[1], to_y),
        ]

    def second_copies(k):
        half = widths[k] // 2
        return [
            remote(k, 3, own[k].at[1 - y, x, :, :, pl.ds(0, half)], second_in[k].at[0], to_y),
            remote(k, 4, own[k].at[y, 1 - x, :, :, pl.ds(half, half)], second_in[k].at[1], to_x),
        ]

    def line_copies(k):
        return [
            remote(
                k,
                4 + step,
                own[k].at[y, x, lax.rem(z + step, 4)],
                line_in[k].at[step - 1],
                to_z[step - 1],
            )
            for step in (1, 2, 3)
        ]

    def start(copies):
        for copy in copies:
            copy.start()

    def arrived(copies):
        for copy in copies:
            copy.wait_recv()

    def products(k, half, store):
        slot = k % 3
        tile = 256

        @pl.loop(0, widths[k] // tile)
        def _(n):
            columns = pl.ds(pl.multiple_of(n * tile, tile), tile)
            left = left_in[slot, :, pl.ds(pl.multiple_of(half * half_rows, BLOCK), half_rows)]
            result = dot_rows(left, right_in[slot, :, columns])
            for i in range(16):
                at = (i // 8, (i // 4) % 2, i % 4, slice(None), columns)
                store(at, result[i * rows : (i + 1) * rows])

    def away_products(k):
        for copy in loads(k):
            copy.wait()
        if k >= 3:
            for copy in core_copies(k - 3):
                copy.wait_send()

        def store(at, value):
            away[(k % 3,) + at] = value.astype(jnp.bfloat16)

        products(k, 1 - c, store)
        start(core_copies(k))

    def own_products(k):
        def store(at, value):
            own[k][at] = (value + own[k][at].astype(jnp.float32)).astype(jnp.bfloat16)

        products(k, c, store)

    def first_sum(k):
        half = widths[k] // 2

        @pl.loop(0, 8)
        def _(i):
            two, at_z = i // 4, i % 4
            a_at = (two, x, at_z, slice(None), pl.ds(0, half))
            b_at = (y, two, at_z, slice(None), pl.ds(half, half))
            own[k][a_at] = own[k][a_at] + first_in[k][0, two, at_z]
            own[k][b_at] = own[k][b_at] + first_in[k][1, two, at_z]

    def second_sum(k):
        half = widths[k] // 2

        @pl.loop(0, 4)
        def _(at_z):
            a_at = (y, x, at_z, slice(None), pl.ds(0, half))
            b_at = (y, x, at_z, slice(None), pl.ds(half, half))
            own[k][a_at] = own[k][a_at] + second_in[k][0, at_z]
            own[k][b_at] = own[k][b_at] + second_in[k][1, at_z]

    all_start(modul_copy)
    for i in range(images):
        every_modul[me * images + i] = modul[i]
    for k in range(min(3, count)):
        start(loads(k))
    away_products(0)
    for t in range(count + 3):
        if t + 1 < count:
            away_products(t + 1)
        if t < count:
            arrived(core_copies(t))
            own_products(t)
            start(first_copies(t))
            if t + 3 < count:
                start(loads(t + 3))
        if 0 <= t - 1 < count:
            arrived(first_copies(t - 1))
            first_sum(t - 1)
            start(second_copies(t - 1))
        if 0 <= t - 2 < count:
            arrived(second_copies(t - 2))
            second_sum(t - 2)
            start(line_copies(t - 2))
        if 0 <= t - 3 < count:
            k = t - 3
            arrived(line_copies(k))
            total = own[k][y, x, z].astype(jnp.float32)
            for step in (1, 2, 3):
                total = total + line_in[k][step - 1].astype(jnp.float32)
            outs[k][...] = total.astype(jnp.bfloat16)
        if t == 3:
            image_parts()
        if t == 6:
            image_sums()
    all_arrived(sum_copy)
    for copy in (modul_copy, part_copy, sum_copy):
        all_sent(copy)
    for k in range(count):
        for copies in (core_copies, first_copies, second_copies, line_copies):
            if copies is core_copies and k + 3 < count:
                continue
            for copy in copies(k):
                copy.wait_send()


class RingPlan:
    def order_rows(self, values):
        shape = values.shape
        split = values.reshape((2, 2, 2, 4, D // 32) + shape[1:])
        return jnp.moveaxis(split, 0, 2).reshape(shape)

    def restore_rows(self, values):
        shape = values.shape
        split = values.reshape((2, 2, 2, 4, D // 32) + shape[1:])
        return jnp.moveaxis(split, 2, 0).reshape(shape)

    def gather(self, pieces, time_piece, info, low_slots):
        pieces = [time_piece] + list(pieces)
        widths = tuple(piece.shape[1] for piece in pieces)
        count, rows = len(pieces), D // 32
        all_images = 32 * info.shape[0]
        slots = low_slots.shape[1]
        room = -(-slots // 8) * 8
        size = sum(4 * D * width for width in widths)
        whole_shape = [(2, 2, 2, 4, rows, width) for width in widths]
        *whole, every_info, cond, modul = pl.pallas_call(
            lambda *refs: gather_kernel(widths, *refs),
            out_shape=[
                jax.ShapeDtypeStruct(shape, piece.dtype)
                for shape, piece in zip(whole_shape, pieces)
            ]
            + [
                jax.ShapeDtypeStruct((all_images,) + info.shape[1:], jnp.float32),
                jax.ShapeDtypeStruct((all_images, D), jnp.float32),
                jax.ShapeDtypeStruct((32, all_images // 32, room, BLOCK), jnp.float32),
            ],
            in_specs=[pl.BlockSpec(memory_space=pltpu.VMEM)] * (count + 2),
            out_specs=[pl.BlockSpec(memory_space=pl.ANY)] * count
            + [pl.BlockSpec(memory_space=pltpu.VMEM)] * 3,
            scratch_shapes=[
                pltpu.VMEM(whole_shape[0], jnp.bfloat16),
                pltpu.VMEM((all_images, room, BLOCK), jnp.float32),
                pltpu.SemaphoreType.DMA((count,)),
                pltpu.SemaphoreType.DMA((count, 8)),
                pltpu.SemaphoreType.DMA((count, 8)),
                pltpu.SemaphoreType.DMA,
                pltpu.SemaphoreType.DMA((2, 32)),
                pltpu.SemaphoreType.DMA((2, 32)),
            ],
            compiler_params=pltpu.CompilerParams(
                collective_id=0, has_side_effects=True, vmem_limit_bytes=GATHER_VMEM
            ),
            cost_estimate=pl.CostEstimate(flops=0, bytes_accessed=size, transcendentals=0),
        )(*pieces, info, jnp.swapaxes(low_slots, 0, 1))
        whole = [part.reshape(D, -1) for part in whole]
        modul = jnp.swapaxes(modul[:, :, :slots], 0, 1).reshape(-1, 32 * slots, BLOCK)
        return whole[1:], whole[0], every_info, cond, modul

    def scatter(self, grads, modul, pick, low_slots, edge, factor):
        lefts = [left.reshape(-1, D) for left, _ in grads]
        rights = [right.reshape(left.shape[0], -1) for (_, right), left in zip(grads, lefts)]
        widths = tuple(right.shape[1] for right in rights)
        count, rows, tokens = len(grads), D // 32, lefts[0].shape[0]
        widest = max(widths)
        images, slots = modul.shape[0], low_slots.shape[1]
        size = sum(4 * D * width for width in widths)
        scratch = [pltpu.VMEM((2, 2, 4, rows, width), jnp.bfloat16) for width in widths]
        scratch += [pltpu.VMEM((2, 2, 4, rows, width // 2), jnp.bfloat16) for width in widths]
        scratch += [pltpu.VMEM((2, 4, rows, width // 2), jnp.bfloat16) for width in widths]
        scratch += [pltpu.VMEM((3, rows, width), jnp.bfloat16) for width in widths]
        *scattered, chosen, shared = pl.pallas_call(
            lambda *refs: scatter_kernel(widths, slots, *refs),
            out_shape=[jax.ShapeDtypeStruct((rows, width), jnp.bfloat16) for width in widths]
            + [
                jax.ShapeDtypeStruct((32 * images, pick.shape[0], BLOCK), jnp.float32),
                jax.ShapeDtypeStruct((32,) + factor.shape, jnp.float32),
            ],
            in_specs=[pl.BlockSpec(memory_space=pl.ANY)] * (2 * count)
            + [pl.BlockSpec(memory_space=pltpu.VMEM)] * 5,
            out_specs=[pl.BlockSpec(memory_space=pltpu.VMEM)] * (count + 2),
            scratch_shapes=scratch
            + [
                pltpu.VMEM((3, tokens, D), jnp.bfloat16),
                pltpu.VMEM((3, tokens, widest), jnp.bfloat16),
                pltpu.VMEM((3, 2, 2, 4, rows, widest), jnp.bfloat16),
                pltpu.VMEM((32 * images,) + modul.shape[1:], jnp.bfloat16),
                pltpu.VMEM(edge.shape, jnp.float32),
                pltpu.VMEM((32,) + factor.shape, jnp.float32),
                pltpu.SemaphoreType.DMA((2, 3)),
                pltpu.SemaphoreType.DMA((count, 8)),
                pltpu.SemaphoreType.DMA((count, 8)),
                pltpu.SemaphoreType.DMA((2, 32)),
                pltpu.SemaphoreType.DMA((2, 32)),
                pltpu.SemaphoreType.DMA((2, 32)),
            ],
            compiler_params=pltpu.CompilerParams(
                collective_id=1, has_side_effects=True, vmem_limit_bytes=SCATTER_VMEM
            ),
            cost_estimate=pl.CostEstimate(flops=0, bytes_accessed=size, transcendentals=0),
        )(*lefts, *rights, modul, pick, jnp.swapaxes(low_slots, 0, 1), edge, factor)
        return scattered, chosen[:, :slots].astype(jnp.bfloat16), shared


class PlainPlan:
    def order_rows(self, values):
        return values

    def restore_rows(self, values):
        return values

    def gather(self, pieces, time_piece, info, low_slots):
        whole = [lax.all_gather(piece, AXES, axis=0, tiled=True) for piece in pieces]
        time_two = lax.all_gather(time_piece, AXES, axis=0, tiled=True)
        every_info = lax.all_gather(info, AXES, axis=0, tiled=True)
        blocks = D // BLOCK
        time_act = every_info[:, :blocks].reshape(-1, D).astype(jnp.bfloat16)
        cond = jnp.dot(time_act, time_two, preferred_element_type=jnp.float32)
        cond = cond + every_info[:, 8 : 8 + blocks].reshape(-1, D)
        modul = dot_low("gd,dsc->gsc", jax.nn.silu(cond).astype(jnp.bfloat16), low_slots)
        modul = lax.all_to_all(modul, AXES, split_axis=0, concat_axis=1, tiled=True)
        return whole, time_two, every_info, cond, modul

    def scatter(self, grads, modul, pick, low_slots, edge, factor):
        scattered = [
            lax.psum_scatter(row_product(*pair), AXES, scatter_dimension=0, tiled=True)
            for pair in grads
        ]
        slots = low_slots.shape[1]
        every = lax.all_gather(modul, AXES, axis=0, tiled=True)
        chosen = dot_low("su,guc->gsc", pick, every)[:, :slots].astype(jnp.bfloat16)
        part = dot_low("gsc,dsc->gd", chosen, low_slots).reshape(-1, D // BLOCK, BLOCK)
        parts = edge.at[:, : D // BLOCK].set(part)
        own = lax.psum_scatter(parts, AXES, scatter_dimension=0, tiled=True) * factor
        shared = lax.all_gather(own, AXES, axis=0, tiled=False)
        return scattered, chosen, shared


def unit_lists():
    dense = np.concatenate(
        [np.arange(l * LAYER_UNITS + ADA_UNITS, (l + 1) * LAYER_UNITS) for l in range(LAYERS)]
    )
    time_units = np.arange(TAIL_FIRST, TAIL_FIRST + TIME_UNITS)
    image_units = np.concatenate(
        [np.arange(l * LAYER_UNITS, l * LAYER_UNITS + ADA_UNITS) for l in range(LAYERS)]
        + [np.arange(TAIL_FIRST + TIME_UNITS, UNITS)]
    )
    return dense, time_units, image_units


def on_device(
    latents,
    noise,
    labels,
    t_index,
    owner,
    master,
    first_moment,
    second_moment,
    small,
    small_first,
    small_second,
):
    count = lax.axis_size("rep") * lax.axis_size("shard")
    me = lax.axis_index(AXES)
    slot_dev = master.shape[1]
    slot_total = count * slot_dev
    rows = D // count
    images = latents.shape[0]
    dense_units, time_units, image_units = unit_lists()

    unit_of_slot = (
        jnp.full((slot_total,), -1, jnp.int32).at[owner].set(jnp.arange(UNITS, dtype=jnp.int32))
    )
    my_unit = lax.dynamic_slice_in_dim(unit_of_slot, me * slot_dev, slot_dev)
    low_slots = master.astype(jnp.bfloat16)

    plan = RingPlan() if (lax.axis_size("rep"), lax.axis_size("shard")) == (8, 4) else PlainPlan()
    spread = lax.all_to_all(
        plan.order_rows(low_slots), AXES, split_axis=0, concat_axis=1, tiled=True
    )
    moved = np.concatenate([dense_units, time_units])
    unit_rows = jnp.take(spread, owner[moved], axis=1).reshape(rows, -1)
    pieces = []
    for l in range(LAYERS):
        base = l * DENSE_COLS
        cuts = (base, base + 4 * D, base + 4 * D + FF, base + DENSE_COLS)
        pieces += [unit_rows[:, cuts[i] : cuts[i + 1]] for i in range(3)]
    x_start = latents.astype(jnp.float32).reshape(-1, PATCHES, CHANNELS)
    noise_f = noise.astype(jnp.float32).reshape(-1, PATCHES, CHANNELS)
    times = (t_index.astype(jnp.float32) + 0.5) / TSTEPS
    noisy = (1.0 - times)[:, None, None] * x_start + times[:, None, None] * noise_f
    target = noise_f - x_start
    loss_weight = 1.0 + 3.0 * times
    small_low = small.astype(jnp.bfloat16)
    patch_w = small_low[:CHANNELS]
    time_w = small_low[CHANNELS : CHANNELS + FREQ]
    table = small[CHANNELS + FREQ : CHANNELS + FREQ + CLASSES]
    head_w = small_low[CHANNELS + FREQ + CLASSES :]
    noisy_low = noisy.astype(jnp.bfloat16)
    hidden = dot_low("gpc,cd->gpd", noisy_low, patch_w) + positions()

    blocks = D // BLOCK
    freq_own = frequencies(times).astype(jnp.bfloat16)
    time_own = jnp.dot(freq_own, time_w, preferred_element_type=jnp.float32)
    act_own = jax.nn.silu(time_own).astype(jnp.bfloat16).astype(jnp.float32)
    label_own = jnp.take(table, labels, axis=0)
    numbers = jnp.stack([t_index, labels], 1).astype(jnp.float32)
    info = jnp.concatenate(
        [
            act_own.reshape(images, blocks, BLOCK),
            jnp.pad(numbers, ((0, 0), (0, BLOCK - 2)))[:, None],
            jnp.zeros((images, 7 - blocks, BLOCK), jnp.float32),
            label_own.reshape(images, blocks, BLOCK),
            jnp.zeros((images, 8 - blocks, BLOCK), jnp.float32),
        ],
        1,
    )
    whole, time_two, every_info, cond_all, slot_modul = plan.gather(
        pieces, unit_rows[:, LAYERS * DENSE_COLS :], info, low_slots
    )
    all_images = cond_all.shape[0]
    every_time = (every_info[:, blocks, 0] + 0.5) / TSTEPS
    every_label = every_info[:, blocks, 1].astype(jnp.int32)
    weight_total = jnp.sum(1.0 + 3.0 * every_time) * PATCHES
    freq_low = frequencies(every_time).astype(jnp.bfloat16)
    time_pre = jnp.dot(freq_low, time_w, preferred_element_type=jnp.float32)
    time_act = every_info[:, :blocks].reshape(all_images, D).astype(jnp.bfloat16)
    weights_all = [
        (whole[3 * l][:, : 3 * D], whole[3 * l][:, 3 * D :], whole[3 * l + 1], whole[3 * l + 2])
        for l in range(LAYERS)
    ]
    cond = lax.dynamic_slice_in_dim(cond_all, me * images, images)
    cond_act = jax.nn.silu(cond_all).astype(jnp.bfloat16)
    modul_all = jnp.take(slot_modul, owner[image_units], axis=1).reshape(images, -1)

    saved_all = []
    for l in range(LAYERS):
        hidden, saved = layer_forward(
            hidden, modul_all[:, l * 6 * D : (l + 1) * 6 * D], weights_all[l]
        )
        saved_all.append(saved)
    shift_f, scale_f = jnp.split(modul_all[:, LAYERS * 6 * D :], 2, -1)
    normed_f = norm_rows(hidden)
    final_in = modulate(normed_f, shift_f, scale_f).astype(jnp.bfloat16)
    predict = dot_low("gpd,cd->gpc", final_in, head_w)
    error = predict - target
    loss_part = jnp.sum(loss_weight[:, None, None] * error * error) / CHANNELS
    grad_pred = (loss_weight[:, None, None] * 2.0 * error / CHANNELS).astype(jnp.bfloat16)
    grad_head = dot_low("gpc,gpd->cd", grad_pred, final_in)
    grad_final_in = dot_low("gpc,cd->gpd", grad_pred, head_w)
    grad_modul_f = jnp.concatenate(
        [jnp.sum(grad_final_in, 1), jnp.sum(grad_final_in * normed_f, 1)], -1
    ).astype(jnp.bfloat16)
    grad_hidden = local_back(norm_rows, hidden, grad_final_in * (1.0 + scale_f[:, None, :]))
    layer_grads = [None] * LAYERS
    grad_moduls = [None] * LAYERS
    for l in reversed(range(LAYERS)):
        grad_hidden, grad_moduls[l], layer_grads[l] = layer_backward(
            grad_hidden, weights_all[l], saved_all[l]
        )
    grad_embed = grad_hidden.astype(jnp.bfloat16)
    grad_patch = dot_low("gpc,gpd->cd", noisy_low, grad_embed)

    image_place = np.full((UNITS + 1,), -1, np.int32)
    image_place[image_units] = np.arange(len(image_units))
    my_place = jnp.asarray(image_place)[my_unit]
    room_slots, room_units = -(-slot_dev // 16) * 16, -(-len(image_units) // 16) * 16
    pick = jnp.pad(my_place, (0, room_slots - slot_dev), constant_values=-1)[:, None]
    pick = (pick == jnp.arange(room_units, dtype=jnp.int32)).astype(jnp.bfloat16)
    modul_grad = jnp.concatenate(grad_moduls + [grad_modul_f], -1).reshape(images, -1, BLOCK)
    modul_grad = jnp.pad(modul_grad, ((0, 0), (0, room_units - len(image_units)), (0, 0)))
    edge = jnp.concatenate([grad_patch, grad_head], 0)
    edge_room = max(all_images, 4 * CHANNELS)
    edge = jnp.concatenate([edge, jnp.broadcast_to(loss_part, (2 * CHANNELS, D))], 0)
    edge = jnp.pad(edge, ((0, edge_room - 4 * CHANNELS), (0, 0)))[:all_images]
    edge = jnp.pad(edge.reshape(all_images, blocks, BLOCK), ((0, 0), (8, 8 - blocks), (0, 0)))
    factor = local_back(jax.nn.silu, cond, jnp.ones_like(cond)).reshape(images, blocks, BLOCK)
    factor = jnp.pad(factor, ((0, 0), (0, 16 - blocks), (0, 0)), constant_values=1.0)
    order = list(reversed(range(LAYERS)))
    scattered, slot_grad_out, shared = plan.scatter(
        [grad for l in order for grad in reversed(layer_grads[l])],
        modul_grad, pick, low_slots, edge, factor,
    )
    grad_rows = {
        (l, 3 - i): scattered[4 * n + i] for n, l in enumerate(order) for i in range(4)
    }
    shared = shared.reshape(all_images, 16, BLOCK)
    grad_cond = shared[:, :blocks].reshape(all_images, D)
    edge = shared[:, 8 : 8 + blocks].reshape(all_images, D)
    grad_patch, grad_head = edge[:CHANNELS], edge[CHANNELS : 2 * CHANNELS]
    loss_sum = edge[2 * CHANNELS, 0]
    grad_time_out = grad_cond.astype(jnp.bfloat16)
    grad_time_act = dot_low("ge,de->gd", grad_time_out, time_two)
    grad_time_pre = local_back(jax.nn.silu, time_pre, grad_time_act).astype(jnp.bfloat16)
    grad_time_w = dot_low("gf,gd->fd", freq_low, grad_time_pre)
    grad_table = jnp.zeros((CLASSES, D), jnp.float32).at[every_label].add(grad_cond)
    small_grad = jnp.concatenate([grad_patch, grad_time_w, grad_table, grad_head], 0)

    my_time = jnp.clip(my_unit - TAIL_FIRST, 0, TIME_UNITS - 1)
    is_time = (my_unit >= TAIL_FIRST) & (my_unit < TAIL_FIRST + TIME_UNITS)
    time_cols = jnp.take(grad_time_out.reshape(all_images, TIME_UNITS, BLOCK), my_time, axis=1)
    is_image = my_place >= 0
    image_grad = dot_low("gd,gsc->dsc", cond_act, slot_grad_out)
    time_grad = dot_low("gd,gsc->dsc", time_act, time_cols)

    dense_place = np.full((UNITS + 1,), 0, np.int32)
    dense_place[dense_units] = np.arange(len(dense_units))
    slot_place = jnp.asarray(dense_place)[unit_of_slot]
    all_rows = jnp.concatenate(
        [
            grad_rows[l, i].reshape(rows, -1, BLOCK)
            for l in range(LAYERS)
            for i in range(4)
        ],
        1,
    )
    slot_rows = jnp.take(all_rows, slot_place, axis=1)
    dense_grad = plan.restore_rows(
        lax.all_to_all(slot_rows, AXES, split_axis=1, concat_axis=0, tiled=True)
    ).astype(jnp.float32)

    owned_grad = jnp.where(
        is_image[None, :, None],
        image_grad,
        jnp.where(is_time[None, :, None], time_grad, dense_grad),
    )
    used = (my_unit >= 0)[None, :, None]
    rate = rate_factor * unit_scale(jnp.maximum(my_unit, 0))[None, :, None]
    new_w, new_first, new_second = adam_update(
        master, first_moment, second_moment, owned_grad, rate
    )
    new_master = jnp.where(used, new_w, master)
    new_first = jnp.where(used, new_first, first_moment)
    new_second = jnp.where(used, new_second, second_moment)
    small_rate = rate_factor * table_scale(jnp.arange(small.shape[0], dtype=jnp.int32))[:, None]
    new_small, new_small_first, new_small_second = adam_update(
        small, small_first, small_second, small_grad, small_rate
    )
    return (
        loss_sum,
        weight_total,
        new_master,
        new_first,
        new_second,
        new_small,
        new_small_first,
        new_small_second,
    )


def solution(mesh):
    return jax.shard_map(
        on_device,
        mesh=mesh,
        in_specs=(
            P(("rep", "shard"), None),
            P(("rep", "shard"), None),
            P(("rep", "shard")),
            P(("rep", "shard")),
            P(),
            P(None, ("rep", "shard"), None),
            P(None, ("rep", "shard"), None),
            P(None, ("rep", "shard"), None),
            P(),
            P(),
            P(),
        ),
        out_specs=(
            P(),
            P(),
            P(None, ("rep", "shard"), None),
            P(None, ("rep", "shard"), None),
            P(None, ("rep", "shard"), None),
            P(),
            P(),
            P(),
        ),
        check_vma=False,
    )
```

```python
import jax
import jax.numpy as jnp
import numpy as np
from jax import lax
from jax.experimental import pallas as pl
from jax.experimental.pallas import tpu as pltpu
from jax.sharding import PartitionSpec as P

D = 768
HEADS = 12
HEAD_DIM = 64
FF = 3072
FREQ = 256
CLASSES = 1000
CHANNELS = 16
GRID = 16
PATCHES = 256
LAYERS = 2
TSTEPS = 1000
STEP = 10
BLOCK = 128
LAYER_COLS = 13824
LAYER_UNITS = 108
UNITS = 234

ADA_UNITS = 6 * D // BLOCK
DENSE_UNITS = LAYER_UNITS - ADA_UNITS
DENSE_COLS = DENSE_UNITS * BLOCK
TIME_UNITS = D // BLOCK
TAIL_FIRST = LAYERS * LAYER_UNITS
AXES = ("rep", "shard")


beta_one = 0.5
beta_two = 0.5
adam_eps = 1e-08
decay_rate = 0.1
rate_factor = 0.5


def gelu_tanh(values):
    return jax.nn.gelu(values, approximate=True)


def norm_rows(hidden):
    centered = hidden - jnp.mean(hidden, -1, keepdims=True)
    return centered * lax.rsqrt(jnp.mean(centered * centered, -1, keepdims=True) + 1e-06)


def local_back(function, primal, upstream):
    return jax.vjp(function, primal)[1](upstream)[0]


def dot_low(pattern, left_side, right_side):
    return jnp.einsum(pattern, left_side, right_side, preferred_element_type=jnp.float32)


def positions():
    quarter = D // 4
    angular = jnp.exp(-jnp.log(10000.0) * jnp.arange(quarter, dtype=jnp.float32) / quarter)
    patch_idx = jnp.arange(PATCHES, dtype=jnp.int32)
    row_pos = (patch_idx // GRID).astype(jnp.float32)[:, None] * angular
    col_pos = (patch_idx % GRID).astype(jnp.float32)[:, None] * angular
    return jnp.concatenate(
        [jnp.sin(col_pos), jnp.cos(col_pos), jnp.sin(row_pos), jnp.cos(row_pos)], -1
    )


def frequencies(times):
    half_size = FREQ // 2
    spacing = jnp.exp(-jnp.log(10000.0) * jnp.arange(half_size, dtype=jnp.float32) / half_size)
    angles = 1000.0 * times[:, None] * spacing
    return jnp.concatenate([jnp.cos(angles), jnp.sin(angles)], -1)


def unit_scale(unit_ids):
    column = unit_ids % LAYER_UNITS * BLOCK
    in_layer = unit_ids < LAYERS * LAYER_UNITS
    is_output = in_layer & (column >= 9 * D) & (column < 10 * D)
    is_down = in_layer & (column >= 10 * D + FF)
    factor = jnp.where(is_output, 4.0, jnp.where(is_down, 1.5 * (D / FF) ** 0.5, 1.0))
    return factor / D**0.5


def table_scale(row_ids):
    return jnp.where(
        row_ids < CHANNELS,
        CHANNELS ** (-0.5),
        jnp.where(
            row_ids < CHANNELS + FREQ,
            FREQ ** (-0.5),
            jnp.where(row_ids < CHANNELS + FREQ + CLASSES, 0.5, D ** (-0.5)),
        ),
    )


def adam_update(weight, first_mom, second, gradient, rate):
    first_new = beta_one * first_mom + (1.0 - beta_one) * gradient
    second_new = beta_two * second + (1.0 - beta_two) * gradient * gradient
    ratio = (
        first_new
        / (1.0 - beta_one**STEP)
        / (jnp.sqrt(second_new / (1.0 - beta_two**STEP)) + adam_eps)
    )
    return (weight - rate * (ratio + decay_rate * weight), first_new, second_new)


def split_heads(qkv_all):
    groups, length = (qkv_all.shape[0], qkv_all.shape[1])
    return tuple(
        (
            qkv_all[..., part_idx * D : (part_idx + 1) * D].reshape(groups, length, HEADS, HEAD_DIM)
            for part_idx in range(3)
        )
    )


def modulate(normed, shift, scale):
    return normed * (1.0 + scale[:, None, :]) + shift[:, None, :]


def layer_forward(hidden, modul, weights):
    w_qkv, w_out, w_up, w_down = weights
    groups = hidden.shape[0]
    shift_a, scale_a, gate_a, shift_b, scale_b, gate_b = jnp.split(modul, 6, -1)
    attn_in = modulate(norm_rows(hidden), shift_a, scale_a).astype(jnp.bfloat16)
    qkv_all = dot_low("gpd,de->gpe", attn_in, w_qkv).astype(jnp.bfloat16)
    queries, keys_all, values = split_heads(qkv_all)
    scores = dot_low("gqhe,gkhe->ghqk", queries, keys_all) * HEAD_DIM ** (-0.5)
    top_score = jnp.max(scores, -1, keepdims=True)
    log_total = top_score + jnp.log(jnp.sum(jnp.exp(scores - top_score), -1, keepdims=True))
    attn_prob = jnp.exp(scores - log_total).astype(jnp.bfloat16)
    heads_out = (
        dot_low("ghqk,gkhe->gqhe", attn_prob, values).astype(jnp.bfloat16).reshape(groups, -1, D)
    )
    branch_a = dot_low("gpd,de->gpe", heads_out, w_out)
    middle = hidden + gate_a[:, None, :] * branch_a
    mlp_in = modulate(norm_rows(middle), shift_b, scale_b).astype(jnp.bfloat16)
    pre_act = dot_low("gpd,df->gpf", mlp_in, w_up)
    post_act = gelu_tanh(pre_act).astype(jnp.bfloat16)
    branch_b = dot_low("gpf,df->gpd", post_act, w_down)
    output = middle + gate_b[:, None, :] * branch_b
    return (
        output,
        (
            hidden,
            modul,
            attn_in,
            qkv_all,
            log_total,
            heads_out,
            branch_a,
            middle,
            mlp_in,
            pre_act,
            post_act,
            branch_b,
        ),
    )


def layer_backward(grad_out, weights, saved):
    w_qkv, w_out, w_up, w_down = weights
    (
        hidden,
        modul,
        attn_in,
        qkv_all,
        log_total,
        heads_out,
        branch_a,
        middle,
        mlp_in,
        pre_act,
        post_act,
        branch_b,
    ) = saved
    groups = hidden.shape[0]
    shift_a, scale_a, gate_a, shift_b, scale_b, gate_b = jnp.split(modul, 6, -1)
    grad_gate_b = jnp.sum(grad_out * branch_b, 1)
    grad_branch_b = (gate_b[:, None, :] * grad_out).astype(jnp.bfloat16)
    grad_down = (grad_branch_b, post_act)
    grad_post = dot_low("gpd,df->gpf", grad_branch_b, w_down)
    grad_pre = local_back(gelu_tanh, pre_act, grad_post).astype(jnp.bfloat16)
    grad_up = (mlp_in, grad_pre)
    grad_mlp_in = dot_low("gpf,df->gpd", grad_pre, w_up)
    normed_b = norm_rows(middle)
    grad_scale_b = jnp.sum(grad_mlp_in * normed_b, 1)
    grad_shift_b = jnp.sum(grad_mlp_in, 1)
    grad_middle = grad_out + local_back(
        norm_rows, middle, grad_mlp_in * (1.0 + scale_b[:, None, :])
    )
    grad_gate_a = jnp.sum(grad_middle * branch_a, 1)
    grad_branch_a = (gate_a[:, None, :] * grad_middle).astype(jnp.bfloat16)
    grad_out_w = (heads_out, grad_branch_a)
    grad_heads = (
        dot_low("gpe,de->gpd", grad_branch_a, w_out)
        .astype(jnp.bfloat16)
        .reshape(groups, -1, HEADS, HEAD_DIM)
    )
    queries, keys_all, values = split_heads(qkv_all)
    scores = dot_low("gqhe,gkhe->ghqk", queries, keys_all) * HEAD_DIM ** (-0.5)
    attn_prob = jnp.exp(scores - log_total)
    grad_prob = dot_low("gqhe,gkhe->ghqk", grad_heads, values)
    grad_values = dot_low("ghqk,gqhe->gkhe", attn_prob.astype(jnp.bfloat16), grad_heads)
    inner_sum = jnp.sum(attn_prob * grad_prob, -1, keepdims=True)
    grad_scores = (HEAD_DIM ** (-0.5) * attn_prob * (grad_prob - inner_sum)).astype(jnp.bfloat16)
    grad_queries = dot_low("ghqk,gkhe->gqhe", grad_scores, keys_all)
    grad_keys = dot_low("ghqk,gqhe->gkhe", grad_scores, queries)
    grad_qkv = jnp.concatenate(
        [
            grad_queries.reshape(groups, -1, D),
            grad_keys.reshape(groups, -1, D),
            grad_values.reshape(groups, -1, D),
        ],
        -1,
    ).astype(jnp.bfloat16)
    grad_qkv_w = (attn_in, grad_qkv)
    grad_attn_in = dot_low("gpe,de->gpd", grad_qkv, w_qkv)
    normed_a = norm_rows(hidden)
    grad_scale_a = jnp.sum(grad_attn_in * normed_a, 1)
    grad_shift_a = jnp.sum(grad_attn_in, 1)
    grad_in = grad_middle + local_back(
        norm_rows, hidden, grad_attn_in * (1.0 + scale_a[:, None, :])
    )
    grad_modul = jnp.concatenate(
        [grad_shift_a, grad_scale_a, grad_gate_a, grad_shift_b, grad_scale_b, grad_gate_b], -1
    ).astype(jnp.bfloat16)
    return (grad_in, grad_modul, [grad_qkv_w, grad_out_w, grad_up, grad_down])


MESH = pl.DeviceIdType.MESH
GATHER_VMEM = 40 * 2**20
SCATTER_VMEM = 56 * 2**20


def dot_rows(left_side, right_side):
    return lax.dot_general(
        left_side, right_side, (((0,), (0,)), ((), ())), preferred_element_type=jnp.float32
    )


def row_product(left_side, right_side):
    left_side = left_side.reshape(-1, left_side.shape[-1])
    right_side = right_side.reshape(-1, right_side.shape[-1])
    return dot_rows(left_side, right_side).astype(jnp.bfloat16)


def place_of():
    rep = lax.axis_index("rep")
    return rep // 4, (rep // 2) % 2, rep % 2, lax.axis_index("shard")


def rep_of(y, x, c):
    return (y * 2 + x) * 2 + c


def device_at(j):
    shards = lax.axis_size("shard")
    devices = lax.axis_size("rep") * shards
    me = lax.axis_index("rep") * shards + lax.axis_index("shard")
    peer = lax.rem(me + j, devices)
    return peer, (peer // shards, lax.rem(peer, shards))


def meet_all(devices):
    barrier = pltpu.get_barrier_semaphore()

    @pl.loop(1, devices)
    def _(j):
        pl.semaphore_signal(barrier, inc=1, device_id=device_at(j)[1], device_id_type=MESH)

    pl.semaphore_wait(barrier, devices - 1)


def neighbours():
    y, x, c, z = place_of()
    to_x = (rep_of(y, 1 - x, c), z)
    to_y = (rep_of(1 - y, x, c), z)
    to_core = (rep_of(y, x, 1 - c), z)
    to_z = [(rep_of(y, x, c), lax.rem(z + step, 4)) for step in (1, 2, 3)]
    return to_x, to_y, to_core, to_z


def gather_kernel(widths, *refs):
    count = len(widths)
    pieces = refs[:count]
    info, low_slots = refs[count : count + 2]
    outs = refs[count + 2 : 2 * count + 2]
    every_info, cond_out, modul_out = refs[2 * count + 2 : 2 * count + 5]
    time_two, parts, own_sem, send_sem, recv_sem, time_sem, modul_sem, info_sem = refs[
        2 * count + 5 :
    ]
    devices, images = modul_out.shape[:2]
    slots = low_slots.shape[0]
    y, x, c, z = place_of()
    to_x, to_y, to_core, to_z = neighbours()
    me = rep_of(y, x, c) * 4 + z
    meet_all(devices)

    def remote(k, number, source, dest, target):
        return pltpu.make_async_remote_copy(
            src_ref=source,
            dst_ref=dest,
            send_sem=send_sem.at[k, number],
            recv_sem=recv_sem.at[k, number],
            device_id=target,
            device_id_type=MESH,
        )

    def own_copy(k):
        return pltpu.make_async_copy(pieces[k], outs[k].at[c, y, x, z], own_sem.at[k])

    def line_copies(k, arriving):
        copies = []
        for step in (1, 2, 3):
            at_z = lax.rem(z + 4 - step, 4) if arriving else z
            copies.append(
                remote(k, step - 1, pieces[k], outs[k].at[c, y, x, at_z], to_z[step - 1])
            )
        return copies

    def first_copies(k, arriving):
        half = widths[k] // 2
        left, right = pl.ds(0, half), pl.ds(half, half)
        at_x = 1 - x if arriving else x
        at_y = 1 - y if arriving else y
        a_block = outs[k].at[c, y, at_x, :, :, left]
        b_block = outs[k].at[c, at_y, x, :, :, right]
        return [remote(k, 3, a_block, a_block, to_x), remote(k, 4, b_block, b_block, to_y)]

    def second_copies(k, arriving):
        half = widths[k] // 2
        left, right = pl.ds(0, half), pl.ds(half, half)
        at_x = 1 - x if arriving else x
        at_y = 1 - y if arriving else y
        a_block = outs[k].at[c, at_y, :, :, :, left]
        b_block = outs[k].at[c, :, at_x, :, :, right]
        return [remote(k, 5, a_block, a_block, to_y), remote(k, 6, b_block, b_block, to_x)]

    def core_copies(k, arriving):
        block = outs[k].at[1 - c if arriving else c]
        return [remote(k, 7, block, block, to_core)]

    def start(copies):
        for copy in copies:
            copy.start()

    def arrived(copies):
        for copy in copies:
            copy.wait_recv()

    def modul_copy(j, arriving):
        peer, where = device_at(devices - j if arriving else j)
        return pltpu.make_async_remote_copy(
            src_ref=parts.at[pl.ds(peer * images, images)],
            dst_ref=modul_out.at[peer if arriving else me],
            send_sem=modul_sem.at[0, j],
            recv_sem=modul_sem.at[1, j],
            device_id=where,
            device_id_type=MESH,
        )

    def info_copy(j, arriving):
        peer, where = device_at(devices - j if arriving else j)
        return pltpu.make_async_remote_copy(
            src_ref=info,
            dst_ref=every_info.at[pl.ds((peer if arriving else me) * images, images)],
            send_sem=info_sem.at[0, j],
            recv_sem=info_sem.at[1, j],
            device_id=where,
            device_id_type=MESH,
        )

    def info_rows(first):
        return jnp.concatenate([every_info[:, first + j, :] for j in range(D // BLOCK)], -1)

    def image_products():
        copy = pltpu.make_async_copy(outs[0], time_two, time_sem)
        copy.start()

        @pl.loop(1, devices)
        def _(j):
            info_copy(j, True).wait_recv()
            info_copy(j, False).wait_send()

        copy.wait()
        weight = time_two[...].astype(jnp.float32).reshape(D, D).astype(jnp.bfloat16)
        cond = jnp.dot(
            info_rows(0).astype(jnp.bfloat16), weight, preferred_element_type=jnp.float32
        )
        cond = cond + info_rows(8)
        cond_out[...] = cond
        act = (cond * jax.nn.sigmoid(cond)).astype(jnp.bfloat16)
        for s in range(slots):
            parts[:, s, :] = jnp.dot(act, low_slots[s], preferred_element_type=jnp.float32)
        for i in range(images):
            modul_out[me, i] = parts[me * images + i]

        @pl.loop(1, devices)
        def _(j):
            modul_copy(j, False).start()

    @pl.loop(1, devices)
    def _(j):
        info_copy(j, False).start()

    for i in range(images):
        every_info[me * images + i] = info[i]
    for k in range(count):
        own_copy(k).start()
    start(line_copies(0, False))
    for t in range(count + 2):
        if t + 1 < count:
            start(line_copies(t + 1, False))
        if t < count:
            own_copy(t).wait()
            arrived(line_copies(t, True))
            start(first_copies(t, False))
        if 0 <= t - 1 < count:
            arrived(first_copies(t - 1, True))
            start(second_copies(t - 1, False))
        if 0 <= t - 2 < count:
            arrived(second_copies(t - 2, True))
            start(core_copies(t - 2, False))
        if t == 3:
            arrived(core_copies(0, True))
            image_products()
    for k in range(1, count):
        arrived(core_copies(k, True))

    @pl.loop(1, devices)
    def _(j):
        modul_copy(j, True).wait_recv()
        modul_copy(j, False).wait_send()

    for k in range(count):
        for copies in (line_copies, first_copies, second_copies, core_copies):
            for copy in copies(k, False):
                copy.wait_send()


def scatter_kernel(widths, slots, *refs):
    count = len(widths)
    lefts, rights = refs[:count], refs[count : 2 * count]
    modul, pick, low_slots, edge, factor = refs[2 * count : 2 * count + 5]
    outs = refs[2 * count + 5 : 3 * count + 5]
    chosen, shared = refs[3 * count + 5 : 3 * count + 7]
    scratch = refs[3 * count + 7 :]
    own, first_in, second_in, line_in = (scratch[i * count : (i + 1) * count] for i in range(4))
    (
        left_in, left_turned, right_in, away, every_modul, parts, landed,
        load_sem, send_sem, recv_sem, modul_sem, part_sem, sum_sem,
    ) = scratch[4 * count :]
    devices, images = shared.shape[:2]
    y, x, c, z = place_of()
    to_x, to_y, to_core, to_z = neighbours()
    me = rep_of(y, x, c) * 4 + z
    rows = D // 32
    half_rows = D // 2
    meet_all(devices)

    def exchange(source, dest, sem, j, arriving):
        peer, where = device_at(devices - j if arriving else j)
        return pltpu.make_async_remote_copy(
            src_ref=source(peer, me),
            dst_ref=dest(peer if arriving else me),
            send_sem=sem.at[0, j],
            recv_sem=sem.at[1, j],
            device_id=where,
            device_id_type=MESH,
        )

    def modul_copies(step, arriving):
        if step == 0:
            copies = []
            for number in (1, 2, 3):
                at_z = lax.rem(z + 4 - number, 4) if arriving else z
                copies.append((modul, every_modul.at[y, x, c, at_z], to_z[number - 1]))
        else:
            at_x = 1 - x if arriving and step == 1 else x
            at_y = 1 - y if arriving and step == 2 else y
            at_c = 1 - c if arriving and step == 3 else c
            block = (
                every_modul.at[y, at_x, c],
                every_modul.at[at_y, :, c],
                every_modul.at[:, :, at_c],
            )[step - 1]
            copies = [(block, block, (to_x, to_y, to_core)[step - 1])]
        return [
            pltpu.make_async_remote_copy(
                src_ref=source,
                dst_ref=dest,
                send_sem=modul_sem.at[0, step, number],
                recv_sem=modul_sem.at[1, step, number],
                device_id=target,
                device_id_type=MESH,
            )
            for number, (source, dest, target) in enumerate(copies)
        ]

    def part_copy(j, arriving):
        return exchange(
            lambda peer, mine: parts.at[pl.ds(peer * images, images)],
            lambda owner: landed.at[owner],
            part_sem, j, arriving,
        )

    def sum_copy(j, arriving):
        return exchange(
            lambda peer, mine: shared.at[mine], lambda owner: shared.at[owner], sum_sem, j, arriving
        )

    def all_start(copy):
        @pl.loop(1, devices)
        def _(j):
            copy(j, False).start()

    def all_arrived(copy):
        @pl.loop(1, devices)
        def _(j):
            copy(j, True).wait_recv()

    def all_sent(copy):
        @pl.loop(1, devices)
        def _(j):
            copy(j, False).wait_send()

    def image_parts():
        arrived(modul_copies(3, True))

        @pl.loop(0, devices // 4)
        def _(i):
            for n in range(4):
                for m in range(images):
                    block = every_modul[i // 4, (i // 2) % 2, i % 2, n, m]
                    chosen[(i * 4 + n) * images + m] = jnp.dot(
                        pick[...], block, preferred_element_type=jnp.float32
                    )

        total = jnp.zeros((devices * images, D), jnp.float32)
        for s in range(slots):
            total = total + lax.dot_general(
                chosen[:, s, :].astype(jnp.bfloat16),
                low_slots[s],
                (((1,), (1,)), ((), ())),
                preferred_element_type=jnp.float32,
            )
        parts[...] = edge[...]
        for j in range(D // BLOCK):
            parts[:, j, :] = total[:, j * BLOCK : (j + 1) * BLOCK]
        all_start(part_copy)
        for i in range(images):
            landed[me, i] = parts[me * images + i]

    def image_sums():
        all_arrived(part_copy)
        shared[me] = jnp.sum(landed[...], 0) * factor[...]
        all_start(sum_copy)

    def remote(k, number, source, dest, target):
        return pltpu.make_async_remote_copy(
            src_ref=source,
            dst_ref=dest,
            send_sem=send_sem.at[k, number],
            recv_sem=recv_sem.at[k, number],
            device_id=target,
            device_id_type=MESH,
        )

    def load_left(k):
        return pltpu.make_async_copy(lefts[k], left_in.at[k % 2], load_sem.at[0, k % 2])

    def load_right(k):
        place = right_in.at[k % 3, :, pl.ds(0, widths[k])]
        return pltpu.make_async_copy(rights[k], place, load_sem.at[1, k % 3])

    def core_copies(k):
        source = away.at[k % 3, :, :, :, :, pl.ds(0, widths[k])]
        return [remote(k, 0, source, own[k], to_core)]

    def first_copies(k):
        half = widths[k] // 2
        return [
            remote(k, 1, own[k].at[:, 1 - x, :, :, pl.ds(0, half)], first_in[k].at[0], to_x),
            remote(k, 2, own[k].at[1 - y, :, :, :, pl.ds(half, half)], first_in[k].at[1], to_y),
        ]

    def second_copies(k):
        half = widths[k] // 2
        return [
            remote(k, 3, own[k].at[1 - y, x, :, :, pl.ds(0, half)], second_in[k].at[0], to_y),
            remote(k, 4, own[k].at[y, 1 - x, :, :, pl.ds(half, half)], second_in[k].at[1], to_x),
        ]

    def line_copies(k):
        return [
            remote(
                k,
                4 + step,
                own[k].at[y, x, lax.rem(z + step, 4)],
                line_in[k].at[step - 1],
                to_z[step - 1],
            )
            for step in (1, 2, 3)
        ]

    def start(copies):
        for copy in copies:
            copy.start()

    def arrived(copies):
        for copy in copies:
            copy.wait_recv()

    def products(k, half, store):
        slot = k % 3
        tile = D

        @pl.loop(0, widths[k] // tile)
        def _(n):
            columns = pl.ds(pl.multiple_of(n * tile, tile), tile)
            left = left_turned[slot, pl.ds(pl.multiple_of(half * half_rows, half_rows), half_rows)]
            result = jnp.dot(left, right_in[slot, :, columns], preferred_element_type=jnp.float32)
            for i in range(16):
                at = (i // 8, (i // 4) % 2, i % 4, slice(None), columns)
                store(at, result[i * rows : (i + 1) * rows])

    def away_products(k):
        load_left(k).wait()
        load_right(k).wait()
        left_turned[k % 3] = left_in[k % 2].T
        if k + 2 < count:
            load_left(k + 2).start()
        if k >= 3:
            for copy in core_copies(k - 3):
                copy.wait_send()

        def store(at, value):
            away[(k % 3,) + at] = value.astype(jnp.bfloat16)

        products(k, 1 - c, store)
        start(core_copies(k))

    def own_products(k):
        def store(at, value):
            own[k][at] = (value + own[k][at].astype(jnp.float32)).astype(jnp.bfloat16)

        products(k, c, store)

    def first_sum(k):
        half = widths[k] // 2

        @pl.loop(0, 8)
        def _(i):
            two, at_z = i // 4, i % 4
            a_at = (two, x, at_z, slice(None), pl.ds(0, half))
            b_at = (y, two, at_z, slice(None), pl.ds(half, half))
            own[k][a_at] = own[k][a_at] + first_in[k][0, two, at_z]
            own[k][b_at] = own[k][b_at] + first_in[k][1, two, at_z]

    def second_sum(k):
        half = widths[k] // 2

        @pl.loop(0, 4)
        def _(at_z):
            a_at = (y, x, at_z, slice(None), pl.ds(0, half))
            b_at = (y, x, at_z, slice(None), pl.ds(half, half))
            own[k][a_at] = own[k][a_at] + second_in[k][0, at_z]
            own[k][b_at] = own[k][b_at] + second_in[k][1, at_z]

    start(modul_copies(0, False))
    every_modul[y, x, c, z] = modul[...]
    for k in range(min(3, count)):
        load_right(k).start()
        if k < 2:
            load_left(k).start()
    away_products(0)
    for t in range(count + 3):
        if t + 1 < count:
            away_products(t + 1)
        if t < count:
            arrived(core_copies(t))
            own_products(t)
            start(first_copies(t))
            if t + 3 < count:
                load_right(t + 3).start()
        if 0 <= t - 1 < count:
            arrived(first_copies(t - 1))
            first_sum(t - 1)
            start(second_copies(t - 1))
        if 0 <= t - 2 < count:
            arrived(second_copies(t - 2))
            second_sum(t - 2)
            start(line_copies(t - 2))
        if 0 <= t - 3 < count:
            k = t - 3
            arrived(line_copies(k))
            total = own[k][y, x, z].astype(jnp.float32)
            for step in (1, 2, 3):
                total = total + line_in[k][step - 1].astype(jnp.float32)
            outs[k][...] = total.astype(jnp.bfloat16)
        if t < 3:
            arrived(modul_copies(t, True))
            start(modul_copies(t + 1, False))
        if t == 3:
            image_parts()
        if t == 6:
            image_sums()
    all_arrived(sum_copy)
    for copy in (part_copy, sum_copy):
        all_sent(copy)
    for step in range(4):
        for copy in modul_copies(step, False):
            copy.wait_send()
    for k in range(count):
        for copies in (core_copies, first_copies, second_copies, line_copies):
            if copies is core_copies and k + 3 < count:
                continue
            for copy in copies(k):
                copy.wait_send()


class RingPlan:
    def order_rows(self, values):
        shape = values.shape
        split = values.reshape((2, 2, 2, 4, D // 32) + shape[1:])
        return jnp.moveaxis(split, 0, 2).reshape(shape)

    def restore_rows(self, values):
        shape = values.shape
        split = values.reshape((2, 2, 2, 4, D // 32) + shape[1:])
        return jnp.moveaxis(split, 2, 0).reshape(shape)

    def gather(self, pieces, time_piece, info, low_slots):
        pieces = [time_piece] + list(pieces)
        widths = tuple(piece.shape[1] for piece in pieces)
        count, rows = len(pieces), D // 32
        all_images = 32 * info.shape[0]
        slots = low_slots.shape[1]
        room = -(-slots // 8) * 8
        size = sum(4 * D * width for width in widths)
        whole_shape = [(2, 2, 2, 4, rows, width) for width in widths]
        *whole, every_info, cond, modul = pl.pallas_call(
            lambda *refs: gather_kernel(widths, *refs),
            out_shape=[
                jax.ShapeDtypeStruct(shape, piece.dtype)
                for shape, piece in zip(whole_shape, pieces)
            ]
            + [
                jax.ShapeDtypeStruct((all_images,) + info.shape[1:], jnp.float32),
                jax.ShapeDtypeStruct((all_images, D), jnp.float32),
                jax.ShapeDtypeStruct((32, all_images // 32, room, BLOCK), jnp.float32),
            ],
            in_specs=[pl.BlockSpec(memory_space=pltpu.VMEM)] * (count + 2),
            out_specs=[pl.BlockSpec(memory_space=pl.ANY)] * count
            + [pl.BlockSpec(memory_space=pltpu.VMEM)] * 3,
            scratch_shapes=[
                pltpu.VMEM(whole_shape[0], jnp.bfloat16),
                pltpu.VMEM((all_images, room, BLOCK), jnp.float32),
                pltpu.SemaphoreType.DMA((count,)),
                pltpu.SemaphoreType.DMA((count, 8)),
                pltpu.SemaphoreType.DMA((count, 8)),
                pltpu.SemaphoreType.DMA,
                pltpu.SemaphoreType.DMA((2, 32)),
                pltpu.SemaphoreType.DMA((2, 32)),
            ],
            compiler_params=pltpu.CompilerParams(
                collective_id=0, has_side_effects=True, vmem_limit_bytes=GATHER_VMEM
            ),
            cost_estimate=pl.CostEstimate(flops=0, bytes_accessed=size, transcendentals=0),
        )(*pieces, info, jnp.swapaxes(low_slots, 0, 1))
        whole = [part.reshape(D, -1) for part in whole]
        modul = jnp.swapaxes(modul[:, :, :slots], 0, 1).reshape(-1, 32 * slots, BLOCK)
        return whole[1:], whole[0], every_info, cond, modul

    def scatter(self, grads, modul, pick, low_slots, edge, factor):
        lefts = [left.reshape(-1, D) for left, _ in grads]
        rights = [right.reshape(left.shape[0], -1) for (_, right), left in zip(grads, lefts)]
        widths = tuple(right.shape[1] for right in rights)
        count, rows, tokens = len(grads), D // 32, lefts[0].shape[0]
        widest = max(widths)
        images, slots = modul.shape[0], low_slots.shape[1]
        size = sum(4 * D * width for width in widths)
        scratch = [pltpu.VMEM((2, 2, 4, rows, width), jnp.bfloat16) for width in widths]
        scratch += [pltpu.VMEM((2, 2, 4, rows, width // 2), jnp.bfloat16) for width in widths]
        scratch += [pltpu.VMEM((2, 4, rows, width // 2), jnp.bfloat16) for width in widths]
        scratch += [pltpu.VMEM((3, rows, width), jnp.bfloat16) for width in widths]
        *scattered, chosen, shared = pl.pallas_call(
            lambda *refs: scatter_kernel(widths, slots, *refs),
            out_shape=[jax.ShapeDtypeStruct((rows, width), jnp.bfloat16) for width in widths]
            + [
                jax.ShapeDtypeStruct((32 * images, pick.shape[0], BLOCK), jnp.float32),
                jax.ShapeDtypeStruct((32,) + factor.shape, jnp.float32),
            ],
            in_specs=[pl.BlockSpec(memory_space=pl.ANY)] * (2 * count)
            + [pl.BlockSpec(memory_space=pltpu.VMEM)] * 5,
            out_specs=[pl.BlockSpec(memory_space=pltpu.VMEM)] * (count + 2),
            scratch_shapes=scratch
            + [
                pltpu.VMEM((2, tokens, D), jnp.bfloat16),
                pltpu.VMEM((3, D, tokens), jnp.bfloat16),
                pltpu.VMEM((3, tokens, widest), jnp.bfloat16),
                pltpu.VMEM((3, 2, 2, 4, rows, widest), jnp.bfloat16),
                pltpu.VMEM((2, 2, 2, 4) + modul.shape, jnp.bfloat16),
                pltpu.VMEM(edge.shape, jnp.float32),
                pltpu.VMEM((32,) + factor.shape, jnp.float32),
                pltpu.SemaphoreType.DMA((2, 3)),
                pltpu.SemaphoreType.DMA((count, 8)),
                pltpu.SemaphoreType.DMA((count, 8)),
                pltpu.SemaphoreType.DMA((2, 4, 3)),
                pltpu.SemaphoreType.DMA((2, 32)),
                pltpu.SemaphoreType.DMA((2, 32)),
            ],
            compiler_params=pltpu.CompilerParams(
                collective_id=1, has_side_effects=True, vmem_limit_bytes=SCATTER_VMEM
            ),
            cost_estimate=pl.CostEstimate(flops=0, bytes_accessed=size, transcendentals=0),
        )(*lefts, *rights, modul, pick, jnp.swapaxes(low_slots, 0, 1), edge, factor)
        return scattered, chosen[:, :slots].astype(jnp.bfloat16), shared


class PlainPlan:
    def order_rows(self, values):
        return values

    def restore_rows(self, values):
        return values

    def gather(self, pieces, time_piece, info, low_slots):
        whole = [lax.all_gather(piece, AXES, axis=0, tiled=True) for piece in pieces]
        time_two = lax.all_gather(time_piece, AXES, axis=0, tiled=True)
        every_info = lax.all_gather(info, AXES, axis=0, tiled=True)
        blocks = D // BLOCK
        time_act = every_info[:, :blocks].reshape(-1, D).astype(jnp.bfloat16)
        cond = jnp.dot(time_act, time_two, preferred_element_type=jnp.float32)
        cond = cond + every_info[:, 8 : 8 + blocks].reshape(-1, D)
        modul = dot_low("gd,dsc->gsc", jax.nn.silu(cond).astype(jnp.bfloat16), low_slots)
        modul = lax.all_to_all(modul, AXES, split_axis=0, concat_axis=1, tiled=True)
        return whole, time_two, every_info, cond, modul

    def scatter(self, grads, modul, pick, low_slots, edge, factor):
        scattered = [
            lax.psum_scatter(row_product(*pair), AXES, scatter_dimension=0, tiled=True)
            for pair in grads
        ]
        slots = low_slots.shape[1]
        every = lax.all_gather(modul, AXES, axis=0, tiled=True)
        chosen = dot_low("su,guc->gsc", pick, every)[:, :slots].astype(jnp.bfloat16)
        part = dot_low("gsc,dsc->gd", chosen, low_slots).reshape(-1, D // BLOCK, BLOCK)
        parts = edge.at[:, : D // BLOCK].set(part)
        own = lax.psum_scatter(parts, AXES, scatter_dimension=0, tiled=True) * factor
        shared = lax.all_gather(own, AXES, axis=0, tiled=False)
        return scattered, chosen, shared


def unit_lists():
    dense = np.concatenate(
        [np.arange(l * LAYER_UNITS + ADA_UNITS, (l + 1) * LAYER_UNITS) for l in range(LAYERS)]
    )
    time_units = np.arange(TAIL_FIRST, TAIL_FIRST + TIME_UNITS)
    image_units = np.concatenate(
        [np.arange(l * LAYER_UNITS, l * LAYER_UNITS + ADA_UNITS) for l in range(LAYERS)]
        + [np.arange(TAIL_FIRST + TIME_UNITS, UNITS)]
    )
    return dense, time_units, image_units


def on_device(
    latents,
    noise,
    labels,
    t_index,
    owner,
    master,
    first_moment,
    second_moment,
    small,
    small_first,
    small_second,
):
    count = lax.axis_size("rep") * lax.axis_size("shard")
    me = lax.axis_index(AXES)
    slot_dev = master.shape[1]
    slot_total = count * slot_dev
    rows = D // count
    images = latents.shape[0]
    dense_units, time_units, image_units = unit_lists()

    unit_of_slot = (
        jnp.full((slot_total,), -1, jnp.int32).at[owner].set(jnp.arange(UNITS, dtype=jnp.int32))
    )
    my_unit = lax.dynamic_slice_in_dim(unit_of_slot, me * slot_dev, slot_dev)
    low_slots = master.astype(jnp.bfloat16)

    plan = RingPlan() if (lax.axis_size("rep"), lax.axis_size("shard")) == (8, 4) else PlainPlan()
    spread = lax.all_to_all(
        plan.order_rows(low_slots), AXES, split_axis=0, concat_axis=1, tiled=True
    )
    moved = np.concatenate([dense_units, time_units])
    unit_rows = jnp.take(spread, owner[moved], axis=1).reshape(rows, -1)
    pieces = []
    for l in range(LAYERS):
        base = l * DENSE_COLS
        cuts = (base, base + 4 * D, base + 4 * D + FF, base + DENSE_COLS)
        pieces += [unit_rows[:, cuts[i] : cuts[i + 1]] for i in range(3)]
    x_start = latents.astype(jnp.float32).reshape(-1, PATCHES, CHANNELS)
    noise_f = noise.astype(jnp.float32).reshape(-1, PATCHES, CHANNELS)
    times = (t_index.astype(jnp.float32) + 0.5) / TSTEPS
    noisy = (1.0 - times)[:, None, None] * x_start + times[:, None, None] * noise_f
    target = noise_f - x_start
    loss_weight = 1.0 + 3.0 * times
    small_low = small.astype(jnp.bfloat16)
    patch_w = small_low[:CHANNELS]
    time_w = small_low[CHANNELS : CHANNELS + FREQ]
    table = small[CHANNELS + FREQ : CHANNELS + FREQ + CLASSES]
    head_w = small_low[CHANNELS + FREQ + CLASSES :]
    noisy_low = noisy.astype(jnp.bfloat16)
    hidden = dot_low("gpc,cd->gpd", noisy_low, patch_w) + positions()

    blocks = D // BLOCK
    freq_own = frequencies(times).astype(jnp.bfloat16)
    time_own = jnp.dot(freq_own, time_w, preferred_element_type=jnp.float32)
    act_own = jax.nn.silu(time_own).astype(jnp.bfloat16).astype(jnp.float32)
    label_own = jnp.take(table, labels, axis=0)
    numbers = jnp.stack([t_index, labels], 1).astype(jnp.float32)
    info = jnp.concatenate(
        [
            act_own.reshape(images, blocks, BLOCK),
            jnp.pad(numbers, ((0, 0), (0, BLOCK - 2)))[:, None],
            jnp.zeros((images, 7 - blocks, BLOCK), jnp.float32),
            label_own.reshape(images, blocks, BLOCK),
            jnp.zeros((images, 8 - blocks, BLOCK), jnp.float32),
        ],
        1,
    )
    whole, time_two, every_info, cond_all, slot_modul = plan.gather(
        pieces, unit_rows[:, LAYERS * DENSE_COLS :], info, low_slots
    )
    all_images = cond_all.shape[0]
    every_time = (every_info[:, blocks, 0] + 0.5) / TSTEPS
    every_label = every_info[:, blocks, 1].astype(jnp.int32)
    weight_total = jnp.sum(1.0 + 3.0 * every_time) * PATCHES
    freq_low = frequencies(every_time).astype(jnp.bfloat16)
    time_pre = jnp.dot(freq_low, time_w, preferred_element_type=jnp.float32)
    time_act = every_info[:, :blocks].reshape(all_images, D).astype(jnp.bfloat16)
    weights_all = [
        (whole[3 * l][:, : 3 * D], whole[3 * l][:, 3 * D :], whole[3 * l + 1], whole[3 * l + 2])
        for l in range(LAYERS)
    ]
    cond = lax.dynamic_slice_in_dim(cond_all, me * images, images)
    cond_act = jax.nn.silu(cond_all).astype(jnp.bfloat16)
    modul_all = jnp.take(slot_modul, owner[image_units], axis=1).reshape(images, -1)

    saved_all = []
    for l in range(LAYERS):
        hidden, saved = layer_forward(
            hidden, modul_all[:, l * 6 * D : (l + 1) * 6 * D], weights_all[l]
        )
        saved_all.append(saved)
    shift_f, scale_f = jnp.split(modul_all[:, LAYERS * 6 * D :], 2, -1)
    normed_f = norm_rows(hidden)
    final_in = modulate(normed_f, shift_f, scale_f).astype(jnp.bfloat16)
    predict = dot_low("gpd,cd->gpc", final_in, head_w)
    error = predict - target
    loss_part = jnp.sum(loss_weight[:, None, None] * error * error) / CHANNELS
    grad_pred = (loss_weight[:, None, None] * 2.0 * error / CHANNELS).astype(jnp.bfloat16)
    grad_head = dot_low("gpc,gpd->cd", grad_pred, final_in)
    grad_final_in = dot_low("gpc,cd->gpd", grad_pred, head_w)
    grad_modul_f = jnp.concatenate(
        [jnp.sum(grad_final_in, 1), jnp.sum(grad_final_in * normed_f, 1)], -1
    ).astype(jnp.bfloat16)
    grad_hidden = local_back(norm_rows, hidden, grad_final_in * (1.0 + scale_f[:, None, :]))
    layer_grads = [None] * LAYERS
    grad_moduls = [None] * LAYERS
    for l in reversed(range(LAYERS)):
        grad_hidden, grad_moduls[l], layer_grads[l] = layer_backward(
            grad_hidden, weights_all[l], saved_all[l]
        )
    grad_embed = grad_hidden.astype(jnp.bfloat16)
    grad_patch = dot_low("gpc,gpd->cd", noisy_low, grad_embed)

    image_place = np.full((UNITS + 1,), -1, np.int32)
    image_place[image_units] = np.arange(len(image_units))
    my_place = jnp.asarray(image_place)[my_unit]
    room_slots, room_units = -(-slot_dev // 16) * 16, -(-len(image_units) // 16) * 16
    pick = jnp.pad(my_place, (0, room_slots - slot_dev), constant_values=-1)[:, None]
    pick = (pick == jnp.arange(room_units, dtype=jnp.int32)).astype(jnp.bfloat16)
    modul_grad = jnp.concatenate(grad_moduls + [grad_modul_f], -1).reshape(images, -1, BLOCK)
    modul_grad = jnp.pad(modul_grad, ((0, 0), (0, room_units - len(image_units)), (0, 0)))
    edge = jnp.concatenate([grad_patch, grad_head], 0)
    edge_room = max(all_images, 4 * CHANNELS)
    edge = jnp.concatenate([edge, jnp.broadcast_to(loss_part, (2 * CHANNELS, D))], 0)
    edge = jnp.pad(edge, ((0, edge_room - 4 * CHANNELS), (0, 0)))[:all_images]
    edge = jnp.pad(edge.reshape(all_images, blocks, BLOCK), ((0, 0), (8, 8 - blocks), (0, 0)))
    factor = local_back(jax.nn.silu, cond, jnp.ones_like(cond)).reshape(images, blocks, BLOCK)
    factor = jnp.pad(factor, ((0, 0), (0, 16 - blocks), (0, 0)), constant_values=1.0)
    order = list(reversed(range(LAYERS)))
    scattered, slot_grad_out, shared = plan.scatter(
        [grad for l in order for grad in reversed(layer_grads[l])],
        modul_grad, pick, low_slots, edge, factor,
    )
    grad_rows = {
        (l, 3 - i): scattered[4 * n + i] for n, l in enumerate(order) for i in range(4)
    }
    shared = shared.reshape(all_images, 16, BLOCK)
    grad_cond = shared[:, :blocks].reshape(all_images, D)
    edge = shared[:, 8 : 8 + blocks].reshape(all_images, D)
    grad_patch, grad_head = edge[:CHANNELS], edge[CHANNELS : 2 * CHANNELS]
    loss_sum = edge[2 * CHANNELS, 0]
    grad_time_out = grad_cond.astype(jnp.bfloat16)
    grad_time_act = dot_low("ge,de->gd", grad_time_out, time_two)
    grad_time_pre = local_back(jax.nn.silu, time_pre, grad_time_act).astype(jnp.bfloat16)
    grad_time_w = dot_low("gf,gd->fd", freq_low, grad_time_pre)
    grad_table = jnp.zeros((CLASSES, D), jnp.float32).at[every_label].add(grad_cond)
    small_grad = jnp.concatenate([grad_patch, grad_time_w, grad_table, grad_head], 0)

    my_time = jnp.clip(my_unit - TAIL_FIRST, 0, TIME_UNITS - 1)
    is_time = (my_unit >= TAIL_FIRST) & (my_unit < TAIL_FIRST + TIME_UNITS)
    time_cols = jnp.take(grad_time_out.reshape(all_images, TIME_UNITS, BLOCK), my_time, axis=1)
    is_image = my_place >= 0
    image_grad = dot_low("gd,gsc->dsc", cond_act, slot_grad_out)
    time_grad = dot_low("gd,gsc->dsc", time_act, time_cols)

    dense_place = np.full((UNITS + 1,), 0, np.int32)
    dense_place[dense_units] = np.arange(len(dense_units))
    slot_place = jnp.asarray(dense_place)[unit_of_slot]
    all_rows = jnp.concatenate(
        [
            grad_rows[l, i].reshape(rows, -1, BLOCK)
            for l in range(LAYERS)
            for i in range(4)
        ],
        1,
    )
    slot_rows = jnp.take(all_rows, slot_place, axis=1)
    dense_grad = plan.restore_rows(
        lax.all_to_all(slot_rows, AXES, split_axis=1, concat_axis=0, tiled=True)
    ).astype(jnp.float32)

    owned_grad = jnp.where(
        is_image[None, :, None],
        image_grad,
        jnp.where(is_time[None, :, None], time_grad, dense_grad),
    )
    used = (my_unit >= 0)[None, :, None]
    rate = rate_factor * unit_scale(jnp.maximum(my_unit, 0))[None, :, None]
    new_w, new_first, new_second = adam_update(
        master, first_moment, second_moment, owned_grad, rate
    )
    new_master = jnp.where(used, new_w, master)
    new_first = jnp.where(used, new_first, first_moment)
    new_second = jnp.where(used, new_second, second_moment)
    small_rate = rate_factor * table_scale(jnp.arange(small.shape[0], dtype=jnp.int32))[:, None]
    new_small, new_small_first, new_small_second = adam_update(
        small, small_first, small_second, small_grad, small_rate
    )
    return (
        loss_sum,
        weight_total,
        new_master,
        new_first,
        new_second,
        new_small,
        new_small_first,
        new_small_second,
    )


def solution(mesh):
    return jax.shard_map(
        on_device,
        mesh=mesh,
        in_specs=(
            P(("rep", "shard"), None),
            P(("rep", "shard"), None),
            P(("rep", "shard")),
            P(("rep", "shard")),
            P(),
            P(None, ("rep", "shard"), None),
            P(None, ("rep", "shard"), None),
            P(None, ("rep", "shard"), None),
            P(),
            P(),
            P(),
        ),
        out_specs=(
            P(),
            P(),
            P(None, ("rep", "shard"), None),
            P(None, ("rep", "shard"), None),
            P(None, ("rep", "shard"), None),
            P(),
            P(),
            P(),
        ),
        check_vma=False,
    )
```

```python
import jax
import jax.numpy as jnp
import numpy as np
from jax import lax
from jax.experimental import pallas as pl
from jax.experimental.pallas import tpu as pltpu
from jax.sharding import PartitionSpec as P

D = 768
HEADS = 12
HEAD_DIM = 64
FF = 3072
FREQ = 256
CLASSES = 1000
CHANNELS = 16
GRID = 16
PATCHES = 256
LAYERS = 2
TSTEPS = 1000
STEP = 10
BLOCK = 128
LAYER_COLS = 13824
LAYER_UNITS = 108
UNITS = 234

ADA_UNITS = 6 * D // BLOCK
DENSE_UNITS = LAYER_UNITS - ADA_UNITS
DENSE_COLS = DENSE_UNITS * BLOCK
TIME_UNITS = D // BLOCK
TAIL_FIRST = LAYERS * LAYER_UNITS
AXES = ("rep", "shard")


beta_one = 0.5
beta_two = 0.5
adam_eps = 1e-08
decay_rate = 0.1
rate_factor = 0.5


def gelu_tanh(values):
    return jax.nn.gelu(values, approximate=True)


def norm_rows(hidden):
    centered = hidden - jnp.mean(hidden, -1, keepdims=True)
    return centered * lax.rsqrt(jnp.mean(centered * centered, -1, keepdims=True) + 1e-06)


def local_back(function, primal, upstream):
    return jax.vjp(function, primal)[1](upstream)[0]


def dot_low(pattern, left_side, right_side):
    return jnp.einsum(pattern, left_side, right_side, preferred_element_type=jnp.float32)


def positions():
    quarter = D // 4
    angular = jnp.exp(-jnp.log(10000.0) * jnp.arange(quarter, dtype=jnp.float32) / quarter)
    patch_idx = jnp.arange(PATCHES, dtype=jnp.int32)
    row_pos = (patch_idx // GRID).astype(jnp.float32)[:, None] * angular
    col_pos = (patch_idx % GRID).astype(jnp.float32)[:, None] * angular
    return jnp.concatenate(
        [jnp.sin(col_pos), jnp.cos(col_pos), jnp.sin(row_pos), jnp.cos(row_pos)], -1
    )


def frequencies(times):
    half_size = FREQ // 2
    spacing = jnp.exp(-jnp.log(10000.0) * jnp.arange(half_size, dtype=jnp.float32) / half_size)
    angles = 1000.0 * times[:, None] * spacing
    return jnp.concatenate([jnp.cos(angles), jnp.sin(angles)], -1)


def unit_scale(unit_ids):
    column = unit_ids % LAYER_UNITS * BLOCK
    in_layer = unit_ids < LAYERS * LAYER_UNITS
    is_output = in_layer & (column >= 9 * D) & (column < 10 * D)
    is_down = in_layer & (column >= 10 * D + FF)
    factor = jnp.where(is_output, 4.0, jnp.where(is_down, 1.5 * (D / FF) ** 0.5, 1.0))
    return factor / D**0.5


def table_scale(row_ids):
    return jnp.where(
        row_ids < CHANNELS,
        CHANNELS ** (-0.5),
        jnp.where(
            row_ids < CHANNELS + FREQ,
            FREQ ** (-0.5),
            jnp.where(row_ids < CHANNELS + FREQ + CLASSES, 0.5, D ** (-0.5)),
        ),
    )


def adam_update(weight, first_mom, second, gradient, rate):
    first_new = beta_one * first_mom + (1.0 - beta_one) * gradient
    second_new = beta_two * second + (1.0 - beta_two) * gradient * gradient
    ratio = (
        first_new
        / (1.0 - beta_one**STEP)
        / (jnp.sqrt(second_new / (1.0 - beta_two**STEP)) + adam_eps)
    )
    return (weight - rate * (ratio + decay_rate * weight), first_new, second_new)


def modulate(normed, shift, scale):
    return normed * (1.0 + scale[:, None, :]) + shift[:, None, :]


def layer_forward(hidden, modul, weights):
    w_qkv, w_out, w_up, w_down = weights
    shift_a, scale_a, gate_a, shift_b, scale_b, gate_b = jnp.split(modul, 6, -1)
    attn_in = modulate(norm_rows(hidden), shift_a, scale_a).astype(jnp.bfloat16)
    qkv_all = dot_low("gpd,de->gpe", attn_in, w_qkv).astype(jnp.bfloat16)
    heads_out = attend(qkv_all)
    branch_a = dot_low("gpd,de->gpe", heads_out, w_out)
    middle = hidden + gate_a[:, None, :] * branch_a
    mlp_in = modulate(norm_rows(middle), shift_b, scale_b).astype(jnp.bfloat16)
    pre_act = dot_low("gpd,df->gpf", mlp_in, w_up)
    post_act = gelu_tanh(pre_act).astype(jnp.bfloat16)
    branch_b = dot_low("gpf,df->gpd", post_act, w_down)
    output = middle + gate_b[:, None, :] * branch_b
    return (
        output,
        (
            hidden,
            modul,
            attn_in,
            qkv_all,
            heads_out,
            branch_a,
            middle,
            mlp_in,
            pre_act,
            post_act,
            branch_b,
        ),
    )


def layer_backward(grad_out, weights, saved):
    w_qkv, w_out, w_up, w_down = weights
    (
        hidden,
        modul,
        attn_in,
        qkv_all,
        heads_out,
        branch_a,
        middle,
        mlp_in,
        pre_act,
        post_act,
        branch_b,
    ) = saved
    shift_a, scale_a, gate_a, shift_b, scale_b, gate_b = jnp.split(modul, 6, -1)
    grad_gate_b = jnp.sum(grad_out * branch_b, 1)
    grad_branch_b = (gate_b[:, None, :] * grad_out).astype(jnp.bfloat16)
    grad_down = (grad_branch_b, post_act)
    grad_post = dot_low("gpd,df->gpf", grad_branch_b, w_down)
    grad_pre = local_back(gelu_tanh, pre_act, grad_post).astype(jnp.bfloat16)
    grad_up = (mlp_in, grad_pre)
    grad_mlp_in = dot_low("gpf,df->gpd", grad_pre, w_up)
    normed_b = norm_rows(middle)
    grad_scale_b = jnp.sum(grad_mlp_in * normed_b, 1)
    grad_shift_b = jnp.sum(grad_mlp_in, 1)
    grad_middle = grad_out + local_back(
        norm_rows, middle, grad_mlp_in * (1.0 + scale_b[:, None, :])
    )
    grad_gate_a = jnp.sum(grad_middle * branch_a, 1)
    grad_branch_a = (gate_a[:, None, :] * grad_middle).astype(jnp.bfloat16)
    grad_out_w = (heads_out, grad_branch_a)
    grad_heads = dot_low("gpe,de->gpd", grad_branch_a, w_out).astype(jnp.bfloat16)
    grad_qkv = attend_back(qkv_all, grad_heads)
    grad_qkv_w = (attn_in, grad_qkv)
    grad_attn_in = dot_low("gpe,de->gpd", grad_qkv, w_qkv)
    normed_a = norm_rows(hidden)
    grad_scale_a = jnp.sum(grad_attn_in * normed_a, 1)
    grad_shift_a = jnp.sum(grad_attn_in, 1)
    grad_in = grad_middle + local_back(
        norm_rows, hidden, grad_attn_in * (1.0 + scale_a[:, None, :])
    )
    grad_modul = jnp.concatenate(
        [grad_shift_a, grad_scale_a, grad_gate_a, grad_shift_b, grad_scale_b, grad_gate_b], -1
    ).astype(jnp.bfloat16)
    return (grad_in, grad_modul, [grad_qkv_w, grad_out_w, grad_up, grad_down])


MESH = pl.DeviceIdType.MESH
GATHER_VMEM = 40 * 2**20
SCATTER_VMEM = 56 * 2**20


def dot_rows(left_side, right_side):
    return lax.dot_general(
        left_side, right_side, (((0,), (0,)), ((), ())), preferred_element_type=jnp.float32
    )


def row_product(left_side, right_side):
    left_side = left_side.reshape(-1, left_side.shape[-1])
    right_side = right_side.reshape(-1, right_side.shape[-1])
    return dot_rows(left_side, right_side).astype(jnp.bfloat16)


def head_mask(number):
    lane = lax.broadcasted_iota(jnp.int32, (PATCHES, 2 * HEAD_DIM), 1)
    return (lane >= number * HEAD_DIM) & (lane < (number + 1) * HEAD_DIM)


def dot_lanes(left_side, right_side):
    return lax.dot_general(
        left_side, right_side, (((1,), (1,)), ((), ())), preferred_element_type=jnp.float32
    )


def attend_kernel(queries, keys_all, values, out):
    result = jnp.zeros((PATCHES, 2 * HEAD_DIM), jnp.float32)
    for number in (0, 1):
        mask = head_mask(number)
        one = jnp.where(mask, queries[0], jnp.zeros((), jnp.bfloat16))
        scores = dot_lanes(one, keys_all[0]) * HEAD_DIM ** (-0.5)
        powers = jnp.exp(scores - jnp.max(scores, -1, keepdims=True))
        prob = (powers * (1.0 / jnp.sum(powers, -1, keepdims=True))).astype(jnp.bfloat16)
        mixed = jnp.dot(prob, values[0], preferred_element_type=jnp.float32)
        result = jnp.where(mask, mixed, result)
    out[0] = result.astype(jnp.bfloat16)


def attend_back_kernel(queries, keys_all, values, grad, out):
    pair = pl.program_id(1)
    results = [jnp.zeros((PATCHES, 2 * HEAD_DIM), jnp.float32)] * 3
    none = jnp.zeros((), jnp.bfloat16)
    for number in (0, 1):
        mask = head_mask(number)
        scores = dot_lanes(keys_all[0], jnp.where(mask, queries[0], none)) * HEAD_DIM ** (-0.5)
        powers = jnp.exp(scores - jnp.max(scores, 0, keepdims=True))
        prob = powers * (1.0 / jnp.sum(powers, 0, keepdims=True))
        grad_prob = dot_lanes(values[0], jnp.where(mask, grad[0], none))
        inner = jnp.sum(prob * grad_prob, 0, keepdims=True)
        grad_scores = (HEAD_DIM ** (-0.5) * prob * (grad_prob - inner)).astype(jnp.bfloat16)
        parts = (
            dot_rows(grad_scores, keys_all[0]),
            jnp.dot(grad_scores, queries[0], preferred_element_type=jnp.float32),
            jnp.dot(prob.astype(jnp.bfloat16), grad[0], preferred_element_type=jnp.float32),
        )
        results = [jnp.where(mask, part, result) for part, result in zip(parts, results)]
    for third, result in enumerate(results):
        first = pl.multiple_of(third * D + pair * 2 * HEAD_DIM, 2 * HEAD_DIM)
        out[0, :, pl.ds(first, 2 * HEAD_DIM)] = result.astype(jnp.bfloat16)


def pair_block(third):
    pairs = HEADS // 2
    return pl.BlockSpec(
        (1, PATCHES, 2 * HEAD_DIM), lambda image, pair: (image, 0, third * pairs + pair)
    )


def attend(qkv_all):
    images = qkv_all.shape[0]
    pairs = HEADS // 2
    return pl.pallas_call(
        attend_kernel,
        grid=(images, pairs),
        out_shape=jax.ShapeDtypeStruct((images, PATCHES, D), jnp.bfloat16),
        in_specs=[pair_block(0), pair_block(1), pair_block(2)],
        out_specs=pair_block(0),
        cost_estimate=pl.CostEstimate(
            flops=4 * images * PATCHES * PATCHES * D,
            bytes_accessed=8 * images * PATCHES * D,
            transcendentals=images * HEADS * PATCHES * PATCHES,
        ),
    )(qkv_all, qkv_all, qkv_all)


def attend_back(qkv_all, grad_heads):
    images = qkv_all.shape[0]
    pairs = HEADS // 2
    return pl.pallas_call(
        attend_back_kernel,
        grid=(images, pairs),
        out_shape=jax.ShapeDtypeStruct((images, PATCHES, 3 * D), jnp.bfloat16),
        in_specs=[pair_block(0), pair_block(1), pair_block(2), pair_block(0)],
        out_specs=pl.BlockSpec((1, PATCHES, 3 * D), lambda image, pair: (image, 0, 0)),
        cost_estimate=pl.CostEstimate(
            flops=10 * images * PATCHES * PATCHES * D,
            bytes_accessed=14 * images * PATCHES * D,
            transcendentals=images * HEADS * PATCHES * PATCHES,
        ),
    )(qkv_all, qkv_all, qkv_all, grad_heads)


def place_of():
    rep = lax.axis_index("rep")
    return rep // 4, (rep // 2) % 2, rep % 2, lax.axis_index("shard")


def rep_of(y, x, c):
    return (y * 2 + x) * 2 + c


def device_at(j):
    shards = lax.axis_size("shard")
    devices = lax.axis_size("rep") * shards
    me = lax.axis_index("rep") * shards + lax.axis_index("shard")
    peer = lax.rem(me + j, devices)
    return peer, (peer // shards, lax.rem(peer, shards))


def meet_all(devices):
    barrier = pltpu.get_barrier_semaphore()

    @pl.loop(1, devices)
    def _(j):
        pl.semaphore_signal(barrier, inc=1, device_id=device_at(j)[1], device_id_type=MESH)

    pl.semaphore_wait(barrier, devices - 1)


def neighbours():
    y, x, c, z = place_of()
    to_x = (rep_of(y, 1 - x, c), z)
    to_y = (rep_of(1 - y, x, c), z)
    to_core = (rep_of(y, x, 1 - c), z)
    to_z = [(rep_of(y, x, c), lax.rem(z + step, 4)) for step in (1, 2, 3)]
    return to_x, to_y, to_core, to_z


def gather_kernel(widths, *refs):
    count = len(widths)
    pieces = refs[:count]
    info, low_slots = refs[count : count + 2]
    outs = refs[count + 2 : 2 * count + 2]
    every_info, cond_out, modul_out = refs[2 * count + 2 : 2 * count + 5]
    time_two, parts, own_sem, send_sem, recv_sem, time_sem, modul_sem, info_sem = refs[
        2 * count + 5 :
    ]
    devices, images = modul_out.shape[:2]
    slots = low_slots.shape[0]
    y, x, c, z = place_of()
    to_x, to_y, to_core, to_z = neighbours()
    me = rep_of(y, x, c) * 4 + z
    meet_all(devices)

    def remote(k, number, source, dest, target):
        return pltpu.make_async_remote_copy(
            src_ref=source,
            dst_ref=dest,
            send_sem=send_sem.at[k, number],
            recv_sem=recv_sem.at[k, number],
            device_id=target,
            device_id_type=MESH,
        )

    def own_copy(k):
        return pltpu.make_async_copy(pieces[k], outs[k].at[c, y, x, z], own_sem.at[k])

    def line_copies(k, arriving):
        copies = []
        for step in (1, 2, 3):
            at_z = lax.rem(z + 4 - step, 4) if arriving else z
            copies.append(
                remote(k, step - 1, pieces[k], outs[k].at[c, y, x, at_z], to_z[step - 1])
            )
        return copies

    def first_copies(k, arriving):
        half = widths[k] // 2
        left, right = pl.ds(0, half), pl.ds(half, half)
        at_x = 1 - x if arriving else x
        at_y = 1 - y if arriving else y
        a_block = outs[k].at[c, y, at_x, :, :, left]
        b_block = outs[k].at[c, at_y, x, :, :, right]
        return [remote(k, 3, a_block, a_block, to_x), remote(k, 4, b_block, b_block, to_y)]

    def second_copies(k, arriving):
        half = widths[k] // 2
        left, right = pl.ds(0, half), pl.ds(half, half)
        at_x = 1 - x if arriving else x
        at_y = 1 - y if arriving else y
        a_block = outs[k].at[c, at_y, :, :, :, left]
        b_block = outs[k].at[c, :, at_x, :, :, right]
        return [remote(k, 5, a_block, a_block, to_y), remote(k, 6, b_block, b_block, to_x)]

    def core_copies(k, arriving):
        block = outs[k].at[1 - c if arriving else c]
        return [remote(k, 7, block, block, to_core)]

    def start(copies):
        for copy in copies:
            copy.start()

    def arrived(copies):
        for copy in copies:
            copy.wait_recv()

    def modul_copy(j, arriving):
        peer, where = device_at(devices - j if arriving else j)
        return pltpu.make_async_remote_copy(
            src_ref=parts.at[pl.ds(peer * images, images)],
            dst_ref=modul_out.at[peer if arriving else me],
            send_sem=modul_sem.at[0, j],
            recv_sem=modul_sem.at[1, j],
            device_id=where,
            device_id_type=MESH,
        )

    def info_copy(j, arriving):
        peer, where = device_at(devices - j if arriving else j)
        return pltpu.make_async_remote_copy(
            src_ref=info,
            dst_ref=every_info.at[pl.ds((peer if arriving else me) * images, images)],
            send_sem=info_sem.at[0, j],
            recv_sem=info_sem.at[1, j],
            device_id=where,
            device_id_type=MESH,
        )

    def info_rows(first):
        return jnp.concatenate([every_info[:, first + j, :] for j in range(D // BLOCK)], -1)

    def image_products():
        copy = pltpu.make_async_copy(outs[0], time_two, time_sem)
        copy.start()

        @pl.loop(1, devices)
        def _(j):
            info_copy(j, True).wait_recv()
            info_copy(j, False).wait_send()

        copy.wait()
        weight = time_two[...].astype(jnp.float32).reshape(D, D).astype(jnp.bfloat16)
        cond = jnp.dot(
            info_rows(0).astype(jnp.bfloat16), weight, preferred_element_type=jnp.float32
        )
        cond = cond + info_rows(8)
        cond_out[...] = cond
        act = (cond * jax.nn.sigmoid(cond)).astype(jnp.bfloat16)
        for s in range(slots):
            parts[:, s, :] = jnp.dot(act, low_slots[s], preferred_element_type=jnp.float32)
        for i in range(images):
            modul_out[me, i] = parts[me * images + i]

        @pl.loop(1, devices)
        def _(j):
            modul_copy(j, False).start()

    @pl.loop(1, devices)
    def _(j):
        info_copy(j, False).start()

    for i in range(images):
        every_info[me * images + i] = info[i]
    for k in range(count):
        own_copy(k).start()
    start(line_copies(0, False))
    for t in range(count + 2):
        if t + 1 < count:
            start(line_copies(t + 1, False))
        if t < count:
            own_copy(t).wait()
            arrived(line_copies(t, True))
            start(first_copies(t, False))
        if 0 <= t - 1 < count:
            arrived(first_copies(t - 1, True))
            start(second_copies(t - 1, False))
        if 0 <= t - 2 < count:
            arrived(second_copies(t - 2, True))
            start(core_copies(t - 2, False))
        if t == 3:
            arrived(core_copies(0, True))
            image_products()
    for k in range(1, count):
        arrived(core_copies(k, True))

    @pl.loop(1, devices)
    def _(j):
        modul_copy(j, True).wait_recv()
        modul_copy(j, False).wait_send()

    for k in range(count):
        for copies in (line_copies, first_copies, second_copies, core_copies):
            for copy in copies(k, False):
                copy.wait_send()


def scatter_kernel(widths, slots, *refs):
    count = len(widths)
    lefts, rights = refs[:count], refs[count : 2 * count]
    modul, pick, low_slots, edge, factor = refs[2 * count : 2 * count + 5]
    outs = refs[2 * count + 5 : 3 * count + 5]
    chosen, shared = refs[3 * count + 5 : 3 * count + 7]
    scratch = refs[3 * count + 7 :]
    own, first_in, second_in, line_in = (scratch[i * count : (i + 1) * count] for i in range(4))
    (
        left_in, left_turned, right_in, away, every_modul, parts, landed,
        load_sem, send_sem, recv_sem, modul_sem, part_sem, sum_sem,
    ) = scratch[4 * count :]
    devices, images = shared.shape[:2]
    y, x, c, z = place_of()
    to_x, to_y, to_core, to_z = neighbours()
    me = rep_of(y, x, c) * 4 + z
    rows = D // 32
    half_rows = D // 2
    meet_all(devices)

    def exchange(source, dest, sem, j, arriving):
        peer, where = device_at(devices - j if arriving else j)
        return pltpu.make_async_remote_copy(
            src_ref=source(peer, me),
            dst_ref=dest(peer if arriving else me),
            send_sem=sem.at[0, j],
            recv_sem=sem.at[1, j],
            device_id=where,
            device_id_type=MESH,
        )

    def modul_copies(step, arriving):
        if step == 0:
            copies = []
            for number in (1, 2, 3):
                at_z = lax.rem(z + 4 - number, 4) if arriving else z
                copies.append((modul, every_modul.at[y, x, c, at_z], to_z[number - 1]))
        else:
            at_x = 1 - x if arriving and step == 1 else x
            at_y = 1 - y if arriving and step == 2 else y
            at_c = 1 - c if arriving and step == 3 else c
            block = (
                every_modul.at[y, at_x, c],
                every_modul.at[at_y, :, c],
                every_modul.at[:, :, at_c],
            )[step - 1]
            copies = [(block, block, (to_x, to_y, to_core)[step - 1])]
        return [
            pltpu.make_async_remote_copy(
                src_ref=source,
                dst_ref=dest,
                send_sem=modul_sem.at[0, step, number],
                recv_sem=modul_sem.at[1, step, number],
                device_id=target,
                device_id_type=MESH,
            )
            for number, (source, dest, target) in enumerate(copies)
        ]

    def part_copy(j, arriving):
        return exchange(
            lambda peer, mine: parts.at[pl.ds(peer * images, images)],
            lambda owner: landed.at[owner],
            part_sem, j, arriving,
        )

    def sum_copy(j, arriving):
        return exchange(
            lambda peer, mine: shared.at[mine], lambda owner: shared.at[owner], sum_sem, j, arriving
        )

    def all_start(copy):
        @pl.loop(1, devices)
        def _(j):
            copy(j, False).start()

    def all_arrived(copy):
        @pl.loop(1, devices)
        def _(j):
            copy(j, True).wait_recv()

    def all_sent(copy):
        @pl.loop(1, devices)
        def _(j):
            copy(j, False).wait_send()

    def image_parts():
        arrived(modul_copies(3, True))

        @pl.loop(0, devices // 4)
        def _(i):
            for n in range(4):
                for m in range(images):
                    block = every_modul[i // 4, (i // 2) % 2, i % 2, n, m]
                    chosen[(i * 4 + n) * images + m] = jnp.dot(
                        pick[...], block, preferred_element_type=jnp.float32
                    )

        total = jnp.zeros((devices * images, D), jnp.float32)
        for s in range(slots):
            total = total + lax.dot_general(
                chosen[:, s, :].astype(jnp.bfloat16),
                low_slots[s],
                (((1,), (1,)), ((), ())),
                preferred_element_type=jnp.float32,
            )
        parts[...] = edge[...]
        for j in range(D // BLOCK):
            parts[:, j, :] = total[:, j * BLOCK : (j + 1) * BLOCK]
        all_start(part_copy)
        for i in range(images):
            landed[me, i] = parts[me * images + i]

    def image_sums():
        all_arrived(part_copy)
        shared[me] = jnp.sum(landed[...], 0) * factor[...]
        all_start(sum_copy)

    def remote(k, number, source, dest, target):
        return pltpu.make_async_remote_copy(
            src_ref=source,
            dst_ref=dest,
            send_sem=send_sem.at[k, number],
            recv_sem=recv_sem.at[k, number],
            device_id=target,
            device_id_type=MESH,
        )

    def load_left(k):
        return pltpu.make_async_copy(lefts[k], left_in.at[k % 2], load_sem.at[0, k % 2])

    def load_right(k):
        place = right_in.at[k % 3, :, pl.ds(0, widths[k])]
        return pltpu.make_async_copy(rights[k], place, load_sem.at[1, k % 3])

    def core_copies(k):
        source = away.at[k % 3, :, :, :, :, pl.ds(0, widths[k])]
        return [remote(k, 0, source, own[k], to_core)]

    def first_copies(k):
        half = widths[k] // 2
        return [
            remote(k, 1, own[k].at[:, 1 - x, :, :, pl.ds(0, half)], first_in[k].at[0], to_x),
            remote(k, 2, own[k].at[1 - y, :, :, :, pl.ds(half, half)], first_in[k].at[1], to_y),
        ]

    def second_copies(k):
        half = widths[k] // 2
        return [
            remote(k, 3, own[k].at[1 - y, x, :, :, pl.ds(0, half)], second_in[k].at[0], to_y),
            remote(k, 4, own[k].at[y, 1 - x, :, :, pl.ds(half, half)], second_in[k].at[1], to_x),
        ]

    def line_copies(k):
        return [
            remote(
                k,
                4 + step,
                own[k].at[y, x, lax.rem(z + step, 4)],
                line_in[k].at[step - 1],
                to_z[step - 1],
            )
            for step in (1, 2, 3)
        ]

    def start(copies):
        for copy in copies:
            copy.start()

    def arrived(copies):
        for copy in copies:
            copy.wait_recv()

    def products(k, half, store):
        slot = k % 3
        tile = D

        @pl.loop(0, widths[k] // tile)
        def _(n):
            columns = pl.ds(pl.multiple_of(n * tile, tile), tile)
            left = left_turned[slot, pl.ds(pl.multiple_of(half * half_rows, half_rows), half_rows)]
            result = jnp.dot(left, right_in[slot, :, columns], preferred_element_type=jnp.float32)
            for i in range(16):
                at = (i // 8, (i // 4) % 2, i % 4, slice(None), columns)
                store(at, result[i * rows : (i + 1) * rows])

    def away_products(k):
        load_left(k).wait()
        load_right(k).wait()
        left_turned[k % 3] = left_in[k % 2].T
        if k + 2 < count:
            load_left(k + 2).start()
        if k >= 3:
            for copy in core_copies(k - 3):
                copy.wait_send()

        def store(at, value):
            away[(k % 3,) + at] = value.astype(jnp.bfloat16)

        products(k, 1 - c, store)
        start(core_copies(k))

    def own_products(k):
        def store(at, value):
            own[k][at] = (value + own[k][at].astype(jnp.float32)).astype(jnp.bfloat16)

        products(k, c, store)

    def first_sum(k):
        half = widths[k] // 2

        @pl.loop(0, 8)
        def _(i):
            two, at_z = i // 4, i % 4
            a_at = (two, x, at_z, slice(None), pl.ds(0, half))
            b_at = (y, two, at_z, slice(None), pl.ds(half, half))
            own[k][a_at] = own[k][a_at] + first_in[k][0, two, at_z]
            own[k][b_at] = own[k][b_at] + first_in[k][1, two, at_z]

    def second_sum(k):
        half = widths[k] // 2

        @pl.loop(0, 4)
        def _(at_z):
            a_at = (y, x, at_z, slice(None), pl.ds(0, half))
            b_at = (y, x, at_z, slice(None), pl.ds(half, half))
            own[k][a_at] = own[k][a_at] + second_in[k][0, at_z]
            own[k][b_at] = own[k][b_at] + second_in[k][1, at_z]

    start(modul_copies(0, False))
    every_modul[y, x, c, z] = modul[...]
    for k in range(min(3, count)):
        load_right(k).start()
        if k < 2:
            load_left(k).start()
    away_products(0)
    for t in range(count + 3):
        if t + 1 < count:
            away_products(t + 1)
        if t < count:
            arrived(core_copies(t))
            own_products(t)
            start(first_copies(t))
            if t + 3 < count:
                load_right(t + 3).start()
        if 0 <= t - 1 < count:
            arrived(first_copies(t - 1))
            first_sum(t - 1)
            start(second_copies(t - 1))
        if 0 <= t - 2 < count:
            arrived(second_copies(t - 2))
            second_sum(t - 2)
            start(line_copies(t - 2))
        if 0 <= t - 3 < count:
            k = t - 3
            arrived(line_copies(k))
            total = own[k][y, x, z].astype(jnp.float32)
            for step in (1, 2, 3):
                total = total + line_in[k][step - 1].astype(jnp.float32)
            outs[k][...] = total.astype(jnp.bfloat16)
        if t < 3:
            arrived(modul_copies(t, True))
            start(modul_copies(t + 1, False))
        if t == 3:
            image_parts()
        if t == 6:
            image_sums()
    all_arrived(sum_copy)
    for copy in (part_copy, sum_copy):
        all_sent(copy)
    for step in range(4):
        for copy in modul_copies(step, False):
            copy.wait_send()
    for k in range(count):
        for copies in (core_copies, first_copies, second_copies, line_copies):
            if copies is core_copies and k + 3 < count:
                continue
            for copy in copies(k):
                copy.wait_send()


class RingPlan:
    def order_rows(self, values):
        shape = values.shape
        split = values.reshape((2, 2, 2, 4, D // 32) + shape[1:])
        return jnp.moveaxis(split, 0, 2).reshape(shape)

    def restore_rows(self, values):
        shape = values.shape
        split = values.reshape((2, 2, 2, 4, D // 32) + shape[1:])
        return jnp.moveaxis(split, 2, 0).reshape(shape)

    def gather(self, pieces, time_piece, info, low_slots):
        turn = sorted(range(len(pieces)), key=lambda n: (n % 4 == 1, n))
        pieces = [time_piece] + [pieces[n] for n in turn]
        widths = tuple(piece.shape[1] for piece in pieces)
        count, rows = len(pieces), D // 32
        all_images = 32 * info.shape[0]
        slots = low_slots.shape[1]
        room = -(-slots // 8) * 8
        size = sum(4 * D * width for width in widths)
        whole_shape = [(2, 2, 2, 4, rows, width) for width in widths]
        *whole, every_info, cond, modul = pl.pallas_call(
            lambda *refs: gather_kernel(widths, *refs),
            out_shape=[
                jax.ShapeDtypeStruct(shape, piece.dtype)
                for shape, piece in zip(whole_shape, pieces)
            ]
            + [
                jax.ShapeDtypeStruct((all_images,) + info.shape[1:], jnp.float32),
                jax.ShapeDtypeStruct((all_images, D), jnp.float32),
                jax.ShapeDtypeStruct((32, all_images // 32, room, BLOCK), jnp.float32),
            ],
            in_specs=[pl.BlockSpec(memory_space=pltpu.VMEM)] * (count + 2),
            out_specs=[pl.BlockSpec(memory_space=pl.ANY)] * count
            + [pl.BlockSpec(memory_space=pltpu.VMEM)] * 3,
            scratch_shapes=[
                pltpu.VMEM(whole_shape[0], jnp.bfloat16),
                pltpu.VMEM((all_images, room, BLOCK), jnp.float32),
                pltpu.SemaphoreType.DMA((count,)),
                pltpu.SemaphoreType.DMA((count, 8)),
                pltpu.SemaphoreType.DMA((count, 8)),
                pltpu.SemaphoreType.DMA,
                pltpu.SemaphoreType.DMA((2, 32)),
                pltpu.SemaphoreType.DMA((2, 32)),
            ],
            compiler_params=pltpu.CompilerParams(
                collective_id=0, has_side_effects=True, vmem_limit_bytes=GATHER_VMEM
            ),
            cost_estimate=pl.CostEstimate(flops=0, bytes_accessed=size, transcendentals=0),
        )(*pieces, info, jnp.swapaxes(low_slots, 0, 1))
        whole = [part.reshape(D, -1) for part in whole]
        modul = jnp.swapaxes(modul[:, :, :slots], 0, 1).reshape(-1, 32 * slots, BLOCK)
        ordered = [whole[1 + turn.index(n)] for n in range(len(turn))]
        return ordered, whole[0], every_info, cond, modul

    def scatter(self, grads, modul, pick, low_slots, edge, factor):
        lefts = [left.reshape(-1, D) for left, _ in grads]
        rights = [right.reshape(left.shape[0], -1) for (_, right), left in zip(grads, lefts)]
        widths = tuple(right.shape[1] for right in rights)
        count, rows, tokens = len(grads), D // 32, lefts[0].shape[0]
        widest = max(widths)
        images, slots = modul.shape[0], low_slots.shape[1]
        size = sum(4 * D * width for width in widths)
        scratch = [pltpu.VMEM((2, 2, 4, rows, width), jnp.bfloat16) for width in widths]
        scratch += [pltpu.VMEM((2, 2, 4, rows, width // 2), jnp.bfloat16) for width in widths]
        scratch += [pltpu.VMEM((2, 4, rows, width // 2), jnp.bfloat16) for width in widths]
        scratch += [pltpu.VMEM((3, rows, width), jnp.bfloat16) for width in widths]
        *scattered, chosen, shared = pl.pallas_call(
            lambda *refs: scatter_kernel(widths, slots, *refs),
            out_shape=[jax.ShapeDtypeStruct((rows, width), jnp.bfloat16) for width in widths]
            + [
                jax.ShapeDtypeStruct((32 * images, pick.shape[0], BLOCK), jnp.float32),
                jax.ShapeDtypeStruct((32,) + factor.shape, jnp.float32),
            ],
            in_specs=[pl.BlockSpec(memory_space=pl.ANY)] * (2 * count)
            + [pl.BlockSpec(memory_space=pltpu.VMEM)] * 5,
            out_specs=[pl.BlockSpec(memory_space=pltpu.VMEM)] * (count + 2),
            scratch_shapes=scratch
            + [
                pltpu.VMEM((2, tokens, D), jnp.bfloat16),
                pltpu.VMEM((3, D, tokens), jnp.bfloat16),
                pltpu.VMEM((3, tokens, widest), jnp.bfloat16),
                pltpu.VMEM((3, 2, 2, 4, rows, widest), jnp.bfloat16),
                pltpu.VMEM((2, 2, 2, 4) + modul.shape, jnp.bfloat16),
                pltpu.VMEM(edge.shape, jnp.float32),
                pltpu.VMEM((32,) + factor.shape, jnp.float32),
                pltpu.SemaphoreType.DMA((2, 3)),
                pltpu.SemaphoreType.DMA((count, 8)),
                pltpu.SemaphoreType.DMA((count, 8)),
                pltpu.SemaphoreType.DMA((2, 4, 3)),
                pltpu.SemaphoreType.DMA((2, 32)),
                pltpu.SemaphoreType.DMA((2, 32)),
            ],
            compiler_params=pltpu.CompilerParams(
                collective_id=1, has_side_effects=True, vmem_limit_bytes=SCATTER_VMEM
            ),
            cost_estimate=pl.CostEstimate(flops=0, bytes_accessed=size, transcendentals=0),
        )(*lefts, *rights, modul, pick, jnp.swapaxes(low_slots, 0, 1), edge, factor)
        return scattered, chosen[:, :slots].astype(jnp.bfloat16), shared


class PlainPlan:
    def order_rows(self, values):
        return values

    def restore_rows(self, values):
        return values

    def gather(self, pieces, time_piece, info, low_slots):
        whole = [lax.all_gather(piece, AXES, axis=0, tiled=True) for piece in pieces]
        time_two = lax.all_gather(time_piece, AXES, axis=0, tiled=True)
        every_info = lax.all_gather(info, AXES, axis=0, tiled=True)
        blocks = D // BLOCK
        time_act = every_info[:, :blocks].reshape(-1, D).astype(jnp.bfloat16)
        cond = jnp.dot(time_act, time_two, preferred_element_type=jnp.float32)
        cond = cond + every_info[:, 8 : 8 + blocks].reshape(-1, D)
        modul = dot_low("gd,dsc->gsc", jax.nn.silu(cond).astype(jnp.bfloat16), low_slots)
        modul = lax.all_to_all(modul, AXES, split_axis=0, concat_axis=1, tiled=True)
        return whole, time_two, every_info, cond, modul

    def scatter(self, grads, modul, pick, low_slots, edge, factor):
        scattered = [
            lax.psum_scatter(row_product(*pair), AXES, scatter_dimension=0, tiled=True)
            for pair in grads
        ]
        slots = low_slots.shape[1]
        every = lax.all_gather(modul, AXES, axis=0, tiled=True)
        chosen = dot_low("su,guc->gsc", pick, every)[:, :slots].astype(jnp.bfloat16)
        part = dot_low("gsc,dsc->gd", chosen, low_slots).reshape(-1, D // BLOCK, BLOCK)
        parts = edge.at[:, : D // BLOCK].set(part)
        own = lax.psum_scatter(parts, AXES, scatter_dimension=0, tiled=True) * factor
        shared = lax.all_gather(own, AXES, axis=0, tiled=False)
        return scattered, chosen, shared


def unit_lists():
    dense = np.concatenate(
        [np.arange(l * LAYER_UNITS + ADA_UNITS, (l + 1) * LAYER_UNITS) for l in range(LAYERS)]
    )
    time_units = np.arange(TAIL_FIRST, TAIL_FIRST + TIME_UNITS)
    image_units = np.concatenate(
        [np.arange(l * LAYER_UNITS, l * LAYER_UNITS + ADA_UNITS) for l in range(LAYERS)]
        + [np.arange(TAIL_FIRST + TIME_UNITS, UNITS)]
    )
    return dense, time_units, image_units


def on_device(
    latents,
    noise,
    labels,
    t_index,
    owner,
    master,
    first_moment,
    second_moment,
    small,
    small_first,
    small_second,
):
    count = lax.axis_size("rep") * lax.axis_size("shard")
    me = lax.axis_index(AXES)
    slot_dev = master.shape[1]
    slot_total = count * slot_dev
    rows = D // count
    images = latents.shape[0]
    dense_units, time_units, image_units = unit_lists()

    unit_of_slot = (
        jnp.full((slot_total,), -1, jnp.int32).at[owner].set(jnp.arange(UNITS, dtype=jnp.int32))
    )
    my_unit = lax.dynamic_slice_in_dim(unit_of_slot, me * slot_dev, slot_dev)
    low_slots = master.astype(jnp.bfloat16)

    plan = RingPlan() if (lax.axis_size("rep"), lax.axis_size("shard")) == (8, 4) else PlainPlan()
    spread = lax.all_to_all(
        plan.order_rows(low_slots), AXES, split_axis=0, concat_axis=1, tiled=True
    )
    moved = np.concatenate([dense_units, time_units])
    unit_rows = jnp.take(spread, owner[moved], axis=1).reshape(rows, -1)
    pieces = []
    for l in range(LAYERS):
        base = l * DENSE_COLS
        cuts = (0, 3 * D, 4 * D, 4 * D + FF, DENSE_COLS)
        pieces += [unit_rows[:, base + cuts[i] : base + cuts[i + 1]] for i in range(4)]
    x_start = latents.astype(jnp.float32).reshape(-1, PATCHES, CHANNELS)
    noise_f = noise.astype(jnp.float32).reshape(-1, PATCHES, CHANNELS)
    times = (t_index.astype(jnp.float32) + 0.5) / TSTEPS
    noisy = (1.0 - times)[:, None, None] * x_start + times[:, None, None] * noise_f
    target = noise_f - x_start
    loss_weight = 1.0 + 3.0 * times
    small_low = small.astype(jnp.bfloat16)
    patch_w = small_low[:CHANNELS]
    time_w = small_low[CHANNELS : CHANNELS + FREQ]
    table = small[CHANNELS + FREQ : CHANNELS + FREQ + CLASSES]
    head_w = small_low[CHANNELS + FREQ + CLASSES :]
    noisy_low = noisy.astype(jnp.bfloat16)
    hidden = dot_low("gpc,cd->gpd", noisy_low, patch_w) + positions()

    blocks = D // BLOCK
    freq_own = frequencies(times).astype(jnp.bfloat16)
    time_own = jnp.dot(freq_own, time_w, preferred_element_type=jnp.float32)
    act_own = jax.nn.silu(time_own).astype(jnp.bfloat16).astype(jnp.float32)
    label_own = jnp.take(table, labels, axis=0)
    numbers = jnp.stack([t_index, labels], 1).astype(jnp.float32)
    info = jnp.concatenate(
        [
            act_own.reshape(images, blocks, BLOCK),
            jnp.pad(numbers, ((0, 0), (0, BLOCK - 2)))[:, None],
            jnp.zeros((images, 7 - blocks, BLOCK), jnp.float32),
            label_own.reshape(images, blocks, BLOCK),
            jnp.zeros((images, 8 - blocks, BLOCK), jnp.float32),
        ],
        1,
    )
    whole, time_two, every_info, cond_all, slot_modul = plan.gather(
        pieces, unit_rows[:, LAYERS * DENSE_COLS :], info, low_slots
    )
    all_images = cond_all.shape[0]
    every_time = (every_info[:, blocks, 0] + 0.5) / TSTEPS
    every_label = every_info[:, blocks, 1].astype(jnp.int32)
    weight_total = jnp.sum(1.0 + 3.0 * every_time) * PATCHES
    freq_low = frequencies(every_time).astype(jnp.bfloat16)
    time_pre = jnp.dot(freq_low, time_w, preferred_element_type=jnp.float32)
    time_act = every_info[:, :blocks].reshape(all_images, D).astype(jnp.bfloat16)
    weights_all = [tuple(whole[4 * l : 4 * l + 4]) for l in range(LAYERS)]
    cond = lax.dynamic_slice_in_dim(cond_all, me * images, images)
    cond_act = jax.nn.silu(cond_all).astype(jnp.bfloat16)
    modul_all = jnp.take(slot_modul, owner[image_units], axis=1).reshape(images, -1)

    saved_all = []
    for l in range(LAYERS):
        hidden, saved = layer_forward(
            hidden, modul_all[:, l * 6 * D : (l + 1) * 6 * D], weights_all[l]
        )
        saved_all.append(saved)
    shift_f, scale_f = jnp.split(modul_all[:, LAYERS * 6 * D :], 2, -1)
    normed_f = norm_rows(hidden)
    final_in = modulate(normed_f, shift_f, scale_f).astype(jnp.bfloat16)
    predict = dot_low("gpd,cd->gpc", final_in, head_w)
    error = predict - target
    loss_part = jnp.sum(loss_weight[:, None, None] * error * error) / CHANNELS
    grad_pred = (loss_weight[:, None, None] * 2.0 * error / CHANNELS).astype(jnp.bfloat16)
    grad_head = dot_low("gpc,gpd->cd", grad_pred, final_in)
    grad_final_in = dot_low("gpc,cd->gpd", grad_pred, head_w)
    grad_modul_f = jnp.concatenate(
        [jnp.sum(grad_final_in, 1), jnp.sum(grad_final_in * normed_f, 1)], -1
    ).astype(jnp.bfloat16)
    grad_hidden = local_back(norm_rows, hidden, grad_final_in * (1.0 + scale_f[:, None, :]))
    layer_grads = [None] * LAYERS
    grad_moduls = [None] * LAYERS
    for l in reversed(range(LAYERS)):
        grad_hidden, grad_moduls[l], layer_grads[l] = layer_backward(
            grad_hidden, weights_all[l], saved_all[l]
        )
    grad_embed = grad_hidden.astype(jnp.bfloat16)
    grad_patch = dot_low("gpc,gpd->cd", noisy_low, grad_embed)

    image_place = np.full((UNITS + 1,), -1, np.int32)
    image_place[image_units] = np.arange(len(image_units))
    my_place = jnp.asarray(image_place)[my_unit]
    room_slots, room_units = -(-slot_dev // 16) * 16, -(-len(image_units) // 16) * 16
    pick = jnp.pad(my_place, (0, room_slots - slot_dev), constant_values=-1)[:, None]
    pick = (pick == jnp.arange(room_units, dtype=jnp.int32)).astype(jnp.bfloat16)
    modul_grad = jnp.concatenate(grad_moduls + [grad_modul_f], -1).reshape(images, -1, BLOCK)
    modul_grad = jnp.pad(modul_grad, ((0, 0), (0, room_units - len(image_units)), (0, 0)))
    edge = jnp.concatenate([grad_patch, grad_head], 0)
    edge_room = max(all_images, 4 * CHANNELS)
    edge = jnp.concatenate([edge, jnp.broadcast_to(loss_part, (2 * CHANNELS, D))], 0)
    edge = jnp.pad(edge, ((0, edge_room - 4 * CHANNELS), (0, 0)))[:all_images]
    edge = jnp.pad(edge.reshape(all_images, blocks, BLOCK), ((0, 0), (8, 8 - blocks), (0, 0)))
    factor = local_back(jax.nn.silu, cond, jnp.ones_like(cond)).reshape(images, blocks, BLOCK)
    factor = jnp.pad(factor, ((0, 0), (0, 16 - blocks), (0, 0)), constant_values=1.0)
    order = [(l, i) for l in range(LAYERS) for i in (0, 2, 3)]
    order = [(LAYERS - 1, 1)] + order + [(l, 1) for l in range(LAYERS - 1)]
    scattered, slot_grad_out, shared = plan.scatter(
        [layer_grads[l][i] for l, i in order],
        modul_grad, pick, low_slots, edge, factor,
    )
    grad_rows = dict(zip(order, scattered))
    shared = shared.reshape(all_images, 16, BLOCK)
    grad_cond = shared[:, :blocks].reshape(all_images, D)
    edge = shared[:, 8 : 8 + blocks].reshape(all_images, D)
    grad_patch, grad_head = edge[:CHANNELS], edge[CHANNELS : 2 * CHANNELS]
    loss_sum = edge[2 * CHANNELS, 0]
    grad_time_out = grad_cond.astype(jnp.bfloat16)
    grad_time_act = dot_low("ge,de->gd", grad_time_out, time_two)
    grad_time_pre = local_back(jax.nn.silu, time_pre, grad_time_act).astype(jnp.bfloat16)
    grad_time_w = dot_low("gf,gd->fd", freq_low, grad_time_pre)
    grad_table = jnp.zeros((CLASSES, D), jnp.float32).at[every_label].add(grad_cond)
    small_grad = jnp.concatenate([grad_patch, grad_time_w, grad_table, grad_head], 0)

    my_time = jnp.clip(my_unit - TAIL_FIRST, 0, TIME_UNITS - 1)
    is_time = (my_unit >= TAIL_FIRST) & (my_unit < TAIL_FIRST + TIME_UNITS)
    time_cols = jnp.take(grad_time_out.reshape(all_images, TIME_UNITS, BLOCK), my_time, axis=1)
    is_image = my_place >= 0
    image_grad = dot_low("gd,gsc->dsc", cond_act, slot_grad_out)
    time_grad = dot_low("gd,gsc->dsc", time_act, time_cols)

    dense_place = np.full((UNITS + 1,), 0, np.int32)
    dense_place[dense_units] = np.arange(len(dense_units))
    slot_place = jnp.asarray(dense_place)[unit_of_slot]
    all_rows = jnp.concatenate(
        [
            grad_rows[l, i].reshape(rows, -1, BLOCK)
            for l in range(LAYERS)
            for i in range(4)
        ],
        1,
    )
    slot_rows = jnp.take(all_rows, slot_place, axis=1)
    dense_grad = plan.restore_rows(
        lax.all_to_all(slot_rows, AXES, split_axis=1, concat_axis=0, tiled=True)
    ).astype(jnp.float32)

    owned_grad = jnp.where(
        is_image[None, :, None],
        image_grad,
        jnp.where(is_time[None, :, None], time_grad, dense_grad),
    )
    used = (my_unit >= 0)[None, :, None]
    rate = rate_factor * unit_scale(jnp.maximum(my_unit, 0))[None, :, None]
    new_w, new_first, new_second = adam_update(
        master, first_moment, second_moment, owned_grad, rate
    )
    new_master = jnp.where(used, new_w, master)
    new_first = jnp.where(used, new_first, first_moment)
    new_second = jnp.where(used, new_second, second_moment)
    small_rate = rate_factor * table_scale(jnp.arange(small.shape[0], dtype=jnp.int32))[:, None]
    new_small, new_small_first, new_small_second = adam_update(
        small, small_first, small_second, small_grad, small_rate
    )
    return (
        loss_sum,
        weight_total,
        new_master,
        new_first,
        new_second,
        new_small,
        new_small_first,
        new_small_second,
    )


def solution(mesh):
    return jax.shard_map(
        on_device,
        mesh=mesh,
        in_specs=(
            P(("rep", "shard"), None),
            P(("rep", "shard"), None),
            P(("rep", "shard")),
            P(("rep", "shard")),
            P(),
            P(None, ("rep", "shard"), None),
            P(None, ("rep", "shard"), None),
            P(None, ("rep", "shard"), None),
            P(),
            P(),
            P(),
        ),
        out_specs=(
            P(),
            P(),
            P(None, ("rep", "shard"), None),
            P(None, ("rep", "shard"), None),
            P(None, ("rep", "shard"), None),
            P(),
            P(),
            P(),
        ),
        check_vma=False,
    )
```

```python
import jax
import jax.numpy as jnp
import numpy as np
from jax import lax
from jax.experimental import pallas as pl
from jax.experimental.pallas import tpu as pltpu
from jax.sharding import PartitionSpec as P

D = 768
HEADS = 12
HEAD_DIM = 64
FF = 3072
FREQ = 256
CLASSES = 1000
CHANNELS = 16
GRID = 16
PATCHES = 256
LAYERS = 2
TSTEPS = 1000
STEP = 10
BLOCK = 128
LAYER_COLS = 13824
LAYER_UNITS = 108
UNITS = 234

ADA_UNITS = 6 * D // BLOCK
DENSE_UNITS = LAYER_UNITS - ADA_UNITS
DENSE_COLS = DENSE_UNITS * BLOCK
TIME_UNITS = D // BLOCK
TAIL_FIRST = LAYERS * LAYER_UNITS
AXES = ("rep", "shard")


beta_one = 0.5
beta_two = 0.5
adam_eps = 1e-08
decay_rate = 0.1
rate_factor = 0.5


def gelu_tanh(values):
    return jax.nn.gelu(values, approximate=True)


def norm_rows(hidden):
    centered = hidden - jnp.mean(hidden, -1, keepdims=True)
    return centered * lax.rsqrt(jnp.mean(centered * centered, -1, keepdims=True) + 1e-06)


def local_back(function, primal, upstream):
    return jax.vjp(function, primal)[1](upstream)[0]


def dot_low(pattern, left_side, right_side):
    return jnp.einsum(pattern, left_side, right_side, preferred_element_type=jnp.float32)


def positions():
    quarter = D // 4
    angular = jnp.exp(-jnp.log(10000.0) * jnp.arange(quarter, dtype=jnp.float32) / quarter)
    patch_idx = jnp.arange(PATCHES, dtype=jnp.int32)
    row_pos = (patch_idx // GRID).astype(jnp.float32)[:, None] * angular
    col_pos = (patch_idx % GRID).astype(jnp.float32)[:, None] * angular
    return jnp.concatenate(
        [jnp.sin(col_pos), jnp.cos(col_pos), jnp.sin(row_pos), jnp.cos(row_pos)], -1
    )


def frequencies(times):
    half_size = FREQ // 2
    spacing = jnp.exp(-jnp.log(10000.0) * jnp.arange(half_size, dtype=jnp.float32) / half_size)
    angles = 1000.0 * times[:, None] * spacing
    return jnp.concatenate([jnp.cos(angles), jnp.sin(angles)], -1)


def unit_scale(unit_ids):
    column = unit_ids % LAYER_UNITS * BLOCK
    in_layer = unit_ids < LAYERS * LAYER_UNITS
    is_output = in_layer & (column >= 9 * D) & (column < 10 * D)
    is_down = in_layer & (column >= 10 * D + FF)
    factor = jnp.where(is_output, 4.0, jnp.where(is_down, 1.5 * (D / FF) ** 0.5, 1.0))
    return factor / D**0.5


def table_scale(row_ids):
    return jnp.where(
        row_ids < CHANNELS,
        CHANNELS ** (-0.5),
        jnp.where(
            row_ids < CHANNELS + FREQ,
            FREQ ** (-0.5),
            jnp.where(row_ids < CHANNELS + FREQ + CLASSES, 0.5, D ** (-0.5)),
        ),
    )


def adam_update(weight, first_mom, second, gradient, rate):
    first_new = beta_one * first_mom + (1.0 - beta_one) * gradient
    second_new = beta_two * second + (1.0 - beta_two) * gradient * gradient
    ratio = (
        first_new
        / (1.0 - beta_one**STEP)
        / (jnp.sqrt(second_new / (1.0 - beta_two**STEP)) + adam_eps)
    )
    return (weight - rate * (ratio + decay_rate * weight), first_new, second_new)


def modulate(normed, shift, scale):
    return normed * (1.0 + scale[:, None, :]) + shift[:, None, :]


def layer_forward(hidden, modul, weights):
    w_qkv, w_out, w_up, w_down = weights
    shift_a, scale_a, gate_a, shift_b, scale_b, gate_b = jnp.split(modul, 6, -1)
    attn_in = modulate(norm_rows(hidden), shift_a, scale_a).astype(jnp.bfloat16)
    qkv_all = dot_low("gpd,de->gpe", attn_in, w_qkv).astype(jnp.bfloat16)
    heads_out = attend(qkv_all)
    branch_a = dot_low("gpd,de->gpe", heads_out, w_out)
    middle = hidden + gate_a[:, None, :] * branch_a
    mlp_in = modulate(norm_rows(middle), shift_b, scale_b).astype(jnp.bfloat16)
    pre_act = dot_low("gpd,df->gpf", mlp_in, w_up)
    post_act = gelu_tanh(pre_act).astype(jnp.bfloat16)
    branch_b = dot_low("gpf,df->gpd", post_act, w_down)
    output = middle + gate_b[:, None, :] * branch_b
    return (
        output,
        (
            hidden,
            modul,
            attn_in,
            qkv_all,
            heads_out,
            branch_a,
            middle,
            mlp_in,
            pre_act.astype(jnp.bfloat16),
            post_act,
            branch_b,
        ),
    )


def layer_backward(grad_out, weights, saved):
    w_qkv, w_out, w_up, w_down = weights
    (
        hidden,
        modul,
        attn_in,
        qkv_all,
        heads_out,
        branch_a,
        middle,
        mlp_in,
        pre_act,
        post_act,
        branch_b,
    ) = saved
    shift_a, scale_a, gate_a, shift_b, scale_b, gate_b = jnp.split(modul, 6, -1)
    grad_gate_b = jnp.sum(grad_out * branch_b, 1)
    grad_branch_b = (gate_b[:, None, :] * grad_out).astype(jnp.bfloat16)
    grad_down = (grad_branch_b, post_act)
    grad_post = dot_low("gpd,df->gpf", grad_branch_b, w_down)
    grad_pre = local_back(gelu_tanh, pre_act.astype(jnp.float32), grad_post).astype(jnp.bfloat16)
    grad_up = (mlp_in, grad_pre)
    grad_mlp_in = dot_low("gpf,df->gpd", grad_pre, w_up)
    normed_b = norm_rows(middle)
    grad_scale_b = jnp.sum(grad_mlp_in * normed_b, 1)
    grad_shift_b = jnp.sum(grad_mlp_in, 1)
    grad_middle = grad_out + local_back(
        norm_rows, middle, grad_mlp_in * (1.0 + scale_b[:, None, :])
    )
    grad_gate_a = jnp.sum(grad_middle * branch_a, 1)
    grad_branch_a = (gate_a[:, None, :] * grad_middle).astype(jnp.bfloat16)
    grad_out_w = (heads_out, grad_branch_a)
    grad_heads = dot_low("gpe,de->gpd", grad_branch_a, w_out).astype(jnp.bfloat16)
    grad_qkv = attend_back(qkv_all, grad_heads)
    grad_qkv_w = (attn_in, grad_qkv)
    grad_attn_in = dot_low("gpe,de->gpd", grad_qkv, w_qkv)
    normed_a = norm_rows(hidden)
    grad_scale_a = jnp.sum(grad_attn_in * normed_a, 1)
    grad_shift_a = jnp.sum(grad_attn_in, 1)
    grad_in = grad_middle + local_back(
        norm_rows, hidden, grad_attn_in * (1.0 + scale_a[:, None, :])
    )
    grad_modul = jnp.concatenate(
        [grad_shift_a, grad_scale_a, grad_gate_a, grad_shift_b, grad_scale_b, grad_gate_b], -1
    ).astype(jnp.bfloat16)
    return (grad_in, grad_modul, [grad_qkv_w, grad_out_w, grad_up, grad_down])


MESH = pl.DeviceIdType.MESH
GATHER_VMEM = 40 * 2**20
SCATTER_VMEM = 56 * 2**20


def dot_rows(left_side, right_side):
    return lax.dot_general(
        left_side, right_side, (((0,), (0,)), ((), ())), preferred_element_type=jnp.float32
    )


def row_product(left_side, right_side):
    left_side = left_side.reshape(-1, left_side.shape[-1])
    right_side = right_side.reshape(-1, right_side.shape[-1])
    return dot_rows(left_side, right_side).astype(jnp.bfloat16)


def unit_groups():
    groups, place = [], 0
    for number in (3 * D, D, FF, FF) * LAYERS + (D,):
        groups.append((place, number // BLOCK))
        place += number // BLOCK
    return groups


def head_mask(number):
    lane = lax.broadcasted_iota(jnp.int32, (PATCHES, 2 * HEAD_DIM), 1)
    return (lane >= number * HEAD_DIM) & (lane < (number + 1) * HEAD_DIM)


def dot_lanes(left_side, right_side):
    return lax.dot_general(
        left_side, right_side, (((1,), (1,)), ((), ())), preferred_element_type=jnp.float32
    )


def attend_kernel(queries, keys_all, values, out):
    row = lax.broadcasted_iota(jnp.int32, (2 * HEAD_DIM, PATCHES), 0)
    scaled = queries[0] * HEAD_DIM ** (-0.5)
    result = jnp.zeros((2 * HEAD_DIM, PATCHES), jnp.float32)
    for number in (0, 1):
        one = jnp.where(head_mask(number), scaled, jnp.zeros((), jnp.bfloat16))
        scores = dot_lanes(keys_all[0], one)
        powers = jnp.exp(scores - jnp.max(scores, 0, keepdims=True))
        prob = (powers * (1.0 / jnp.sum(powers, 0, keepdims=True))).astype(jnp.bfloat16)
        result = jnp.where(row // HEAD_DIM == number, dot_rows(values[0], prob), result)
    out[0] = result.T.astype(jnp.bfloat16)


def attend_back_kernel(queries, keys_all, values, grad, out):
    pair = pl.program_id(1)
    row = lax.broadcasted_iota(jnp.int32, (2 * HEAD_DIM, PATCHES), 0)
    scaled = queries[0] * HEAD_DIM ** (-0.5)
    grad_queries = jnp.zeros((2 * HEAD_DIM, PATCHES), jnp.float32)
    grad_keys = jnp.zeros((PATCHES, 2 * HEAD_DIM), jnp.float32)
    grad_values = grad_keys
    none = jnp.zeros((), jnp.bfloat16)
    for number in (0, 1):
        mask = head_mask(number)
        scores = dot_lanes(keys_all[0], jnp.where(mask, scaled, none))
        powers = jnp.exp(scores - jnp.max(scores, 0, keepdims=True))
        prob = powers * (1.0 / jnp.sum(powers, 0, keepdims=True))
        grad_prob = dot_lanes(values[0], jnp.where(mask, grad[0], none))
        inner = jnp.sum(prob * grad_prob, 0, keepdims=True)
        grad_scores = (prob * (grad_prob - inner)).astype(jnp.bfloat16)
        part = dot_rows(keys_all[0], grad_scores)
        grad_queries = jnp.where(row // HEAD_DIM == number, part, grad_queries)
        part = jnp.dot(grad_scores, scaled, preferred_element_type=jnp.float32)
        grad_keys = jnp.where(mask, part, grad_keys)
        part = jnp.dot(prob.astype(jnp.bfloat16), grad[0], preferred_element_type=jnp.float32)
        grad_values = jnp.where(mask, part, grad_values)
    grad_queries = grad_queries.T * HEAD_DIM ** (-0.5)
    for third, result in enumerate((grad_queries, grad_keys, grad_values)):
        first = pl.multiple_of(third * D + pair * 2 * HEAD_DIM, 2 * HEAD_DIM)
        out[0, :, pl.ds(first, 2 * HEAD_DIM)] = result.astype(jnp.bfloat16)


def pair_block(third):
    pairs = HEADS // 2
    return pl.BlockSpec(
        (1, PATCHES, 2 * HEAD_DIM), lambda image, pair: (image, 0, third * pairs + pair)
    )


def attend(qkv_all):
    images = qkv_all.shape[0]
    pairs = HEADS // 2
    return pl.pallas_call(
        attend_kernel,
        grid=(images, pairs),
        out_shape=jax.ShapeDtypeStruct((images, PATCHES, D), jnp.bfloat16),
        in_specs=[pair_block(0), pair_block(1), pair_block(2)],
        out_specs=pair_block(0),
        cost_estimate=pl.CostEstimate(
            flops=4 * images * PATCHES * PATCHES * D,
            bytes_accessed=8 * images * PATCHES * D,
            transcendentals=images * HEADS * PATCHES * PATCHES,
        ),
    )(qkv_all, qkv_all, qkv_all)


def attend_back(qkv_all, grad_heads):
    images = qkv_all.shape[0]
    pairs = HEADS // 2
    return pl.pallas_call(
        attend_back_kernel,
        grid=(images, pairs),
        out_shape=jax.ShapeDtypeStruct((images, PATCHES, 3 * D), jnp.bfloat16),
        in_specs=[pair_block(0), pair_block(1), pair_block(2), pair_block(0)],
        out_specs=pl.BlockSpec((1, PATCHES, 3 * D), lambda image, pair: (image, 0, 0)),
        cost_estimate=pl.CostEstimate(
            flops=10 * images * PATCHES * PATCHES * D,
            bytes_accessed=14 * images * PATCHES * D,
            transcendentals=images * HEADS * PATCHES * PATCHES,
        ),
    )(qkv_all, qkv_all, qkv_all, grad_heads)


def place_of():
    rep = lax.axis_index("rep")
    return rep // 4, (rep // 2) % 2, rep % 2, lax.axis_index("shard")


def rep_of(y, x, c):
    return (y * 2 + x) * 2 + c


def device_at(j):
    shards = lax.axis_size("shard")
    devices = lax.axis_size("rep") * shards
    me = lax.axis_index("rep") * shards + lax.axis_index("shard")
    peer = lax.rem(me + j, devices)
    return peer, (peer // shards, lax.rem(peer, shards))


def meet_all(devices):
    barrier = pltpu.get_barrier_semaphore()

    @pl.loop(1, devices)
    def _(j):
        pl.semaphore_signal(barrier, inc=1, device_id=device_at(j)[1], device_id_type=MESH)

    pl.semaphore_wait(barrier, devices - 1)


def neighbours():
    y, x, c, z = place_of()
    to_x = (rep_of(y, 1 - x, c), z)
    to_y = (rep_of(1 - y, x, c), z)
    to_core = (rep_of(y, x, 1 - c), z)
    to_z = [(rep_of(y, x, c), lax.rem(z + step, 4)) for step in (1, 2, 3)]
    return to_x, to_y, to_core, to_z


def gather_kernel(widths, bases, *refs):
    count = len(widths)
    units, info, low_slots = refs[:3]
    outs = refs[3 : count + 3]
    every_info, cond_out, modul_out = refs[count + 3 : count + 6]
    pieces = refs[count + 6 : 2 * count + 6]
    time_two, parts, own_sem, send_sem, recv_sem, time_sem, modul_sem, info_sem = refs[
        2 * count + 6 :
    ]
    devices, images = modul_out.shape[:2]
    slots = low_slots.shape[0]
    y, x, c, z = place_of()
    to_x, to_y, to_core, to_z = neighbours()
    me = rep_of(y, x, c) * 4 + z
    meet_all(devices)

    def remote(k, number, source, dest, target):
        return pltpu.make_async_remote_copy(
            src_ref=source,
            dst_ref=dest,
            send_sem=send_sem.at[k, number],
            recv_sem=recv_sem.at[k, number],
            device_id=target,
            device_id_type=MESH,
        )

    def own_copy(k):
        return pltpu.make_async_copy(pieces[k], outs[k].at[c, y, x, z], own_sem.at[k])

    def line_copies(k, arriving):
        copies = []
        for step in (1, 2, 3):
            at_z = lax.rem(z + 4 - step, 4) if arriving else z
            copies.append(
                remote(k, step - 1, pieces[k], outs[k].at[c, y, x, at_z], to_z[step - 1])
            )
        return copies

    def first_copies(k, arriving):
        half = widths[k] // 2
        left, right = pl.ds(0, half), pl.ds(half, half)
        at_x = 1 - x if arriving else x
        at_y = 1 - y if arriving else y
        a_block = outs[k].at[c, y, at_x, :, :, left]
        b_block = outs[k].at[c, at_y, x, :, :, right]
        return [remote(k, 3, a_block, a_block, to_x), remote(k, 4, b_block, b_block, to_y)]

    def second_copies(k, arriving):
        half = widths[k] // 2
        left, right = pl.ds(0, half), pl.ds(half, half)
        at_x = 1 - x if arriving else x
        at_y = 1 - y if arriving else y
        a_block = outs[k].at[c, at_y, :, :, :, left]
        b_block = outs[k].at[c, :, at_x, :, :, right]
        return [remote(k, 5, a_block, a_block, to_y), remote(k, 6, b_block, b_block, to_x)]

    def core_copies(k, arriving):
        block = outs[k].at[1 - c if arriving else c]
        return [remote(k, 7, block, block, to_core)]

    def start(copies):
        for copy in copies:
            copy.start()

    def arrived(copies):
        for copy in copies:
            copy.wait_recv()

    def modul_copy(j, arriving):
        peer, where = device_at(devices - j if arriving else j)
        return pltpu.make_async_remote_copy(
            src_ref=parts.at[pl.ds(peer * images, images)],
            dst_ref=modul_out.at[peer if arriving else me],
            send_sem=modul_sem.at[0, j],
            recv_sem=modul_sem.at[1, j],
            device_id=where,
            device_id_type=MESH,
        )

    def info_copy(j, arriving):
        peer, where = device_at(devices - j if arriving else j)
        return pltpu.make_async_remote_copy(
            src_ref=info,
            dst_ref=every_info.at[pl.ds((peer if arriving else me) * images, images)],
            send_sem=info_sem.at[0, j],
            recv_sem=info_sem.at[1, j],
            device_id=where,
            device_id_type=MESH,
        )

    def info_rows(first):
        return jnp.concatenate([every_info[:, first + j, :] for j in range(D // BLOCK)], -1)

    def image_products():
        copy = pltpu.make_async_copy(outs[0], time_two, time_sem)
        copy.start()

        @pl.loop(1, devices)
        def _(j):
            info_copy(j, True).wait_recv()
            info_copy(j, False).wait_send()

        copy.wait()
        weight = time_two[...].astype(jnp.float32).reshape(D, D).astype(jnp.bfloat16)
        cond = jnp.dot(
            info_rows(0).astype(jnp.bfloat16), weight, preferred_element_type=jnp.float32
        )
        cond = cond + info_rows(8)
        cond_out[...] = cond
        act = (cond * jax.nn.sigmoid(cond)).astype(jnp.bfloat16)
        for s in range(slots):
            parts[:, s, :] = jnp.dot(act, low_slots[s], preferred_element_type=jnp.float32)
        for i in range(images):
            modul_out[me, i] = parts[me * images + i]

        @pl.loop(1, devices)
        def _(j):
            modul_copy(j, False).start()

    @pl.loop(1, devices)
    def _(j):
        info_copy(j, False).start()

    for i in range(images):
        every_info[me * images + i] = info[i]
    def send_piece(k):
        for n in range(widths[k] // BLOCK):
            pieces[k][:, n * BLOCK : (n + 1) * BLOCK] = units[bases[k] + n]
        start(line_copies(k, False))
        own_copy(k).start()

    send_piece(0)
    for t in range(count + 2):
        if t + 1 < count:
            send_piece(t + 1)
        if t < count:
            own_copy(t).wait()
            arrived(line_copies(t, True))
            start(first_copies(t, False))
        if 0 <= t - 1 < count:
            arrived(first_copies(t - 1, True))
            start(second_copies(t - 1, False))
        if 0 <= t - 2 < count:
            arrived(second_copies(t - 2, True))
            start(core_copies(t - 2, False))
        if t == 3:
            arrived(core_copies(0, True))
            image_products()
    for k in range(1, count):
        arrived(core_copies(k, True))

    @pl.loop(1, devices)
    def _(j):
        modul_copy(j, True).wait_recv()
        modul_copy(j, False).wait_send()

    for k in range(count):
        for copies in (line_copies, first_copies, second_copies, core_copies):
            for copy in copies(k, False):
                copy.wait_send()


def scatter_kernel(widths, bases, slots, *refs):
    count = len(widths)
    lefts, rights = refs[:count], refs[count : 2 * count]
    modul, pick, low_slots, edge, factor = refs[2 * count : 2 * count + 5]
    units, chosen, shared = refs[2 * count + 5 : 2 * count + 8]
    scratch = refs[2 * count + 8 :]
    own, first_in, second_in, line_in = (scratch[i * count : (i + 1) * count] for i in range(4))
    (
        left_in, left_turned, right_in, away, every_modul, parts, landed,
        load_sem, send_sem, recv_sem, modul_sem, part_sem, sum_sem,
    ) = scratch[4 * count :]
    devices, images = shared.shape[:2]
    y, x, c, z = place_of()
    to_x, to_y, to_core, to_z = neighbours()
    me = rep_of(y, x, c) * 4 + z
    rows = D // 32
    half_rows = D // 2
    meet_all(devices)

    def exchange(source, dest, sem, j, arriving):
        peer, where = device_at(devices - j if arriving else j)
        return pltpu.make_async_remote_copy(
            src_ref=source(peer, me),
            dst_ref=dest(peer if arriving else me),
            send_sem=sem.at[0, j],
            recv_sem=sem.at[1, j],
            device_id=where,
            device_id_type=MESH,
        )

    def modul_copies(step, arriving):
        if step == 0:
            copies = []
            for number in (1, 2, 3):
                at_z = lax.rem(z + 4 - number, 4) if arriving else z
                copies.append((modul, every_modul.at[y, x, c, at_z], to_z[number - 1]))
        else:
            at_x = 1 - x if arriving and step == 1 else x
            at_y = 1 - y if arriving and step == 2 else y
            at_c = 1 - c if arriving and step == 3 else c
            block = (
                every_modul.at[y, at_x, c],
                every_modul.at[at_y, :, c],
                every_modul.at[:, :, at_c],
            )[step - 1]
            copies = [(block, block, (to_x, to_y, to_core)[step - 1])]
        return [
            pltpu.make_async_remote_copy(
                src_ref=source,
                dst_ref=dest,
                send_sem=modul_sem.at[0, step, number],
                recv_sem=modul_sem.at[1, step, number],
                device_id=target,
                device_id_type=MESH,
            )
            for number, (source, dest, target) in enumerate(copies)
        ]

    def part_copy(j, arriving):
        return exchange(
            lambda peer, mine: parts.at[pl.ds(peer * images, images)],
            lambda owner: landed.at[owner],
            part_sem, j, arriving,
        )

    def sum_copy(j, arriving):
        return exchange(
            lambda peer, mine: shared.at[mine], lambda owner: shared.at[owner], sum_sem, j, arriving
        )

    def all_start(copy):
        @pl.loop(1, devices)
        def _(j):
            copy(j, False).start()

    def all_arrived(copy):
        @pl.loop(1, devices)
        def _(j):
            copy(j, True).wait_recv()

    def all_sent(copy):
        @pl.loop(1, devices)
        def _(j):
            copy(j, False).wait_send()

    def image_parts():
        arrived(modul_copies(3, True))

        @pl.loop(0, devices // 4)
        def _(i):
            for n in range(4):
                for m in range(images):
                    block = every_modul[i // 4, (i // 2) % 2, i % 2, n, m]
                    chosen[(i * 4 + n) * images + m] = jnp.dot(
                        pick[...], block, preferred_element_type=jnp.float32
                    )

        total = jnp.zeros((devices * images, D), jnp.float32)
        for s in range(slots):
            total = total + lax.dot_general(
                chosen[:, s, :].astype(jnp.bfloat16),
                low_slots[s],
                (((1,), (1,)), ((), ())),
                preferred_element_type=jnp.float32,
            )
        parts[...] = edge[...]
        for j in range(D // BLOCK):
            parts[:, j, :] = total[:, j * BLOCK : (j + 1) * BLOCK]
        all_start(part_copy)
        for i in range(images):
            landed[me, i] = parts[me * images + i]

    def image_sums():
        all_arrived(part_copy)
        shared[me] = jnp.sum(landed[...], 0) * factor[...]
        all_start(sum_copy)

    def remote(k, number, source, dest, target):
        return pltpu.make_async_remote_copy(
            src_ref=source,
            dst_ref=dest,
            send_sem=send_sem.at[k, number],
            recv_sem=recv_sem.at[k, number],
            device_id=target,
            device_id_type=MESH,
        )

    def load_left(k):
        return pltpu.make_async_copy(lefts[k], left_in.at[k % 2], load_sem.at[0, k % 2])

    def load_right(k):
        place = right_in.at[k % 3, :, pl.ds(0, widths[k])]
        return pltpu.make_async_copy(rights[k], place, load_sem.at[1, k % 3])

    def core_copies(k):
        source = away.at[k % 3, :, :, :, :, pl.ds(0, widths[k])]
        return [remote(k, 0, source, own[k], to_core)]

    def first_copies(k):
        half = widths[k] // 2
        return [
            remote(k, 1, own[k].at[:, 1 - x, :, :, pl.ds(0, half)], first_in[k].at[0], to_x),
            remote(k, 2, own[k].at[1 - y, :, :, :, pl.ds(half, half)], first_in[k].at[1], to_y),
        ]

    def second_copies(k):
        half = widths[k] // 2
        return [
            remote(k, 3, own[k].at[1 - y, x, :, :, pl.ds(0, half)], second_in[k].at[0], to_y),
            remote(k, 4, own[k].at[y, 1 - x, :, :, pl.ds(half, half)], second_in[k].at[1], to_x),
        ]

    def line_copies(k):
        return [
            remote(
                k,
                4 + step,
                own[k].at[y, x, lax.rem(z + step, 4)],
                line_in[k].at[step - 1],
                to_z[step - 1],
            )
            for step in (1, 2, 3)
        ]

    def start(copies):
        for copy in copies:
            copy.start()

    def arrived(copies):
        for copy in copies:
            copy.wait_recv()

    def products(k, half, store):
        slot = k % 3
        tile = D

        @pl.loop(0, widths[k] // tile)
        def _(n):
            columns = pl.ds(pl.multiple_of(n * tile, tile), tile)
            left = left_turned[slot, pl.ds(pl.multiple_of(half * half_rows, half_rows), half_rows)]
            result = jnp.dot(left, right_in[slot, :, columns], preferred_element_type=jnp.float32)
            for i in range(16):
                at = (i // 8, (i // 4) % 2, i % 4, slice(None), columns)
                store(at, result[i * rows : (i + 1) * rows])

    def away_products(k):
        load_left(k).wait()
        load_right(k).wait()
        left_turned[k % 3] = left_in[k % 2].T
        if k + 2 < count:
            load_left(k + 2).start()
        if k >= 3:
            for copy in core_copies(k - 3):
                copy.wait_send()

        def store(at, value):
            away[(k % 3,) + at] = value.astype(jnp.bfloat16)

        products(k, 1 - c, store)
        start(core_copies(k))

    def own_products(k):
        def store(at, value):
            own[k][at] = (value + own[k][at].astype(jnp.float32)).astype(jnp.bfloat16)

        products(k, c, store)

    def first_sum(k):
        half = widths[k] // 2

        @pl.loop(0, 8)
        def _(i):
            two, at_z = i // 4, i % 4
            a_at = (two, x, at_z, slice(None), pl.ds(0, half))
            b_at = (y, two, at_z, slice(None), pl.ds(half, half))
            own[k][a_at] = own[k][a_at] + first_in[k][0, two, at_z]
            own[k][b_at] = own[k][b_at] + first_in[k][1, two, at_z]

    def second_sum(k):
        half = widths[k] // 2

        @pl.loop(0, 4)
        def _(at_z):
            a_at = (y, x, at_z, slice(None), pl.ds(0, half))
            b_at = (y, x, at_z, slice(None), pl.ds(half, half))
            own[k][a_at] = own[k][a_at] + second_in[k][0, at_z]
            own[k][b_at] = own[k][b_at] + second_in[k][1, at_z]

    start(modul_copies(0, False))
    every_modul[y, x, c, z] = modul[...]
    for k in range(min(3, count)):
        load_right(k).start()
        if k < 2:
            load_left(k).start()
    away_products(0)
    for t in range(count + 3):
        if t + 1 < count:
            away_products(t + 1)
        if t < count:
            arrived(core_copies(t))
            own_products(t)
            start(first_copies(t))
            if t + 3 < count:
                load_right(t + 3).start()
        if 0 <= t - 1 < count:
            arrived(first_copies(t - 1))
            first_sum(t - 1)
            start(second_copies(t - 1))
        if 0 <= t - 2 < count:
            arrived(second_copies(t - 2))
            second_sum(t - 2)
            start(line_copies(t - 2))
        if 0 <= t - 3 < count:
            k = t - 3
            arrived(line_copies(k))
            total = own[k][y, x, z].astype(jnp.float32)
            for step in (1, 2, 3):
                total = total + line_in[k][step - 1].astype(jnp.float32)
            for n in range(widths[k] // BLOCK):
                part = total[:, n * BLOCK : (n + 1) * BLOCK]
                units[bases[k] + n] = part.astype(jnp.bfloat16)
        if t < 3:
            arrived(modul_copies(t, True))
            start(modul_copies(t + 1, False))
        if t == 3:
            image_parts()
        if t == 6:
            image_sums()
    all_arrived(sum_copy)
    for copy in (part_copy, sum_copy):
        all_sent(copy)
    for step in range(4):
        for copy in modul_copies(step, False):
            copy.wait_send()
    for k in range(count):
        for copies in (core_copies, first_copies, second_copies, line_copies):
            if copies is core_copies and k + 3 < count:
                continue
            for copy in copies(k):
                copy.wait_send()


class RingPlan:
    def split_rows(self, values):
        slots = values.shape[0]
        split = values.reshape(slots, 2, 2, 2, 4, D // 32, BLOCK)
        return split.transpose(2, 3, 1, 4, 0, 5, 6).reshape(32, slots, D // 32, BLOCK)

    def join_rows(self, values):
        slots = values.shape[1]
        split = values.reshape(2, 2, 2, 4, slots, D // 32, BLOCK)
        return split.transpose(4, 2, 0, 1, 3, 5, 6).reshape(slots, D, BLOCK)

    def gather(self, units, info, low_slots):
        names = unit_groups()
        turn = [len(names) - 1] + sorted(range(len(names) - 1), key=lambda n: (n % 4 == 1, n))
        bases = tuple(names[n][0] for n in turn)
        widths = tuple(names[n][1] * BLOCK for n in turn)
        count, rows = len(turn), D // 32
        all_images = 32 * info.shape[0]
        slots = low_slots.shape[0]
        room = -(-slots // 8) * 8
        size = sum(4 * D * width for width in widths)
        whole_shape = [(2, 2, 2, 4, rows, width) for width in widths]
        *whole, every_info, cond, modul = pl.pallas_call(
            lambda *refs: gather_kernel(widths, bases, *refs),
            out_shape=[
                jax.ShapeDtypeStruct(shape, jnp.bfloat16) for shape in whole_shape
            ]
            + [
                jax.ShapeDtypeStruct((all_images,) + info.shape[1:], jnp.float32),
                jax.ShapeDtypeStruct((all_images, D), jnp.float32),
                jax.ShapeDtypeStruct((32, all_images // 32, room, BLOCK), jnp.float32),
            ],
            in_specs=[pl.BlockSpec(memory_space=pltpu.VMEM)] * 3,
            out_specs=[pl.BlockSpec(memory_space=pl.ANY)] * count
            + [pl.BlockSpec(memory_space=pltpu.VMEM)] * 3,
            scratch_shapes=[pltpu.VMEM((rows, width), jnp.bfloat16) for width in widths]
            + [
                pltpu.VMEM(whole_shape[0], jnp.bfloat16),
                pltpu.VMEM((all_images, room, BLOCK), jnp.float32),
                pltpu.SemaphoreType.DMA((count,)),
                pltpu.SemaphoreType.DMA((count, 8)),
                pltpu.SemaphoreType.DMA((count, 8)),
                pltpu.SemaphoreType.DMA,
                pltpu.SemaphoreType.DMA((2, 32)),
                pltpu.SemaphoreType.DMA((2, 32)),
            ],
            compiler_params=pltpu.CompilerParams(
                collective_id=0, has_side_effects=True, vmem_limit_bytes=GATHER_VMEM
            ),
            cost_estimate=pl.CostEstimate(flops=0, bytes_accessed=size, transcendentals=0),
        )(units, info, low_slots)
        whole = [part.reshape(D, -1) for part in whole]
        modul = jnp.swapaxes(modul[:, :, :slots], 0, 1).reshape(-1, 32 * slots, BLOCK)
        ordered = [whole[turn.index(n)] for n in range(count)]
        return ordered[:-1], ordered[-1], every_info, cond, modul

    def scatter(self, layer_grads, modul, pick, low_slots, edge, factor):
        turn = [(l, n) for l in range(LAYERS) for n in (0, 2, 3)]
        turn = [(LAYERS - 1, 1)] + turn + [(l, 1) for l in range(LAYERS - 1)]
        grads = [layer_grads[l][n] for l, n in turn]
        names = unit_groups()
        bases = tuple(names[4 * l + n][0] for l, n in turn)
        lefts = [left.reshape(-1, D) for left, _ in grads]
        rights = [right.reshape(left.shape[0], -1) for (_, right), left in zip(grads, lefts)]
        widths = tuple(right.shape[1] for right in rights)
        count, rows, tokens = len(grads), D // 32, lefts[0].shape[0]
        widest = max(widths)
        images, slots = modul.shape[0], low_slots.shape[0]
        size = sum(4 * D * width for width in widths)
        scratch = [pltpu.VMEM((2, 2, 4, rows, width), jnp.bfloat16) for width in widths]
        scratch += [pltpu.VMEM((2, 2, 4, rows, width // 2), jnp.bfloat16) for width in widths]
        scratch += [pltpu.VMEM((2, 4, rows, width // 2), jnp.bfloat16) for width in widths]
        scratch += [pltpu.VMEM((3, rows, width), jnp.bfloat16) for width in widths]
        units, chosen, shared = pl.pallas_call(
            lambda *refs: scatter_kernel(widths, bases, slots, *refs),
            out_shape=[
                jax.ShapeDtypeStruct((sum(widths) // BLOCK, rows, BLOCK), jnp.bfloat16),
                jax.ShapeDtypeStruct((32 * images, pick.shape[0], BLOCK), jnp.float32),
                jax.ShapeDtypeStruct((32,) + factor.shape, jnp.float32),
            ],
            in_specs=[pl.BlockSpec(memory_space=pl.ANY)] * (2 * count)
            + [pl.BlockSpec(memory_space=pltpu.VMEM)] * 5,
            out_specs=[pl.BlockSpec(memory_space=pltpu.VMEM)] * 3,
            scratch_shapes=scratch
            + [
                pltpu.VMEM((2, tokens, D), jnp.bfloat16),
                pltpu.VMEM((3, D, tokens), jnp.bfloat16),
                pltpu.VMEM((3, tokens, widest), jnp.bfloat16),
                pltpu.VMEM((3, 2, 2, 4, rows, widest), jnp.bfloat16),
                pltpu.VMEM((2, 2, 2, 4) + modul.shape, jnp.bfloat16),
                pltpu.VMEM(edge.shape, jnp.float32),
                pltpu.VMEM((32,) + factor.shape, jnp.float32),
                pltpu.SemaphoreType.DMA((2, 3)),
                pltpu.SemaphoreType.DMA((count, 8)),
                pltpu.SemaphoreType.DMA((count, 8)),
                pltpu.SemaphoreType.DMA((2, 4, 3)),
                pltpu.SemaphoreType.DMA((2, 32)),
                pltpu.SemaphoreType.DMA((2, 32)),
            ],
            compiler_params=pltpu.CompilerParams(
                collective_id=1, has_side_effects=True, vmem_limit_bytes=SCATTER_VMEM
            ),
            cost_estimate=pl.CostEstimate(flops=0, bytes_accessed=size, transcendentals=0),
        )(*lefts, *rights, modul, pick, low_slots, edge, factor)
        return units, chosen[:, :slots].astype(jnp.bfloat16), shared


class PlainPlan:
    def split_rows(self, values):
        slots, devices = values.shape[0], lax.axis_size("rep") * lax.axis_size("shard")
        return jnp.swapaxes(values.reshape(slots, devices, -1, BLOCK), 0, 1)

    def join_rows(self, values):
        return jnp.swapaxes(values, 0, 1).reshape(-1, D, BLOCK)

    def gather(self, units, info, low_slots):
        whole = []
        for first, number in unit_groups():
            piece = jnp.swapaxes(units[first : first + number], 0, 1)
            piece = piece.reshape(-1, number * BLOCK)
            whole.append(lax.all_gather(piece, AXES, axis=0, tiled=True))
        every_info = lax.all_gather(info, AXES, axis=0, tiled=True)
        blocks = D // BLOCK
        time_act = every_info[:, :blocks].reshape(-1, D).astype(jnp.bfloat16)
        cond = jnp.dot(time_act, whole[-1], preferred_element_type=jnp.float32)
        cond = cond + every_info[:, 8 : 8 + blocks].reshape(-1, D)
        modul = dot_low("gd,sdc->gsc", jax.nn.silu(cond).astype(jnp.bfloat16), low_slots)
        modul = lax.all_to_all(modul, AXES, split_axis=0, concat_axis=1, tiled=True)
        return whole[:-1], whole[-1], every_info, cond, modul

    def scatter(self, layer_grads, modul, pick, low_slots, edge, factor):
        units = []
        for pair in (pair for grads in layer_grads for pair in grads):
            own = lax.psum_scatter(row_product(*pair), AXES, scatter_dimension=0, tiled=True)
            units.append(jnp.swapaxes(own.reshape(own.shape[0], -1, BLOCK), 0, 1))
        slots = low_slots.shape[0]
        every = lax.all_gather(modul, AXES, axis=0, tiled=True)
        chosen = dot_low("su,guc->gsc", pick, every)[:, :slots].astype(jnp.bfloat16)
        part = dot_low("gsc,sdc->gd", chosen, low_slots).reshape(-1, D // BLOCK, BLOCK)
        parts = edge.at[:, : D // BLOCK].set(part)
        own = lax.psum_scatter(parts, AXES, scatter_dimension=0, tiled=True) * factor
        shared = lax.all_gather(own, AXES, axis=0, tiled=False)
        return jnp.concatenate(units, 0), chosen, shared


def unit_lists():
    dense = np.concatenate(
        [np.arange(l * LAYER_UNITS + ADA_UNITS, (l + 1) * LAYER_UNITS) for l in range(LAYERS)]
    )
    time_units = np.arange(TAIL_FIRST, TAIL_FIRST + TIME_UNITS)
    image_units = np.concatenate(
        [np.arange(l * LAYER_UNITS, l * LAYER_UNITS + ADA_UNITS) for l in range(LAYERS)]
        + [np.arange(TAIL_FIRST + TIME_UNITS, UNITS)]
    )
    return dense, time_units, image_units


def on_device(
    latents,
    noise,
    labels,
    t_index,
    owner,
    master,
    first_moment,
    second_moment,
    small,
    small_first,
    small_second,
):
    count = lax.axis_size("rep") * lax.axis_size("shard")
    me = lax.axis_index(AXES)
    slot_dev = master.shape[1]
    slot_total = count * slot_dev
    rows = D // count
    images = latents.shape[0]
    dense_units, time_units, image_units = unit_lists()

    unit_of_slot = (
        jnp.full((slot_total,), -1, jnp.int32).at[owner].set(jnp.arange(UNITS, dtype=jnp.int32))
    )
    my_unit = lax.dynamic_slice_in_dim(unit_of_slot, me * slot_dev, slot_dev)
    low_slots = jnp.swapaxes(master.astype(jnp.bfloat16), 0, 1)

    plan = RingPlan() if (lax.axis_size("rep"), lax.axis_size("shard")) == (8, 4) else PlainPlan()
    spread = lax.all_to_all(
        plan.split_rows(low_slots), AXES, split_axis=0, concat_axis=0, tiled=True
    ).reshape(slot_total, rows, BLOCK)
    moved = np.concatenate([dense_units, time_units])
    units = jnp.take(spread, owner[moved], axis=0, mode="clip")

    x_start = latents.astype(jnp.float32).reshape(-1, PATCHES, CHANNELS)
    noise_f = noise.astype(jnp.float32).reshape(-1, PATCHES, CHANNELS)
    times = (t_index.astype(jnp.float32) + 0.5) / TSTEPS
    noisy = (1.0 - times)[:, None, None] * x_start + times[:, None, None] * noise_f
    target = noise_f - x_start
    loss_weight = 1.0 + 3.0 * times
    small_low = small.astype(jnp.bfloat16)
    patch_w = small_low[:CHANNELS]
    time_w = small_low[CHANNELS : CHANNELS + FREQ]
    table = small[CHANNELS + FREQ : CHANNELS + FREQ + CLASSES]
    head_w = small_low[CHANNELS + FREQ + CLASSES :]
    noisy_low = noisy.astype(jnp.bfloat16)
    hidden = dot_low("gpc,cd->gpd", noisy_low, patch_w) + positions()

    blocks = D // BLOCK
    freq_own = frequencies(times).astype(jnp.bfloat16)
    time_own = jnp.dot(freq_own, time_w, preferred_element_type=jnp.float32)
    act_own = jax.nn.silu(time_own).astype(jnp.bfloat16).astype(jnp.float32)
    label_own = jnp.take(table, labels, axis=0)
    numbers = jnp.stack([t_index, labels], 1).astype(jnp.float32)
    info = jnp.concatenate(
        [
            act_own.reshape(images, blocks, BLOCK),
            jnp.pad(numbers, ((0, 0), (0, BLOCK - 2)))[:, None],
            jnp.zeros((images, 7 - blocks, BLOCK), jnp.float32),
            label_own.reshape(images, blocks, BLOCK),
            jnp.zeros((images, 8 - blocks, BLOCK), jnp.float32),
        ],
        1,
    )
    whole, time_two, every_info, cond_all, slot_modul = plan.gather(
        units, info, low_slots
    )
    all_images = cond_all.shape[0]
    every_time = (every_info[:, blocks, 0] + 0.5) / TSTEPS
    every_label = every_info[:, blocks, 1].astype(jnp.int32)
    weight_total = jnp.sum(1.0 + 3.0 * every_time) * PATCHES
    freq_low = frequencies(every_time).astype(jnp.bfloat16)
    time_pre = jnp.dot(freq_low, time_w, preferred_element_type=jnp.float32)
    time_act = every_info[:, :blocks].reshape(all_images, D).astype(jnp.bfloat16)
    weights_all = [tuple(whole[4 * l : 4 * l + 4]) for l in range(LAYERS)]
    cond = lax.dynamic_slice_in_dim(cond_all, me * images, images)
    cond_act = jax.nn.silu(cond_all).astype(jnp.bfloat16)
    modul_all = jnp.take(slot_modul, owner[image_units], axis=1, mode="clip").reshape(images, -1)

    saved_all = []
    for l in range(LAYERS):
        hidden, saved = layer_forward(
            hidden, modul_all[:, l * 6 * D : (l + 1) * 6 * D], weights_all[l]
        )
        saved_all.append(saved)
    shift_f, scale_f = jnp.split(modul_all[:, LAYERS * 6 * D :], 2, -1)
    normed_f = norm_rows(hidden)
    final_in = modulate(normed_f, shift_f, scale_f).astype(jnp.bfloat16)
    predict = dot_low("gpd,cd->gpc", final_in, head_w)
    error = predict - target
    loss_part = jnp.sum(loss_weight[:, None, None] * error * error) / CHANNELS
    grad_pred = (loss_weight[:, None, None] * 2.0 * error / CHANNELS).astype(jnp.bfloat16)
    grad_head = dot_low("gpc,gpd->cd", grad_pred, final_in)
    grad_final_in = dot_low("gpc,cd->gpd", grad_pred, head_w)
    grad_modul_f = jnp.concatenate(
        [jnp.sum(grad_final_in, 1), jnp.sum(grad_final_in * normed_f, 1)], -1
    ).astype(jnp.bfloat16)
    grad_hidden = local_back(norm_rows, hidden, grad_final_in * (1.0 + scale_f[:, None, :]))
    layer_grads = [None] * LAYERS
    grad_moduls = [None] * LAYERS
    for l in reversed(range(LAYERS)):
        grad_hidden, grad_moduls[l], layer_grads[l] = layer_backward(
            grad_hidden, weights_all[l], saved_all[l]
        )
    grad_embed = grad_hidden.astype(jnp.bfloat16)
    grad_patch = dot_low("gpc,gpd->cd", noisy_low, grad_embed)

    image_place = np.full((UNITS + 1,), -1, np.int32)
    image_place[image_units] = np.arange(len(image_units))
    my_place = jnp.asarray(image_place)[my_unit]
    room_slots, room_units = -(-slot_dev // 16) * 16, -(-len(image_units) // 16) * 16
    pick = jnp.pad(my_place, (0, room_slots - slot_dev), constant_values=-1)[:, None]
    pick = (pick == jnp.arange(room_units, dtype=jnp.int32)).astype(jnp.bfloat16)
    modul_grad = jnp.concatenate(grad_moduls + [grad_modul_f], -1).reshape(images, -1, BLOCK)
    modul_grad = jnp.pad(modul_grad, ((0, 0), (0, room_units - len(image_units)), (0, 0)))
    edge = jnp.concatenate([grad_patch, grad_head], 0)
    edge_room = max(all_images, 4 * CHANNELS)
    edge = jnp.concatenate([edge, jnp.broadcast_to(loss_part, (2 * CHANNELS, D))], 0)
    edge = jnp.pad(edge, ((0, edge_room - 4 * CHANNELS), (0, 0)))[:all_images]
    edge = jnp.pad(edge.reshape(all_images, blocks, BLOCK), ((0, 0), (8, 8 - blocks), (0, 0)))
    factor = local_back(jax.nn.silu, cond, jnp.ones_like(cond)).reshape(images, blocks, BLOCK)
    factor = jnp.pad(factor, ((0, 0), (0, 16 - blocks), (0, 0)), constant_values=1.0)
    unit_grads, slot_grad_out, shared = plan.scatter(
        layer_grads, modul_grad, pick, low_slots, edge, factor
    )
    shared = shared.reshape(all_images, 16, BLOCK)
    grad_cond = shared[:, :blocks].reshape(all_images, D)
    edge = shared[:, 8 : 8 + blocks].reshape(all_images, D)
    grad_patch, grad_head = edge[:CHANNELS], edge[CHANNELS : 2 * CHANNELS]
    loss_sum = edge[2 * CHANNELS, 0]
    grad_time_out = grad_cond.astype(jnp.bfloat16)
    grad_time_act = dot_low("ge,de->gd", grad_time_out, time_two)
    grad_time_pre = local_back(jax.nn.silu, time_pre, grad_time_act).astype(jnp.bfloat16)
    grad_time_w = dot_low("gf,gd->fd", freq_low, grad_time_pre)
    grad_table = jnp.zeros((CLASSES, D), jnp.float32).at[every_label].add(grad_cond)
    small_grad = jnp.concatenate([grad_patch, grad_time_w, grad_table, grad_head], 0)

    my_time = jnp.clip(my_unit - TAIL_FIRST, 0, TIME_UNITS - 1)
    is_time = (my_unit >= TAIL_FIRST) & (my_unit < TAIL_FIRST + TIME_UNITS)
    time_cols = jnp.take(grad_time_out.reshape(all_images, TIME_UNITS, BLOCK), my_time, axis=1)
    is_image = my_place >= 0
    image_grad = dot_low("gd,gsc->dsc", cond_act, slot_grad_out)
    time_grad = dot_low("gd,gsc->dsc", time_act, time_cols)

    dense_place = np.full((UNITS + 1,), 0, np.int32)
    dense_place[dense_units] = np.arange(len(dense_units))
    slot_place = jnp.asarray(dense_place)[unit_of_slot]
    slot_rows = jnp.take(unit_grads, slot_place, axis=0, mode="clip")
    dense_grad = plan.join_rows(
        lax.all_to_all(
            slot_rows.reshape(count, slot_dev, rows, BLOCK),
            AXES,
            split_axis=0,
            concat_axis=0,
            tiled=True,
        )
    )
    dense_grad = jnp.swapaxes(dense_grad, 0, 1).astype(jnp.float32)

    owned_grad = jnp.where(
        is_image[None, :, None],
        image_grad,
        jnp.where(is_time[None, :, None], time_grad, dense_grad),
    )
    used = (my_unit >= 0)[None, :, None]
    rate = rate_factor * unit_scale(jnp.maximum(my_unit, 0))[None, :, None]
    new_w, new_first, new_second = adam_update(
        master, first_moment, second_moment, owned_grad, rate
    )
    new_master = jnp.where(used, new_w, master)
    new_first = jnp.where(used, new_first, first_moment)
    new_second = jnp.where(used, new_second, second_moment)
    small_rate = rate_factor * table_scale(jnp.arange(small.shape[0], dtype=jnp.int32))[:, None]
    new_small, new_small_first, new_small_second = adam_update(
        small, small_first, small_second, small_grad, small_rate
    )
    return (
        loss_sum,
        weight_total,
        new_master,
        new_first,
        new_second,
        new_small,
        new_small_first,
        new_small_second,
    )


def solution(mesh):
    return jax.shard_map(
        on_device,
        mesh=mesh,
        in_specs=(
            P(("rep", "shard"), None),
            P(("rep", "shard"), None),
            P(("rep", "shard")),
            P(("rep", "shard")),
            P(),
            P(None, ("rep", "shard"), None),
            P(None, ("rep", "shard"), None),
            P(None, ("rep", "shard"), None),
            P(),
            P(),
            P(),
        ),
        out_specs=(
            P(),
            P(),
            P(None, ("rep", "shard"), None),
            P(None, ("rep", "shard"), None),
            P(None, ("rep", "shard"), None),
            P(),
            P(),
            P(),
        ),
        check_vma=False,
    )
```

```python
import jax
import jax.numpy as jnp
import numpy as np
from jax import lax
from jax.experimental import pallas as pl
from jax.experimental.pallas import tpu as pltpu
from jax.sharding import PartitionSpec as P

D = 768
HEADS = 12
HEAD_DIM = 64
FF = 3072
FREQ = 256
CLASSES = 1000
CHANNELS = 16
GRID = 16
PATCHES = 256
LAYERS = 2
TSTEPS = 1000
STEP = 10
BLOCK = 128
LAYER_COLS = 13824
LAYER_UNITS = 108
UNITS = 234

ADA_UNITS = 6 * D // BLOCK
DENSE_UNITS = LAYER_UNITS - ADA_UNITS
DENSE_COLS = DENSE_UNITS * BLOCK
TIME_UNITS = D // BLOCK
TAIL_FIRST = LAYERS * LAYER_UNITS
AXES = ("rep", "shard")


beta_one = 0.5
beta_two = 0.5
adam_eps = 1e-08
decay_rate = 0.1
rate_factor = 0.5


def gelu_tanh(values):
    return jax.nn.gelu(values, approximate=True)


def norm_rows(hidden):
    centered = hidden - jnp.mean(hidden, -1, keepdims=True)
    return centered * lax.rsqrt(jnp.mean(centered * centered, -1, keepdims=True) + 1e-06)


def local_back(function, primal, upstream):
    return jax.vjp(function, primal)[1](upstream)[0]


def dot_low(pattern, left_side, right_side):
    return jnp.einsum(pattern, left_side, right_side, preferred_element_type=jnp.float32)


def positions():
    quarter = D // 4
    angular = jnp.exp(-jnp.log(10000.0) * jnp.arange(quarter, dtype=jnp.float32) / quarter)
    patch_idx = jnp.arange(PATCHES, dtype=jnp.int32)
    row_pos = (patch_idx // GRID).astype(jnp.float32)[:, None] * angular
    col_pos = (patch_idx % GRID).astype(jnp.float32)[:, None] * angular
    return jnp.concatenate(
        [jnp.sin(col_pos), jnp.cos(col_pos), jnp.sin(row_pos), jnp.cos(row_pos)], -1
    )


def frequencies(times):
    half_size = FREQ // 2
    spacing = jnp.exp(-jnp.log(10000.0) * jnp.arange(half_size, dtype=jnp.float32) / half_size)
    angles = 1000.0 * times[:, None] * spacing
    return jnp.concatenate([jnp.cos(angles), jnp.sin(angles)], -1)


def unit_scale(unit_ids):
    column = unit_ids % LAYER_UNITS * BLOCK
    in_layer = unit_ids < LAYERS * LAYER_UNITS
    is_output = in_layer & (column >= 9 * D) & (column < 10 * D)
    is_down = in_layer & (column >= 10 * D + FF)
    factor = jnp.where(is_output, 4.0, jnp.where(is_down, 1.5 * (D / FF) ** 0.5, 1.0))
    return factor / D**0.5


def table_scale(row_ids):
    return jnp.where(
        row_ids < CHANNELS,
        CHANNELS ** (-0.5),
        jnp.where(
            row_ids < CHANNELS + FREQ,
            FREQ ** (-0.5),
            jnp.where(row_ids < CHANNELS + FREQ + CLASSES, 0.5, D ** (-0.5)),
        ),
    )


def adam_update(weight, first_mom, second, gradient, rate):
    first_new = beta_one * first_mom + (1.0 - beta_one) * gradient
    second_new = beta_two * second + (1.0 - beta_two) * gradient * gradient
    ratio = (
        first_new
        / (1.0 - beta_one**STEP)
        / (jnp.sqrt(second_new / (1.0 - beta_two**STEP)) + adam_eps)
    )
    return (weight - rate * (ratio + decay_rate * weight), first_new, second_new)


def modulate(normed, shift, scale):
    return normed * (1.0 + scale[:, None, :]) + shift[:, None, :]


def layer_forward(hidden, modul, weights):
    w_qkv, w_out, w_up, w_down = weights
    shift_a, scale_a, gate_a, shift_b, scale_b, gate_b = jnp.split(modul, 6, -1)
    attn_in = modulate(norm_rows(hidden), shift_a, scale_a).astype(jnp.bfloat16)
    qkv_all = dot_low("gpd,de->gpe", attn_in, w_qkv).astype(jnp.bfloat16)
    heads_out = attend(qkv_all)
    branch_a = dot_low("gpd,de->gpe", heads_out, w_out)
    middle = hidden + gate_a[:, None, :] * branch_a
    mlp_in = modulate(norm_rows(middle), shift_b, scale_b).astype(jnp.bfloat16)
    pre_act = dot_low("gpd,df->gpf", mlp_in, w_up)
    post_act = gelu_tanh(pre_act).astype(jnp.bfloat16)
    branch_b = dot_low("gpf,df->gpd", post_act, w_down)
    output = middle + gate_b[:, None, :] * branch_b
    return (
        output,
        (
            hidden,
            modul,
            attn_in,
            qkv_all,
            heads_out,
            branch_a,
            middle,
            mlp_in,
            pre_act.astype(jnp.bfloat16),
            post_act,
            branch_b,
        ),
    )


def layer_backward(grad_out, weights, saved):
    w_qkv, w_out, w_up, w_down = weights
    (
        hidden,
        modul,
        attn_in,
        qkv_all,
        heads_out,
        branch_a,
        middle,
        mlp_in,
        pre_act,
        post_act,
        branch_b,
    ) = saved
    shift_a, scale_a, gate_a, shift_b, scale_b, gate_b = jnp.split(modul, 6, -1)
    grad_gate_b = jnp.sum(grad_out * branch_b, 1)
    grad_branch_b = (gate_b[:, None, :] * grad_out).astype(jnp.bfloat16)
    grad_down = (grad_branch_b, post_act)
    grad_post = dot_low("gpd,df->gpf", grad_branch_b, w_down)
    grad_pre = local_back(gelu_tanh, pre_act.astype(jnp.float32), grad_post).astype(jnp.bfloat16)
    grad_up = (mlp_in, grad_pre)
    grad_mlp_in = dot_low("gpf,df->gpd", grad_pre, w_up)
    normed_b = norm_rows(middle)
    grad_scale_b = jnp.sum(grad_mlp_in * normed_b, 1)
    grad_shift_b = jnp.sum(grad_mlp_in, 1)
    grad_middle = grad_out + local_back(
        norm_rows, middle, grad_mlp_in * (1.0 + scale_b[:, None, :])
    )
    grad_gate_a = jnp.sum(grad_middle * branch_a, 1)
    grad_branch_a = (gate_a[:, None, :] * grad_middle).astype(jnp.bfloat16)
    grad_out_w = (heads_out, grad_branch_a)
    grad_heads = dot_low("gpe,de->gpd", grad_branch_a, w_out).astype(jnp.bfloat16)
    grad_qkv = attend_back(qkv_all, grad_heads)
    grad_qkv_w = (attn_in, grad_qkv)
    grad_attn_in = dot_low("gpe,de->gpd", grad_qkv, w_qkv)
    normed_a = norm_rows(hidden)
    grad_scale_a = jnp.sum(grad_attn_in * normed_a, 1)
    grad_shift_a = jnp.sum(grad_attn_in, 1)
    grad_in = grad_middle + local_back(
        norm_rows, hidden, grad_attn_in * (1.0 + scale_a[:, None, :])
    )
    grad_modul = jnp.concatenate(
        [grad_shift_a, grad_scale_a, grad_gate_a, grad_shift_b, grad_scale_b, grad_gate_b], -1
    ).astype(jnp.bfloat16)
    return (grad_in, grad_modul, [grad_qkv_w, grad_out_w, grad_up, grad_down])


MESH = pl.DeviceIdType.MESH
GATHER_VMEM = 40 * 2**20
SCATTER_VMEM = 56 * 2**20


def dot_rows(left_side, right_side):
    return lax.dot_general(
        left_side, right_side, (((0,), (0,)), ((), ())), preferred_element_type=jnp.float32
    )


def row_product(left_side, right_side):
    left_side = left_side.reshape(-1, left_side.shape[-1])
    right_side = right_side.reshape(-1, right_side.shape[-1])
    return dot_rows(left_side, right_side).astype(jnp.bfloat16)


def unit_groups():
    groups, place = [], 0
    for number in (3 * D, D, FF, FF) * LAYERS + (D,):
        groups.append((place, number // BLOCK))
        place += number // BLOCK
    return groups


PAIR = 2 * HEAD_DIM
SPAN = 3


def head_mask(number):
    lane = lax.broadcasted_iota(jnp.int32, (PATCHES, PAIR), 1)
    return (lane >= number * HEAD_DIM) & (lane < (number + 1) * HEAD_DIM)


def dot_lanes(left_side, right_side):
    return lax.dot_general(
        left_side, right_side, (((1,), (1,)), ((), ())), preferred_element_type=jnp.float32
    )


def attend_kernel(queries, keys_all, values, out):
    row = lax.broadcasted_iota(jnp.int32, (PAIR, PATCHES), 0)
    for pair in range(SPAN):
        lanes = slice(pair * PAIR, (pair + 1) * PAIR)
        scaled = queries[0, :, lanes] * HEAD_DIM ** (-0.5)
        keys, vals = keys_all[0, :, lanes], values[0, :, lanes]
        result = jnp.zeros((PAIR, PATCHES), jnp.float32)
        for number in (0, 1):
            one = jnp.where(head_mask(number), scaled, jnp.zeros((), jnp.bfloat16))
            scores = dot_lanes(keys, one)
            powers = jnp.exp(scores - jnp.max(scores, 0, keepdims=True))
            prob = (powers * (1.0 / jnp.sum(powers, 0, keepdims=True))).astype(jnp.bfloat16)
            result = jnp.where(row // HEAD_DIM == number, dot_rows(vals, prob), result)
        out[0, :, lanes] = result.T.astype(jnp.bfloat16)


def attend_back_kernel(queries, keys_all, values, grads, out):
    step = pl.program_id(1)
    row = lax.broadcasted_iota(jnp.int32, (PAIR, PATCHES), 0)
    none = jnp.zeros((), jnp.bfloat16)
    for pair in range(SPAN):
        lanes = slice(pair * PAIR, (pair + 1) * PAIR)
        scaled = queries[0, :, lanes] * HEAD_DIM ** (-0.5)
        keys, vals, grad = (ref[0, :, lanes] for ref in (keys_all, values, grads))
        grad_queries = jnp.zeros((PAIR, PATCHES), jnp.float32)
        grad_keys = jnp.zeros((PATCHES, PAIR), jnp.float32)
        grad_values = grad_keys
        for number in (0, 1):
            mask = head_mask(number)
            scores = dot_lanes(keys, jnp.where(mask, scaled, none))
            powers = jnp.exp(scores - jnp.max(scores, 0, keepdims=True))
            prob = powers * (1.0 / jnp.sum(powers, 0, keepdims=True))
            grad_prob = dot_lanes(vals, jnp.where(mask, grad, none))
            inner = jnp.sum(prob * grad_prob, 0, keepdims=True)
            grad_scores = (prob * (grad_prob - inner)).astype(jnp.bfloat16)
            part = dot_rows(keys, grad_scores)
            grad_queries = jnp.where(row // HEAD_DIM == number, part, grad_queries)
            part = jnp.dot(grad_scores, scaled, preferred_element_type=jnp.float32)
            grad_keys = jnp.where(mask, part, grad_keys)
            part = jnp.dot(prob.astype(jnp.bfloat16), grad, preferred_element_type=jnp.float32)
            grad_values = jnp.where(mask, part, grad_values)
        grad_queries = grad_queries.T * HEAD_DIM ** (-0.5)
        for third, result in enumerate((grad_queries, grad_keys, grad_values)):
            first = pl.multiple_of(third * D + (step * SPAN + pair) * PAIR, PAIR)
            out[0, :, pl.ds(first, PAIR)] = result.astype(jnp.bfloat16)


def pair_block(third):
    steps = HEADS // 2 // SPAN
    return pl.BlockSpec(
        (1, PATCHES, SPAN * PAIR), lambda image, step: (image, 0, third * steps + step)
    )


def attend(qkv_all):
    images = qkv_all.shape[0]
    steps = HEADS // 2 // SPAN
    return pl.pallas_call(
        attend_kernel,
        grid=(images, steps),
        out_shape=jax.ShapeDtypeStruct((images, PATCHES, D), jnp.bfloat16),
        in_specs=[pair_block(0), pair_block(1), pair_block(2)],
        out_specs=pair_block(0),
        cost_estimate=pl.CostEstimate(
            flops=4 * images * PATCHES * PATCHES * D,
            bytes_accessed=8 * images * PATCHES * D,
            transcendentals=images * HEADS * PATCHES * PATCHES,
        ),
    )(qkv_all, qkv_all, qkv_all)


def attend_back(qkv_all, grad_heads):
    images = qkv_all.shape[0]
    steps = HEADS // 2 // SPAN
    return pl.pallas_call(
        attend_back_kernel,
        grid=(images, steps),
        out_shape=jax.ShapeDtypeStruct((images, PATCHES, 3 * D), jnp.bfloat16),
        in_specs=[pair_block(0), pair_block(1), pair_block(2), pair_block(0)],
        out_specs=pl.BlockSpec((1, PATCHES, 3 * D), lambda image, step: (image, 0, 0)),
        cost_estimate=pl.CostEstimate(
            flops=10 * images * PATCHES * PATCHES * D,
            bytes_accessed=14 * images * PATCHES * D,
            transcendentals=images * HEADS * PATCHES * PATCHES,
        ),
    )(qkv_all, qkv_all, qkv_all, grad_heads)


def adam_kernel(starts, flags, dense, left, right, master, first, second, *refs):
    new_master, new_first, new_second, image_grad = refs
    slot = pl.program_id(0)
    rate, used, is_dense = flags[slot, 0], flags[slot, 1], flags[slot, 2]
    image_grad[...] = jnp.dot(left[0], right[0], preferred_element_type=jnp.float32)
    rows = dense.shape[2]
    for n, start in enumerate(starts):
        at = (0, slice(start, start + rows))
        grad = jnp.where(is_dense > 0.0, dense[n, 0].astype(jnp.float32), image_grad[at[1]])
        old = (master[at], first[at], second[at])
        new = adam_update(*old, grad, rate)
        for ref, value, kept in zip((new_master, new_first, new_second), new, old):
            ref[at] = jnp.where(used > 0.0, value, kept)


def adam_slots(dense, starts, flags, left, right, *state):
    slots = state[0].shape[0]
    block = pl.BlockSpec((1, D, BLOCK), lambda slot: (slot, 0, 0))
    side = left.shape[2]
    return pl.pallas_call(
        lambda *refs: adam_kernel(starts, *refs),
        grid=(slots,),
        out_shape=[jax.ShapeDtypeStruct((slots, D, BLOCK), jnp.float32)] * 3,
        in_specs=[
            pl.BlockSpec(memory_space=pltpu.SMEM),
            pl.BlockSpec(
                (dense.shape[0], 1) + dense.shape[2:], lambda slot: (0, slot, 0, 0)
            ),
            pl.BlockSpec((1, D, side), lambda slot: (slot, 0, 0)),
            pl.BlockSpec((1, side, BLOCK), lambda slot: (slot, 0, 0)),
        ]
        + [block] * 3,
        out_specs=[block] * 3,
        scratch_shapes=[pltpu.VMEM((D, BLOCK), jnp.float32)],
        cost_estimate=pl.CostEstimate(
            flops=40 * slots * D * BLOCK, bytes_accessed=26 * slots * D * BLOCK, transcendentals=0
        ),
    )(flags, dense, left, right, *state)


def place_of():
    rep = lax.axis_index("rep")
    return rep // 4, (rep // 2) % 2, rep % 2, lax.axis_index("shard")


def rep_of(y, x, c):
    return (y * 2 + x) * 2 + c


def device_at(j):
    shards = lax.axis_size("shard")
    devices = lax.axis_size("rep") * shards
    me = lax.axis_index("rep") * shards + lax.axis_index("shard")
    peer = lax.rem(me + j, devices)
    return peer, (peer // shards, lax.rem(peer, shards))


def meet_all(devices):
    barrier = pltpu.get_barrier_semaphore()

    @pl.loop(1, devices)
    def _(j):
        pl.semaphore_signal(barrier, inc=1, device_id=device_at(j)[1], device_id_type=MESH)

    pl.semaphore_wait(barrier, devices - 1)


def neighbours():
    y, x, c, z = place_of()
    to_x = (rep_of(y, 1 - x, c), z)
    to_y = (rep_of(1 - y, x, c), z)
    to_core = (rep_of(y, x, 1 - c), z)
    to_z = [(rep_of(y, x, c), lax.rem(z + step, 4)) for step in (1, 2, 3)]
    return to_x, to_y, to_core, to_z


def gather_kernel(widths, bases, *refs):
    count = len(widths)
    units, info, low_slots = refs[:3]
    outs = refs[3 : count + 3]
    every_info, cond_out, modul_out = refs[count + 3 : count + 6]
    pieces = refs[count + 6 : 2 * count + 6]
    time_two, parts, own_sem, send_sem, recv_sem, time_sem, modul_sem, info_sem = refs[
        2 * count + 6 :
    ]
    devices, images = modul_out.shape[:2]
    slots = low_slots.shape[0]
    y, x, c, z = place_of()
    to_x, to_y, to_core, to_z = neighbours()
    me = rep_of(y, x, c) * 4 + z
    meet_all(devices)

    def remote(k, number, source, dest, target):
        return pltpu.make_async_remote_copy(
            src_ref=source,
            dst_ref=dest,
            send_sem=send_sem.at[k, number],
            recv_sem=recv_sem.at[k, number],
            device_id=target,
            device_id_type=MESH,
        )

    def own_copy(k):
        return pltpu.make_async_copy(pieces[k], outs[k].at[c, y, x, z], own_sem.at[k])

    def line_copies(k, arriving):
        copies = []
        for step in (1, 2, 3):
            at_z = lax.rem(z + 4 - step, 4) if arriving else z
            copies.append(
                remote(k, step - 1, pieces[k], outs[k].at[c, y, x, at_z], to_z[step - 1])
            )
        return copies

    def first_copies(k, arriving):
        half = widths[k] // 2
        left, right = pl.ds(0, half), pl.ds(half, half)
        at_x = 1 - x if arriving else x
        at_y = 1 - y if arriving else y
        a_block = outs[k].at[c, y, at_x, :, :, left]
        b_block = outs[k].at[c, at_y, x, :, :, right]
        return [remote(k, 3, a_block, a_block, to_x), remote(k, 4, b_block, b_block, to_y)]

    def second_copies(k, arriving):
        half = widths[k] // 2
        left, right = pl.ds(0, half), pl.ds(half, half)
        at_x = 1 - x if arriving else x
        at_y = 1 - y if arriving else y
        a_block = outs[k].at[c, at_y, :, :, :, left]
        b_block = outs[k].at[c, :, at_x, :, :, right]
        return [remote(k, 5, a_block, a_block, to_y), remote(k, 6, b_block, b_block, to_x)]

    def core_copies(k, arriving):
        block = outs[k].at[1 - c if arriving else c]
        return [remote(k, 7, block, block, to_core)]

    def start(copies):
        for copy in copies:
            copy.start()

    def arrived(copies):
        for copy in copies:
            copy.wait_recv()

    def modul_copy(j, arriving):
        peer, where = device_at(devices - j if arriving else j)
        return pltpu.make_async_remote_copy(
            src_ref=parts.at[pl.ds(peer * images, images)],
            dst_ref=modul_out.at[peer if arriving else me],
            send_sem=modul_sem.at[0, j],
            recv_sem=modul_sem.at[1, j],
            device_id=where,
            device_id_type=MESH,
        )

    def info_copy(j, arriving):
        peer, where = device_at(devices - j if arriving else j)
        return pltpu.make_async_remote_copy(
            src_ref=info,
            dst_ref=every_info.at[pl.ds((peer if arriving else me) * images, images)],
            send_sem=info_sem.at[0, j],
            recv_sem=info_sem.at[1, j],
            device_id=where,
            device_id_type=MESH,
        )

    def info_rows(first):
        return jnp.concatenate([every_info[:, first + j, :] for j in range(D // BLOCK)], -1)

    def image_products():
        copy = pltpu.make_async_copy(outs[0], time_two, time_sem)
        copy.start()

        @pl.loop(1, devices)
        def _(j):
            info_copy(j, True).wait_recv()
            info_copy(j, False).wait_send()

        copy.wait()
        weight = time_two[...].astype(jnp.float32).reshape(D, D).astype(jnp.bfloat16)
        cond = jnp.dot(
            info_rows(0).astype(jnp.bfloat16), weight, preferred_element_type=jnp.float32
        )
        cond = cond + info_rows(8)
        cond_out[...] = cond
        act = (cond * jax.nn.sigmoid(cond)).astype(jnp.bfloat16)
        for s in range(slots):
            parts[:, s, :] = jnp.dot(act, low_slots[s], preferred_element_type=jnp.float32)
        for i in range(images):
            modul_out[me, i] = parts[me * images + i]

        @pl.loop(1, devices)
        def _(j):
            modul_copy(j, False).start()

    @pl.loop(1, devices)
    def _(j):
        info_copy(j, False).start()

    for i in range(images):
        every_info[me * images + i] = info[i]
    def send_piece(k):
        for n in range(widths[k] // BLOCK):
            pieces[k][:, n * BLOCK : (n + 1) * BLOCK] = units[bases[k] + n]
        start(line_copies(k, False))
        own_copy(k).start()

    send_piece(0)
    for t in range(count + 2):
        if t + 1 < count:
            send_piece(t + 1)
        if t < count:
            own_copy(t).wait()
            arrived(line_copies(t, True))
            start(first_copies(t, False))
        if 0 <= t - 1 < count:
            arrived(first_copies(t - 1, True))
            start(second_copies(t - 1, False))
        if 0 <= t - 2 < count:
            arrived(second_copies(t - 2, True))
            start(core_copies(t - 2, False))
        if t == 3:
            arrived(core_copies(0, True))
            image_products()
    for k in range(1, count):
        arrived(core_copies(k, True))

    @pl.loop(1, devices)
    def _(j):
        modul_copy(j, True).wait_recv()
        modul_copy(j, False).wait_send()

    for k in range(count):
        for copies in (line_copies, first_copies, second_copies, core_copies):
            for copy in copies(k, False):
                copy.wait_send()


def scatter_kernel(widths, bases, slots, *refs):
    count = len(widths)
    lefts, rights = refs[:count], refs[count : 2 * count]
    modul, pick, low_slots, edge, factor = refs[2 * count : 2 * count + 5]
    units, chosen, shared = refs[2 * count + 5 : 2 * count + 8]
    scratch = refs[2 * count + 8 :]
    own, first_in, second_in, line_in = (scratch[i * count : (i + 1) * count] for i in range(4))
    (
        left_in, left_turned, right_in, away, every_modul, parts, landed,
        load_sem, send_sem, recv_sem, modul_sem, part_sem, sum_sem,
    ) = scratch[4 * count :]
    devices, images = shared.shape[:2]
    y, x, c, z = place_of()
    to_x, to_y, to_core, to_z = neighbours()
    me = rep_of(y, x, c) * 4 + z
    rows = D // 32
    half_rows = D // 2
    meet_all(devices)

    def exchange(source, dest, sem, j, arriving):
        peer, where = device_at(devices - j if arriving else j)
        return pltpu.make_async_remote_copy(
            src_ref=source(peer, me),
            dst_ref=dest(peer if arriving else me),
            send_sem=sem.at[0, j],
            recv_sem=sem.at[1, j],
            device_id=where,
            device_id_type=MESH,
        )

    def modul_copies(step, arriving):
        if step == 0:
            copies = []
            for number in (1, 2, 3):
                at_z = lax.rem(z + 4 - number, 4) if arriving else z
                copies.append((modul, every_modul.at[y, x, c, at_z], to_z[number - 1]))
        else:
            at_x = 1 - x if arriving and step == 1 else x
            at_y = 1 - y if arriving and step == 2 else y
            at_c = 1 - c if arriving and step == 3 else c
            block = (
                every_modul.at[y, at_x, c],
                every_modul.at[at_y, :, c],
                every_modul.at[:, :, at_c],
            )[step - 1]
            copies = [(block, block, (to_x, to_y, to_core)[step - 1])]
        return [
            pltpu.make_async_remote_copy(
                src_ref=source,
                dst_ref=dest,
                send_sem=modul_sem.at[0, step, number],
                recv_sem=modul_sem.at[1, step, number],
                device_id=target,
                device_id_type=MESH,
            )
            for number, (source, dest, target) in enumerate(copies)
        ]

    def part_copy(j, arriving):
        return exchange(
            lambda peer, mine: parts.at[pl.ds(peer * images, images)],
            lambda owner: landed.at[owner],
            part_sem, j, arriving,
        )

    def sum_copy(j, arriving):
        return exchange(
            lambda peer, mine: shared.at[mine], lambda owner: shared.at[owner], sum_sem, j, arriving
        )

    def all_start(copy):
        @pl.loop(1, devices)
        def _(j):
            copy(j, False).start()

    def all_arrived(copy):
        @pl.loop(1, devices)
        def _(j):
            copy(j, True).wait_recv()

    def all_sent(copy):
        @pl.loop(1, devices)
        def _(j):
            copy(j, False).wait_send()

    def image_parts():
        arrived(modul_copies(3, True))

        @pl.loop(0, devices // 4)
        def _(i):
            for n in range(4):
                for m in range(images):
                    block = every_modul[i // 4, (i // 2) % 2, i % 2, n, m]
                    chosen[(i * 4 + n) * images + m] = jnp.dot(
                        pick[...], block, preferred_element_type=jnp.float32
                    )

        total = jnp.zeros((devices * images, D), jnp.float32)
        for s in range(slots):
            total = total + lax.dot_general(
                chosen[:, s, :].astype(jnp.bfloat16),
                low_slots[s],
                (((1,), (1,)), ((), ())),
                preferred_element_type=jnp.float32,
            )
        parts[...] = edge[...]
        for j in range(D // BLOCK):
            parts[:, j, :] = total[:, j * BLOCK : (j + 1) * BLOCK]
        all_start(part_copy)
        for i in range(images):
            landed[me, i] = parts[me * images + i]

    def image_sums():
        all_arrived(part_copy)
        shared[me] = jnp.sum(landed[...], 0) * factor[...]
        all_start(sum_copy)

    def remote(k, number, source, dest, target):
        return pltpu.make_async_remote_copy(
            src_ref=source,
            dst_ref=dest,
            send_sem=send_sem.at[k, number],
            recv_sem=recv_sem.at[k, number],
            device_id=target,
            device_id_type=MESH,
        )

    def load_left(k):
        return pltpu.make_async_copy(lefts[k], left_in.at[k % 2], load_sem.at[0, k % 2])

    def load_right(k):
        place = right_in.at[k % 3, :, pl.ds(0, widths[k])]
        return pltpu.make_async_copy(rights[k], place, load_sem.at[1, k % 3])

    def core_copies(k):
        source = away.at[k % 3, :, :, :, :, pl.ds(0, widths[k])]
        return [remote(k, 0, source, own[k], to_core)]

    def first_copies(k):
        half = widths[k] // 2
        return [
            remote(k, 1, own[k].at[:, 1 - x, :, :, pl.ds(0, half)], first_in[k].at[0], to_x),
            remote(k, 2, own[k].at[1 - y, :, :, :, pl.ds(half, half)], first_in[k].at[1], to_y),
        ]

    def second_copies(k):
        half = widths[k] // 2
        return [
            remote(k, 3, own[k].at[1 - y, x, :, :, pl.ds(0, half)], second_in[k].at[0], to_y),
            remote(k, 4, own[k].at[y, 1 - x, :, :, pl.ds(half, half)], second_in[k].at[1], to_x),
        ]

    def line_copies(k):
        return [
            remote(
                k,
                4 + step,
                own[k].at[y, x, lax.rem(z + step, 4)],
                line_in[k].at[step - 1],
                to_z[step - 1],
            )
            for step in (1, 2, 3)
        ]

    def start(copies):
        for copy in copies:
            copy.start()

    def arrived(copies):
        for copy in copies:
            copy.wait_recv()

    def products(k, half, store):
        slot = k % 3
        tile = D

        @pl.loop(0, widths[k] // tile)
        def _(n):
            columns = pl.ds(pl.multiple_of(n * tile, tile), tile)
            left = left_turned[slot, pl.ds(pl.multiple_of(half * half_rows, half_rows), half_rows)]
            result = jnp.dot(left, right_in[slot, :, columns], preferred_element_type=jnp.float32)
            for i in range(16):
                at = (i // 8, (i // 4) % 2, i % 4, slice(None), columns)
                store(at, result[i * rows : (i + 1) * rows])

    def away_products(k):
        load_left(k).wait()
        load_right(k).wait()
        left_turned[k % 3] = left_in[k % 2].T
        if k + 2 < count:
            load_left(k + 2).start()
        if k >= 3:
            for copy in core_copies(k - 3):
                copy.wait_send()

        def store(at, value):
            away[(k % 3,) + at] = value.astype(jnp.bfloat16)

        products(k, 1 - c, store)
        start(core_copies(k))

    def own_products(k):
        def store(at, value):
            own[k][at] = (value + own[k][at].astype(jnp.float32)).astype(jnp.bfloat16)

        products(k, c, store)

    def first_sum(k):
        half = widths[k] // 2

        @pl.loop(0, 8)
        def _(i):
            two, at_z = i // 4, i % 4
            a_at = (two, x, at_z, slice(None), pl.ds(0, half))
            b_at = (y, two, at_z, slice(None), pl.ds(half, half))
            own[k][a_at] = own[k][a_at] + first_in[k][0, two, at_z]
            own[k][b_at] = own[k][b_at] + first_in[k][1, two, at_z]

    def second_sum(k):
        half = widths[k] // 2

        @pl.loop(0, 4)
        def _(at_z):
            a_at = (y, x, at_z, slice(None), pl.ds(0, half))
            b_at = (y, x, at_z, slice(None), pl.ds(half, half))
            own[k][a_at] = own[k][a_at] + second_in[k][0, at_z]
            own[k][b_at] = own[k][b_at] + second_in[k][1, at_z]

    start(modul_copies(0, False))
    every_modul[y, x, c, z] = modul[...]
    for k in range(min(3, count)):
        load_right(k).start()
        if k < 2:
            load_left(k).start()
    away_products(0)
    for t in range(count + 3):
        if t + 1 < count:
            away_products(t + 1)
        if t < count:
            arrived(core_copies(t))
            own_products(t)
            start(first_copies(t))
            if t + 3 < count:
                load_right(t + 3).start()
        if 0 <= t - 1 < count:
            arrived(first_copies(t - 1))
            first_sum(t - 1)
            start(second_copies(t - 1))
        if 0 <= t - 2 < count:
            arrived(second_copies(t - 2))
            second_sum(t - 2)
            start(line_copies(t - 2))
        if 0 <= t - 3 < count:
            k = t - 3
            arrived(line_copies(k))
            total = own[k][y, x, z].astype(jnp.float32)
            for step in (1, 2, 3):
                total = total + line_in[k][step - 1].astype(jnp.float32)
            for n in range(widths[k] // BLOCK):
                part = total[:, n * BLOCK : (n + 1) * BLOCK]
                units[bases[k] + n] = part.astype(jnp.bfloat16)
        if t < 3:
            arrived(modul_copies(t, True))
            start(modul_copies(t + 1, False))
        if t == 3:
            image_parts()
        if t == 6:
            image_sums()
    all_arrived(sum_copy)
    for copy in (part_copy, sum_copy):
        all_sent(copy)
    for step in range(4):
        for copy in modul_copies(step, False):
            copy.wait_send()
    for k in range(count):
        for copies in (core_copies, first_copies, second_copies, line_copies):
            if copies is core_copies and k + 3 < count:
                continue
            for copy in copies(k):
                copy.wait_send()


class RingPlan:
    def split_rows(self, values):
        slots = values.shape[0]
        split = values.reshape(slots, 2, 2, 2, 4, D // 32, BLOCK)
        return split.transpose(2, 3, 1, 4, 0, 5, 6).reshape(32, slots, D // 32, BLOCK)

    def join_rows(self, values):
        starts = []
        for device in range(32):
            y, x, c, z = device // 16, device // 8 % 2, device // 4 % 2, device % 4
            starts.append(((((c * 2 + y) * 2 + x) * 4) + z) * (D // 32))
        return values, starts

    def gather(self, units, info, low_slots):
        names = unit_groups()
        turn = [len(names) - 1] + sorted(range(len(names) - 1), key=lambda n: (n % 4 == 1, n))
        bases = tuple(names[n][0] for n in turn)
        widths = tuple(names[n][1] * BLOCK for n in turn)
        count, rows = len(turn), D // 32
        all_images = 32 * info.shape[0]
        slots = low_slots.shape[0]
        room = -(-slots // 8) * 8
        size = sum(4 * D * width for width in widths)
        whole_shape = [(2, 2, 2, 4, rows, width) for width in widths]
        *whole, every_info, cond, modul = pl.pallas_call(
            lambda *refs: gather_kernel(widths, bases, *refs),
            out_shape=[
                jax.ShapeDtypeStruct(shape, jnp.bfloat16) for shape in whole_shape
            ]
            + [
                jax.ShapeDtypeStruct((all_images,) + info.shape[1:], jnp.float32),
                jax.ShapeDtypeStruct((all_images, D), jnp.float32),
                jax.ShapeDtypeStruct((32, all_images // 32, room, BLOCK), jnp.float32),
            ],
            in_specs=[pl.BlockSpec(memory_space=pltpu.VMEM)] * 3,
            out_specs=[pl.BlockSpec(memory_space=pl.ANY)] * count
            + [pl.BlockSpec(memory_space=pltpu.VMEM)] * 3,
            scratch_shapes=[pltpu.VMEM((rows, width), jnp.bfloat16) for width in widths]
            + [
                pltpu.VMEM(whole_shape[0], jnp.bfloat16),
                pltpu.VMEM((all_images, room, BLOCK), jnp.float32),
                pltpu.SemaphoreType.DMA((count,)),
                pltpu.SemaphoreType.DMA((count, 8)),
                pltpu.SemaphoreType.DMA((count, 8)),
                pltpu.SemaphoreType.DMA,
                pltpu.SemaphoreType.DMA((2, 32)),
                pltpu.SemaphoreType.DMA((2, 32)),
            ],
            compiler_params=pltpu.CompilerParams(
                collective_id=0, has_side_effects=True, vmem_limit_bytes=GATHER_VMEM
            ),
            cost_estimate=pl.CostEstimate(flops=0, bytes_accessed=size, transcendentals=0),
        )(units, info, low_slots)
        whole = [part.reshape(D, -1) for part in whole]
        modul = jnp.swapaxes(modul[:, :, :slots], 0, 1).reshape(-1, 32 * slots, BLOCK)
        ordered = [whole[turn.index(n)] for n in range(count)]
        return ordered[:-1], ordered[-1], every_info, cond, modul

    def scatter(self, layer_grads, modul, pick, low_slots, edge, factor):
        turn = [(l, n) for l in range(LAYERS) for n in (0, 2, 3)]
        turn = [(LAYERS - 1, 1)] + turn + [(l, 1) for l in range(LAYERS - 1)]
        grads = [layer_grads[l][n] for l, n in turn]
        names = unit_groups()
        bases = tuple(names[4 * l + n][0] for l, n in turn)
        lefts = [left.reshape(-1, D) for left, _ in grads]
        rights = [right.reshape(left.shape[0], -1) for (_, right), left in zip(grads, lefts)]
        widths = tuple(right.shape[1] for right in rights)
        count, rows, tokens = len(grads), D // 32, lefts[0].shape[0]
        widest = max(widths)
        images, slots = modul.shape[0], low_slots.shape[0]
        size = sum(4 * D * width for width in widths)
        scratch = [pltpu.VMEM((2, 2, 4, rows, width), jnp.bfloat16) for width in widths]
        scratch += [pltpu.VMEM((2, 2, 4, rows, width // 2), jnp.bfloat16) for width in widths]
        scratch += [pltpu.VMEM((2, 4, rows, width // 2), jnp.bfloat16) for width in widths]
        scratch += [pltpu.VMEM((3, rows, width), jnp.bfloat16) for width in widths]
        units, chosen, shared = pl.pallas_call(
            lambda *refs: scatter_kernel(widths, bases, slots, *refs),
            out_shape=[
                jax.ShapeDtypeStruct((sum(widths) // BLOCK, rows, BLOCK), jnp.bfloat16),
                jax.ShapeDtypeStruct((32 * images, pick.shape[0], BLOCK), jnp.float32),
                jax.ShapeDtypeStruct((32,) + factor.shape, jnp.float32),
            ],
            in_specs=[pl.BlockSpec(memory_space=pl.ANY)] * (2 * count)
            + [pl.BlockSpec(memory_space=pltpu.VMEM)] * 5,
            out_specs=[pl.BlockSpec(memory_space=pltpu.VMEM)] * 3,
            scratch_shapes=scratch
            + [
                pltpu.VMEM((2, tokens, D), jnp.bfloat16),
                pltpu.VMEM((3, D, tokens), jnp.bfloat16),
                pltpu.VMEM((3, tokens, widest), jnp.bfloat16),
                pltpu.VMEM((3, 2, 2, 4, rows, widest), jnp.bfloat16),
                pltpu.VMEM((2, 2, 2, 4) + modul.shape, jnp.bfloat16),
                pltpu.VMEM(edge.shape, jnp.float32),
                pltpu.VMEM((32,) + factor.shape, jnp.float32),
                pltpu.SemaphoreType.DMA((2, 3)),
                pltpu.SemaphoreType.DMA((count, 8)),
                pltpu.SemaphoreType.DMA((count, 8)),
                pltpu.SemaphoreType.DMA((2, 4, 3)),
                pltpu.SemaphoreType.DMA((2, 32)),
                pltpu.SemaphoreType.DMA((2, 32)),
            ],
            compiler_params=pltpu.CompilerParams(
                collective_id=1, has_side_effects=True, vmem_limit_bytes=SCATTER_VMEM
            ),
            cost_estimate=pl.CostEstimate(flops=0, bytes_accessed=size, transcendentals=0),
        )(*lefts, *rights, modul, pick, low_slots, edge, factor)
        return units, chosen[:, :slots].astype(jnp.bfloat16), shared


class PlainPlan:
    def split_rows(self, values):
        slots, devices = values.shape[0], lax.axis_size("rep") * lax.axis_size("shard")
        return jnp.swapaxes(values.reshape(slots, devices, -1, BLOCK), 0, 1)

    def join_rows(self, values):
        return jnp.swapaxes(values, 0, 1).reshape(1, -1, D, BLOCK), [0]

    def gather(self, units, info, low_slots):
        whole = []
        for first, number in unit_groups():
            piece = jnp.swapaxes(units[first : first + number], 0, 1)
            piece = piece.reshape(-1, number * BLOCK)
            whole.append(lax.all_gather(piece, AXES, axis=0, tiled=True))
        every_info = lax.all_gather(info, AXES, axis=0, tiled=True)
        blocks = D // BLOCK
        time_act = every_info[:, :blocks].reshape(-1, D).astype(jnp.bfloat16)
        cond = jnp.dot(time_act, whole[-1], preferred_element_type=jnp.float32)
        cond = cond + every_info[:, 8 : 8 + blocks].reshape(-1, D)
        modul = dot_low("gd,sdc->gsc", jax.nn.silu(cond).astype(jnp.bfloat16), low_slots)
        modul = lax.all_to_all(modul, AXES, split_axis=0, concat_axis=1, tiled=True)
        return whole[:-1], whole[-1], every_info, cond, modul

    def scatter(self, layer_grads, modul, pick, low_slots, edge, factor):
        units = []
        for pair in (pair for grads in layer_grads for pair in grads):
            own = lax.psum_scatter(row_product(*pair), AXES, scatter_dimension=0, tiled=True)
            units.append(jnp.swapaxes(own.reshape(own.shape[0], -1, BLOCK), 0, 1))
        slots = low_slots.shape[0]
        every = lax.all_gather(modul, AXES, axis=0, tiled=True)
        chosen = dot_low("su,guc->gsc", pick, every)[:, :slots].astype(jnp.bfloat16)
        part = dot_low("gsc,sdc->gd", chosen, low_slots).reshape(-1, D // BLOCK, BLOCK)
        parts = edge.at[:, : D // BLOCK].set(part)
        own = lax.psum_scatter(parts, AXES, scatter_dimension=0, tiled=True) * factor
        shared = lax.all_gather(own, AXES, axis=0, tiled=False)
        return jnp.concatenate(units, 0), chosen, shared


def unit_lists():
    dense = np.concatenate(
        [np.arange(l * LAYER_UNITS + ADA_UNITS, (l + 1) * LAYER_UNITS) for l in range(LAYERS)]
    )
    time_units = np.arange(TAIL_FIRST, TAIL_FIRST + TIME_UNITS)
    image_units = np.concatenate(
        [np.arange(l * LAYER_UNITS, l * LAYER_UNITS + ADA_UNITS) for l in range(LAYERS)]
        + [np.arange(TAIL_FIRST + TIME_UNITS, UNITS)]
    )
    return dense, time_units, image_units


def on_device(
    latents,
    noise,
    labels,
    t_index,
    owner,
    master,
    first_moment,
    second_moment,
    small,
    small_first,
    small_second,
):
    count = lax.axis_size("rep") * lax.axis_size("shard")
    me = lax.axis_index(AXES)
    slot_dev = master.shape[1]
    slot_total = count * slot_dev
    rows = D // count
    images = latents.shape[0]
    dense_units, time_units, image_units = unit_lists()

    unit_of_slot = (
        jnp.full((slot_total,), -1, jnp.int32).at[owner].set(jnp.arange(UNITS, dtype=jnp.int32))
    )
    my_unit = lax.dynamic_slice_in_dim(unit_of_slot, me * slot_dev, slot_dev)
    low_slots = jnp.swapaxes(master.astype(jnp.bfloat16), 0, 1)

    plan = RingPlan() if (lax.axis_size("rep"), lax.axis_size("shard")) == (8, 4) else PlainPlan()
    spread = lax.all_to_all(
        plan.split_rows(low_slots), AXES, split_axis=0, concat_axis=0, tiled=True
    ).reshape(slot_total, rows, BLOCK)
    moved = np.concatenate([dense_units, time_units])
    units = jnp.take(spread, owner[moved], axis=0, mode="clip")

    x_start = latents.astype(jnp.float32).reshape(-1, PATCHES, CHANNELS)
    noise_f = noise.astype(jnp.float32).reshape(-1, PATCHES, CHANNELS)
    times = (t_index.astype(jnp.float32) + 0.5) / TSTEPS
    noisy = (1.0 - times)[:, None, None] * x_start + times[:, None, None] * noise_f
    target = noise_f - x_start
    loss_weight = 1.0 + 3.0 * times
    small_low = small.astype(jnp.bfloat16)
    patch_w = small_low[:CHANNELS]
    time_w = small_low[CHANNELS : CHANNELS + FREQ]
    table = small[CHANNELS + FREQ : CHANNELS + FREQ + CLASSES]
    head_w = small_low[CHANNELS + FREQ + CLASSES :]
    noisy_low = noisy.astype(jnp.bfloat16)
    hidden = dot_low("gpc,cd->gpd", noisy_low, patch_w) + positions()

    blocks = D // BLOCK
    freq_own = frequencies(times).astype(jnp.bfloat16)
    time_own = jnp.dot(freq_own, time_w, preferred_element_type=jnp.float32)
    act_own = jax.nn.silu(time_own).astype(jnp.bfloat16).astype(jnp.float32)
    label_own = jnp.take(table, labels, axis=0)
    numbers = jnp.stack([t_index, labels], 1).astype(jnp.float32)
    info = jnp.concatenate(
        [
            act_own.reshape(images, blocks, BLOCK),
            jnp.pad(numbers, ((0, 0), (0, BLOCK - 2)))[:, None],
            jnp.zeros((images, 7 - blocks, BLOCK), jnp.float32),
            label_own.reshape(images, blocks, BLOCK),
            jnp.zeros((images, 8 - blocks, BLOCK), jnp.float32),
        ],
        1,
    )
    whole, time_two, every_info, cond_all, slot_modul = plan.gather(
        units, info, low_slots
    )
    all_images = cond_all.shape[0]
    every_time = (every_info[:, blocks, 0] + 0.5) / TSTEPS
    every_label = every_info[:, blocks, 1].astype(jnp.int32)
    weight_total = jnp.sum(1.0 + 3.0 * every_time) * PATCHES
    freq_low = frequencies(every_time).astype(jnp.bfloat16)
    time_pre = jnp.dot(freq_low, time_w, preferred_element_type=jnp.float32)
    time_act = every_info[:, :blocks].reshape(all_images, D).astype(jnp.bfloat16)
    weights_all = [tuple(whole[4 * l : 4 * l + 4]) for l in range(LAYERS)]
    cond = lax.dynamic_slice_in_dim(cond_all, me * images, images)
    cond_act = jax.nn.silu(cond_all).astype(jnp.bfloat16)
    modul_all = jnp.take(slot_modul, owner[image_units], axis=1, mode="clip").reshape(images, -1)

    saved_all = []
    for l in range(LAYERS):
        hidden, saved = layer_forward(
            hidden, modul_all[:, l * 6 * D : (l + 1) * 6 * D], weights_all[l]
        )
        saved_all.append(saved)
    shift_f, scale_f = jnp.split(modul_all[:, LAYERS * 6 * D :], 2, -1)
    normed_f = norm_rows(hidden)
    final_in = modulate(normed_f, shift_f, scale_f).astype(jnp.bfloat16)
    predict = dot_low("gpd,cd->gpc", final_in, head_w)
    error = predict - target
    loss_part = jnp.sum(loss_weight[:, None, None] * error * error) / CHANNELS
    grad_pred = (loss_weight[:, None, None] * 2.0 * error / CHANNELS).astype(jnp.bfloat16)
    grad_head = dot_low("gpc,gpd->cd", grad_pred, final_in)
    grad_final_in = dot_low("gpc,cd->gpd", grad_pred, head_w)
    grad_modul_f = jnp.concatenate(
        [jnp.sum(grad_final_in, 1), jnp.sum(grad_final_in * normed_f, 1)], -1
    ).astype(jnp.bfloat16)
    grad_hidden = local_back(norm_rows, hidden, grad_final_in * (1.0 + scale_f[:, None, :]))
    layer_grads = [None] * LAYERS
    grad_moduls = [None] * LAYERS
    for l in reversed(range(LAYERS)):
        grad_hidden, grad_moduls[l], layer_grads[l] = layer_backward(
            grad_hidden, weights_all[l], saved_all[l]
        )
    grad_embed = grad_hidden.astype(jnp.bfloat16)
    grad_patch = dot_low("gpc,gpd->cd", noisy_low, grad_embed)

    image_place = np.full((UNITS + 1,), -1, np.int32)
    image_place[image_units] = np.arange(len(image_units))
    my_place = jnp.asarray(image_place)[my_unit]
    room_slots, room_units = -(-slot_dev // 16) * 16, -(-len(image_units) // 16) * 16
    pick = jnp.pad(my_place, (0, room_slots - slot_dev), constant_values=-1)[:, None]
    pick = (pick == jnp.arange(room_units, dtype=jnp.int32)).astype(jnp.bfloat16)
    modul_grad = jnp.concatenate(grad_moduls + [grad_modul_f], -1).reshape(images, -1, BLOCK)
    modul_grad = jnp.pad(modul_grad, ((0, 0), (0, room_units - len(image_units)), (0, 0)))
    edge = jnp.concatenate([grad_patch, grad_head], 0)
    edge_room = max(all_images, 4 * CHANNELS)
    edge = jnp.concatenate([edge, jnp.broadcast_to(loss_part, (2 * CHANNELS, D))], 0)
    edge = jnp.pad(edge, ((0, edge_room - 4 * CHANNELS), (0, 0)))[:all_images]
    edge = jnp.pad(edge.reshape(all_images, blocks, BLOCK), ((0, 0), (8, 8 - blocks), (0, 0)))
    factor = local_back(jax.nn.silu, cond, jnp.ones_like(cond)).reshape(images, blocks, BLOCK)
    factor = jnp.pad(factor, ((0, 0), (0, 16 - blocks), (0, 0)), constant_values=1.0)
    unit_grads, slot_grad_out, shared = plan.scatter(
        layer_grads, modul_grad, pick, low_slots, edge, factor
    )
    shared = shared.reshape(all_images, 16, BLOCK)
    grad_cond = shared[:, :blocks].reshape(all_images, D)
    edge = shared[:, 8 : 8 + blocks].reshape(all_images, D)
    grad_patch, grad_head = edge[:CHANNELS], edge[CHANNELS : 2 * CHANNELS]
    loss_sum = edge[2 * CHANNELS, 0]
    grad_time_out = grad_cond.astype(jnp.bfloat16)
    grad_time_act = dot_low("ge,de->gd", grad_time_out, time_two)
    grad_time_pre = local_back(jax.nn.silu, time_pre, grad_time_act).astype(jnp.bfloat16)
    grad_time_w = dot_low("gf,gd->fd", freq_low, grad_time_pre)
    grad_table = jnp.zeros((CLASSES, D), jnp.float32).at[every_label].add(grad_cond)
    small_grad = jnp.concatenate([grad_patch, grad_time_w, grad_table, grad_head], 0)

    my_time = jnp.clip(my_unit - TAIL_FIRST, 0, TIME_UNITS - 1)
    is_time = (my_unit >= TAIL_FIRST) & (my_unit < TAIL_FIRST + TIME_UNITS)
    time_cols = jnp.take(grad_time_out.reshape(all_images, TIME_UNITS, BLOCK), my_time, axis=1)
    dense_place = np.full((UNITS + 1,), 0, np.int32)
    dense_place[dense_units] = np.arange(len(dense_units))
    slot_place = jnp.asarray(dense_place)[unit_of_slot]
    slot_rows = jnp.take(unit_grads, slot_place, axis=0, mode="clip")
    dense_grad, starts = plan.join_rows(
        lax.all_to_all(
            slot_rows.reshape(count, slot_dev, rows, BLOCK),
            AXES,
            split_axis=0,
            concat_axis=0,
            tiled=True,
        )
    )
    is_dense = (my_unit >= 0) & (my_place < 0) & ~is_time
    right = jnp.where(is_time[None, :, None], time_cols, slot_grad_out)
    left = jnp.where(is_time[:, None, None], time_act.T[None], cond_act.T[None])
    flags = [rate_factor * unit_scale(jnp.maximum(my_unit, 0)), my_unit >= 0, is_dense]
    flags = jnp.stack([flag.astype(jnp.float32) for flag in flags], 1)
    new_slots = adam_slots(
        dense_grad,
        starts,
        flags,
        left,
        jnp.swapaxes(right, 0, 1),
        *[jnp.swapaxes(values, 0, 1) for values in (master, first_moment, second_moment)],
    )
    new_master, new_first, new_second = [jnp.swapaxes(values, 0, 1) for values in new_slots]
    small_rate = rate_factor * table_scale(jnp.arange(small.shape[0], dtype=jnp.int32))[:, None]
    new_small, new_small_first, new_small_second = adam_update(
        small, small_first, small_second, small_grad, small_rate
    )
    return (
        loss_sum,
        weight_total,
        new_master,
        new_first,
        new_second,
        new_small,
        new_small_first,
        new_small_second,
    )


def solution(mesh):
    return jax.shard_map(
        on_device,
        mesh=mesh,
        in_specs=(
            P(("rep", "shard"), None),
            P(("rep", "shard"), None),
            P(("rep", "shard")),
            P(("rep", "shard")),
            P(),
            P(None, ("rep", "shard"), None),
            P(None, ("rep", "shard"), None),
            P(None, ("rep", "shard"), None),
            P(),
            P(),
            P(),
        ),
        out_specs=(
            P(),
            P(),
            P(None, ("rep", "shard"), None),
            P(None, ("rep", "shard"), None),
            P(None, ("rep", "shard"), None),
            P(),
            P(),
            P(),
        ),
        check_vma=False,
    )
```

```python
import jax
import jax.numpy as jnp
import numpy as np
from jax import lax
from jax.experimental import pallas as pl
from jax.experimental.pallas import tpu as pltpu
from jax.sharding import PartitionSpec as P

D = 768
HEADS = 12
HEAD_DIM = 64
FF = 3072
FREQ = 256
CLASSES = 1000
CHANNELS = 16
GRID = 16
PATCHES = 256
LAYERS = 2
TSTEPS = 1000
STEP = 10
BLOCK = 128
LAYER_COLS = 13824
LAYER_UNITS = 108
UNITS = 234

ADA_UNITS = 6 * D // BLOCK
DENSE_UNITS = LAYER_UNITS - ADA_UNITS
DENSE_COLS = DENSE_UNITS * BLOCK
TIME_UNITS = D // BLOCK
TAIL_FIRST = LAYERS * LAYER_UNITS
AXES = ("rep", "shard")


beta_one = 0.5
beta_two = 0.5
adam_eps = 1e-08
decay_rate = 0.1
rate_factor = 0.5


def gelu_tanh(values):
    return jax.nn.gelu(values, approximate=True)


def norm_rows(hidden):
    centered = hidden - jnp.mean(hidden, -1, keepdims=True)
    return centered * lax.rsqrt(jnp.mean(centered * centered, -1, keepdims=True) + 1e-06)


def local_back(function, primal, upstream):
    return jax.vjp(function, primal)[1](upstream)[0]


def dot_low(pattern, left_side, right_side):
    return jnp.einsum(pattern, left_side, right_side, preferred_element_type=jnp.float32)


def positions():
    quarter = D // 4
    angular = jnp.exp(-jnp.log(10000.0) * jnp.arange(quarter, dtype=jnp.float32) / quarter)
    patch_idx = jnp.arange(PATCHES, dtype=jnp.int32)
    row_pos = (patch_idx // GRID).astype(jnp.float32)[:, None] * angular
    col_pos = (patch_idx % GRID).astype(jnp.float32)[:, None] * angular
    return jnp.concatenate(
        [jnp.sin(col_pos), jnp.cos(col_pos), jnp.sin(row_pos), jnp.cos(row_pos)], -1
    )


def frequencies(times):
    half_size = FREQ // 2
    spacing = jnp.exp(-jnp.log(10000.0) * jnp.arange(half_size, dtype=jnp.float32) / half_size)
    angles = 1000.0 * times[:, None] * spacing
    return jnp.concatenate([jnp.cos(angles), jnp.sin(angles)], -1)


def unit_scale(unit_ids):
    column = unit_ids % LAYER_UNITS * BLOCK
    in_layer = unit_ids < LAYERS * LAYER_UNITS
    is_output = in_layer & (column >= 9 * D) & (column < 10 * D)
    is_down = in_layer & (column >= 10 * D + FF)
    factor = jnp.where(is_output, 4.0, jnp.where(is_down, 1.5 * (D / FF) ** 0.5, 1.0))
    return factor / D**0.5


def table_scale(row_ids):
    return jnp.where(
        row_ids < CHANNELS,
        CHANNELS ** (-0.5),
        jnp.where(
            row_ids < CHANNELS + FREQ,
            FREQ ** (-0.5),
            jnp.where(row_ids < CHANNELS + FREQ + CLASSES, 0.5, D ** (-0.5)),
        ),
    )


def adam_update(weight, first_mom, second, gradient, rate):
    first_new = beta_one * first_mom + (1.0 - beta_one) * gradient
    second_new = beta_two * second + (1.0 - beta_two) * gradient * gradient
    ratio = (
        first_new
        / (1.0 - beta_one**STEP)
        / (jnp.sqrt(second_new / (1.0 - beta_two**STEP)) + adam_eps)
    )
    return (weight - rate * (ratio + decay_rate * weight), first_new, second_new)


def modulate(normed, shift, scale):
    return normed * (1.0 + scale[:, None, :]) + shift[:, None, :]


def layer_forward(hidden, modul, weights):
    w_qkv, w_out, w_up, w_down = weights
    shift_a, scale_a, gate_a, shift_b, scale_b, gate_b = jnp.split(modul, 6, -1)
    attn_in = modulate(norm_rows(hidden), shift_a, scale_a).astype(jnp.bfloat16)
    qkv_all = dot_low("gpd,de->gpe", attn_in, w_qkv).astype(jnp.bfloat16)
    heads_out = attend(qkv_all)
    branch_a = dot_low("gpd,de->gpe", heads_out, w_out)
    middle = hidden + gate_a[:, None, :] * branch_a
    mlp_in = modulate(norm_rows(middle), shift_b, scale_b).astype(jnp.bfloat16)
    pre_act = dot_low("gpd,df->gpf", mlp_in, w_up)
    post_act = gelu_tanh(pre_act).astype(jnp.bfloat16)
    branch_b = dot_low("gpf,df->gpd", post_act, w_down)
    output = middle + gate_b[:, None, :] * branch_b
    return (
        output,
        (
            hidden,
            modul,
            attn_in,
            qkv_all,
            heads_out,
            branch_a,
            middle,
            mlp_in,
            pre_act.astype(jnp.bfloat16),
            post_act,
            branch_b,
        ),
    )


def layer_backward(grad_out, weights, saved):
    w_qkv, w_out, w_up, w_down = weights
    (
        hidden,
        modul,
        attn_in,
        qkv_all,
        heads_out,
        branch_a,
        middle,
        mlp_in,
        pre_act,
        post_act,
        branch_b,
    ) = saved
    shift_a, scale_a, gate_a, shift_b, scale_b, gate_b = jnp.split(modul, 6, -1)
    grad_gate_b = jnp.sum(grad_out * branch_b, 1)
    grad_branch_b = (gate_b[:, None, :] * grad_out).astype(jnp.bfloat16)
    grad_down = (grad_branch_b, post_act)
    grad_post = dot_low("gpd,df->gpf", grad_branch_b, w_down)
    grad_pre = local_back(gelu_tanh, pre_act.astype(jnp.float32), grad_post).astype(jnp.bfloat16)
    grad_up = (mlp_in, grad_pre)
    grad_mlp_in = dot_low("gpf,df->gpd", grad_pre, w_up)
    normed_b = norm_rows(middle)
    grad_scale_b = jnp.sum(grad_mlp_in * normed_b, 1)
    grad_shift_b = jnp.sum(grad_mlp_in, 1)
    grad_middle = grad_out + local_back(
        norm_rows, middle, grad_mlp_in * (1.0 + scale_b[:, None, :])
    )
    grad_gate_a = jnp.sum(grad_middle * branch_a, 1)
    grad_branch_a = (gate_a[:, None, :] * grad_middle).astype(jnp.bfloat16)
    grad_out_w = (heads_out, grad_branch_a)
    grad_heads = dot_low("gpe,de->gpd", grad_branch_a, w_out).astype(jnp.bfloat16)
    grad_qkv = attend_back(qkv_all, grad_heads)
    grad_qkv_w = (attn_in, grad_qkv)
    grad_attn_in = dot_low("gpe,de->gpd", grad_qkv, w_qkv)
    normed_a = norm_rows(hidden)
    grad_scale_a = jnp.sum(grad_attn_in * normed_a, 1)
    grad_shift_a = jnp.sum(grad_attn_in, 1)
    grad_in = grad_middle + local_back(
        norm_rows, hidden, grad_attn_in * (1.0 + scale_a[:, None, :])
    )
    grad_modul = jnp.concatenate(
        [grad_shift_a, grad_scale_a, grad_gate_a, grad_shift_b, grad_scale_b, grad_gate_b], -1
    ).astype(jnp.bfloat16)
    return (grad_in, grad_modul, [grad_qkv_w, grad_out_w, grad_up, grad_down])


MESH = pl.DeviceIdType.MESH
GATHER_VMEM = 60 * 2**20
SCATTER_VMEM = 56 * 2**20


def dot_rows(left_side, right_side):
    return lax.dot_general(
        left_side, right_side, (((0,), (0,)), ((), ())), preferred_element_type=jnp.float32
    )


def row_product(left_side, right_side):
    left_side = left_side.reshape(-1, left_side.shape[-1])
    right_side = right_side.reshape(-1, right_side.shape[-1])
    return dot_rows(left_side, right_side).astype(jnp.bfloat16)


def unit_groups():
    groups, place = [], 0
    for number in (3 * D, D, FF, FF) * LAYERS + (D,):
        groups.append((place, number // BLOCK))
        place += number // BLOCK
    return groups


PAIR = 2 * HEAD_DIM
SPAN = 3


def head_mask(number):
    lane = lax.broadcasted_iota(jnp.int32, (PATCHES, PAIR), 1)
    return (lane >= number * HEAD_DIM) & (lane < (number + 1) * HEAD_DIM)


def dot_lanes(left_side, right_side):
    return lax.dot_general(
        left_side, right_side, (((1,), (1,)), ((), ())), preferred_element_type=jnp.float32
    )


def attend_kernel(queries, keys_all, values, out):
    row = lax.broadcasted_iota(jnp.int32, (PAIR, PATCHES), 0)
    for pair in range(SPAN):
        lanes = slice(pair * PAIR, (pair + 1) * PAIR)
        scaled = queries[0, :, lanes] * HEAD_DIM ** (-0.5)
        keys, vals = keys_all[0, :, lanes], values[0, :, lanes]
        result = jnp.zeros((PAIR, PATCHES), jnp.float32)
        for number in (0, 1):
            one = jnp.where(head_mask(number), scaled, jnp.zeros((), jnp.bfloat16))
            scores = dot_lanes(keys, one)
            powers = jnp.exp(scores - jnp.max(scores, 0, keepdims=True))
            prob = (powers * (1.0 / jnp.sum(powers, 0, keepdims=True))).astype(jnp.bfloat16)
            result = jnp.where(row // HEAD_DIM == number, dot_rows(vals, prob), result)
        out[0, :, lanes] = result.T.astype(jnp.bfloat16)


def attend_back_kernel(queries, keys_all, values, grads, out):
    step = pl.program_id(1)
    row = lax.broadcasted_iota(jnp.int32, (PAIR, PATCHES), 0)
    none = jnp.zeros((), jnp.bfloat16)
    for pair in range(SPAN):
        lanes = slice(pair * PAIR, (pair + 1) * PAIR)
        scaled = queries[0, :, lanes] * HEAD_DIM ** (-0.5)
        keys, vals, grad = (ref[0, :, lanes] for ref in (keys_all, values, grads))
        grad_queries = jnp.zeros((PAIR, PATCHES), jnp.float32)
        grad_keys = jnp.zeros((PATCHES, PAIR), jnp.float32)
        grad_values = grad_keys
        for number in (0, 1):
            mask = head_mask(number)
            scores = dot_lanes(keys, jnp.where(mask, scaled, none))
            powers = jnp.exp(scores - jnp.max(scores, 0, keepdims=True))
            prob = powers * (1.0 / jnp.sum(powers, 0, keepdims=True))
            grad_prob = dot_lanes(vals, jnp.where(mask, grad, none))
            inner = jnp.sum(prob * grad_prob, 0, keepdims=True)
            grad_scores = (prob * (grad_prob - inner)).astype(jnp.bfloat16)
            part = dot_rows(keys, grad_scores)
            grad_queries = jnp.where(row // HEAD_DIM == number, part, grad_queries)
            part = jnp.dot(grad_scores, scaled, preferred_element_type=jnp.float32)
            grad_keys = jnp.where(mask, part, grad_keys)
            part = jnp.dot(prob.astype(jnp.bfloat16), grad, preferred_element_type=jnp.float32)
            grad_values = jnp.where(mask, part, grad_values)
        grad_queries = grad_queries.T * HEAD_DIM ** (-0.5)
        for third, result in enumerate((grad_queries, grad_keys, grad_values)):
            first = pl.multiple_of(third * D + (step * SPAN + pair) * PAIR, PAIR)
            out[0, :, pl.ds(first, PAIR)] = result.astype(jnp.bfloat16)


def pair_block(third):
    steps = HEADS // 2 // SPAN
    return pl.BlockSpec(
        (1, PATCHES, SPAN * PAIR), lambda image, step: (image, 0, third * steps + step)
    )


def attend(qkv_all):
    images = qkv_all.shape[0]
    steps = HEADS // 2 // SPAN
    return pl.pallas_call(
        attend_kernel,
        grid=(images, steps),
        out_shape=jax.ShapeDtypeStruct((images, PATCHES, D), jnp.bfloat16),
        in_specs=[pair_block(0), pair_block(1), pair_block(2)],
        out_specs=pair_block(0),
        cost_estimate=pl.CostEstimate(
            flops=4 * images * PATCHES * PATCHES * D,
            bytes_accessed=8 * images * PATCHES * D,
            transcendentals=images * HEADS * PATCHES * PATCHES,
        ),
    )(qkv_all, qkv_all, qkv_all)


def attend_back(qkv_all, grad_heads):
    images = qkv_all.shape[0]
    steps = HEADS // 2 // SPAN
    return pl.pallas_call(
        attend_back_kernel,
        grid=(images, steps),
        out_shape=jax.ShapeDtypeStruct((images, PATCHES, 3 * D), jnp.bfloat16),
        in_specs=[pair_block(0), pair_block(1), pair_block(2), pair_block(0)],
        out_specs=pl.BlockSpec((1, PATCHES, 3 * D), lambda image, step: (image, 0, 0)),
        cost_estimate=pl.CostEstimate(
            flops=10 * images * PATCHES * PATCHES * D,
            bytes_accessed=14 * images * PATCHES * D,
            transcendentals=images * HEADS * PATCHES * PATCHES,
        ),
    )(qkv_all, qkv_all, qkv_all, grad_heads)


def adam_kernel(starts, flags, dense, left, right, master, first, second, *refs):
    new_master, new_first, new_second, image_grad = refs
    slot = pl.program_id(0)
    rate, used, is_dense = flags[slot, 0], flags[slot, 1], flags[slot, 2]
    image_grad[...] = jnp.dot(left[0], right[0], preferred_element_type=jnp.float32)
    rows = dense.shape[2]
    for n, start in enumerate(starts):
        at = (0, slice(start, start + rows))
        grad = jnp.where(is_dense > 0.0, dense[n, 0].astype(jnp.float32), image_grad[at[1]])
        old = (master[at], first[at], second[at])
        first_new = beta_one * old[1] + (1.0 - beta_one) * grad
        second_new = beta_two * old[2] + (1.0 - beta_two) * grad * grad
        root = jnp.sqrt(second_new * (1.0 / (1.0 - beta_two**STEP))) + adam_eps
        ratio = first_new * (1.0 / (1.0 - beta_one**STEP)) / root
        new = (old[0] - rate * (ratio + decay_rate * old[0]), first_new, second_new)
        for ref, value, kept in zip((new_master, new_first, new_second), new, old):
            ref[at] = jnp.where(used > 0.0, value, kept)


def adam_slots(dense, starts, flags, left, right, *state):
    slots = state[0].shape[0]
    block = pl.BlockSpec((1, D, BLOCK), lambda slot: (slot, 0, 0))
    side = left.shape[2]
    return pl.pallas_call(
        lambda *refs: adam_kernel(starts, *refs),
        grid=(slots,),
        out_shape=[jax.ShapeDtypeStruct((slots, D, BLOCK), jnp.float32)] * 3,
        in_specs=[
            pl.BlockSpec(memory_space=pltpu.SMEM),
            pl.BlockSpec(
                (dense.shape[0], 1) + dense.shape[2:], lambda slot: (0, slot, 0, 0)
            ),
            pl.BlockSpec((1, D, side), lambda slot: (slot, 0, 0)),
            pl.BlockSpec((1, side, BLOCK), lambda slot: (slot, 0, 0)),
        ]
        + [block] * 3,
        out_specs=[block] * 3,
        scratch_shapes=[pltpu.VMEM((D, BLOCK), jnp.float32)],
        cost_estimate=pl.CostEstimate(
            flops=40 * slots * D * BLOCK, bytes_accessed=26 * slots * D * BLOCK, transcendentals=0
        ),
    )(flags, dense, left, right, *state)


def place_of():
    rep = lax.axis_index("rep")
    return rep // 4, (rep // 2) % 2, rep % 2, lax.axis_index("shard")


def rep_of(y, x, c):
    return (y * 2 + x) * 2 + c


def device_at(j):
    shards = lax.axis_size("shard")
    devices = lax.axis_size("rep") * shards
    me = lax.axis_index("rep") * shards + lax.axis_index("shard")
    peer = lax.rem(me + j, devices)
    return peer, (peer // shards, lax.rem(peer, shards))


def meet_all(devices):
    barrier = pltpu.get_barrier_semaphore()

    @pl.loop(1, devices)
    def _(j):
        pl.semaphore_signal(barrier, inc=1, device_id=device_at(j)[1], device_id_type=MESH)

    pl.semaphore_wait(barrier, devices - 1)


def neighbours():
    y, x, c, z = place_of()
    to_x = (rep_of(y, 1 - x, c), z)
    to_y = (rep_of(1 - y, x, c), z)
    to_core = (rep_of(y, x, 1 - c), z)
    to_z = [(rep_of(y, x, c), lax.rem(z + step, 4)) for step in (1, 2, 3)]
    return to_x, to_y, to_core, to_z


def round_copies(step, source, held, sem, arriving):
    y, x, c, z = place_of()
    to_x, to_y, to_core, to_z = neighbours()
    if step == 0:
        copies = []
        for number in (1, 2, 3):
            at_z = lax.rem(z + 4 - number, 4) if arriving else z
            copies.append((source, held.at[y, x, c, at_z], to_z[number - 1]))
    else:
        at_x = 1 - x if arriving and step == 1 else x
        at_y = 1 - y if arriving and step == 2 else y
        at_c = 1 - c if arriving and step == 3 else c
        block = (held.at[y, at_x, c], held.at[at_y, :, c], held.at[:, :, at_c])[step - 1]
        copies = [(block, block, (to_x, to_y, to_core)[step - 1])]
    return [
        pltpu.make_async_remote_copy(
            src_ref=start,
            dst_ref=dest,
            send_sem=sem.at[0, step, number],
            recv_sem=sem.at[1, step, number],
            device_id=target,
            device_id_type=MESH,
        )
        for number, (start, dest, target) in enumerate(copies)
    ]


def gather_kernel(widths, bases, *refs):
    count = len(widths)
    places, spread, info, low_slots = refs[:4]
    outs = refs[4 : count + 4]
    every_info, cond_out, modul_out = refs[count + 4 : count + 7]
    pieces = refs[count + 7 : 2 * count + 7]
    time_two, parts, own_sem, send_sem, recv_sem, time_sem, modul_sem, info_sem = refs[
        2 * count + 7 :
    ]
    devices, images = modul_out.shape[:2]
    slots = low_slots.shape[0]
    y, x, c, z = place_of()
    to_x, to_y, to_core, to_z = neighbours()
    me = rep_of(y, x, c) * 4 + z
    meet_all(devices)

    def remote(k, number, source, dest, target):
        return pltpu.make_async_remote_copy(
            src_ref=source,
            dst_ref=dest,
            send_sem=send_sem.at[k, number],
            recv_sem=recv_sem.at[k, number],
            device_id=target,
            device_id_type=MESH,
        )

    def own_copy(k):
        return pltpu.make_async_copy(pieces[k], outs[k].at[c, y, x, z], own_sem.at[k])

    def line_copies(k, arriving):
        copies = []
        for step in (1, 2, 3):
            at_z = lax.rem(z + 4 - step, 4) if arriving else z
            copies.append(
                remote(k, step - 1, pieces[k], outs[k].at[c, y, x, at_z], to_z[step - 1])
            )
        return copies

    def first_copies(k, arriving):
        half = widths[k] // 2
        left, right = pl.ds(0, half), pl.ds(half, half)
        at_x = 1 - x if arriving else x
        at_y = 1 - y if arriving else y
        a_block = outs[k].at[c, y, at_x, :, :, left]
        b_block = outs[k].at[c, at_y, x, :, :, right]
        return [remote(k, 3, a_block, a_block, to_x), remote(k, 4, b_block, b_block, to_y)]

    def second_copies(k, arriving):
        half = widths[k] // 2
        left, right = pl.ds(0, half), pl.ds(half, half)
        at_x = 1 - x if arriving else x
        at_y = 1 - y if arriving else y
        a_block = outs[k].at[c, at_y, :, :, :, left]
        b_block = outs[k].at[c, :, at_x, :, :, right]
        return [remote(k, 5, a_block, a_block, to_y), remote(k, 6, b_block, b_block, to_x)]

    def core_copies(k, arriving):
        block = outs[k].at[1 - c if arriving else c]
        return [remote(k, 7, block, block, to_core)]

    def start(copies):
        for copy in copies:
            copy.start()

    def arrived(copies):
        for copy in copies:
            copy.wait_recv()

    def modul_copy(j, arriving):
        peer, where = device_at(devices - j if arriving else j)
        return pltpu.make_async_remote_copy(
            src_ref=parts.at[pl.ds(peer * images, images)],
            dst_ref=modul_out.at[peer if arriving else me],
            send_sem=modul_sem.at[0, j],
            recv_sem=modul_sem.at[1, j],
            device_id=where,
            device_id_type=MESH,
        )

    def info_copies(step, arriving):
        return round_copies(step, info, every_info, info_sem, arriving)

    def info_rows(first):
        rows = [every_info[:, :, :, :, :, first + j, :] for j in range(D // BLOCK)]
        return jnp.concatenate([row.reshape(devices * images, BLOCK) for row in rows], -1)

    def image_products():
        copy = pltpu.make_async_copy(outs[0], time_two, time_sem)
        copy.start()
        arrived(info_copies(3, True))
        for step in range(4):
            for sent in info_copies(step, False):
                sent.wait_send()
        copy.wait()
        weight = time_two[...].astype(jnp.float32).reshape(D, D).astype(jnp.bfloat16)
        cond = jnp.dot(
            info_rows(0).astype(jnp.bfloat16), weight, preferred_element_type=jnp.float32
        )
        cond = cond + info_rows(8)
        cond_out[...] = cond
        act = (cond * jax.nn.sigmoid(cond)).astype(jnp.bfloat16)
        for s in range(slots):
            parts[:, s, :] = jnp.dot(act, low_slots[s], preferred_element_type=jnp.float32)
        for i in range(images):
            modul_out[me, i] = parts[me * images + i]

        @pl.loop(1, devices)
        def _(j):
            modul_copy(j, False).start()

    start(info_copies(0, False))
    every_info[y, x, c, z] = info[...]
    def send_piece(k):
        for n in range(widths[k] // BLOCK):
            pieces[k][:, n * BLOCK : (n + 1) * BLOCK] = spread[places[bases[k] + n]]
        start(line_copies(k, False))
        own_copy(k).start()

    send_piece(0)
    for t in range(count + 2):
        if t + 1 < count:
            send_piece(t + 1)
        if t < count:
            own_copy(t).wait()
            arrived(line_copies(t, True))
            start(first_copies(t, False))
        if 0 <= t - 1 < count:
            arrived(first_copies(t - 1, True))
            start(second_copies(t - 1, False))
        if 0 <= t - 2 < count:
            arrived(second_copies(t - 2, True))
            start(core_copies(t - 2, False))
        if t < 3:
            arrived(info_copies(t, True))
            start(info_copies(t + 1, False))
        if t == 3:
            arrived(core_copies(0, True))
            image_products()
    for k in range(1, count):
        arrived(core_copies(k, True))

    @pl.loop(1, devices)
    def _(j):
        modul_copy(j, True).wait_recv()
        modul_copy(j, False).wait_send()

    for k in range(count):
        for copies in (line_copies, first_copies, second_copies, core_copies):
            for copy in copies(k, False):
                copy.wait_send()


def scatter_kernel(widths, bases, slots, *refs):
    count = len(widths)
    lefts, rights = refs[:count], refs[count : 2 * count]
    modul, pick, low_slots, edge, factor = refs[2 * count : 2 * count + 5]
    units, chosen, shared = refs[2 * count + 5 : 2 * count + 8]
    scratch = refs[2 * count + 8 :]
    own, first_in, second_in, line_in = (scratch[i * count : (i + 1) * count] for i in range(4))
    (
        left_in, left_turned, right_in, away, every_modul, parts, landed,
        load_sem, send_sem, recv_sem, modul_sem, part_sem, sum_sem,
    ) = scratch[4 * count :]
    devices, images = 32, shared.shape[4]
    y, x, c, z = place_of()
    to_x, to_y, to_core, to_z = neighbours()
    me = rep_of(y, x, c) * 4 + z
    rows = D // 32
    half_rows = D // 2
    meet_all(devices)

    def exchange(source, dest, sem, j, arriving):
        peer, where = device_at(devices - j if arriving else j)
        return pltpu.make_async_remote_copy(
            src_ref=source(peer, me),
            dst_ref=dest(peer if arriving else me),
            send_sem=sem.at[0, j],
            recv_sem=sem.at[1, j],
            device_id=where,
            device_id_type=MESH,
        )

    def modul_copies(step, arriving):
        return round_copies(step, modul, every_modul, modul_sem, arriving)

    def sum_copies(step, arriving):
        return round_copies(step, shared.at[y, x, c, z], shared, sum_sem, arriving)

    def part_copy(j, arriving):
        return exchange(
            lambda peer, mine: parts.at[pl.ds(peer * images, images)],
            lambda owner: landed.at[owner],
            part_sem, j, arriving,
        )

    def all_start(copy):
        @pl.loop(1, devices)
        def _(j):
            copy(j, False).start()

    def all_arrived(copy):
        @pl.loop(1, devices)
        def _(j):
            copy(j, True).wait_recv()

    def all_sent(copy):
        @pl.loop(1, devices)
        def _(j):
            copy(j, False).wait_send()

    def image_parts():
        arrived(modul_copies(3, True))

        @pl.loop(0, devices // 4)
        def _(i):
            for n in range(4):
                for m in range(images):
                    block = every_modul[i // 4, (i // 2) % 2, i % 2, n, m]
                    chosen[(i * 4 + n) * images + m] = jnp.dot(
                        pick[...], block, preferred_element_type=jnp.float32
                    )

        total = jnp.zeros((devices * images, D), jnp.float32)
        for s in range(slots):
            total = total + lax.dot_general(
                chosen[:, s, :].astype(jnp.bfloat16),
                low_slots[s],
                (((1,), (1,)), ((), ())),
                preferred_element_type=jnp.float32,
            )
        parts[...] = edge[...]
        for j in range(D // BLOCK):
            parts[:, j, :] = total[:, j * BLOCK : (j + 1) * BLOCK]
        all_start(part_copy)
        for i in range(images):
            landed[me, i] = parts[me * images + i]

    def image_sums():
        all_arrived(part_copy)
        shared[y, x, c, z] = jnp.sum(landed[...], 0) * factor[...]
        start(sum_copies(0, False))

    def remote(k, number, source, dest, target):
        return pltpu.make_async_remote_copy(
            src_ref=source,
            dst_ref=dest,
            send_sem=send_sem.at[k, number],
            recv_sem=recv_sem.at[k, number],
            device_id=target,
            device_id_type=MESH,
        )

    def load_left(k):
        return pltpu.make_async_copy(lefts[k], left_in.at[k % 2], load_sem.at[0, k % 2])

    def load_right(k):
        place = right_in.at[k % 3, :, pl.ds(0, widths[k])]
        return pltpu.make_async_copy(rights[k], place, load_sem.at[1, k % 3])

    def core_copies(k):
        source = away.at[k % 3, :, :, :, :, pl.ds(0, widths[k])]
        return [remote(k, 0, source, own[k], to_core)]

    def first_copies(k):
        half = widths[k] // 2
        return [
            remote(k, 1, own[k].at[:, 1 - x, :, :, pl.ds(0, half)], first_in[k].at[0], to_x),
            remote(k, 2, own[k].at[1 - y, :, :, :, pl.ds(half, half)], first_in[k].at[1], to_y),
        ]

    def second_copies(k):
        half = widths[k] // 2
        return [
            remote(k, 3, own[k].at[1 - y, x, :, :, pl.ds(0, half)], second_in[k].at[0], to_y),
            remote(k, 4, own[k].at[y, 1 - x, :, :, pl.ds(half, half)], second_in[k].at[1], to_x),
        ]

    def line_copies(k):
        return [
            remote(
                k,
                4 + step,
                own[k].at[y, x, lax.rem(z + step, 4)],
                line_in[k].at[step - 1],
                to_z[step - 1],
            )
            for step in (1, 2, 3)
        ]

    def start(copies):
        for copy in copies:
            copy.start()

    def arrived(copies):
        for copy in copies:
            copy.wait_recv()

    def products(k, half, store):
        slot = k % 3
        tile = D

        @pl.loop(0, widths[k] // tile)
        def _(n):
            columns = pl.ds(pl.multiple_of(n * tile, tile), tile)
            left = left_turned[slot, pl.ds(pl.multiple_of(half * half_rows, half_rows), half_rows)]
            result = jnp.dot(left, right_in[slot, :, columns], preferred_element_type=jnp.float32)
            for i in range(16):
                at = (i // 8, (i // 4) % 2, i % 4, slice(None), columns)
                store(at, result[i * rows : (i + 1) * rows])

    def away_products(k):
        load_left(k).wait()
        load_right(k).wait()
        left_turned[k % 3] = left_in[k % 2].T
        if k + 2 < count:
            load_left(k + 2).start()
        if k >= 3:
            for copy in core_copies(k - 3):
                copy.wait_send()

        def store(at, value):
            away[(k % 3,) + at] = value.astype(jnp.bfloat16)

        products(k, 1 - c, store)
        start(core_copies(k))

    def own_products(k):
        def store(at, value):
            own[k][at] = (value + own[k][at].astype(jnp.float32)).astype(jnp.bfloat16)

        products(k, c, store)

    def first_sum(k):
        half = widths[k] // 2

        @pl.loop(0, 8)
        def _(i):
            two, at_z = i // 4, i % 4
            a_at = (two, x, at_z, slice(None), pl.ds(0, half))
            b_at = (y, two, at_z, slice(None), pl.ds(half, half))
            own[k][a_at] = own[k][a_at] + first_in[k][0, two, at_z]
            own[k][b_at] = own[k][b_at] + first_in[k][1, two, at_z]

    def second_sum(k):
        half = widths[k] // 2

        @pl.loop(0, 4)
        def _(at_z):
            a_at = (y, x, at_z, slice(None), pl.ds(0, half))
            b_at = (y, x, at_z, slice(None), pl.ds(half, half))
            own[k][a_at] = own[k][a_at] + second_in[k][0, at_z]
            own[k][b_at] = own[k][b_at] + second_in[k][1, at_z]

    start(modul_copies(0, False))
    every_modul[y, x, c, z] = modul[...]
    for k in range(min(3, count)):
        load_right(k).start()
        if k < 2:
            load_left(k).start()
    away_products(0)
    for t in range(count + 3):
        if t + 1 < count:
            away_products(t + 1)
        if t < count:
            arrived(core_copies(t))
            own_products(t)
            start(first_copies(t))
            if t + 3 < count:
                load_right(t + 3).start()
        if 0 <= t - 1 < count:
            arrived(first_copies(t - 1))
            first_sum(t - 1)
            start(second_copies(t - 1))
        if 0 <= t - 2 < count:
            arrived(second_copies(t - 2))
            second_sum(t - 2)
            start(line_copies(t - 2))
        if 0 <= t - 3 < count:
            k = t - 3
            arrived(line_copies(k))
            total = own[k][y, x, z].astype(jnp.float32)
            for step in (1, 2, 3):
                total = total + line_in[k][step - 1].astype(jnp.float32)
            for n in range(widths[k] // BLOCK):
                part = total[:, n * BLOCK : (n + 1) * BLOCK]
                units[bases[k] + n] = part.astype(jnp.bfloat16)
        if t < 3:
            arrived(modul_copies(t, True))
            start(modul_copies(t + 1, False))
        if t == 3:
            image_parts()
        if t == 6:
            image_sums()
        if 7 <= t < 10:
            arrived(sum_copies(t - 7, True))
            start(sum_copies(t - 6, False))
    arrived(sum_copies(3, True))
    all_sent(part_copy)
    for step in range(4):
        for copy in modul_copies(step, False) + sum_copies(step, False):
            copy.wait_send()
    for k in range(count):
        for copies in (core_copies, first_copies, second_copies, line_copies):
            if copies is core_copies and k + 3 < count:
                continue
            for copy in copies(k):
                copy.wait_send()


class RingPlan:
    def split_rows(self, values):
        slots = values.shape[0]
        split = values.reshape(slots, 2, 2, 2, 4, D // 32, BLOCK)
        return split.transpose(2, 3, 1, 4, 0, 5, 6).reshape(32, slots, D // 32, BLOCK)

    def join_rows(self, values):
        starts = []
        for device in range(32):
            y, x, c, z = device // 16, device // 8 % 2, device // 4 % 2, device % 4
            starts.append(((((c * 2 + y) * 2 + x) * 4) + z) * (D // 32))
        return values, starts

    def gather(self, places, spread, info, low_slots):
        names = unit_groups()
        turn = [len(names) - 1] + sorted(range(len(names) - 1), key=lambda n: (n % 4 == 1, n))
        bases = tuple(names[n][0] for n in turn)
        widths = tuple(names[n][1] * BLOCK for n in turn)
        count, rows = len(turn), D // 32
        all_images = 32 * info.shape[0]
        slots = low_slots.shape[0]
        room = -(-slots // 8) * 8
        size = sum(4 * D * width for width in widths)
        whole_shape = [(2, 2, 2, 4, rows, width) for width in widths]
        *whole, every_info, cond, modul = pl.pallas_call(
            lambda *refs: gather_kernel(widths, bases, *refs),
            out_shape=[
                jax.ShapeDtypeStruct(shape, jnp.bfloat16) for shape in whole_shape
            ]
            + [
                jax.ShapeDtypeStruct((2, 2, 2, 4) + info.shape, jnp.float32),
                jax.ShapeDtypeStruct((all_images, D), jnp.float32),
                jax.ShapeDtypeStruct((32, all_images // 32, room, BLOCK), jnp.float32),
            ],
            in_specs=[pl.BlockSpec(memory_space=pltpu.SMEM)]
            + [pl.BlockSpec(memory_space=pltpu.VMEM)] * 3,
            out_specs=[pl.BlockSpec(memory_space=pl.ANY)] * count
            + [pl.BlockSpec(memory_space=pltpu.VMEM)] * 3,
            scratch_shapes=[pltpu.VMEM((rows, width), jnp.bfloat16) for width in widths]
            + [
                pltpu.VMEM(whole_shape[0], jnp.bfloat16),
                pltpu.VMEM((all_images, room, BLOCK), jnp.float32),
                pltpu.SemaphoreType.DMA((count,)),
                pltpu.SemaphoreType.DMA((count, 8)),
                pltpu.SemaphoreType.DMA((count, 8)),
                pltpu.SemaphoreType.DMA,
                pltpu.SemaphoreType.DMA((2, 32)),
                pltpu.SemaphoreType.DMA((2, 4, 3)),
            ],
            compiler_params=pltpu.CompilerParams(
                collective_id=0, has_side_effects=True, vmem_limit_bytes=GATHER_VMEM
            ),
            cost_estimate=pl.CostEstimate(flops=0, bytes_accessed=size, transcendentals=0),
        )(places, spread, info, low_slots)
        whole = [part.reshape(D, -1) for part in whole]
        modul = jnp.swapaxes(modul[:, :, :slots], 0, 1).reshape(-1, 32 * slots, BLOCK)
        ordered = [whole[turn.index(n)] for n in range(count)]
        every_info = every_info.reshape((all_images,) + info.shape[1:])
        return ordered[:-1], ordered[-1], every_info, cond, modul

    def scatter(self, layer_grads, modul, pick, low_slots, edge, factor):
        turn = [(l, n) for l in range(LAYERS) for n in (0, 2, 3)]
        turn = [(LAYERS - 1, 1)] + turn + [(l, 1) for l in range(LAYERS - 1)]
        grads = [layer_grads[l][n] for l, n in turn]
        names = unit_groups()
        bases = tuple(names[4 * l + n][0] for l, n in turn)
        lefts = [left.reshape(-1, D) for left, _ in grads]
        rights = [right.reshape(left.shape[0], -1) for (_, right), left in zip(grads, lefts)]
        widths = tuple(right.shape[1] for right in rights)
        count, rows, tokens = len(grads), D // 32, lefts[0].shape[0]
        widest = max(widths)
        images, slots = modul.shape[0], low_slots.shape[0]
        size = sum(4 * D * width for width in widths)
        scratch = [pltpu.VMEM((2, 2, 4, rows, width), jnp.bfloat16) for width in widths]
        scratch += [pltpu.VMEM((2, 2, 4, rows, width // 2), jnp.bfloat16) for width in widths]
        scratch += [pltpu.VMEM((2, 4, rows, width // 2), jnp.bfloat16) for width in widths]
        scratch += [pltpu.VMEM((3, rows, width), jnp.bfloat16) for width in widths]
        units, chosen, shared = pl.pallas_call(
            lambda *refs: scatter_kernel(widths, bases, slots, *refs),
            out_shape=[
                jax.ShapeDtypeStruct((sum(widths) // BLOCK, rows, BLOCK), jnp.bfloat16),
                jax.ShapeDtypeStruct((32 * images, pick.shape[0], BLOCK), jnp.float32),
                jax.ShapeDtypeStruct((2, 2, 2, 4) + factor.shape, jnp.float32),
            ],
            in_specs=[pl.BlockSpec(memory_space=pl.ANY)] * (2 * count)
            + [pl.BlockSpec(memory_space=pltpu.VMEM)] * 5,
            out_specs=[pl.BlockSpec(memory_space=pltpu.VMEM)] * 3,
            scratch_shapes=scratch
            + [
                pltpu.VMEM((2, tokens, D), jnp.bfloat16),
                pltpu.VMEM((3, D, tokens), jnp.bfloat16),
                pltpu.VMEM((3, tokens, widest), jnp.bfloat16),
                pltpu.VMEM((3, 2, 2, 4, rows, widest), jnp.bfloat16),
                pltpu.VMEM((2, 2, 2, 4) + modul.shape, jnp.bfloat16),
                pltpu.VMEM(edge.shape, jnp.float32),
                pltpu.VMEM((32,) + factor.shape, jnp.float32),
                pltpu.SemaphoreType.DMA((2, 3)),
                pltpu.SemaphoreType.DMA((count, 8)),
                pltpu.SemaphoreType.DMA((count, 8)),
                pltpu.SemaphoreType.DMA((2, 4, 3)),
                pltpu.SemaphoreType.DMA((2, 32)),
                pltpu.SemaphoreType.DMA((2, 4, 3)),
            ],
            compiler_params=pltpu.CompilerParams(
                collective_id=1, has_side_effects=True, vmem_limit_bytes=SCATTER_VMEM
            ),
            cost_estimate=pl.CostEstimate(flops=0, bytes_accessed=size, transcendentals=0),
        )(*lefts, *rights, modul, pick, low_slots, edge, factor)
        return units, chosen[:, :slots].astype(jnp.bfloat16), shared


class PlainPlan:
    def split_rows(self, values):
        slots, devices = values.shape[0], lax.axis_size("rep") * lax.axis_size("shard")
        return jnp.swapaxes(values.reshape(slots, devices, -1, BLOCK), 0, 1)

    def join_rows(self, values):
        return jnp.swapaxes(values, 0, 1).reshape(1, -1, D, BLOCK), [0]

    def gather(self, places, spread, info, low_slots):
        units = jnp.take(spread, places, axis=0, mode="clip")
        whole = []
        for first, number in unit_groups():
            piece = jnp.swapaxes(units[first : first + number], 0, 1)
            piece = piece.reshape(-1, number * BLOCK)
            whole.append(lax.all_gather(piece, AXES, axis=0, tiled=True))
        every_info = lax.all_gather(info, AXES, axis=0, tiled=True)
        blocks = D // BLOCK
        time_act = every_info[:, :blocks].reshape(-1, D).astype(jnp.bfloat16)
        cond = jnp.dot(time_act, whole[-1], preferred_element_type=jnp.float32)
        cond = cond + every_info[:, 8 : 8 + blocks].reshape(-1, D)
        modul = dot_low("gd,sdc->gsc", jax.nn.silu(cond).astype(jnp.bfloat16), low_slots)
        modul = lax.all_to_all(modul, AXES, split_axis=0, concat_axis=1, tiled=True)
        return whole[:-1], whole[-1], every_info, cond, modul

    def scatter(self, layer_grads, modul, pick, low_slots, edge, factor):
        units = []
        for pair in (pair for grads in layer_grads for pair in grads):
            own = lax.psum_scatter(row_product(*pair), AXES, scatter_dimension=0, tiled=True)
            units.append(jnp.swapaxes(own.reshape(own.shape[0], -1, BLOCK), 0, 1))
        slots = low_slots.shape[0]
        every = lax.all_gather(modul, AXES, axis=0, tiled=True)
        chosen = dot_low("su,guc->gsc", pick, every)[:, :slots].astype(jnp.bfloat16)
        part = dot_low("gsc,sdc->gd", chosen, low_slots).reshape(-1, D // BLOCK, BLOCK)
        parts = edge.at[:, : D // BLOCK].set(part)
        own = lax.psum_scatter(parts, AXES, scatter_dimension=0, tiled=True) * factor
        shared = lax.all_gather(own, AXES, axis=0, tiled=False)
        return jnp.concatenate(units, 0), chosen, shared


def unit_lists():
    dense = np.concatenate(
        [np.arange(l * LAYER_UNITS + ADA_UNITS, (l + 1) * LAYER_UNITS) for l in range(LAYERS)]
    )
    time_units = np.arange(TAIL_FIRST, TAIL_FIRST + TIME_UNITS)
    image_units = np.concatenate(
        [np.arange(l * LAYER_UNITS, l * LAYER_UNITS + ADA_UNITS) for l in range(LAYERS)]
        + [np.arange(TAIL_FIRST + TIME_UNITS, UNITS)]
    )
    return dense, time_units, image_units


def on_device(
    latents,
    noise,
    labels,
    t_index,
    owner,
    master,
    first_moment,
    second_moment,
    small,
    small_first,
    small_second,
):
    count = lax.axis_size("rep") * lax.axis_size("shard")
    me = lax.axis_index(AXES)
    slot_dev = master.shape[1]
    slot_total = count * slot_dev
    rows = D // count
    images = latents.shape[0]
    dense_units, time_units, image_units = unit_lists()

    unit_of_slot = (
        jnp.full((slot_total,), -1, jnp.int32).at[owner].set(jnp.arange(UNITS, dtype=jnp.int32))
    )
    my_unit = lax.dynamic_slice_in_dim(unit_of_slot, me * slot_dev, slot_dev)
    low_slots = jnp.swapaxes(master.astype(jnp.bfloat16), 0, 1)

    plan = RingPlan() if (lax.axis_size("rep"), lax.axis_size("shard")) == (8, 4) else PlainPlan()
    spread = lax.all_to_all(
        plan.split_rows(low_slots), AXES, split_axis=0, concat_axis=0, tiled=True
    ).reshape(slot_total, rows, BLOCK)
    moved = np.concatenate([dense_units, time_units])
    places = owner[moved]

    x_start = latents.astype(jnp.float32).reshape(-1, PATCHES, CHANNELS)
    noise_f = noise.astype(jnp.float32).reshape(-1, PATCHES, CHANNELS)
    times = (t_index.astype(jnp.float32) + 0.5) / TSTEPS
    noisy = (1.0 - times)[:, None, None] * x_start + times[:, None, None] * noise_f
    target = noise_f - x_start
    loss_weight = 1.0 + 3.0 * times
    small_low = small.astype(jnp.bfloat16)
    patch_w = small_low[:CHANNELS]
    time_w = small_low[CHANNELS : CHANNELS + FREQ]
    table = small[CHANNELS + FREQ : CHANNELS + FREQ + CLASSES]
    head_w = small_low[CHANNELS + FREQ + CLASSES :]
    noisy_low = noisy.astype(jnp.bfloat16)
    hidden = dot_low("gpc,cd->gpd", noisy_low, patch_w) + positions()

    blocks = D // BLOCK
    freq_own = frequencies(times).astype(jnp.bfloat16)
    time_own = jnp.dot(freq_own, time_w, preferred_element_type=jnp.float32)
    act_own = jax.nn.silu(time_own).astype(jnp.bfloat16).astype(jnp.float32)
    label_own = jnp.take(table, labels, axis=0)
    numbers = jnp.stack([t_index, labels], 1).astype(jnp.float32)
    info = jnp.concatenate(
        [
            act_own.reshape(images, blocks, BLOCK),
            jnp.pad(numbers, ((0, 0), (0, BLOCK - 2)))[:, None],
            jnp.zeros((images, 7 - blocks, BLOCK), jnp.float32),
            label_own.reshape(images, blocks, BLOCK),
            jnp.zeros((images, 8 - blocks, BLOCK), jnp.float32),
        ],
        1,
    )
    whole, time_two, every_info, cond_all, slot_modul = plan.gather(
        places, spread, info, low_slots
    )
    all_images = cond_all.shape[0]
    every_time = (every_info[:, blocks, 0] + 0.5) / TSTEPS
    every_label = every_info[:, blocks, 1].astype(jnp.int32)
    weight_total = jnp.sum(1.0 + 3.0 * every_time) * PATCHES
    freq_low = frequencies(every_time).astype(jnp.bfloat16)
    time_pre = jnp.dot(freq_low, time_w, preferred_element_type=jnp.float32)
    time_act = every_info[:, :blocks].reshape(all_images, D).astype(jnp.bfloat16)
    weights_all = [tuple(whole[4 * l : 4 * l + 4]) for l in range(LAYERS)]
    cond = lax.dynamic_slice_in_dim(cond_all, me * images, images)
    cond_act = jax.nn.silu(cond_all).astype(jnp.bfloat16)
    modul_all = jnp.take(slot_modul, owner[image_units], axis=1, mode="clip").reshape(images, -1)

    saved_all = []
    for l in range(LAYERS):
        hidden, saved = layer_forward(
            hidden, modul_all[:, l * 6 * D : (l + 1) * 6 * D], weights_all[l]
        )
        saved_all.append(saved)
    shift_f, scale_f = jnp.split(modul_all[:, LAYERS * 6 * D :], 2, -1)
    normed_f = norm_rows(hidden)
    final_in = modulate(normed_f, shift_f, scale_f).astype(jnp.bfloat16)
    predict = dot_low("gpd,cd->gpc", final_in, head_w)
    error = predict - target
    loss_part = jnp.sum(loss_weight[:, None, None] * error * error) / CHANNELS
    grad_pred = (loss_weight[:, None, None] * 2.0 * error / CHANNELS).astype(jnp.bfloat16)
    grad_head = dot_low("gpc,gpd->cd", grad_pred, final_in)
    grad_final_in = dot_low("gpc,cd->gpd", grad_pred, head_w)
    grad_modul_f = jnp.concatenate(
        [jnp.sum(grad_final_in, 1), jnp.sum(grad_final_in * normed_f, 1)], -1
    ).astype(jnp.bfloat16)
    grad_hidden = local_back(norm_rows, hidden, grad_final_in * (1.0 + scale_f[:, None, :]))
    layer_grads = [None] * LAYERS
    grad_moduls = [None] * LAYERS
    for l in reversed(range(LAYERS)):
        grad_hidden, grad_moduls[l], layer_grads[l] = layer_backward(
            grad_hidden, weights_all[l], saved_all[l]
        )
    grad_embed = grad_hidden.astype(jnp.bfloat16)
    grad_patch = dot_low("gpc,gpd->cd", noisy_low, grad_embed)

    image_place = np.full((UNITS + 1,), -1, np.int32)
    image_place[image_units] = np.arange(len(image_units))
    my_place = jnp.asarray(image_place)[my_unit]
    room_slots, room_units = -(-slot_dev // 16) * 16, -(-len(image_units) // 16) * 16
    pick = jnp.pad(my_place, (0, room_slots - slot_dev), constant_values=-1)[:, None]
    pick = (pick == jnp.arange(room_units, dtype=jnp.int32)).astype(jnp.bfloat16)
    modul_grad = jnp.concatenate(grad_moduls + [grad_modul_f], -1).reshape(images, -1, BLOCK)
    modul_grad = jnp.pad(modul_grad, ((0, 0), (0, room_units - len(image_units)), (0, 0)))
    edge = jnp.concatenate([grad_patch, grad_head], 0)
    edge_room = max(all_images, 4 * CHANNELS)
    edge = jnp.concatenate([edge, jnp.broadcast_to(loss_part, (2 * CHANNELS, D))], 0)
    edge = jnp.pad(edge, ((0, edge_room - 4 * CHANNELS), (0, 0)))[:all_images]
    edge = jnp.pad(edge.reshape(all_images, blocks, BLOCK), ((0, 0), (8, 8 - blocks), (0, 0)))
    factor = local_back(jax.nn.silu, cond, jnp.ones_like(cond)).reshape(images, blocks, BLOCK)
    factor = jnp.pad(factor, ((0, 0), (0, 16 - blocks), (0, 0)), constant_values=1.0)
    unit_grads, slot_grad_out, shared = plan.scatter(
        layer_grads, modul_grad, pick, low_slots, edge, factor
    )
    shared = shared.reshape(all_images, 16, BLOCK)
    grad_cond = shared[:, :blocks].reshape(all_images, D)
    edge = shared[:, 8 : 8 + blocks].reshape(all_images, D)
    grad_patch, grad_head = edge[:CHANNELS], edge[CHANNELS : 2 * CHANNELS]
    loss_sum = edge[2 * CHANNELS, 0]
    grad_time_out = grad_cond.astype(jnp.bfloat16)
    grad_time_act = dot_low("ge,de->gd", grad_time_out, time_two)
    grad_time_pre = local_back(jax.nn.silu, time_pre, grad_time_act).astype(jnp.bfloat16)
    grad_time_w = dot_low("gf,gd->fd", freq_low, grad_time_pre)
    grad_table = jnp.zeros((CLASSES, D), jnp.float32).at[every_label].add(grad_cond)
    small_grad = jnp.concatenate([grad_patch, grad_time_w, grad_table, grad_head], 0)

    my_time = jnp.clip(my_unit - TAIL_FIRST, 0, TIME_UNITS - 1)
    is_time = (my_unit >= TAIL_FIRST) & (my_unit < TAIL_FIRST + TIME_UNITS)
    time_cols = jnp.take(grad_time_out.reshape(all_images, TIME_UNITS, BLOCK), my_time, axis=1)
    dense_place = np.full((UNITS + 1,), 0, np.int32)
    dense_place[dense_units] = np.arange(len(dense_units))
    slot_place = jnp.asarray(dense_place)[unit_of_slot]
    slot_rows = jnp.take(unit_grads, slot_place, axis=0, mode="clip")
    dense_grad, starts = plan.join_rows(
        lax.all_to_all(
            slot_rows.reshape(count, slot_dev, rows, BLOCK),
            AXES,
            split_axis=0,
            concat_axis=0,
            tiled=True,
        )
    )
    is_dense = (my_unit >= 0) & (my_place < 0) & ~is_time
    right = jnp.where(is_time[None, :, None], time_cols, slot_grad_out)
    left = jnp.where(is_time[:, None, None], time_act.T[None], cond_act.T[None])
    flags = [rate_factor * unit_scale(jnp.maximum(my_unit, 0)), my_unit >= 0, is_dense]
    flags = jnp.stack([flag.astype(jnp.float32) for flag in flags], 1)
    new_slots = adam_slots(
        dense_grad,
        starts,
        flags,
        left,
        jnp.swapaxes(right, 0, 1),
        *[jnp.swapaxes(values, 0, 1) for values in (master, first_moment, second_moment)],
    )
    new_master, new_first, new_second = [jnp.swapaxes(values, 0, 1) for values in new_slots]
    small_rate = rate_factor * table_scale(jnp.arange(small.shape[0], dtype=jnp.int32))[:, None]
    new_small, new_small_first, new_small_second = adam_update(
        small, small_first, small_second, small_grad, small_rate
    )
    return (
        loss_sum,
        weight_total,
        new_master,
        new_first,
        new_second,
        new_small,
        new_small_first,
        new_small_second,
    )


def solution(mesh):
    return jax.shard_map(
        on_device,
        mesh=mesh,
        in_specs=(
            P(("rep", "shard"), None),
            P(("rep", "shard"), None),
            P(("rep", "shard")),
            P(("rep", "shard")),
            P(),
            P(None, ("rep", "shard"), None),
            P(None, ("rep", "shard"), None),
            P(None, ("rep", "shard"), None),
            P(),
            P(),
            P(),
        ),
        out_specs=(
            P(),
            P(),
            P(None, ("rep", "shard"), None),
            P(None, ("rep", "shard"), None),
            P(None, ("rep", "shard"), None),
            P(),
            P(),
            P(),
        ),
        check_vma=False,
    )
```

```python
import jax
import jax.numpy as jnp
import numpy as np
from jax import lax
from jax.experimental import pallas as pl
from jax.experimental.pallas import tpu as pltpu
from jax.sharding import PartitionSpec as P

D = 768
HEADS = 12
HEAD_DIM = 64
FF = 3072
FREQ = 256
CLASSES = 1000
CHANNELS = 16
GRID = 16
PATCHES = 256
LAYERS = 2
TSTEPS = 1000
STEP = 10
BLOCK = 128
LAYER_COLS = 13824
LAYER_UNITS = 108
UNITS = 234

ADA_UNITS = 6 * D // BLOCK
DENSE_UNITS = LAYER_UNITS - ADA_UNITS
DENSE_COLS = DENSE_UNITS * BLOCK
TIME_UNITS = D // BLOCK
TAIL_FIRST = LAYERS * LAYER_UNITS
AXES = ("rep", "shard")


beta_one = 0.5
beta_two = 0.5
adam_eps = 1e-08
decay_rate = 0.1
rate_factor = 0.5


def gelu_tanh(values):
    return jax.nn.gelu(values, approximate=True)


def norm_rows(hidden):
    centered = hidden - jnp.mean(hidden, -1, keepdims=True)
    return centered * lax.rsqrt(jnp.mean(centered * centered, -1, keepdims=True) + 1e-06)


def local_back(function, primal, upstream):
    return jax.vjp(function, primal)[1](upstream)[0]


def dot_low(pattern, left_side, right_side):
    return jnp.einsum(pattern, left_side, right_side, preferred_element_type=jnp.float32)


def positions():
    quarter = D // 4
    angular = jnp.exp(-jnp.log(10000.0) * jnp.arange(quarter, dtype=jnp.float32) / quarter)
    patch_idx = jnp.arange(PATCHES, dtype=jnp.int32)
    row_pos = (patch_idx // GRID).astype(jnp.float32)[:, None] * angular
    col_pos = (patch_idx % GRID).astype(jnp.float32)[:, None] * angular
    return jnp.concatenate(
        [jnp.sin(col_pos), jnp.cos(col_pos), jnp.sin(row_pos), jnp.cos(row_pos)], -1
    )


def frequencies(times):
    half_size = FREQ // 2
    spacing = jnp.exp(-jnp.log(10000.0) * jnp.arange(half_size, dtype=jnp.float32) / half_size)
    angles = 1000.0 * times[:, None] * spacing
    return jnp.concatenate([jnp.cos(angles), jnp.sin(angles)], -1)


def unit_scale(unit_ids):
    column = unit_ids % LAYER_UNITS * BLOCK
    in_layer = unit_ids < LAYERS * LAYER_UNITS
    is_output = in_layer & (column >= 9 * D) & (column < 10 * D)
    is_down = in_layer & (column >= 10 * D + FF)
    factor = jnp.where(is_output, 4.0, jnp.where(is_down, 1.5 * (D / FF) ** 0.5, 1.0))
    return factor / D**0.5


def table_scale(row_ids):
    return jnp.where(
        row_ids < CHANNELS,
        CHANNELS ** (-0.5),
        jnp.where(
            row_ids < CHANNELS + FREQ,
            FREQ ** (-0.5),
            jnp.where(row_ids < CHANNELS + FREQ + CLASSES, 0.5, D ** (-0.5)),
        ),
    )


def adam_update(weight, first_mom, second, gradient, rate):
    first_new = beta_one * first_mom + (1.0 - beta_one) * gradient
    second_new = beta_two * second + (1.0 - beta_two) * gradient * gradient
    ratio = (
        first_new
        / (1.0 - beta_one**STEP)
        / (jnp.sqrt(second_new / (1.0 - beta_two**STEP)) + adam_eps)
    )
    return (weight - rate * (ratio + decay_rate * weight), first_new, second_new)


def modulate(normed, shift, scale):
    return normed * (1.0 + scale[:, None, :]) + shift[:, None, :]


def layer_forward(hidden, modul, weights):
    w_qkv, w_out, w_up, w_down = weights
    shift_a, scale_a, gate_a, shift_b, scale_b, gate_b = jnp.split(modul, 6, -1)
    attn_in = modulate(norm_rows(hidden), shift_a, scale_a).astype(jnp.bfloat16)
    qkv_all = dot_low("gpd,de->gpe", attn_in, w_qkv).astype(jnp.bfloat16)
    heads_out = attend(qkv_all)
    branch_a = dot_low("gpd,de->gpe", heads_out, w_out)
    middle = hidden + gate_a[:, None, :] * branch_a
    mlp_in = modulate(norm_rows(middle), shift_b, scale_b).astype(jnp.bfloat16)
    pre_act = dot_low("gpd,df->gpf", mlp_in, w_up)
    post_act = gelu_tanh(pre_act).astype(jnp.bfloat16)
    branch_b = dot_low("gpf,df->gpd", post_act, w_down)
    output = middle + gate_b[:, None, :] * branch_b
    return (
        output,
        (
            hidden,
            modul,
            attn_in,
            qkv_all,
            heads_out,
            branch_a,
            middle,
            mlp_in,
            pre_act.astype(jnp.bfloat16),
            post_act,
            branch_b,
        ),
    )


def layer_backward(grad_out, weights, saved):
    w_qkv, w_out, w_up, w_down = weights
    (
        hidden,
        modul,
        attn_in,
        qkv_all,
        heads_out,
        branch_a,
        middle,
        mlp_in,
        pre_act,
        post_act,
        branch_b,
    ) = saved
    shift_a, scale_a, gate_a, shift_b, scale_b, gate_b = jnp.split(modul, 6, -1)
    grad_gate_b = jnp.sum(grad_out * branch_b, 1)
    grad_branch_b = (gate_b[:, None, :] * grad_out).astype(jnp.bfloat16)
    grad_down = (grad_branch_b, post_act)
    grad_post = dot_low("gpd,df->gpf", grad_branch_b, w_down)
    grad_pre = local_back(gelu_tanh, pre_act.astype(jnp.float32), grad_post).astype(jnp.bfloat16)
    grad_up = (mlp_in, grad_pre)
    grad_mlp_in = dot_low("gpf,df->gpd", grad_pre, w_up)
    normed_b = norm_rows(middle)
    grad_scale_b = jnp.sum(grad_mlp_in * normed_b, 1)
    grad_shift_b = jnp.sum(grad_mlp_in, 1)
    grad_middle = grad_out + local_back(
        norm_rows, middle, grad_mlp_in * (1.0 + scale_b[:, None, :])
    )
    grad_gate_a = jnp.sum(grad_middle * branch_a, 1)
    grad_branch_a = (gate_a[:, None, :] * grad_middle).astype(jnp.bfloat16)
    grad_out_w = (heads_out, grad_branch_a)
    grad_heads = dot_low("gpe,de->gpd", grad_branch_a, w_out).astype(jnp.bfloat16)
    grad_qkv = attend_back(qkv_all, grad_heads)
    grad_qkv_w = (attn_in, grad_qkv)
    grad_attn_in = dot_low("gpe,de->gpd", grad_qkv, w_qkv)
    normed_a = norm_rows(hidden)
    grad_scale_a = jnp.sum(grad_attn_in * normed_a, 1)
    grad_shift_a = jnp.sum(grad_attn_in, 1)
    grad_in = grad_middle + local_back(
        norm_rows, hidden, grad_attn_in * (1.0 + scale_a[:, None, :])
    )
    grad_modul = jnp.concatenate(
        [grad_shift_a, grad_scale_a, grad_gate_a, grad_shift_b, grad_scale_b, grad_gate_b], -1
    ).astype(jnp.bfloat16)
    return (grad_in, grad_modul, [grad_qkv_w, grad_out_w, grad_up, grad_down])


MESH = pl.DeviceIdType.MESH
GATHER_VMEM = 60 * 2**20
SCATTER_VMEM = 56 * 2**20


def dot_rows(left_side, right_side):
    return lax.dot_general(
        left_side, right_side, (((0,), (0,)), ((), ())), preferred_element_type=jnp.float32
    )


def row_product(left_side, right_side):
    left_side = left_side.reshape(-1, left_side.shape[-1])
    right_side = right_side.reshape(-1, right_side.shape[-1])
    return dot_rows(left_side, right_side).astype(jnp.bfloat16)


def unit_groups():
    groups, place = [], 0
    for number in (3 * D, D, FF, FF) * LAYERS + (D,):
        groups.append((place, number // BLOCK))
        place += number // BLOCK
    return groups


PAIR = 2 * HEAD_DIM
SPAN = 6


def head_mask(number):
    lane = lax.broadcasted_iota(jnp.int32, (PATCHES, PAIR), 1)
    return (lane >= number * HEAD_DIM) & (lane < (number + 1) * HEAD_DIM)


def dot_lanes(left_side, right_side):
    return lax.dot_general(
        left_side, right_side, (((1,), (1,)), ((), ())), preferred_element_type=jnp.float32
    )


def attend_kernel(queries, keys_all, values, out):
    row = lax.broadcasted_iota(jnp.int32, (PAIR, PATCHES), 0)
    for pair in range(SPAN):
        lanes = slice(pair * PAIR, (pair + 1) * PAIR)
        scaled = queries[0, :, lanes] * HEAD_DIM ** (-0.5)
        keys, vals = keys_all[0, :, lanes], values[0, :, lanes]
        result = jnp.zeros((PAIR, PATCHES), jnp.float32)
        for number in (0, 1):
            one = jnp.where(head_mask(number), scaled, jnp.zeros((), jnp.bfloat16))
            scores = dot_lanes(keys, one)
            powers = jnp.exp(scores - jnp.max(scores, 0, keepdims=True))
            prob = (powers * (1.0 / jnp.sum(powers, 0, keepdims=True))).astype(jnp.bfloat16)
            result = jnp.where(row // HEAD_DIM == number, dot_rows(vals, prob), result)
        out[0, :, lanes] = result.T.astype(jnp.bfloat16)


def attend_back_kernel(queries, keys_all, values, grads, out):
    step = pl.program_id(1)
    row = lax.broadcasted_iota(jnp.int32, (PAIR, PATCHES), 0)
    none = jnp.zeros((), jnp.bfloat16)
    for pair in range(SPAN):
        lanes = slice(pair * PAIR, (pair + 1) * PAIR)
        scaled = queries[0, :, lanes] * HEAD_DIM ** (-0.5)
        keys, vals, grad = (ref[0, :, lanes] for ref in (keys_all, values, grads))
        grad_queries = jnp.zeros((PAIR, PATCHES), jnp.float32)
        grad_keys = jnp.zeros((PATCHES, PAIR), jnp.float32)
        grad_values = grad_keys
        for number in (0, 1):
            mask = head_mask(number)
            scores = dot_lanes(keys, jnp.where(mask, scaled, none))
            powers = jnp.exp(scores - jnp.max(scores, 0, keepdims=True))
            prob = powers * (1.0 / jnp.sum(powers, 0, keepdims=True))
            grad_prob = dot_lanes(vals, jnp.where(mask, grad, none))
            inner = jnp.sum(prob * grad_prob, 0, keepdims=True)
            grad_scores = (prob * (grad_prob - inner)).astype(jnp.bfloat16)
            part = dot_rows(keys, grad_scores)
            grad_queries = jnp.where(row // HEAD_DIM == number, part, grad_queries)
            part = jnp.dot(grad_scores, scaled, preferred_element_type=jnp.float32)
            grad_keys = jnp.where(mask, part, grad_keys)
            part = jnp.dot(prob.astype(jnp.bfloat16), grad, preferred_element_type=jnp.float32)
            grad_values = jnp.where(mask, part, grad_values)
        grad_queries = grad_queries.T * HEAD_DIM ** (-0.5)
        for third, result in enumerate((grad_queries, grad_keys, grad_values)):
            first = pl.multiple_of(third * D + (step * SPAN + pair) * PAIR, PAIR)
            out[0, :, pl.ds(first, PAIR)] = result.astype(jnp.bfloat16)


def pair_block(third):
    steps = HEADS // 2 // SPAN
    return pl.BlockSpec(
        (1, PATCHES, SPAN * PAIR), lambda image, step: (image, 0, third * steps + step)
    )


def attend(qkv_all):
    images = qkv_all.shape[0]
    steps = HEADS // 2 // SPAN
    return pl.pallas_call(
        attend_kernel,
        grid=(images, steps),
        out_shape=jax.ShapeDtypeStruct((images, PATCHES, D), jnp.bfloat16),
        in_specs=[pair_block(0), pair_block(1), pair_block(2)],
        out_specs=pair_block(0),
        cost_estimate=pl.CostEstimate(
            flops=4 * images * PATCHES * PATCHES * D,
            bytes_accessed=8 * images * PATCHES * D,
            transcendentals=images * HEADS * PATCHES * PATCHES,
        ),
    )(qkv_all, qkv_all, qkv_all)


def attend_back(qkv_all, grad_heads):
    images = qkv_all.shape[0]
    steps = HEADS // 2 // SPAN
    return pl.pallas_call(
        attend_back_kernel,
        grid=(images, steps),
        out_shape=jax.ShapeDtypeStruct((images, PATCHES, 3 * D), jnp.bfloat16),
        in_specs=[pair_block(0), pair_block(1), pair_block(2), pair_block(0)],
        out_specs=pl.BlockSpec((1, PATCHES, 3 * D), lambda image, step: (image, 0, 0)),
        cost_estimate=pl.CostEstimate(
            flops=10 * images * PATCHES * PATCHES * D,
            bytes_accessed=14 * images * PATCHES * D,
            transcendentals=images * HEADS * PATCHES * PATCHES,
        ),
    )(qkv_all, qkv_all, qkv_all, grad_heads)


def adam_kernel(starts, flags, picks, dense, extra, left, right, master, first, second, *refs):
    new_master, new_first, new_second, image_grad = refs
    group = pl.program_id(0)
    size, rows = master.shape[0], dense.shape[2]

    @pl.loop(0, size)
    def _(s):
        slot = group * size + s
        rate, used = flags[slot, 0], flags[slot, 1]
        from_dense, from_extra, from_images = (flags[slot, n] for n in (2, 3, 4))
        image_grad[...] = jnp.dot(left[s], right[s], preferred_element_type=jnp.float32)
        for n, start in enumerate(starts):
            at = (s, slice(start, start + rows))
            grad = jnp.where(from_images > 0.0, image_grad[at[1]], 0.0)
            part = dense[n, picks[slot, 0]].astype(jnp.float32)
            grad = jnp.where(from_dense > 0.0, part, grad)
            part = extra[n, picks[slot, 1]].astype(jnp.float32)
            grad = jnp.where(from_extra > 0.0, part, grad)
            old = (master[at], first[at], second[at])
            first_new = beta_one * old[1] + (1.0 - beta_one) * grad
            second_new = beta_two * old[2] + (1.0 - beta_two) * grad * grad
            root = jnp.sqrt(second_new * (1.0 / (1.0 - beta_two**STEP))) + adam_eps
            turned = pl.reciprocal(root, approx=True)
            turned = turned * (2.0 - root * turned)
            turned = turned * (2.0 - root * turned)
            ratio = first_new * (1.0 / (1.0 - beta_one**STEP)) * turned
            new = (old[0] - rate * (ratio + decay_rate * old[0]), first_new, second_new)
            for ref, value, kept in zip((new_master, new_first, new_second), new, old):
                ref[at] = jnp.where(used > 0.0, value, kept)


def adam_slots(dense, extra, starts, flags, picks, left, right, *state):
    slots = state[0].shape[0]
    size = next(size for size in (3, 2, 1) if slots % size == 0)
    block = pl.BlockSpec((size, D, BLOCK), lambda group: (group, 0, 0))
    side = left.shape[2]
    return pl.pallas_call(
        lambda *refs: adam_kernel(starts, *refs),
        grid=(slots // size,),
        out_shape=[jax.ShapeDtypeStruct((slots, D, BLOCK), jnp.float32)] * 3,
        in_specs=[
            pl.BlockSpec(memory_space=pltpu.SMEM),
            pl.BlockSpec(memory_space=pltpu.SMEM),
            pl.BlockSpec(memory_space=pltpu.VMEM),
            pl.BlockSpec(memory_space=pltpu.VMEM),
            pl.BlockSpec((size, D, side), lambda group: (group, 0, 0)),
            pl.BlockSpec((size, side, BLOCK), lambda group: (group, 0, 0)),
        ]
        + [block] * 3,
        out_specs=[block] * 3,
        scratch_shapes=[pltpu.VMEM((D, BLOCK), jnp.float32)],
        compiler_params=pltpu.CompilerParams(vmem_limit_bytes=40 * 2**20),
        cost_estimate=pl.CostEstimate(
            flops=40 * slots * D * BLOCK, bytes_accessed=26 * slots * D * BLOCK, transcendentals=0
        ),
    )(flags, picks, dense, extra, left, right, *state)


def place_of():
    rep = lax.axis_index("rep")
    return rep // 4, (rep // 2) % 2, rep % 2, lax.axis_index("shard")


def rep_of(y, x, c):
    return (y * 2 + x) * 2 + c


def device_at(j):
    shards = lax.axis_size("shard")
    devices = lax.axis_size("rep") * shards
    me = lax.axis_index("rep") * shards + lax.axis_index("shard")
    peer = lax.rem(me + j, devices)
    return peer, (peer // shards, lax.rem(peer, shards))


def meet_all(devices):
    barrier = pltpu.get_barrier_semaphore()

    @pl.loop(1, devices)
    def _(j):
        pl.semaphore_signal(barrier, inc=1, device_id=device_at(j)[1], device_id_type=MESH)

    pl.semaphore_wait(barrier, devices - 1)


def neighbours():
    y, x, c, z = place_of()
    to_x = (rep_of(y, 1 - x, c), z)
    to_y = (rep_of(1 - y, x, c), z)
    to_core = (rep_of(y, x, 1 - c), z)
    to_z = [(rep_of(y, x, c), lax.rem(z + step, 4)) for step in (1, 2, 3)]
    return to_x, to_y, to_core, to_z


def round_copies(step, source, held, sem, arriving):
    y, x, c, z = place_of()
    to_x, to_y, to_core, to_z = neighbours()
    if step == 0:
        copies = []
        for number in (1, 2, 3):
            at_z = lax.rem(z + 4 - number, 4) if arriving else z
            copies.append((source, held.at[y, x, c, at_z], to_z[number - 1]))
    else:
        at_x = 1 - x if arriving and step == 1 else x
        at_y = 1 - y if arriving and step == 2 else y
        at_c = 1 - c if arriving and step == 3 else c
        block = (held.at[y, at_x, c], held.at[at_y, :, c], held.at[:, :, at_c])[step - 1]
        copies = [(block, block, (to_x, to_y, to_core)[step - 1])]
    return [
        pltpu.make_async_remote_copy(
            src_ref=start,
            dst_ref=dest,
            send_sem=sem.at[0, step, number],
            recv_sem=sem.at[1, step, number],
            device_id=target,
            device_id_type=MESH,
        )
        for number, (start, dest, target) in enumerate(copies)
    ]


def gather_kernel(widths, bases, *refs):
    count = len(widths)
    places, share, spread, extra, info, low_slots = refs[:6]
    outs = refs[6 : count + 6]
    every_info, cond_out, modul_out = refs[count + 6 : count + 9]
    pieces = refs[count + 9 : 2 * count + 9]
    time_two, parts, own_sem, send_sem, recv_sem, time_sem, modul_sem, info_sem = refs[
        2 * count + 9 :
    ]
    devices, images = modul_out.shape[:2]
    slots = low_slots.shape[0]
    y, x, c, z = place_of()
    to_x, to_y, to_core, to_z = neighbours()
    me = rep_of(y, x, c) * 4 + z
    meet_all(devices)

    def remote(k, number, source, dest, target):
        return pltpu.make_async_remote_copy(
            src_ref=source,
            dst_ref=dest,
            send_sem=send_sem.at[k, number],
            recv_sem=recv_sem.at[k, number],
            device_id=target,
            device_id_type=MESH,
        )

    def own_copy(k):
        return pltpu.make_async_copy(pieces[k], outs[k].at[c, y, x, z], own_sem.at[k])

    def line_copies(k, arriving):
        copies = []
        for step in (1, 2, 3):
            at_z = lax.rem(z + 4 - step, 4) if arriving else z
            copies.append(
                remote(k, step - 1, pieces[k], outs[k].at[c, y, x, at_z], to_z[step - 1])
            )
        return copies

    def first_copies(k, arriving):
        half = widths[k] // 2
        left, right = pl.ds(0, half), pl.ds(half, half)
        at_x = 1 - x if arriving else x
        at_y = 1 - y if arriving else y
        a_block = outs[k].at[c, y, at_x, :, :, left]
        b_block = outs[k].at[c, at_y, x, :, :, right]
        return [remote(k, 3, a_block, a_block, to_x), remote(k, 4, b_block, b_block, to_y)]

    def second_copies(k, arriving):
        half = widths[k] // 2
        left, right = pl.ds(0, half), pl.ds(half, half)
        at_x = 1 - x if arriving else x
        at_y = 1 - y if arriving else y
        a_block = outs[k].at[c, at_y, :, :, :, left]
        b_block = outs[k].at[c, :, at_x, :, :, right]
        return [remote(k, 5, a_block, a_block, to_y), remote(k, 6, b_block, b_block, to_x)]

    def core_copies(k, arriving):
        block = outs[k].at[1 - c if arriving else c]
        return [remote(k, 7, block, block, to_core)]

    def start(copies):
        for copy in copies:
            copy.start()

    def arrived(copies):
        for copy in copies:
            copy.wait_recv()

    def modul_copy(j, arriving):
        peer, where = device_at(devices - j if arriving else j)
        return pltpu.make_async_remote_copy(
            src_ref=parts.at[pl.ds(peer * images, images)],
            dst_ref=modul_out.at[peer if arriving else me],
            send_sem=modul_sem.at[0, j],
            recv_sem=modul_sem.at[1, j],
            device_id=where,
            device_id_type=MESH,
        )

    def info_copies(step, arriving):
        return round_copies(step, info, every_info, info_sem, arriving)

    def info_rows(first):
        rows = [every_info[:, :, :, :, :, first + j, :] for j in range(D // BLOCK)]
        return jnp.concatenate([row.reshape(devices * images, BLOCK) for row in rows], -1)

    def image_products():
        copy = pltpu.make_async_copy(outs[0], time_two, time_sem)
        copy.start()
        arrived(info_copies(3, True))
        for step in range(4):
            for sent in info_copies(step, False):
                sent.wait_send()
        copy.wait()
        weight = time_two[...].astype(jnp.float32).reshape(D, D).astype(jnp.bfloat16)
        cond = jnp.dot(
            info_rows(0).astype(jnp.bfloat16), weight, preferred_element_type=jnp.float32
        )
        cond = cond + info_rows(8)
        cond_out[...] = cond
        act = (cond * jax.nn.sigmoid(cond)).astype(jnp.bfloat16)
        for s in range(slots):
            parts[:, s, :] = jnp.dot(act, low_slots[s], preferred_element_type=jnp.float32)
        for i in range(images):
            modul_out[me, i] = parts[me * images + i]

        @pl.loop(1, devices)
        def _(j):
            modul_copy(j, False).start()

    start(info_copies(0, False))
    every_info[y, x, c, z] = info[...]
    def send_piece(k):
        for n in range(widths[k] // BLOCK):
            unit = bases[k] + n
            value = spread[places[0, unit]].astype(jnp.float32) * share[0, unit]
            value = value + extra[places[1, unit]].astype(jnp.float32) * share[1, unit]
            pieces[k][:, n * BLOCK : (n + 1) * BLOCK] = value.astype(jnp.bfloat16)
        start(line_copies(k, False))
        own_copy(k).start()

    send_piece(0)
    for t in range(count + 2):
        if t + 1 < count:
            send_piece(t + 1)
        if t < count:
            own_copy(t).wait()
            arrived(line_copies(t, True))
            start(first_copies(t, False))
        if 0 <= t - 1 < count:
            arrived(first_copies(t - 1, True))
            start(second_copies(t - 1, False))
        if 0 <= t - 2 < count:
            arrived(second_copies(t - 2, True))
            start(core_copies(t - 2, False))
        if t < 3:
            arrived(info_copies(t, True))
            start(info_copies(t + 1, False))
        if t == 3:
            arrived(core_copies(0, True))
            image_products()
    for k in range(1, count):
        arrived(core_copies(k, True))

    @pl.loop(1, devices)
    def _(j):
        modul_copy(j, True).wait_recv()
        modul_copy(j, False).wait_send()

    for k in range(count):
        for copies in (line_copies, first_copies, second_copies, core_copies):
            for copy in copies(k, False):
                copy.wait_send()


def scatter_kernel(widths, bases, slots, *refs):
    count = len(widths)
    lefts, rights = refs[:count], refs[count : 2 * count]
    modul, pick, low_slots, edge, factor = refs[2 * count : 2 * count + 5]
    units, chosen, shared = refs[2 * count + 5 : 2 * count + 8]
    scratch = refs[2 * count + 8 :]
    own, first_in, second_in, line_in = (scratch[i * count : (i + 1) * count] for i in range(4))
    (
        left_in, left_turned, right_in, away, every_modul, parts, landed,
        load_sem, send_sem, recv_sem, modul_sem, part_sem, sum_sem,
    ) = scratch[4 * count :]
    devices, images = 32, shared.shape[4]
    y, x, c, z = place_of()
    to_x, to_y, to_core, to_z = neighbours()
    me = rep_of(y, x, c) * 4 + z
    rows = D // 32
    half_rows = D // 2
    meet_all(devices)

    def exchange(source, dest, sem, j, arriving):
        peer, where = device_at(devices - j if arriving else j)
        return pltpu.make_async_remote_copy(
            src_ref=source(peer, me),
            dst_ref=dest(peer if arriving else me),
            send_sem=sem.at[0, j],
            recv_sem=sem.at[1, j],
            device_id=where,
            device_id_type=MESH,
        )

    def modul_copies(step, arriving):
        return round_copies(step, modul, every_modul, modul_sem, arriving)

    def sum_copies(step, arriving):
        return round_copies(step, shared.at[y, x, c, z], shared, sum_sem, arriving)

    def part_copy(j, arriving):
        return exchange(
            lambda peer, mine: parts.at[pl.ds(peer * images, images)],
            lambda owner: landed.at[owner],
            part_sem, j, arriving,
        )

    def all_start(copy):
        @pl.loop(1, devices)
        def _(j):
            copy(j, False).start()

    def all_arrived(copy):
        @pl.loop(1, devices)
        def _(j):
            copy(j, True).wait_recv()

    def all_sent(copy):
        @pl.loop(1, devices)
        def _(j):
            copy(j, False).wait_send()

    def image_parts():
        arrived(modul_copies(3, True))

        @pl.loop(0, devices // 4)
        def _(i):
            for n in range(4):
                for m in range(images):
                    block = every_modul[i // 4, (i // 2) % 2, i % 2, n, m]
                    chosen[(i * 4 + n) * images + m] = jnp.dot(
                        pick[...], block, preferred_element_type=jnp.float32
                    )

        total = jnp.zeros((devices * images, D), jnp.float32)
        for s in range(slots):
            total = total + lax.dot_general(
                chosen[:, s, :].astype(jnp.bfloat16),
                low_slots[s],
                (((1,), (1,)), ((), ())),
                preferred_element_type=jnp.float32,
            )
        parts[...] = edge[...]
        for j in range(D // BLOCK):
            parts[:, j, :] = total[:, j * BLOCK : (j + 1) * BLOCK]
        all_start(part_copy)
        for i in range(images):
            landed[me, i] = parts[me * images + i]

    def image_sums():
        all_arrived(part_copy)
        shared[y, x, c, z] = jnp.sum(landed[...], 0) * factor[...]
        start(sum_copies(0, False))

    def remote(k, number, source, dest, target):
        return pltpu.make_async_remote_copy(
            src_ref=source,
            dst_ref=dest,
            send_sem=send_sem.at[k, number],
            recv_sem=recv_sem.at[k, number],
            device_id=target,
            device_id_type=MESH,
        )

    def load_left(k):
        return pltpu.make_async_copy(lefts[k], left_in.at[k % 2], load_sem.at[0, k % 2])

    def load_right(k):
        place = right_in.at[k % 3, :, pl.ds(0, widths[k])]
        return pltpu.make_async_copy(rights[k], place, load_sem.at[1, k % 3])

    def core_copies(k):
        source = away.at[k % 3, :, :, :, :, pl.ds(0, widths[k])]
        return [remote(k, 0, source, own[k], to_core)]

    def first_copies(k):
        half = widths[k] // 2
        return [
            remote(k, 1, own[k].at[:, 1 - x, :, :, pl.ds(0, half)], first_in[k].at[0], to_x),
            remote(k, 2, own[k].at[1 - y, :, :, :, pl.ds(half, half)], first_in[k].at[1], to_y),
        ]

    def second_copies(k):
        half = widths[k] // 2
        return [
            remote(k, 3, own[k].at[1 - y, x, :, :, pl.ds(0, half)], second_in[k].at[0], to_y),
            remote(k, 4, own[k].at[y, 1 - x, :, :, pl.ds(half, half)], second_in[k].at[1], to_x),
        ]

    def line_copies(k):
        return [
            remote(
                k,
                4 + step,
                own[k].at[y, x, lax.rem(z + step, 4)],
                line_in[k].at[step - 1],
                to_z[step - 1],
            )
            for step in (1, 2, 3)
        ]

    def start(copies):
        for copy in copies:
            copy.start()

    def arrived(copies):
        for copy in copies:
            copy.wait_recv()

    def products(k, half, store):
        slot = k % 3
        tile = D

        @pl.loop(0, widths[k] // tile)
        def _(n):
            columns = pl.ds(pl.multiple_of(n * tile, tile), tile)
            left = left_turned[slot, pl.ds(pl.multiple_of(half * half_rows, half_rows), half_rows)]
            result = jnp.dot(left, right_in[slot, :, columns], preferred_element_type=jnp.float32)
            for i in range(16):
                at = (i // 8, (i // 4) % 2, i % 4, slice(None), columns)
                store(at, result[i * rows : (i + 1) * rows])

    def away_products(k):
        load_left(k).wait()
        load_right(k).wait()
        left_turned[k % 3] = left_in[k % 2].T
        if k + 2 < count:
            load_left(k + 2).start()
        if k >= 3:
            for copy in core_copies(k - 3):
                copy.wait_send()

        def store(at, value):
            away[(k % 3,) + at] = value.astype(jnp.bfloat16)

        products(k, 1 - c, store)
        start(core_copies(k))

    def own_products(k):
        def store(at, value):
            own[k][at] = (value + own[k][at].astype(jnp.float32)).astype(jnp.bfloat16)

        products(k, c, store)

    def first_sum(k):
        half = widths[k] // 2

        @pl.loop(0, 8)
        def _(i):
            two, at_z = i // 4, i % 4
            a_at = (two, x, at_z, slice(None), pl.ds(0, half))
            b_at = (y, two, at_z, slice(None), pl.ds(half, half))
            own[k][a_at] = own[k][a_at] + first_in[k][0, two, at_z]
            own[k][b_at] = own[k][b_at] + first_in[k][1, two, at_z]

    def second_sum(k):
        half = widths[k] // 2

        @pl.loop(0, 4)
        def _(at_z):
            a_at = (y, x, at_z, slice(None), pl.ds(0, half))
            b_at = (y, x, at_z, slice(None), pl.ds(half, half))
            own[k][a_at] = own[k][a_at] + second_in[k][0, at_z]
            own[k][b_at] = own[k][b_at] + second_in[k][1, at_z]

    start(modul_copies(0, False))
    every_modul[y, x, c, z] = modul[...]
    for k in range(min(3, count)):
        load_right(k).start()
        if k < 2:
            load_left(k).start()
    away_products(0)
    for t in range(count + 3):
        if t + 1 < count:
            away_products(t + 1)
        if t < count:
            arrived(core_copies(t))
            own_products(t)
            start(first_copies(t))
            if t + 3 < count:
                load_right(t + 3).start()
        if 0 <= t - 1 < count:
            arrived(first_copies(t - 1))
            first_sum(t - 1)
            start(second_copies(t - 1))
        if 0 <= t - 2 < count:
            arrived(second_copies(t - 2))
            second_sum(t - 2)
            start(line_copies(t - 2))
        if 0 <= t - 3 < count:
            k = t - 3
            arrived(line_copies(k))
            total = own[k][y, x, z].astype(jnp.float32)
            for step in (1, 2, 3):
                total = total + line_in[k][step - 1].astype(jnp.float32)
            for n in range(widths[k] // BLOCK):
                part = total[:, n * BLOCK : (n + 1) * BLOCK]
                units[bases[k] + n] = part.astype(jnp.bfloat16)
        if t < 3:
            arrived(modul_copies(t, True))
            start(modul_copies(t + 1, False))
        if t == 3:
            image_parts()
        if t == 6:
            image_sums()
        if 7 <= t < 10:
            arrived(sum_copies(t - 7, True))
            start(sum_copies(t - 6, False))
    arrived(sum_copies(3, True))
    all_sent(part_copy)
    for step in range(4):
        for copy in modul_copies(step, False) + sum_copies(step, False):
            copy.wait_send()
    for k in range(count):
        for copies in (core_copies, first_copies, second_copies, line_copies):
            if copies is core_copies and k + 3 < count:
                continue
            for copy in copies(k):
                copy.wait_send()


class RingPlan:
    def split_rows(self, values):
        slots = values.shape[0]
        split = values.reshape(slots, 2, 2, 2, 4, D // 32, BLOCK)
        return split.transpose(2, 3, 1, 4, 0, 5, 6).reshape(32, slots, D // 32, BLOCK)

    def join_rows(self, values):
        starts = []
        for device in range(32):
            y, x, c, z = device // 16, device // 8 % 2, device // 4 % 2, device % 4
            starts.append(((((c * 2 + y) * 2 + x) * 4) + z) * (D // 32))
        return values, starts

    def gather(self, places, share, spread, extra, info, low_slots):
        names = unit_groups()
        turn = [len(names) - 1] + sorted(range(len(names) - 1), key=lambda n: (n % 4 == 1, n))
        bases = tuple(names[n][0] for n in turn)
        widths = tuple(names[n][1] * BLOCK for n in turn)
        count, rows = len(turn), D // 32
        all_images = 32 * info.shape[0]
        slots = low_slots.shape[0]
        room = -(-slots // 8) * 8
        size = sum(4 * D * width for width in widths)
        whole_shape = [(2, 2, 2, 4, rows, width) for width in widths]
        *whole, every_info, cond, modul = pl.pallas_call(
            lambda *refs: gather_kernel(widths, bases, *refs),
            out_shape=[
                jax.ShapeDtypeStruct(shape, jnp.bfloat16) for shape in whole_shape
            ]
            + [
                jax.ShapeDtypeStruct((2, 2, 2, 4) + info.shape, jnp.float32),
                jax.ShapeDtypeStruct((all_images, D), jnp.float32),
                jax.ShapeDtypeStruct((32, all_images // 32, room, BLOCK), jnp.float32),
            ],
            in_specs=[pl.BlockSpec(memory_space=pltpu.SMEM)] * 2
            + [pl.BlockSpec(memory_space=pltpu.VMEM)] * 4,
            out_specs=[pl.BlockSpec(memory_space=pl.ANY)] * count
            + [pl.BlockSpec(memory_space=pltpu.VMEM)] * 3,
            scratch_shapes=[pltpu.VMEM((rows, width), jnp.bfloat16) for width in widths]
            + [
                pltpu.VMEM(whole_shape[0], jnp.bfloat16),
                pltpu.VMEM((all_images, room, BLOCK), jnp.float32),
                pltpu.SemaphoreType.DMA((count,)),
                pltpu.SemaphoreType.DMA((count, 8)),
                pltpu.SemaphoreType.DMA((count, 8)),
                pltpu.SemaphoreType.DMA,
                pltpu.SemaphoreType.DMA((2, 32)),
                pltpu.SemaphoreType.DMA((2, 4, 3)),
            ],
            compiler_params=pltpu.CompilerParams(
                collective_id=0, has_side_effects=True, vmem_limit_bytes=GATHER_VMEM
            ),
            cost_estimate=pl.CostEstimate(flops=0, bytes_accessed=size, transcendentals=0),
        )(places, share, spread, extra, info, low_slots)
        whole = [part.reshape(D, -1) for part in whole]
        modul = jnp.swapaxes(modul[:, :, :slots], 0, 1).reshape(-1, 32 * slots, BLOCK)
        ordered = [whole[turn.index(n)] for n in range(count)]
        every_info = every_info.reshape((all_images,) + info.shape[1:])
        return ordered[:-1], ordered[-1], every_info, cond, modul

    def scatter(self, layer_grads, modul, pick, low_slots, edge, factor):
        turn = [(l, n) for l in range(LAYERS) for n in (0, 2, 3)]
        turn = [(LAYERS - 1, 1)] + turn + [(l, 1) for l in range(LAYERS - 1)]
        grads = [layer_grads[l][n] for l, n in turn]
        names = unit_groups()
        bases = tuple(names[4 * l + n][0] for l, n in turn)
        lefts = [left.reshape(-1, D) for left, _ in grads]
        rights = [right.reshape(left.shape[0], -1) for (_, right), left in zip(grads, lefts)]
        widths = tuple(right.shape[1] for right in rights)
        count, rows, tokens = len(grads), D // 32, lefts[0].shape[0]
        widest = max(widths)
        images, slots = modul.shape[0], low_slots.shape[0]
        size = sum(4 * D * width for width in widths)
        scratch = [pltpu.VMEM((2, 2, 4, rows, width), jnp.bfloat16) for width in widths]
        scratch += [pltpu.VMEM((2, 2, 4, rows, width // 2), jnp.bfloat16) for width in widths]
        scratch += [pltpu.VMEM((2, 4, rows, width // 2), jnp.bfloat16) for width in widths]
        scratch += [pltpu.VMEM((3, rows, width), jnp.bfloat16) for width in widths]
        units, chosen, shared = pl.pallas_call(
            lambda *refs: scatter_kernel(widths, bases, slots, *refs),
            out_shape=[
                jax.ShapeDtypeStruct((sum(widths) // BLOCK, rows, BLOCK), jnp.bfloat16),
                jax.ShapeDtypeStruct((32 * images, pick.shape[0], BLOCK), jnp.float32),
                jax.ShapeDtypeStruct((2, 2, 2, 4) + factor.shape, jnp.float32),
            ],
            in_specs=[pl.BlockSpec(memory_space=pl.ANY)] * (2 * count)
            + [pl.BlockSpec(memory_space=pltpu.VMEM)] * 5,
            out_specs=[pl.BlockSpec(memory_space=pltpu.VMEM)] * 3,
            scratch_shapes=scratch
            + [
                pltpu.VMEM((2, tokens, D), jnp.bfloat16),
                pltpu.VMEM((3, D, tokens), jnp.bfloat16),
                pltpu.VMEM((3, tokens, widest), jnp.bfloat16),
                pltpu.VMEM((3, 2, 2, 4, rows, widest), jnp.bfloat16),
                pltpu.VMEM((2, 2, 2, 4) + modul.shape, jnp.bfloat16),
                pltpu.VMEM(edge.shape, jnp.float32),
                pltpu.VMEM((32,) + factor.shape, jnp.float32),
                pltpu.SemaphoreType.DMA((2, 3)),
                pltpu.SemaphoreType.DMA((count, 8)),
                pltpu.SemaphoreType.DMA((count, 8)),
                pltpu.SemaphoreType.DMA((2, 4, 3)),
                pltpu.SemaphoreType.DMA((2, 32)),
                pltpu.SemaphoreType.DMA((2, 4, 3)),
            ],
            compiler_params=pltpu.CompilerParams(
                collective_id=1, has_side_effects=True, vmem_limit_bytes=SCATTER_VMEM
            ),
            cost_estimate=pl.CostEstimate(flops=0, bytes_accessed=size, transcendentals=0),
        )(*lefts, *rights, modul, pick, low_slots, edge, factor)
        return units, chosen[:, :slots].astype(jnp.bfloat16), shared


class PlainPlan:
    def split_rows(self, values):
        slots, devices = values.shape[0], lax.axis_size("rep") * lax.axis_size("shard")
        return jnp.swapaxes(values.reshape(slots, devices, -1, BLOCK), 0, 1)

    def join_rows(self, values):
        return jnp.swapaxes(values, 0, 1).reshape(1, -1, D, BLOCK), [0]

    def gather(self, places, share, spread, extra, info, low_slots):
        units = jnp.take(spread, places[0], axis=0, mode="clip") * share[0, :, None, None]
        units = units + jnp.take(extra, places[1], axis=0, mode="clip") * share[1, :, None, None]
        units = units.astype(jnp.bfloat16)
        whole = []
        for first, number in unit_groups():
            piece = jnp.swapaxes(units[first : first + number], 0, 1)
            piece = piece.reshape(-1, number * BLOCK)
            whole.append(lax.all_gather(piece, AXES, axis=0, tiled=True))
        every_info = lax.all_gather(info, AXES, axis=0, tiled=True)
        blocks = D // BLOCK
        time_act = every_info[:, :blocks].reshape(-1, D).astype(jnp.bfloat16)
        cond = jnp.dot(time_act, whole[-1], preferred_element_type=jnp.float32)
        cond = cond + every_info[:, 8 : 8 + blocks].reshape(-1, D)
        modul = dot_low("gd,sdc->gsc", jax.nn.silu(cond).astype(jnp.bfloat16), low_slots)
        modul = lax.all_to_all(modul, AXES, split_axis=0, concat_axis=1, tiled=True)
        return whole[:-1], whole[-1], every_info, cond, modul

    def scatter(self, layer_grads, modul, pick, low_slots, edge, factor):
        units = []
        for pair in (pair for grads in layer_grads for pair in grads):
            own = lax.psum_scatter(row_product(*pair), AXES, scatter_dimension=0, tiled=True)
            units.append(jnp.swapaxes(own.reshape(own.shape[0], -1, BLOCK), 0, 1))
        slots = low_slots.shape[0]
        every = lax.all_gather(modul, AXES, axis=0, tiled=True)
        chosen = dot_low("su,guc->gsc", pick, every)[:, :slots].astype(jnp.bfloat16)
        part = dot_low("gsc,sdc->gd", chosen, low_slots).reshape(-1, D // BLOCK, BLOCK)
        parts = edge.at[:, : D // BLOCK].set(part)
        own = lax.psum_scatter(parts, AXES, scatter_dimension=0, tiled=True) * factor
        shared = lax.all_gather(own, AXES, axis=0, tiled=False)
        return jnp.concatenate(units, 0), chosen, shared


def unit_lists():
    dense = np.concatenate(
        [np.arange(l * LAYER_UNITS + ADA_UNITS, (l + 1) * LAYER_UNITS) for l in range(LAYERS)]
    )
    time_units = np.arange(TAIL_FIRST, TAIL_FIRST + TIME_UNITS)
    image_units = np.concatenate(
        [np.arange(l * LAYER_UNITS, l * LAYER_UNITS + ADA_UNITS) for l in range(LAYERS)]
        + [np.arange(TAIL_FIRST + TIME_UNITS, UNITS)]
    )
    return dense, time_units, image_units


def on_device(
    latents,
    noise,
    labels,
    t_index,
    owner,
    master,
    first_moment,
    second_moment,
    small,
    small_first,
    small_second,
):
    count = lax.axis_size("rep") * lax.axis_size("shard")
    me = lax.axis_index(AXES)
    slot_dev = master.shape[1]
    slot_total = count * slot_dev
    rows = D // count
    images = latents.shape[0]
    dense_units, time_units, image_units = unit_lists()

    unit_of_slot = (
        jnp.full((slot_total,), -1, jnp.int32).at[owner].set(jnp.arange(UNITS, dtype=jnp.int32))
    )
    my_unit = lax.dynamic_slice_in_dim(unit_of_slot, me * slot_dev, slot_dev)
    low_slots = jnp.swapaxes(master.astype(jnp.bfloat16), 0, 1)

    plan = RingPlan() if (lax.axis_size("rep"), lax.axis_size("shard")) == (8, 4) else PlainPlan()
    moved = np.concatenate([dense_units, time_units])
    is_moved = np.zeros((UNITS + 1,), np.int32)
    is_moved[moved] = 1
    needed = jnp.asarray(is_moved)[unit_of_slot].reshape(count, slot_dev)
    total_needed = jnp.sum(needed, 1, keepdims=True)
    before = jnp.cumsum(needed, 1)
    turn = jnp.arange(slot_dev, dtype=jnp.int32)[None]
    rank = jnp.where(needed > 0, before - 1, total_needed + turn - before)
    first_slots = max(1, 3 * slot_dev // 4)
    last_slots = slot_dev - first_slots
    overflow = jnp.max(total_needed) > first_slots
    by_rank = (rank[:, :, None] == turn[:, None]).astype(jnp.int32)
    my_rank = lax.dynamic_index_in_dim(rank, me, 0, False)
    my_order = jnp.sum(lax.dynamic_index_in_dim(by_rank, me, 0, False) * turn.T, 0)

    def exchange(blocks):
        return lax.all_to_all(blocks, AXES, split_axis=0, concat_axis=0, tiled=True)

    def exchange_last(blocks):
        return lax.cond(overflow, exchange, jnp.zeros_like, blocks)

    sorted_rows = plan.split_rows(jnp.take(low_slots, my_order, axis=0, mode="clip"))
    spread = exchange(sorted_rows[:, :first_slots]).reshape(-1, rows, BLOCK)
    extra = exchange_last(sorted_rows[:, first_slots:]).reshape(-1, rows, BLOCK)
    moved_rank = rank.reshape(-1)[owner[moved]]
    moved_device = owner[moved] // slot_dev
    in_first = moved_rank < first_slots
    places = jnp.stack(
        [
            moved_device * first_slots + jnp.minimum(moved_rank, first_slots - 1),
            moved_device * last_slots + jnp.maximum(moved_rank - first_slots, 0),
        ]
    )
    share = jnp.stack([in_first, ~in_first]).astype(jnp.float32)

    x_start = latents.astype(jnp.float32).reshape(-1, PATCHES, CHANNELS)
    noise_f = noise.astype(jnp.float32).reshape(-1, PATCHES, CHANNELS)
    times = (t_index.astype(jnp.float32) + 0.5) / TSTEPS
    noisy = (1.0 - times)[:, None, None] * x_start + times[:, None, None] * noise_f
    target = noise_f - x_start
    loss_weight = 1.0 + 3.0 * times
    small_low = small.astype(jnp.bfloat16)
    patch_w = small_low[:CHANNELS]
    time_w = small_low[CHANNELS : CHANNELS + FREQ]
    table = small[CHANNELS + FREQ : CHANNELS + FREQ + CLASSES]
    head_w = small_low[CHANNELS + FREQ + CLASSES :]
    noisy_low = noisy.astype(jnp.bfloat16)
    hidden = dot_low("gpc,cd->gpd", noisy_low, patch_w) + positions()

    blocks = D // BLOCK
    freq_own = frequencies(times).astype(jnp.bfloat16)
    time_own = jnp.dot(freq_own, time_w, preferred_element_type=jnp.float32)
    act_own = jax.nn.silu(time_own).astype(jnp.bfloat16).astype(jnp.float32)
    label_own = jnp.take(table, labels, axis=0)
    numbers = jnp.stack([t_index, labels], 1).astype(jnp.float32)
    info = jnp.concatenate(
        [
            act_own.reshape(images, blocks, BLOCK),
            jnp.pad(numbers, ((0, 0), (0, BLOCK - 2)))[:, None],
            jnp.zeros((images, 7 - blocks, BLOCK), jnp.float32),
            label_own.reshape(images, blocks, BLOCK),
            jnp.zeros((images, 8 - blocks, BLOCK), jnp.float32),
        ],
        1,
    )
    whole, time_two, every_info, cond_all, slot_modul = plan.gather(
        places, share, spread, extra, info, low_slots
    )
    all_images = cond_all.shape[0]
    every_time = (every_info[:, blocks, 0] + 0.5) / TSTEPS
    every_label = every_info[:, blocks, 1].astype(jnp.int32)
    weight_total = jnp.sum(1.0 + 3.0 * every_time) * PATCHES
    freq_low = frequencies(every_time).astype(jnp.bfloat16)
    time_pre = jnp.dot(freq_low, time_w, preferred_element_type=jnp.float32)
    time_act = every_info[:, :blocks].reshape(all_images, D).astype(jnp.bfloat16)
    weights_all = [tuple(whole[4 * l : 4 * l + 4]) for l in range(LAYERS)]
    cond = lax.dynamic_slice_in_dim(cond_all, me * images, images)
    cond_act = jax.nn.silu(cond_all).astype(jnp.bfloat16)
    modul_all = jnp.take(slot_modul, owner[image_units], axis=1, mode="clip").reshape(images, -1)

    saved_all = []
    for l in range(LAYERS):
        hidden, saved = layer_forward(
            hidden, modul_all[:, l * 6 * D : (l + 1) * 6 * D], weights_all[l]
        )
        saved_all.append(saved)
    shift_f, scale_f = jnp.split(modul_all[:, LAYERS * 6 * D :], 2, -1)
    normed_f = norm_rows(hidden)
    final_in = modulate(normed_f, shift_f, scale_f).astype(jnp.bfloat16)
    predict = dot_low("gpd,cd->gpc", final_in, head_w)
    error = predict - target
    loss_part = jnp.sum(loss_weight[:, None, None] * error * error) / CHANNELS
    grad_pred = (loss_weight[:, None, None] * 2.0 * error / CHANNELS).astype(jnp.bfloat16)
    grad_head = dot_low("gpc,gpd->cd", grad_pred, final_in)
    grad_final_in = dot_low("gpc,cd->gpd", grad_pred, head_w)
    grad_modul_f = jnp.concatenate(
        [jnp.sum(grad_final_in, 1), jnp.sum(grad_final_in * normed_f, 1)], -1
    ).astype(jnp.bfloat16)
    grad_hidden = local_back(norm_rows, hidden, grad_final_in * (1.0 + scale_f[:, None, :]))
    layer_grads = [None] * LAYERS
    grad_moduls = [None] * LAYERS
    for l in reversed(range(LAYERS)):
        grad_hidden, grad_moduls[l], layer_grads[l] = layer_backward(
            grad_hidden, weights_all[l], saved_all[l]
        )
    grad_embed = grad_hidden.astype(jnp.bfloat16)
    grad_patch = dot_low("gpc,gpd->cd", noisy_low, grad_embed)

    image_place = np.full((UNITS + 1,), -1, np.int32)
    image_place[image_units] = np.arange(len(image_units))
    my_place = jnp.asarray(image_place)[my_unit]
    room_slots, room_units = -(-slot_dev // 16) * 16, -(-len(image_units) // 16) * 16
    pick = jnp.pad(my_place, (0, room_slots - slot_dev), constant_values=-1)[:, None]
    pick = (pick == jnp.arange(room_units, dtype=jnp.int32)).astype(jnp.bfloat16)
    modul_grad = jnp.concatenate(grad_moduls + [grad_modul_f], -1).reshape(images, -1, BLOCK)
    modul_grad = jnp.pad(modul_grad, ((0, 0), (0, room_units - len(image_units)), (0, 0)))
    edge = jnp.concatenate([grad_patch, grad_head], 0)
    edge_room = max(all_images, 4 * CHANNELS)
    edge = jnp.concatenate([edge, jnp.broadcast_to(loss_part, (2 * CHANNELS, D))], 0)
    edge = jnp.pad(edge, ((0, edge_room - 4 * CHANNELS), (0, 0)))[:all_images]
    edge = jnp.pad(edge.reshape(all_images, blocks, BLOCK), ((0, 0), (8, 8 - blocks), (0, 0)))
    factor = local_back(jax.nn.silu, cond, jnp.ones_like(cond)).reshape(images, blocks, BLOCK)
    factor = jnp.pad(factor, ((0, 0), (0, 16 - blocks), (0, 0)), constant_values=1.0)
    unit_grads, slot_grad_out, shared = plan.scatter(
        layer_grads, modul_grad, pick, low_slots, edge, factor
    )
    shared = shared.reshape(all_images, 16, BLOCK)
    grad_cond = shared[:, :blocks].reshape(all_images, D)
    edge = shared[:, 8 : 8 + blocks].reshape(all_images, D)
    grad_patch, grad_head = edge[:CHANNELS], edge[CHANNELS : 2 * CHANNELS]
    loss_sum = edge[2 * CHANNELS, 0]
    grad_time_out = grad_cond.astype(jnp.bfloat16)
    grad_time_act = dot_low("ge,de->gd", grad_time_out, time_two)
    grad_time_pre = local_back(jax.nn.silu, time_pre, grad_time_act).astype(jnp.bfloat16)
    grad_time_w = dot_low("gf,gd->fd", freq_low, grad_time_pre)
    grad_table = jnp.zeros((CLASSES, D), jnp.float32).at[every_label].add(grad_cond)
    small_grad = jnp.concatenate([grad_patch, grad_time_w, grad_table, grad_head], 0)

    my_time = jnp.clip(my_unit - TAIL_FIRST, 0, TIME_UNITS - 1)
    is_time = (my_unit >= TAIL_FIRST) & (my_unit < TAIL_FIRST + TIME_UNITS)
    time_cols = jnp.take(grad_time_out.reshape(all_images, TIME_UNITS, BLOCK), my_time, axis=1)
    dense_place = np.full((UNITS + 1,), 0, np.int32)
    dense_place[dense_units] = np.arange(len(dense_units))
    slot_place = jnp.asarray(dense_place)[unit_of_slot]
    packed = jnp.sum(by_rank * slot_place.reshape(count, slot_dev, 1), 1)

    def rows_of(places_of):
        picked = jnp.take(unit_grads, places_of.reshape(-1), axis=0, mode="clip")
        return picked.reshape(count, -1, rows, BLOCK)

    dense_grad, starts = plan.join_rows(exchange(rows_of(packed[:, :first_slots])))
    extra_grad, starts = plan.join_rows(exchange_last(rows_of(packed[:, first_slots:])))
    is_dense = (my_unit >= 0) & (my_place < 0) & ~is_time
    right = jnp.where(is_time[None, :, None], time_cols, slot_grad_out)
    left = jnp.where(is_time[:, None, None], time_act.T[None], cond_act.T[None])
    in_first = my_rank < first_slots
    flags = [rate_factor * unit_scale(jnp.maximum(my_unit, 0)), my_unit >= 0]
    flags += [is_dense & in_first, is_dense & ~in_first, ~is_dense]
    picks = [jnp.minimum(my_rank, first_slots - 1), jnp.maximum(my_rank - first_slots, 0)]
    flags = jnp.stack([flag.astype(jnp.float32) for flag in flags], 1)
    new_slots = adam_slots(
        dense_grad,
        extra_grad,
        starts,
        flags,
        jnp.stack(picks, 1),
        left,
        jnp.swapaxes(right, 0, 1),
        *[jnp.swapaxes(values, 0, 1) for values in (master, first_moment, second_moment)],
    )
    new_master, new_first, new_second = [jnp.swapaxes(values, 0, 1) for values in new_slots]
    small_rate = rate_factor * table_scale(jnp.arange(small.shape[0], dtype=jnp.int32))[:, None]
    new_small, new_small_first, new_small_second = adam_update(
        small, small_first, small_second, small_grad, small_rate
    )
    return (
        loss_sum,
        weight_total,
        new_master,
        new_first,
        new_second,
        new_small,
        new_small_first,
        new_small_second,
    )


def solution(mesh):
    return jax.shard_map(
        on_device,
        mesh=mesh,
        in_specs=(
            P(("rep", "shard"), None),
            P(("rep", "shard"), None),
            P(("rep", "shard")),
            P(("rep", "shard")),
            P(),
            P(None, ("rep", "shard"), None),
            P(None, ("rep", "shard"), None),
            P(None, ("rep", "shard"), None),
            P(),
            P(),
            P(),
        ),
        out_specs=(
            P(),
            P(),
            P(None, ("rep", "shard"), None),
            P(None, ("rep", "shard"), None),
            P(None, ("rep", "shard"), None),
            P(),
            P(),
            P(),
        ),
        check_vma=False,
    )
```

```python
import jax
import jax.numpy as jnp
import numpy as np
from jax import lax
from jax.experimental import pallas as pl
from jax.experimental.pallas import tpu as pltpu
from jax.sharding import PartitionSpec as P

D = 768
HEADS = 12
HEAD_DIM = 64
FF = 3072
FREQ = 256
CLASSES = 1000
CHANNELS = 16
GRID = 16
PATCHES = 256
LAYERS = 2
TSTEPS = 1000
STEP = 10
BLOCK = 128
LAYER_COLS = 13824
LAYER_UNITS = 108
UNITS = 234

ADA_UNITS = 6 * D // BLOCK
DENSE_UNITS = LAYER_UNITS - ADA_UNITS
DENSE_COLS = DENSE_UNITS * BLOCK
TIME_UNITS = D // BLOCK
TAIL_FIRST = LAYERS * LAYER_UNITS
AXES = ("rep", "shard")


beta_one = 0.5
beta_two = 0.5
adam_eps = 1e-08
decay_rate = 0.1
rate_factor = 0.5


def gelu_tanh(values):
    return jax.nn.gelu(values, approximate=True)


def norm_rows(hidden):
    centered = hidden - jnp.mean(hidden, -1, keepdims=True)
    return centered * lax.rsqrt(jnp.mean(centered * centered, -1, keepdims=True) + 1e-06)


def local_back(function, primal, upstream):
    return jax.vjp(function, primal)[1](upstream)[0]


def dot_low(pattern, left_side, right_side):
    return jnp.einsum(pattern, left_side, right_side, preferred_element_type=jnp.float32)


def positions():
    quarter = D // 4
    angular = jnp.exp(-jnp.log(10000.0) * jnp.arange(quarter, dtype=jnp.float32) / quarter)
    patch_idx = jnp.arange(PATCHES, dtype=jnp.int32)
    row_pos = (patch_idx // GRID).astype(jnp.float32)[:, None] * angular
    col_pos = (patch_idx % GRID).astype(jnp.float32)[:, None] * angular
    return jnp.concatenate(
        [jnp.sin(col_pos), jnp.cos(col_pos), jnp.sin(row_pos), jnp.cos(row_pos)], -1
    )


def frequencies(times):
    half_size = FREQ // 2
    spacing = jnp.exp(-jnp.log(10000.0) * jnp.arange(half_size, dtype=jnp.float32) / half_size)
    angles = 1000.0 * times[:, None] * spacing
    return jnp.concatenate([jnp.cos(angles), jnp.sin(angles)], -1)


def unit_scale(unit_ids):
    column = unit_ids % LAYER_UNITS * BLOCK
    in_layer = unit_ids < LAYERS * LAYER_UNITS
    is_output = in_layer & (column >= 9 * D) & (column < 10 * D)
    is_down = in_layer & (column >= 10 * D + FF)
    factor = jnp.where(is_output, 4.0, jnp.where(is_down, 1.5 * (D / FF) ** 0.5, 1.0))
    return factor / D**0.5


def table_scale(row_ids):
    return jnp.where(
        row_ids < CHANNELS,
        CHANNELS ** (-0.5),
        jnp.where(
            row_ids < CHANNELS + FREQ,
            FREQ ** (-0.5),
            jnp.where(row_ids < CHANNELS + FREQ + CLASSES, 0.5, D ** (-0.5)),
        ),
    )


def adam_update(weight, first_mom, second, gradient, rate):
    first_new = beta_one * first_mom + (1.0 - beta_one) * gradient
    second_new = beta_two * second + (1.0 - beta_two) * gradient * gradient
    ratio = (
        first_new
        / (1.0 - beta_one**STEP)
        / (jnp.sqrt(second_new / (1.0 - beta_two**STEP)) + adam_eps)
    )
    return (weight - rate * (ratio + decay_rate * weight), first_new, second_new)


def modulate(normed, shift, scale):
    return normed * (1.0 + scale[:, None, :]) + shift[:, None, :]


def layer_forward(hidden, modul, weights):
    w_qkv, w_out, w_up, w_down = weights
    shift_a, scale_a, gate_a, shift_b, scale_b, gate_b = jnp.split(modul, 6, -1)
    attn_in = modulate(norm_rows(hidden), shift_a, scale_a).astype(jnp.bfloat16)
    qkv_all = dot_low("gpd,de->gpe", attn_in, w_qkv).astype(jnp.bfloat16)
    heads_out = attend(qkv_all)
    branch_a = dot_low("gpd,de->gpe", heads_out, w_out)
    middle = hidden + gate_a[:, None, :] * branch_a
    mlp_in = modulate(norm_rows(middle), shift_b, scale_b).astype(jnp.bfloat16)
    pre_act = dot_low("gpd,df->gpf", mlp_in, w_up)
    post_act = gelu_tanh(pre_act).astype(jnp.bfloat16)
    branch_b = dot_low("gpf,df->gpd", post_act, w_down)
    output = middle + gate_b[:, None, :] * branch_b
    return (
        output,
        (
            hidden,
            modul,
            attn_in,
            qkv_all,
            heads_out,
            branch_a,
            middle,
            mlp_in,
            pre_act.astype(jnp.bfloat16),
            post_act,
            branch_b,
        ),
    )


def layer_backward(grad_out, weights, saved):
    w_qkv, w_out, w_up, w_down = weights
    (
        hidden,
        modul,
        attn_in,
        qkv_all,
        heads_out,
        branch_a,
        middle,
        mlp_in,
        pre_act,
        post_act,
        branch_b,
    ) = saved
    shift_a, scale_a, gate_a, shift_b, scale_b, gate_b = jnp.split(modul, 6, -1)
    grad_gate_b = jnp.sum(grad_out * branch_b, 1)
    grad_branch_b = (gate_b[:, None, :] * grad_out).astype(jnp.bfloat16)
    grad_down = (grad_branch_b, post_act)
    grad_post = dot_low("gpd,df->gpf", grad_branch_b, w_down)
    grad_pre = local_back(gelu_tanh, pre_act.astype(jnp.float32), grad_post).astype(jnp.bfloat16)
    grad_up = (mlp_in, grad_pre)
    grad_mlp_in = dot_low("gpf,df->gpd", grad_pre, w_up)
    normed_b = norm_rows(middle)
    grad_scale_b = jnp.sum(grad_mlp_in * normed_b, 1)
    grad_shift_b = jnp.sum(grad_mlp_in, 1)
    grad_middle = grad_out + local_back(
        norm_rows, middle, grad_mlp_in * (1.0 + scale_b[:, None, :])
    )
    grad_gate_a = jnp.sum(grad_middle * branch_a, 1)
    grad_branch_a = (gate_a[:, None, :] * grad_middle).astype(jnp.bfloat16)
    grad_out_w = (heads_out, grad_branch_a)
    grad_heads = dot_low("gpe,de->gpd", grad_branch_a, w_out).astype(jnp.bfloat16)
    grad_qkv = attend_back(qkv_all, grad_heads)
    grad_qkv_w = (attn_in, grad_qkv)
    grad_attn_in = dot_low("gpe,de->gpd", grad_qkv, w_qkv)
    normed_a = norm_rows(hidden)
    grad_scale_a = jnp.sum(grad_attn_in * normed_a, 1)
    grad_shift_a = jnp.sum(grad_attn_in, 1)
    grad_in = grad_middle + local_back(
        norm_rows, hidden, grad_attn_in * (1.0 + scale_a[:, None, :])
    )
    grad_modul = jnp.concatenate(
        [grad_shift_a, grad_scale_a, grad_gate_a, grad_shift_b, grad_scale_b, grad_gate_b], -1
    ).astype(jnp.bfloat16)
    return (grad_in, grad_modul, [grad_qkv_w, grad_out_w, grad_up, grad_down])


MESH = pl.DeviceIdType.MESH
GATHER_VMEM = 60 * 2**20
SCATTER_VMEM = 56 * 2**20


def dot_rows(left_side, right_side):
    return lax.dot_general(
        left_side, right_side, (((0,), (0,)), ((), ())), preferred_element_type=jnp.float32
    )


def row_product(left_side, right_side):
    left_side = left_side.reshape(-1, left_side.shape[-1])
    right_side = right_side.reshape(-1, right_side.shape[-1])
    return dot_rows(left_side, right_side).astype(jnp.bfloat16)


def unit_groups():
    groups, place = [], 0
    for number in (3 * D, D, FF, FF) * LAYERS + (D,):
        groups.append((place, number // BLOCK))
        place += number // BLOCK
    return groups


PAIR = 2 * HEAD_DIM
SPAN = 6


def head_mask(number):
    lane = lax.broadcasted_iota(jnp.int32, (PATCHES, PAIR), 1)
    return (lane >= number * HEAD_DIM) & (lane < (number + 1) * HEAD_DIM)


def dot_lanes(left_side, right_side):
    return lax.dot_general(
        left_side, right_side, (((1,), (1,)), ((), ())), preferred_element_type=jnp.float32
    )


def attend_kernel(queries, keys_all, values, out):
    row = lax.broadcasted_iota(jnp.int32, (PAIR, PATCHES), 0)
    for pair in range(SPAN):
        lanes = slice(pair * PAIR, (pair + 1) * PAIR)
        scaled = queries[0, :, lanes] * HEAD_DIM ** (-0.5)
        keys, vals = keys_all[0, :, lanes], values[0, :, lanes]
        result = jnp.zeros((PAIR, PATCHES), jnp.float32)
        for number in (0, 1):
            one = jnp.where(head_mask(number), scaled, jnp.zeros((), jnp.bfloat16))
            scores = dot_lanes(keys, one)
            powers = jnp.exp(scores - jnp.max(scores, 0, keepdims=True))
            prob = (powers * (1.0 / jnp.sum(powers, 0, keepdims=True))).astype(jnp.bfloat16)
            result = jnp.where(row // HEAD_DIM == number, dot_rows(vals, prob), result)
        out[0, :, lanes] = result.T.astype(jnp.bfloat16)


def attend_back_kernel(queries, keys_all, values, grads, out):
    step = pl.program_id(1)
    row = lax.broadcasted_iota(jnp.int32, (PAIR, PATCHES), 0)
    none = jnp.zeros((), jnp.bfloat16)
    for pair in range(SPAN):
        lanes = slice(pair * PAIR, (pair + 1) * PAIR)
        scaled = queries[0, :, lanes] * HEAD_DIM ** (-0.5)
        keys, vals, grad = (ref[0, :, lanes] for ref in (keys_all, values, grads))
        grad_queries = jnp.zeros((PAIR, PATCHES), jnp.float32)
        grad_keys = jnp.zeros((PATCHES, PAIR), jnp.float32)
        grad_values = grad_keys
        for number in (0, 1):
            mask = head_mask(number)
            scores = dot_lanes(keys, jnp.where(mask, scaled, none))
            powers = jnp.exp(scores - jnp.max(scores, 0, keepdims=True))
            prob = powers * (1.0 / jnp.sum(powers, 0, keepdims=True))
            grad_prob = dot_lanes(vals, jnp.where(mask, grad, none))
            inner = jnp.sum(prob * grad_prob, 0, keepdims=True)
            grad_scores = (prob * (grad_prob - inner)).astype(jnp.bfloat16)
            part = dot_rows(keys, grad_scores)
            grad_queries = jnp.where(row // HEAD_DIM == number, part, grad_queries)
            part = jnp.dot(grad_scores, scaled, preferred_element_type=jnp.float32)
            grad_keys = jnp.where(mask, part, grad_keys)
            part = jnp.dot(prob.astype(jnp.bfloat16), grad, preferred_element_type=jnp.float32)
            grad_values = jnp.where(mask, part, grad_values)
        grad_queries = grad_queries.T * HEAD_DIM ** (-0.5)
        for third, result in enumerate((grad_queries, grad_keys, grad_values)):
            first = pl.multiple_of(third * D + (step * SPAN + pair) * PAIR, PAIR)
            out[0, :, pl.ds(first, PAIR)] = result.astype(jnp.bfloat16)


def pair_block(third):
    steps = HEADS // 2 // SPAN
    return pl.BlockSpec(
        (1, PATCHES, SPAN * PAIR), lambda image, step: (image, 0, third * steps + step)
    )


def attend(qkv_all):
    images = qkv_all.shape[0]
    steps = HEADS // 2 // SPAN
    return pl.pallas_call(
        attend_kernel,
        grid=(images, steps),
        out_shape=jax.ShapeDtypeStruct((images, PATCHES, D), jnp.bfloat16),
        in_specs=[pair_block(0), pair_block(1), pair_block(2)],
        out_specs=pair_block(0),
        cost_estimate=pl.CostEstimate(
            flops=4 * images * PATCHES * PATCHES * D,
            bytes_accessed=8 * images * PATCHES * D,
            transcendentals=images * HEADS * PATCHES * PATCHES,
        ),
    )(qkv_all, qkv_all, qkv_all)


def attend_back(qkv_all, grad_heads):
    images = qkv_all.shape[0]
    steps = HEADS // 2 // SPAN
    return pl.pallas_call(
        attend_back_kernel,
        grid=(images, steps),
        out_shape=jax.ShapeDtypeStruct((images, PATCHES, 3 * D), jnp.bfloat16),
        in_specs=[pair_block(0), pair_block(1), pair_block(2), pair_block(0)],
        out_specs=pl.BlockSpec((1, PATCHES, 3 * D), lambda image, step: (image, 0, 0)),
        cost_estimate=pl.CostEstimate(
            flops=10 * images * PATCHES * PATCHES * D,
            bytes_accessed=14 * images * PATCHES * D,
            transcendentals=images * HEADS * PATCHES * PATCHES,
        ),
    )(qkv_all, qkv_all, qkv_all, grad_heads)


def adam_kernel(starts, flags, picks, dense, extra, left, right, master, first, second, *refs):
    new_master, new_first, new_second, image_grad = refs
    group = pl.program_id(0)
    size, rows = master.shape[0], dense.shape[2]

    @pl.loop(0, size)
    def _(s):
        slot = group * size + s
        rate, used = flags[slot, 0], flags[slot, 1]
        from_dense, from_extra, from_images = (flags[slot, n] for n in (2, 3, 4))
        image_grad[...] = jnp.dot(left[s], right[s], preferred_element_type=jnp.float32)
        for n, start in enumerate(starts):
            at = (s, slice(start, start + rows))
            grad = jnp.where(from_images > 0.0, image_grad[at[1]], 0.0)
            part = dense[n, picks[slot, 0]].astype(jnp.float32)
            grad = jnp.where(from_dense > 0.0, part, grad)
            part = extra[n, picks[slot, 1]].astype(jnp.float32)
            grad = jnp.where(from_extra > 0.0, part, grad)
            old = (master[at], first[at], second[at])
            first_new = beta_one * old[1] + (1.0 - beta_one) * grad
            second_new = beta_two * old[2] + (1.0 - beta_two) * grad * grad
            root = jnp.sqrt(second_new * (1.0 / (1.0 - beta_two**STEP))) + adam_eps
            turned = pl.reciprocal(root, approx=True)
            turned = turned * (2.0 - root * turned)
            turned = turned * (2.0 - root * turned)
            ratio = first_new * (1.0 / (1.0 - beta_one**STEP)) * turned
            new = (old[0] - rate * (ratio + decay_rate * old[0]), first_new, second_new)
            for ref, value, kept in zip((new_master, new_first, new_second), new, old):
                ref[at] = jnp.where(used > 0.0, value, kept)


def adam_slots(dense, extra, starts, flags, picks, left, right, *state):
    slots = state[0].shape[0]
    size = next(size for size in (3, 2, 1) if slots % size == 0)
    block = pl.BlockSpec((size, D, BLOCK), lambda group: (group, 0, 0))
    side = left.shape[2]
    return pl.pallas_call(
        lambda *refs: adam_kernel(starts, *refs),
        grid=(slots // size,),
        out_shape=[jax.ShapeDtypeStruct((slots, D, BLOCK), jnp.float32)] * 3,
        in_specs=[
            pl.BlockSpec(memory_space=pltpu.SMEM),
            pl.BlockSpec(memory_space=pltpu.SMEM),
            pl.BlockSpec(memory_space=pltpu.VMEM),
            pl.BlockSpec(memory_space=pltpu.VMEM),
            pl.BlockSpec((size, D, side), lambda group: (group, 0, 0)),
            pl.BlockSpec((size, side, BLOCK), lambda group: (group, 0, 0)),
        ]
        + [block] * 3,
        out_specs=[block] * 3,
        scratch_shapes=[pltpu.VMEM((D, BLOCK), jnp.float32)],
        compiler_params=pltpu.CompilerParams(vmem_limit_bytes=40 * 2**20),
        cost_estimate=pl.CostEstimate(
            flops=40 * slots * D * BLOCK, bytes_accessed=26 * slots * D * BLOCK, transcendentals=0
        ),
    )(flags, picks, dense, extra, left, right, *state)


def place_of():
    rep = lax.axis_index("rep")
    return rep // 4, (rep // 2) % 2, rep % 2, lax.axis_index("shard")


def rep_of(y, x, c):
    return (y * 2 + x) * 2 + c


def device_at(j):
    shards = lax.axis_size("shard")
    devices = lax.axis_size("rep") * shards
    me = lax.axis_index("rep") * shards + lax.axis_index("shard")
    peer = lax.rem(me + j, devices)
    return peer, (peer // shards, lax.rem(peer, shards))


def meet_all(devices):
    barrier = pltpu.get_barrier_semaphore()

    @pl.loop(1, devices)
    def _(j):
        pl.semaphore_signal(barrier, inc=1, device_id=device_at(j)[1], device_id_type=MESH)

    pl.semaphore_wait(barrier, devices - 1)


def neighbours():
    y, x, c, z = place_of()
    to_x = (rep_of(y, 1 - x, c), z)
    to_y = (rep_of(1 - y, x, c), z)
    to_core = (rep_of(y, x, 1 - c), z)
    to_z = [(rep_of(y, x, c), lax.rem(z + step, 4)) for step in (1, 2, 3)]
    return to_x, to_y, to_core, to_z


def round_copies(step, source, held, sem, arriving):
    y, x, c, z = place_of()
    to_x, to_y, to_core, to_z = neighbours()
    if step == 0:
        copies = []
        for number in (1, 2, 3):
            at_z = lax.rem(z + 4 - number, 4) if arriving else z
            copies.append((source, held.at[y, x, c, at_z], to_z[number - 1]))
    else:
        at_x = 1 - x if arriving and step == 1 else x
        at_y = 1 - y if arriving and step == 2 else y
        at_c = 1 - c if arriving and step == 3 else c
        block = (held.at[y, at_x, c], held.at[at_y, :, c], held.at[:, :, at_c])[step - 1]
        copies = [(block, block, (to_x, to_y, to_core)[step - 1])]
    return [
        pltpu.make_async_remote_copy(
            src_ref=start,
            dst_ref=dest,
            send_sem=sem.at[0, step, number],
            recv_sem=sem.at[1, step, number],
            device_id=target,
            device_id_type=MESH,
        )
        for number, (start, dest, target) in enumerate(copies)
    ]


def gather_kernel(widths, bases, *refs):
    count = len(widths)
    places, share, spread, extra, info, low_slots = refs[:6]
    outs = refs[6 : count + 6]
    every_info, cond_out, modul_out = refs[count + 6 : count + 9]
    pieces = refs[count + 9 : 2 * count + 9]
    time_two, parts, own_sem, send_sem, recv_sem, time_sem, modul_sem, info_sem = refs[
        2 * count + 9 :
    ]
    devices, images = modul_out.shape[:2]
    slots = low_slots.shape[0]
    y, x, c, z = place_of()
    to_x, to_y, to_core, to_z = neighbours()
    me = rep_of(y, x, c) * 4 + z
    meet_all(devices)

    def remote(k, number, source, dest, target):
        return pltpu.make_async_remote_copy(
            src_ref=source,
            dst_ref=dest,
            send_sem=send_sem.at[k, number],
            recv_sem=recv_sem.at[k, number],
            device_id=target,
            device_id_type=MESH,
        )

    def own_copy(k):
        return pltpu.make_async_copy(pieces[k], outs[k].at[c, y, x, z], own_sem.at[k])

    def line_copies(k, arriving):
        copies = []
        for step in (1, 2, 3):
            at_z = lax.rem(z + 4 - step, 4) if arriving else z
            copies.append(
                remote(k, step - 1, pieces[k], outs[k].at[c, y, x, at_z], to_z[step - 1])
            )
        return copies

    def first_copies(k, arriving):
        half = widths[k] // 2
        left, right = pl.ds(0, half), pl.ds(half, half)
        at_x = 1 - x if arriving else x
        at_y = 1 - y if arriving else y
        a_block = outs[k].at[c, y, at_x, :, :, left]
        b_block = outs[k].at[c, at_y, x, :, :, right]
        return [remote(k, 3, a_block, a_block, to_x), remote(k, 4, b_block, b_block, to_y)]

    def second_copies(k, arriving):
        half = widths[k] // 2
        left, right = pl.ds(0, half), pl.ds(half, half)
        at_x = 1 - x if arriving else x
        at_y = 1 - y if arriving else y
        a_block = outs[k].at[c, at_y, :, :, :, left]
        b_block = outs[k].at[c, :, at_x, :, :, right]
        return [remote(k, 5, a_block, a_block, to_y), remote(k, 6, b_block, b_block, to_x)]

    def core_copies(k, arriving):
        block = outs[k].at[1 - c if arriving else c]
        return [remote(k, 7, block, block, to_core)]

    def start(copies):
        for copy in copies:
            copy.start()

    def arrived(copies):
        for copy in copies:
            copy.wait_recv()

    def modul_copy(j, arriving):
        peer, where = device_at(devices - j if arriving else j)
        return pltpu.make_async_remote_copy(
            src_ref=parts.at[pl.ds(peer * images, images)],
            dst_ref=modul_out.at[peer if arriving else me],
            send_sem=modul_sem.at[0, j],
            recv_sem=modul_sem.at[1, j],
            device_id=where,
            device_id_type=MESH,
        )

    def info_copies(step, arriving):
        return round_copies(step, info, every_info, info_sem, arriving)

    def info_rows(first):
        rows = [every_info[:, :, :, :, :, first + j, :] for j in range(D // BLOCK)]
        return jnp.concatenate([row.reshape(devices * images, BLOCK) for row in rows], -1)

    def image_products():
        copy = pltpu.make_async_copy(outs[0], time_two, time_sem)
        copy.start()
        arrived(info_copies(3, True))
        for step in range(4):
            for sent in info_copies(step, False):
                sent.wait_send()
        copy.wait()
        weight = time_two[...].astype(jnp.float32).reshape(D, D).astype(jnp.bfloat16)
        cond = jnp.dot(
            info_rows(0).astype(jnp.bfloat16), weight, preferred_element_type=jnp.float32
        )
        cond = cond + info_rows(8)
        cond_out[...] = cond
        act = (cond * jax.nn.sigmoid(cond)).astype(jnp.bfloat16)
        for s in range(slots):
            parts[:, s, :] = jnp.dot(act, low_slots[s], preferred_element_type=jnp.float32)
        for i in range(images):
            modul_out[me, i] = parts[me * images + i]

        @pl.loop(1, devices)
        def _(j):
            modul_copy(j, False).start()

    start(info_copies(0, False))
    every_info[y, x, c, z] = info[...]
    def send_piece(k):
        for n in range(widths[k] // BLOCK):
            unit = bases[k] + n
            value = spread[places[0, unit]].astype(jnp.float32) * share[0, unit]
            value = value + extra[places[1, unit]].astype(jnp.float32) * share[1, unit]
            pieces[k][:, n * BLOCK : (n + 1) * BLOCK] = value.astype(jnp.bfloat16)
        start(line_copies(k, False))
        own_copy(k).start()

    send_piece(0)
    for t in range(count + 2):
        if t + 1 < count:
            send_piece(t + 1)
        if t < count:
            own_copy(t).wait()
            arrived(line_copies(t, True))
            start(first_copies(t, False))
        if 0 <= t - 1 < count:
            arrived(first_copies(t - 1, True))
            start(second_copies(t - 1, False))
        if 0 <= t - 2 < count:
            arrived(second_copies(t - 2, True))
            start(core_copies(t - 2, False))
        if t < 3:
            arrived(info_copies(t, True))
            start(info_copies(t + 1, False))
        if t == 3:
            arrived(core_copies(0, True))
            image_products()
    for k in range(1, count):
        arrived(core_copies(k, True))

    @pl.loop(1, devices)
    def _(j):
        modul_copy(j, True).wait_recv()
        modul_copy(j, False).wait_send()

    for k in range(count):
        for copies in (line_copies, first_copies, second_copies, core_copies):
            for copy in copies(k, False):
                copy.wait_send()


def scatter_kernel(widths, bases, slots, *refs):
    count = len(widths)
    lefts, rights = refs[:count], refs[count : 2 * count]
    modul, pick, low_slots, edge, factor = refs[2 * count : 2 * count + 5]
    units, chosen, shared = refs[2 * count + 5 : 2 * count + 8]
    scratch = refs[2 * count + 8 :]
    own, first_in, second_in, line_in = (scratch[i * count : (i + 1) * count] for i in range(4))
    (
        left_in, left_turned, right_in, away, every_modul, parts, landed,
        load_sem, send_sem, recv_sem, modul_sem, part_sem, sum_sem,
    ) = scratch[4 * count :]
    devices, images = 32, shared.shape[4]
    y, x, c, z = place_of()
    to_x, to_y, to_core, to_z = neighbours()
    me = rep_of(y, x, c) * 4 + z
    rows = D // 32
    half_rows = D // 2
    meet_all(devices)

    def exchange(source, dest, sem, j, arriving):
        peer, where = device_at(devices - j if arriving else j)
        return pltpu.make_async_remote_copy(
            src_ref=source(peer, me),
            dst_ref=dest(peer if arriving else me),
            send_sem=sem.at[0, j],
            recv_sem=sem.at[1, j],
            device_id=where,
            device_id_type=MESH,
        )

    def modul_copies(step, arriving):
        return round_copies(step, modul, every_modul, modul_sem, arriving)

    def sum_copies(step, arriving):
        return round_copies(step, shared.at[y, x, c, z], shared, sum_sem, arriving)

    def part_copy(j, arriving):
        return exchange(
            lambda peer, mine: parts.at[pl.ds(peer * images, images)],
            lambda owner: landed.at[owner],
            part_sem, j, arriving,
        )

    def all_start(copy):
        @pl.loop(1, devices)
        def _(j):
            copy(j, False).start()

    def all_arrived(copy):
        @pl.loop(1, devices)
        def _(j):
            copy(j, True).wait_recv()

    def all_sent(copy):
        @pl.loop(1, devices)
        def _(j):
            copy(j, False).wait_send()

    def image_parts():
        arrived(modul_copies(3, True))

        @pl.loop(0, devices // 4)
        def _(i):
            for n in range(4):
                for m in range(images):
                    block = every_modul[i // 4, (i // 2) % 2, i % 2, n, m]
                    chosen[(i * 4 + n) * images + m] = jnp.dot(
                        pick[...], block, preferred_element_type=jnp.float32
                    )

        total = jnp.zeros((devices * images, D), jnp.float32)
        for s in range(slots):
            total = total + lax.dot_general(
                chosen[:, s, :].astype(jnp.bfloat16),
                low_slots[s],
                (((1,), (1,)), ((), ())),
                preferred_element_type=jnp.float32,
            )
        parts[...] = edge[...]
        for j in range(D // BLOCK):
            parts[:, j, :] = total[:, j * BLOCK : (j + 1) * BLOCK]
        all_start(part_copy)
        for i in range(images):
            landed[me, i] = parts[me * images + i]

    def image_sums():
        all_arrived(part_copy)
        shared[y, x, c, z] = jnp.sum(landed[...], 0) * factor[...]
        start(sum_copies(0, False))

    def remote(k, number, source, dest, target):
        return pltpu.make_async_remote_copy(
            src_ref=source,
            dst_ref=dest,
            send_sem=send_sem.at[k, number],
            recv_sem=recv_sem.at[k, number],
            device_id=target,
            device_id_type=MESH,
        )

    def load_left(k):
        return pltpu.make_async_copy(lefts[k], left_in.at[k % 2], load_sem.at[0, k % 2])

    def load_right(k):
        place = right_in.at[k % 3, :, pl.ds(0, widths[k])]
        return pltpu.make_async_copy(rights[k], place, load_sem.at[1, k % 3])

    def core_copies(k):
        source = away.at[k % 3, :, :, :, :, pl.ds(0, widths[k])]
        return [remote(k, 0, source, own[k], to_core)]

    def first_copies(k):
        half = widths[k] // 2
        return [
            remote(k, 1, own[k].at[:, 1 - x, :, :, pl.ds(0, half)], first_in[k].at[0], to_x),
            remote(k, 2, own[k].at[1 - y, :, :, :, pl.ds(half, half)], first_in[k].at[1], to_y),
        ]

    def second_copies(k):
        half = widths[k] // 2
        return [
            remote(k, 3, own[k].at[1 - y, x, :, :, pl.ds(0, half)], second_in[k].at[0], to_y),
            remote(k, 4, own[k].at[y, 1 - x, :, :, pl.ds(half, half)], second_in[k].at[1], to_x),
        ]

    def line_copies(k):
        return [
            remote(
                k,
                4 + step,
                own[k].at[y, x, lax.rem(z + step, 4)],
                line_in[k].at[step - 1],
                to_z[step - 1],
            )
            for step in (1, 2, 3)
        ]

    def start(copies):
        for copy in copies:
            copy.start()

    def arrived(copies):
        for copy in copies:
            copy.wait_recv()

    def products(k, half, store):
        slot = k % 3
        tile = D

        @pl.loop(0, widths[k] // tile)
        def _(n):
            columns = pl.ds(pl.multiple_of(n * tile, tile), tile)
            left = left_turned[slot, pl.ds(pl.multiple_of(half * half_rows, half_rows), half_rows)]
            result = jnp.dot(left, right_in[slot, :, columns], preferred_element_type=jnp.float32)
            for i in range(16):
                at = (i // 8, (i // 4) % 2, i % 4, slice(None), columns)
                store(at, result[i * rows : (i + 1) * rows])

    def away_products(k):
        load_left(k).wait()
        load_right(k).wait()
        left_turned[k % 3] = left_in[k % 2].T
        if k + 2 < count:
            load_left(k + 2).start()
        if k >= 3:
            for copy in core_copies(k - 3):
                copy.wait_send()

        def store(at, value):
            away[(k % 3,) + at] = value.astype(jnp.bfloat16)

        products(k, 1 - c, store)
        start(core_copies(k))

    def own_products(k):
        def store(at, value):
            own[k][at] = (value + own[k][at].astype(jnp.float32)).astype(jnp.bfloat16)

        products(k, c, store)

    def first_sum(k):
        half = widths[k] // 2

        @pl.loop(0, 8)
        def _(i):
            two, at_z = i // 4, i % 4
            a_at = (two, x, at_z, slice(None), pl.ds(0, half))
            b_at = (y, two, at_z, slice(None), pl.ds(half, half))
            own[k][a_at] = own[k][a_at] + first_in[k][0, two, at_z]
            own[k][b_at] = own[k][b_at] + first_in[k][1, two, at_z]

    def second_sum(k):
        half = widths[k] // 2

        @pl.loop(0, 4)
        def _(at_z):
            a_at = (y, x, at_z, slice(None), pl.ds(0, half))
            b_at = (y, x, at_z, slice(None), pl.ds(half, half))
            own[k][a_at] = own[k][a_at] + second_in[k][0, at_z]
            own[k][b_at] = own[k][b_at] + second_in[k][1, at_z]

    start(modul_copies(0, False))
    every_modul[y, x, c, z] = modul[...]
    for k in range(min(3, count)):
        load_right(k).start()
        if k < 2:
            load_left(k).start()
    away_products(0)
    for t in range(count + 3):
        if t + 1 < count:
            away_products(t + 1)
        if t < count:
            arrived(core_copies(t))
            own_products(t)
            start(first_copies(t))
            if t + 3 < count:
                load_right(t + 3).start()
        if 0 <= t - 1 < count:
            arrived(first_copies(t - 1))
            first_sum(t - 1)
            start(second_copies(t - 1))
        if 0 <= t - 2 < count:
            arrived(second_copies(t - 2))
            second_sum(t - 2)
            start(line_copies(t - 2))
        if 0 <= t - 3 < count:
            k = t - 3
            arrived(line_copies(k))
            total = own[k][y, x, z].astype(jnp.float32)
            for step in (1, 2, 3):
                total = total + line_in[k][step - 1].astype(jnp.float32)
            for n in range(widths[k] // BLOCK):
                part = total[:, n * BLOCK : (n + 1) * BLOCK]
                units[bases[k] + n] = part.astype(jnp.bfloat16)
        if t < 3:
            arrived(modul_copies(t, True))
            start(modul_copies(t + 1, False))
        if t == 3:
            image_parts()
        if t == 6:
            image_sums()
        if 7 <= t < 10:
            arrived(sum_copies(t - 7, True))
            start(sum_copies(t - 6, False))
    arrived(sum_copies(3, True))
    all_sent(part_copy)
    for step in range(4):
        for copy in modul_copies(step, False) + sum_copies(step, False):
            copy.wait_send()
    for k in range(count):
        for copies in (core_copies, first_copies, second_copies, line_copies):
            if copies is core_copies and k + 3 < count:
                continue
            for copy in copies(k):
                copy.wait_send()


class RingPlan:
    def split_rows(self, values):
        slots = values.shape[0]
        split = values.reshape(slots, 2, 2, 2, 4, D // 32, BLOCK)
        return split.transpose(2, 3, 1, 4, 0, 5, 6).reshape(32, slots, D // 32, BLOCK)

    def join_rows(self, values):
        starts = []
        for device in range(32):
            y, x, c, z = device // 16, device // 8 % 2, device // 4 % 2, device % 4
            starts.append(((((c * 2 + y) * 2 + x) * 4) + z) * (D // 32))
        return values, starts

    def gather(self, places, share, spread, extra, info, low_slots):
        names = unit_groups()
        turn = [len(names) - 1] + sorted(range(len(names) - 1), key=lambda n: (n % 4 == 1, n))
        bases = tuple(names[n][0] for n in turn)
        widths = tuple(names[n][1] * BLOCK for n in turn)
        count, rows = len(turn), D // 32
        all_images = 32 * info.shape[0]
        slots = low_slots.shape[0]
        room = -(-slots // 8) * 8
        size = sum(4 * D * width for width in widths)
        whole_shape = [(2, 2, 2, 4, rows, width) for width in widths]
        *whole, every_info, cond, modul = pl.pallas_call(
            lambda *refs: gather_kernel(widths, bases, *refs),
            out_shape=[
                jax.ShapeDtypeStruct(shape, jnp.bfloat16) for shape in whole_shape
            ]
            + [
                jax.ShapeDtypeStruct((2, 2, 2, 4) + info.shape, jnp.float32),
                jax.ShapeDtypeStruct((all_images, D), jnp.float32),
                jax.ShapeDtypeStruct((32, all_images // 32, room, BLOCK), jnp.float32),
            ],
            in_specs=[pl.BlockSpec(memory_space=pltpu.SMEM)] * 2
            + [pl.BlockSpec(memory_space=pltpu.VMEM)] * 4,
            out_specs=[pl.BlockSpec(memory_space=pl.ANY)] * count
            + [pl.BlockSpec(memory_space=pltpu.VMEM)] * 3,
            scratch_shapes=[pltpu.VMEM((rows, width), jnp.bfloat16) for width in widths]
            + [
                pltpu.VMEM(whole_shape[0], jnp.bfloat16),
                pltpu.VMEM((all_images, room, BLOCK), jnp.float32),
                pltpu.SemaphoreType.DMA((count,)),
                pltpu.SemaphoreType.DMA((count, 8)),
                pltpu.SemaphoreType.DMA((count, 8)),
                pltpu.SemaphoreType.DMA,
                pltpu.SemaphoreType.DMA((2, 32)),
                pltpu.SemaphoreType.DMA((2, 4, 3)),
            ],
            compiler_params=pltpu.CompilerParams(
                collective_id=0, has_side_effects=True, vmem_limit_bytes=GATHER_VMEM
            ),
            cost_estimate=pl.CostEstimate(flops=0, bytes_accessed=size, transcendentals=0),
        )(places, share, spread, extra, info, low_slots)
        whole = [part.reshape(D, -1) for part in whole]
        modul = jnp.swapaxes(modul[:, :, :slots], 0, 1).reshape(-1, 32 * slots, BLOCK)
        ordered = [whole[turn.index(n)] for n in range(count)]
        every_info = every_info.reshape((all_images,) + info.shape[1:])
        return ordered[:-1], ordered[-1], every_info, cond, modul

    def scatter(self, layer_grads, modul, pick, low_slots, edge, factor):
        turn = [(l, n) for l in range(LAYERS) for n in (0, 2, 3)]
        turn = [(LAYERS - 1, 1)] + turn + [(l, 1) for l in range(LAYERS - 1)]
        grads = [layer_grads[l][n] for l, n in turn]
        names = unit_groups()
        bases = tuple(names[4 * l + n][0] for l, n in turn)
        lefts = [left.reshape(-1, D) for left, _ in grads]
        rights = [right.reshape(left.shape[0], -1) for (_, right), left in zip(grads, lefts)]
        widths = tuple(right.shape[1] for right in rights)
        count, rows, tokens = len(grads), D // 32, lefts[0].shape[0]
        widest = max(widths)
        images, slots = modul.shape[0], low_slots.shape[0]
        size = sum(4 * D * width for width in widths)
        scratch = [pltpu.VMEM((2, 2, 4, rows, width), jnp.bfloat16) for width in widths]
        scratch += [pltpu.VMEM((2, 2, 4, rows, width // 2), jnp.bfloat16) for width in widths]
        scratch += [pltpu.VMEM((2, 4, rows, width // 2), jnp.bfloat16) for width in widths]
        scratch += [pltpu.VMEM((3, rows, width), jnp.bfloat16) for width in widths]
        units, chosen, shared = pl.pallas_call(
            lambda *refs: scatter_kernel(widths, bases, slots, *refs),
            out_shape=[
                jax.ShapeDtypeStruct((sum(widths) // BLOCK, rows, BLOCK), jnp.bfloat16),
                jax.ShapeDtypeStruct((32 * images, pick.shape[0], BLOCK), jnp.float32),
                jax.ShapeDtypeStruct((2, 2, 2, 4) + factor.shape, jnp.float32),
            ],
            in_specs=[pl.BlockSpec(memory_space=pl.ANY)] * (2 * count)
            + [pl.BlockSpec(memory_space=pltpu.VMEM)] * 5,
            out_specs=[pl.BlockSpec(memory_space=pltpu.VMEM)] * 3,
            scratch_shapes=scratch
            + [
                pltpu.VMEM((2, tokens, D), jnp.bfloat16),
                pltpu.VMEM((3, D, tokens), jnp.bfloat16),
                pltpu.VMEM((3, tokens, widest), jnp.bfloat16),
                pltpu.VMEM((3, 2, 2, 4, rows, widest), jnp.bfloat16),
                pltpu.VMEM((2, 2, 2, 4) + modul.shape, jnp.bfloat16),
                pltpu.VMEM(edge.shape, jnp.float32),
                pltpu.VMEM((32,) + factor.shape, jnp.float32),
                pltpu.SemaphoreType.DMA((2, 3)),
                pltpu.SemaphoreType.DMA((count, 8)),
                pltpu.SemaphoreType.DMA((count, 8)),
                pltpu.SemaphoreType.DMA((2, 4, 3)),
                pltpu.SemaphoreType.DMA((2, 32)),
                pltpu.SemaphoreType.DMA((2, 4, 3)),
            ],
            compiler_params=pltpu.CompilerParams(
                collective_id=1, has_side_effects=True, vmem_limit_bytes=SCATTER_VMEM
            ),
            cost_estimate=pl.CostEstimate(flops=0, bytes_accessed=size, transcendentals=0),
        )(*lefts, *rights, modul, pick, low_slots, edge, factor)
        return units, chosen[:, :slots].astype(jnp.bfloat16), shared


class PlainPlan:
    def split_rows(self, values):
        slots, devices = values.shape[0], lax.axis_size("rep") * lax.axis_size("shard")
        return jnp.swapaxes(values.reshape(slots, devices, -1, BLOCK), 0, 1)

    def join_rows(self, values):
        return jnp.swapaxes(values, 0, 1).reshape(1, -1, D, BLOCK), [0]

    def gather(self, places, share, spread, extra, info, low_slots):
        units = jnp.take(spread, places[0], axis=0, mode="clip") * share[0, :, None, None]
        units = units + jnp.take(extra, places[1], axis=0, mode="clip") * share[1, :, None, None]
        units = units.astype(jnp.bfloat16)
        whole = []
        for first, number in unit_groups():
            piece = jnp.swapaxes(units[first : first + number], 0, 1)
            piece = piece.reshape(-1, number * BLOCK)
            whole.append(lax.all_gather(piece, AXES, axis=0, tiled=True))
        every_info = lax.all_gather(info, AXES, axis=0, tiled=True)
        blocks = D // BLOCK
        time_act = every_info[:, :blocks].reshape(-1, D).astype(jnp.bfloat16)
        cond = jnp.dot(time_act, whole[-1], preferred_element_type=jnp.float32)
        cond = cond + every_info[:, 8 : 8 + blocks].reshape(-1, D)
        modul = dot_low("gd,sdc->gsc", jax.nn.silu(cond).astype(jnp.bfloat16), low_slots)
        modul = lax.all_to_all(modul, AXES, split_axis=0, concat_axis=1, tiled=True)
        return whole[:-1], whole[-1], every_info, cond, modul

    def scatter(self, layer_grads, modul, pick, low_slots, edge, factor):
        units = []
        for pair in (pair for grads in layer_grads for pair in grads):
            own = lax.psum_scatter(row_product(*pair), AXES, scatter_dimension=0, tiled=True)
            units.append(jnp.swapaxes(own.reshape(own.shape[0], -1, BLOCK), 0, 1))
        slots = low_slots.shape[0]
        every = lax.all_gather(modul, AXES, axis=0, tiled=True)
        chosen = dot_low("su,guc->gsc", pick, every)[:, :slots].astype(jnp.bfloat16)
        part = dot_low("gsc,sdc->gd", chosen, low_slots).reshape(-1, D // BLOCK, BLOCK)
        parts = edge.at[:, : D // BLOCK].set(part)
        own = lax.psum_scatter(parts, AXES, scatter_dimension=0, tiled=True) * factor
        shared = lax.all_gather(own, AXES, axis=0, tiled=False)
        return jnp.concatenate(units, 0), chosen, shared


def unit_lists():
    dense = np.concatenate(
        [np.arange(l * LAYER_UNITS + ADA_UNITS, (l + 1) * LAYER_UNITS) for l in range(LAYERS)]
    )
    time_units = np.arange(TAIL_FIRST, TAIL_FIRST + TIME_UNITS)
    image_units = np.concatenate(
        [np.arange(l * LAYER_UNITS, l * LAYER_UNITS + ADA_UNITS) for l in range(LAYERS)]
        + [np.arange(TAIL_FIRST + TIME_UNITS, UNITS)]
    )
    return dense, time_units, image_units


def on_device(
    latents,
    noise,
    labels,
    t_index,
    owner,
    master,
    first_moment,
    second_moment,
    small,
    small_first,
    small_second,
):
    count = lax.axis_size("rep") * lax.axis_size("shard")
    me = lax.axis_index(AXES)
    slot_dev = master.shape[1]
    slot_total = count * slot_dev
    rows = D // count
    images = latents.shape[0]
    dense_units, time_units, image_units = unit_lists()

    unit_of_slot = (
        jnp.full((slot_total,), -1, jnp.int32).at[owner].set(jnp.arange(UNITS, dtype=jnp.int32))
    )
    my_unit = lax.dynamic_slice_in_dim(unit_of_slot, me * slot_dev, slot_dev)
    low_slots = jnp.swapaxes(master.astype(jnp.bfloat16), 0, 1)

    plan = RingPlan() if (lax.axis_size("rep"), lax.axis_size("shard")) == (8, 4) else PlainPlan()
    moved = np.concatenate([dense_units, time_units])
    in_layers = (unit_of_slot >= 0) & (unit_of_slot < TAIL_FIRST)
    needed = in_layers & (unit_of_slot % LAYER_UNITS >= ADA_UNITS)
    slot_place = unit_of_slot // LAYER_UNITS * DENSE_UNITS + unit_of_slot % LAYER_UNITS
    slot_place = jnp.where(needed, slot_place - ADA_UNITS, 0)
    needed = needed | (unit_of_slot >= TAIL_FIRST) & (unit_of_slot < TAIL_FIRST + TIME_UNITS)
    needed = needed.astype(jnp.int32).reshape(count, slot_dev)
    total_needed = jnp.sum(needed, 1, keepdims=True)
    before = jnp.cumsum(needed, 1)
    turn = jnp.arange(slot_dev, dtype=jnp.int32)[None]
    rank = jnp.where(needed > 0, before - 1, total_needed + turn - before)
    first_slots = max(1, 2 * slot_dev // 3)
    last_slots = slot_dev - first_slots
    overflow = jnp.max(total_needed) > first_slots
    by_rank = (rank[:, :, None] == turn[:, None]).astype(jnp.int32)
    my_rank = lax.dynamic_index_in_dim(rank, me, 0, False)
    my_order = jnp.sum(lax.dynamic_index_in_dim(by_rank, me, 0, False) * turn.T, 0)

    def exchange(blocks):
        return lax.all_to_all(blocks, AXES, split_axis=0, concat_axis=0, tiled=True)

    def exchange_last(blocks):
        return lax.cond(overflow, exchange, jnp.zeros_like, blocks)

    sorted_rows = plan.split_rows(jnp.take(low_slots, my_order, axis=0, mode="clip"))
    spread = exchange(sorted_rows[:, :first_slots]).reshape(-1, rows, BLOCK)
    extra = exchange_last(sorted_rows[:, first_slots:]).reshape(-1, rows, BLOCK)
    moved_rank = rank.reshape(-1)[owner[moved]]
    moved_device = owner[moved] // slot_dev
    in_first = moved_rank < first_slots
    places = jnp.stack(
        [
            moved_device * first_slots + jnp.minimum(moved_rank, first_slots - 1),
            moved_device * last_slots + jnp.maximum(moved_rank - first_slots, 0),
        ]
    )
    share = jnp.stack([in_first, ~in_first]).astype(jnp.float32)

    x_start = latents.astype(jnp.float32).reshape(-1, PATCHES, CHANNELS)
    noise_f = noise.astype(jnp.float32).reshape(-1, PATCHES, CHANNELS)
    times = (t_index.astype(jnp.float32) + 0.5) / TSTEPS
    noisy = (1.0 - times)[:, None, None] * x_start + times[:, None, None] * noise_f
    target = noise_f - x_start
    loss_weight = 1.0 + 3.0 * times
    small_low = small.astype(jnp.bfloat16)
    patch_w = small_low[:CHANNELS]
    time_w = small_low[CHANNELS : CHANNELS + FREQ]
    table = small[CHANNELS + FREQ : CHANNELS + FREQ + CLASSES]
    head_w = small_low[CHANNELS + FREQ + CLASSES :]
    noisy_low = noisy.astype(jnp.bfloat16)
    hidden = dot_low("gpc,cd->gpd", noisy_low, patch_w) + positions()

    blocks = D // BLOCK
    freq_own = frequencies(times).astype(jnp.bfloat16)
    time_own = jnp.dot(freq_own, time_w, preferred_element_type=jnp.float32)
    act_own = jax.nn.silu(time_own).astype(jnp.bfloat16).astype(jnp.float32)
    label_own = jnp.take(table, labels, axis=0)
    numbers = jnp.stack([t_index, labels], 1).astype(jnp.float32)
    info = jnp.concatenate(
        [
            act_own.reshape(images, blocks, BLOCK),
            jnp.pad(numbers, ((0, 0), (0, BLOCK - 2)))[:, None],
            jnp.zeros((images, 7 - blocks, BLOCK), jnp.float32),
            label_own.reshape(images, blocks, BLOCK),
            jnp.zeros((images, 8 - blocks, BLOCK), jnp.float32),
        ],
        1,
    )
    whole, time_two, every_info, cond_all, slot_modul = plan.gather(
        places, share, spread, extra, info, low_slots
    )
    all_images = cond_all.shape[0]
    every_time = (every_info[:, blocks, 0] + 0.5) / TSTEPS
    every_label = every_info[:, blocks, 1].astype(jnp.int32)
    weight_total = jnp.sum(1.0 + 3.0 * every_time) * PATCHES
    freq_low = frequencies(every_time).astype(jnp.bfloat16)
    time_pre = jnp.dot(freq_low, time_w, preferred_element_type=jnp.float32)
    time_act = every_info[:, :blocks].reshape(all_images, D).astype(jnp.bfloat16)
    weights_all = [tuple(whole[4 * l : 4 * l + 4]) for l in range(LAYERS)]
    cond = lax.dynamic_slice_in_dim(cond_all, me * images, images)
    cond_act = jax.nn.silu(cond_all).astype(jnp.bfloat16)
    modul_all = jnp.take(slot_modul, owner[image_units], axis=1, mode="clip").reshape(images, -1)

    saved_all = []
    for l in range(LAYERS):
        hidden, saved = layer_forward(
            hidden, modul_all[:, l * 6 * D : (l + 1) * 6 * D], weights_all[l]
        )
        saved_all.append(saved)
    shift_f, scale_f = jnp.split(modul_all[:, LAYERS * 6 * D :], 2, -1)
    normed_f = norm_rows(hidden)
    final_in = modulate(normed_f, shift_f, scale_f).astype(jnp.bfloat16)
    predict = dot_low("gpd,cd->gpc", final_in, head_w)
    error = predict - target
    loss_part = jnp.sum(loss_weight[:, None, None] * error * error) / CHANNELS
    grad_pred = (loss_weight[:, None, None] * 2.0 * error / CHANNELS).astype(jnp.bfloat16)
    grad_head = dot_low("gpc,gpd->cd", grad_pred, final_in)
    grad_final_in = dot_low("gpc,cd->gpd", grad_pred, head_w)
    grad_modul_f = jnp.concatenate(
        [jnp.sum(grad_final_in, 1), jnp.sum(grad_final_in * normed_f, 1)], -1
    ).astype(jnp.bfloat16)
    grad_hidden = local_back(norm_rows, hidden, grad_final_in * (1.0 + scale_f[:, None, :]))
    layer_grads = [None] * LAYERS
    grad_moduls = [None] * LAYERS
    for l in reversed(range(LAYERS)):
        grad_hidden, grad_moduls[l], layer_grads[l] = layer_backward(
            grad_hidden, weights_all[l], saved_all[l]
        )
    grad_embed = grad_hidden.astype(jnp.bfloat16)
    grad_patch = dot_low("gpc,gpd->cd", noisy_low, grad_embed)

    image_place = np.full((UNITS + 1,), -1, np.int32)
    image_place[image_units] = np.arange(len(image_units))
    my_place = jnp.asarray(image_place)[my_unit]
    room_slots, room_units = -(-slot_dev // 16) * 16, -(-len(image_units) // 16) * 16
    pick = jnp.pad(my_place, (0, room_slots - slot_dev), constant_values=-1)[:, None]
    pick = (pick == jnp.arange(room_units, dtype=jnp.int32)).astype(jnp.bfloat16)
    modul_grad = jnp.concatenate(grad_moduls + [grad_modul_f], -1).reshape(images, -1, BLOCK)
    modul_grad = jnp.pad(modul_grad, ((0, 0), (0, room_units - len(image_units)), (0, 0)))
    edge = jnp.concatenate([grad_patch, grad_head], 0)
    edge_room = max(all_images, 4 * CHANNELS)
    edge = jnp.concatenate([edge, jnp.broadcast_to(loss_part, (2 * CHANNELS, D))], 0)
    edge = jnp.pad(edge, ((0, edge_room - 4 * CHANNELS), (0, 0)))[:all_images]
    edge = jnp.pad(edge.reshape(all_images, blocks, BLOCK), ((0, 0), (8, 8 - blocks), (0, 0)))
    factor = local_back(jax.nn.silu, cond, jnp.ones_like(cond)).reshape(images, blocks, BLOCK)
    factor = jnp.pad(factor, ((0, 0), (0, 16 - blocks), (0, 0)), constant_values=1.0)
    unit_grads, slot_grad_out, shared = plan.scatter(
        layer_grads, modul_grad, pick, low_slots, edge, factor
    )
    shared = shared.reshape(all_images, 16, BLOCK)
    grad_cond = shared[:, :blocks].reshape(all_images, D)
    edge = shared[:, 8 : 8 + blocks].reshape(all_images, D)
    grad_patch, grad_head = edge[:CHANNELS], edge[CHANNELS : 2 * CHANNELS]
    loss_sum = edge[2 * CHANNELS, 0]
    grad_time_out = grad_cond.astype(jnp.bfloat16)
    grad_time_act = dot_low("ge,de->gd", grad_time_out, time_two)
    grad_time_pre = local_back(jax.nn.silu, time_pre, grad_time_act).astype(jnp.bfloat16)
    grad_time_w = dot_low("gf,gd->fd", freq_low, grad_time_pre)
    grad_table = jnp.zeros((CLASSES, D), jnp.float32).at[every_label].add(grad_cond)
    small_grad = jnp.concatenate([grad_patch, grad_time_w, grad_table, grad_head], 0)

    my_time = jnp.clip(my_unit - TAIL_FIRST, 0, TIME_UNITS - 1)
    is_time = (my_unit >= TAIL_FIRST) & (my_unit < TAIL_FIRST + TIME_UNITS)
    time_cols = jnp.take(grad_time_out.reshape(all_images, TIME_UNITS, BLOCK), my_time, axis=1)
    packed = jnp.sum(by_rank * slot_place.reshape(count, slot_dev, 1), 1)

    def rows_of(places_of):
        picked = jnp.take(unit_grads, places_of.reshape(-1), axis=0, mode="clip")
        return picked.reshape(count, -1, rows, BLOCK)

    dense_grad, starts = plan.join_rows(exchange(rows_of(packed[:, :first_slots])))
    extra_grad, starts = plan.join_rows(exchange_last(rows_of(packed[:, first_slots:])))
    is_dense = (my_unit >= 0) & (my_place < 0) & ~is_time
    right = jnp.where(is_time[None, :, None], time_cols, slot_grad_out)
    left = jnp.where(is_time[:, None, None], time_act.T[None], cond_act.T[None])
    in_first = my_rank < first_slots
    flags = [rate_factor * unit_scale(jnp.maximum(my_unit, 0)), my_unit >= 0]
    flags += [is_dense & in_first, is_dense & ~in_first, ~is_dense]
    picks = [jnp.minimum(my_rank, first_slots - 1), jnp.maximum(my_rank - first_slots, 0)]
    flags = jnp.stack([flag.astype(jnp.float32) for flag in flags], 1)
    new_slots = adam_slots(
        dense_grad,
        extra_grad,
        starts,
        flags,
        jnp.stack(picks, 1),
        left,
        jnp.swapaxes(right, 0, 1),
        *[jnp.swapaxes(values, 0, 1) for values in (master, first_moment, second_moment)],
    )
    new_master, new_first, new_second = [jnp.swapaxes(values, 0, 1) for values in new_slots]
    small_rate = rate_factor * table_scale(jnp.arange(small.shape[0], dtype=jnp.int32))[:, None]
    new_small, new_small_first, new_small_second = adam_update(
        small, small_first, small_second, small_grad, small_rate
    )
    return (
        loss_sum,
        weight_total,
        new_master,
        new_first,
        new_second,
        new_small,
        new_small_first,
        new_small_second,
    )


def solution(mesh):
    return jax.shard_map(
        on_device,
        mesh=mesh,
        in_specs=(
            P(("rep", "shard"), None),
            P(("rep", "shard"), None),
            P(("rep", "shard")),
            P(("rep", "shard")),
            P(),
            P(None, ("rep", "shard"), None),
            P(None, ("rep", "shard"), None),
            P(None, ("rep", "shard"), None),
            P(),
            P(),
            P(),
        ),
        out_specs=(
            P(),
            P(),
            P(None, ("rep", "shard"), None),
            P(None, ("rep", "shard"), None),
            P(None, ("rep", "shard"), None),
            P(),
            P(),
            P(),
        ),
        check_vma=False,
    )
```

```python
import jax
import jax.numpy as jnp
import numpy as np
from jax import lax
from jax.experimental import pallas as pl
from jax.experimental.pallas import tpu as pltpu
from jax.sharding import PartitionSpec as P

D = 768
HEADS = 12
HEAD_DIM = 64
FF = 3072
FREQ = 256
CLASSES = 1000
CHANNELS = 16
GRID = 16
PATCHES = 256
LAYERS = 2
TSTEPS = 1000
STEP = 10
BLOCK = 128
LAYER_COLS = 13824
LAYER_UNITS = 108
UNITS = 234

ADA_UNITS = 6 * D // BLOCK
DENSE_UNITS = LAYER_UNITS - ADA_UNITS
DENSE_COLS = DENSE_UNITS * BLOCK
TIME_UNITS = D // BLOCK
TAIL_FIRST = LAYERS * LAYER_UNITS
AXES = ("rep", "shard")


beta_one = 0.5
beta_two = 0.5
adam_eps = 1e-08
decay_rate = 0.1
rate_factor = 0.5


def gelu_tanh(values):
    return jax.nn.gelu(values, approximate=True)


def norm_rows(hidden):
    centered = hidden - jnp.mean(hidden, -1, keepdims=True)
    return centered * lax.rsqrt(jnp.mean(centered * centered, -1, keepdims=True) + 1e-06)


def local_back(function, primal, upstream):
    return jax.vjp(function, primal)[1](upstream)[0]


def dot_low(pattern, left_side, right_side):
    return jnp.einsum(pattern, left_side, right_side, preferred_element_type=jnp.float32)


def positions():
    quarter = D // 4
    angular = jnp.exp(-jnp.log(10000.0) * jnp.arange(quarter, dtype=jnp.float32) / quarter)
    patch_idx = jnp.arange(PATCHES, dtype=jnp.int32)
    row_pos = (patch_idx // GRID).astype(jnp.float32)[:, None] * angular
    col_pos = (patch_idx % GRID).astype(jnp.float32)[:, None] * angular
    return jnp.concatenate(
        [jnp.sin(col_pos), jnp.cos(col_pos), jnp.sin(row_pos), jnp.cos(row_pos)], -1
    )


def frequencies(times):
    half_size = FREQ // 2
    spacing = jnp.exp(-jnp.log(10000.0) * jnp.arange(half_size, dtype=jnp.float32) / half_size)
    angles = 1000.0 * times[:, None] * spacing
    return jnp.concatenate([jnp.cos(angles), jnp.sin(angles)], -1)


def unit_scale(unit_ids):
    column = unit_ids % LAYER_UNITS * BLOCK
    in_layer = unit_ids < LAYERS * LAYER_UNITS
    is_output = in_layer & (column >= 9 * D) & (column < 10 * D)
    is_down = in_layer & (column >= 10 * D + FF)
    factor = jnp.where(is_output, 4.0, jnp.where(is_down, 1.5 * (D / FF) ** 0.5, 1.0))
    return factor / D**0.5


def table_scale(row_ids):
    return jnp.where(
        row_ids < CHANNELS,
        CHANNELS ** (-0.5),
        jnp.where(
            row_ids < CHANNELS + FREQ,
            FREQ ** (-0.5),
            jnp.where(row_ids < CHANNELS + FREQ + CLASSES, 0.5, D ** (-0.5)),
        ),
    )


def adam_update(weight, first_mom, second, gradient, rate):
    first_new = beta_one * first_mom + (1.0 - beta_one) * gradient
    second_new = beta_two * second + (1.0 - beta_two) * gradient * gradient
    ratio = (
        first_new
        / (1.0 - beta_one**STEP)
        / (jnp.sqrt(second_new / (1.0 - beta_two**STEP)) + adam_eps)
    )
    return (weight - rate * (ratio + decay_rate * weight), first_new, second_new)


def modulate(normed, shift, scale):
    return normed * (1.0 + scale[:, None, :]) + shift[:, None, :]


def layer_forward(hidden, modul, weights):
    w_qkv, w_out, w_up, w_down = weights
    shift_a, scale_a, gate_a, shift_b, scale_b, gate_b = jnp.split(modul, 6, -1)
    attn_in = modulate(norm_rows(hidden), shift_a, scale_a).astype(jnp.bfloat16)
    qkv_all = dot_low("gpd,de->gpe", attn_in, w_qkv).astype(jnp.bfloat16)
    heads_out = attend(qkv_all)
    branch_a = dot_low("gpd,de->gpe", heads_out, w_out)
    middle = hidden + gate_a[:, None, :] * branch_a
    mlp_in = modulate(norm_rows(middle), shift_b, scale_b).astype(jnp.bfloat16)
    pre_act = dot_low("gpd,df->gpf", mlp_in, w_up)
    post_act = gelu_tanh(pre_act).astype(jnp.bfloat16)
    branch_b = dot_low("gpf,df->gpd", post_act, w_down)
    output = middle + gate_b[:, None, :] * branch_b
    return (
        output,
        (
            hidden,
            modul,
            attn_in,
            qkv_all,
            heads_out,
            branch_a,
            middle,
            mlp_in,
            pre_act.astype(jnp.bfloat16),
            post_act,
            branch_b,
        ),
    )


def layer_backward(grad_out, weights, saved):
    w_qkv, w_out, w_up, w_down = weights
    (
        hidden,
        modul,
        attn_in,
        qkv_all,
        heads_out,
        branch_a,
        middle,
        mlp_in,
        pre_act,
        post_act,
        branch_b,
    ) = saved
    shift_a, scale_a, gate_a, shift_b, scale_b, gate_b = jnp.split(modul, 6, -1)
    grad_gate_b = jnp.sum(grad_out * branch_b, 1)
    grad_branch_b = (gate_b[:, None, :] * grad_out).astype(jnp.bfloat16)
    grad_down = (grad_branch_b, post_act)
    grad_post = dot_low("gpd,df->gpf", grad_branch_b, w_down)
    grad_pre = local_back(gelu_tanh, pre_act.astype(jnp.float32), grad_post).astype(jnp.bfloat16)
    grad_up = (mlp_in, grad_pre)
    grad_mlp_in = dot_low("gpf,df->gpd", grad_pre, w_up)
    normed_b = norm_rows(middle)
    grad_scale_b = jnp.sum(grad_mlp_in * normed_b, 1)
    grad_shift_b = jnp.sum(grad_mlp_in, 1)
    grad_middle = grad_out + local_back(
        norm_rows, middle, grad_mlp_in * (1.0 + scale_b[:, None, :])
    )
    grad_gate_a = jnp.sum(grad_middle * branch_a, 1)
    grad_branch_a = (gate_a[:, None, :] * grad_middle).astype(jnp.bfloat16)
    grad_out_w = (heads_out, grad_branch_a)
    grad_heads = dot_low("gpe,de->gpd", grad_branch_a, w_out).astype(jnp.bfloat16)
    grad_qkv = attend_back(qkv_all, grad_heads)
    grad_qkv_w = (attn_in, grad_qkv)
    grad_attn_in = dot_low("gpe,de->gpd", grad_qkv, w_qkv)
    normed_a = norm_rows(hidden)
    grad_scale_a = jnp.sum(grad_attn_in * normed_a, 1)
    grad_shift_a = jnp.sum(grad_attn_in, 1)
    grad_in = grad_middle + local_back(
        norm_rows, hidden, grad_attn_in * (1.0 + scale_a[:, None, :])
    )
    grad_modul = jnp.concatenate(
        [grad_shift_a, grad_scale_a, grad_gate_a, grad_shift_b, grad_scale_b, grad_gate_b], -1
    ).astype(jnp.bfloat16)
    return (grad_in, grad_modul, [grad_qkv_w, grad_out_w, grad_up, grad_down])


MESH = pl.DeviceIdType.MESH
GATHER_VMEM = 60 * 2**20
SCATTER_VMEM = 56 * 2**20


def dot_rows(left_side, right_side):
    return lax.dot_general(
        left_side, right_side, (((0,), (0,)), ((), ())), preferred_element_type=jnp.float32
    )


def row_product(left_side, right_side):
    left_side = left_side.reshape(-1, left_side.shape[-1])
    right_side = right_side.reshape(-1, right_side.shape[-1])
    return dot_rows(left_side, right_side).astype(jnp.bfloat16)


def unit_groups():
    groups, place = [], 0
    for number in (3 * D, D, FF, FF) * LAYERS + (D,):
        groups.append((place, number // BLOCK))
        place += number // BLOCK
    return groups


PAIR = 2 * HEAD_DIM
SPAN = 6


def head_mask(number):
    lane = lax.broadcasted_iota(jnp.int32, (PATCHES, PAIR), 1)
    return (lane >= number * HEAD_DIM) & (lane < (number + 1) * HEAD_DIM)


def dot_lanes(left_side, right_side):
    return lax.dot_general(
        left_side, right_side, (((1,), (1,)), ((), ())), preferred_element_type=jnp.float32
    )


def attend_kernel(queries, keys_all, values, out):
    row = lax.broadcasted_iota(jnp.int32, (PAIR, PATCHES), 0)
    for pair in range(SPAN):
        lanes = slice(pair * PAIR, (pair + 1) * PAIR)
        scaled = queries[0, :, lanes] * HEAD_DIM ** (-0.5)
        keys, vals = keys_all[0, :, lanes], values[0, :, lanes]
        result = jnp.zeros((PAIR, PATCHES), jnp.float32)
        for number in (0, 1):
            one = jnp.where(head_mask(number), scaled, jnp.zeros((), jnp.bfloat16))
            scores = dot_lanes(keys, one)
            powers = jnp.exp(scores - jnp.max(scores, 0, keepdims=True))
            prob = (powers * (1.0 / jnp.sum(powers, 0, keepdims=True))).astype(jnp.bfloat16)
            result = jnp.where(row // HEAD_DIM == number, dot_rows(vals, prob), result)
        out[0, :, lanes] = result.T.astype(jnp.bfloat16)


def attend_back_kernel(queries, keys_all, values, grads, out):
    step = pl.program_id(1)
    row = lax.broadcasted_iota(jnp.int32, (PAIR, PATCHES), 0)
    none = jnp.zeros((), jnp.bfloat16)
    for pair in range(SPAN):
        lanes = slice(pair * PAIR, (pair + 1) * PAIR)
        scaled = queries[0, :, lanes] * HEAD_DIM ** (-0.5)
        keys, vals, grad = (ref[0, :, lanes] for ref in (keys_all, values, grads))
        grad_queries = jnp.zeros((PAIR, PATCHES), jnp.float32)
        grad_keys = jnp.zeros((PATCHES, PAIR), jnp.float32)
        grad_values = grad_keys
        for number in (0, 1):
            mask = head_mask(number)
            scores = dot_lanes(keys, jnp.where(mask, scaled, none))
            powers = jnp.exp(scores - jnp.max(scores, 0, keepdims=True))
            prob = powers * (1.0 / jnp.sum(powers, 0, keepdims=True))
            grad_prob = dot_lanes(vals, jnp.where(mask, grad, none))
            inner = jnp.sum(prob * grad_prob, 0, keepdims=True)
            grad_scores = (prob * (grad_prob - inner)).astype(jnp.bfloat16)
            part = dot_rows(keys, grad_scores)
            grad_queries = jnp.where(row // HEAD_DIM == number, part, grad_queries)
            part = jnp.dot(grad_scores, scaled, preferred_element_type=jnp.float32)
            grad_keys = jnp.where(mask, part, grad_keys)
            part = jnp.dot(prob.astype(jnp.bfloat16), grad, preferred_element_type=jnp.float32)
            grad_values = jnp.where(mask, part, grad_values)
        grad_queries = grad_queries.T * HEAD_DIM ** (-0.5)
        for third, result in enumerate((grad_queries, grad_keys, grad_values)):
            first = pl.multiple_of(third * D + (step * SPAN + pair) * PAIR, PAIR)
            out[0, :, pl.ds(first, PAIR)] = result.astype(jnp.bfloat16)


def pair_block(third):
    steps = HEADS // 2 // SPAN
    return pl.BlockSpec(
        (1, PATCHES, SPAN * PAIR), lambda image, step: (image, 0, third * steps + step)
    )


def attend(qkv_all):
    images = qkv_all.shape[0]
    steps = HEADS // 2 // SPAN
    return pl.pallas_call(
        attend_kernel,
        grid=(images, steps),
        out_shape=jax.ShapeDtypeStruct((images, PATCHES, D), jnp.bfloat16),
        in_specs=[pair_block(0), pair_block(1), pair_block(2)],
        out_specs=pair_block(0),
        cost_estimate=pl.CostEstimate(
            flops=4 * images * PATCHES * PATCHES * D,
            bytes_accessed=8 * images * PATCHES * D,
            transcendentals=images * HEADS * PATCHES * PATCHES,
        ),
    )(qkv_all, qkv_all, qkv_all)


def attend_back(qkv_all, grad_heads):
    images = qkv_all.shape[0]
    steps = HEADS // 2 // SPAN
    return pl.pallas_call(
        attend_back_kernel,
        grid=(images, steps),
        out_shape=jax.ShapeDtypeStruct((images, PATCHES, 3 * D), jnp.bfloat16),
        in_specs=[pair_block(0), pair_block(1), pair_block(2), pair_block(0)],
        out_specs=pl.BlockSpec((1, PATCHES, 3 * D), lambda image, step: (image, 0, 0)),
        cost_estimate=pl.CostEstimate(
            flops=10 * images * PATCHES * PATCHES * D,
            bytes_accessed=14 * images * PATCHES * D,
            transcendentals=images * HEADS * PATCHES * PATCHES,
        ),
    )(qkv_all, qkv_all, qkv_all, grad_heads)


def adam_kernel(starts, flags, picks, dense, extra, left, right, master, first, second, *refs):
    new_master, new_first, new_second, image_grad = refs
    group = pl.program_id(0)
    size, rows = master.shape[0], dense.shape[2]

    @pl.loop(0, size)
    def _(s):
        slot = group * size + s
        rate, used = flags[slot, 0], flags[slot, 1]
        from_dense, from_extra, from_images = (flags[slot, n] for n in (2, 3, 4))
        image_grad[...] = jnp.dot(left[s], right[s], preferred_element_type=jnp.float32)
        for n, start in enumerate(starts):
            at = (s, slice(start, start + rows))
            grad = jnp.where(from_images > 0.0, image_grad[at[1]], 0.0)
            part = dense[n, picks[slot, 0]].astype(jnp.float32)
            grad = jnp.where(from_dense > 0.0, part, grad)
            part = extra[n, picks[slot, 1]].astype(jnp.float32)
            grad = jnp.where(from_extra > 0.0, part, grad)
            old = (master[at], first[at], second[at])
            first_new = beta_one * old[1] + (1.0 - beta_one) * grad
            second_new = beta_two * old[2] + (1.0 - beta_two) * grad * grad
            root = jnp.sqrt(second_new * (1.0 / (1.0 - beta_two**STEP))) + adam_eps
            turned = pl.reciprocal(root, approx=True)
            turned = turned * (2.0 - root * turned)
            turned = turned * (2.0 - root * turned)
            ratio = first_new * (1.0 / (1.0 - beta_one**STEP)) * turned
            new = (old[0] - rate * (ratio + decay_rate * old[0]), first_new, second_new)
            for ref, value, kept in zip((new_master, new_first, new_second), new, old):
                ref[at] = jnp.where(used > 0.0, value, kept)


def adam_slots(dense, extra, starts, flags, picks, left, right, *state):
    slots = state[0].shape[0]
    size = next(size for size in (3, 2, 1) if slots % size == 0)
    block = pl.BlockSpec((size, D, BLOCK), lambda group: (group, 0, 0))
    side = left.shape[2]
    return pl.pallas_call(
        lambda *refs: adam_kernel(starts, *refs),
        grid=(slots // size,),
        out_shape=[jax.ShapeDtypeStruct((slots, D, BLOCK), jnp.float32)] * 3,
        in_specs=[
            pl.BlockSpec(memory_space=pltpu.SMEM),
            pl.BlockSpec(memory_space=pltpu.SMEM),
            pl.BlockSpec(memory_space=pltpu.VMEM),
            pl.BlockSpec(memory_space=pltpu.VMEM),
            pl.BlockSpec((size, D, side), lambda group: (group, 0, 0)),
            pl.BlockSpec((size, side, BLOCK), lambda group: (group, 0, 0)),
        ]
        + [block] * 3,
        out_specs=[block] * 3,
        scratch_shapes=[pltpu.VMEM((D, BLOCK), jnp.float32)],
        compiler_params=pltpu.CompilerParams(vmem_limit_bytes=40 * 2**20),
        cost_estimate=pl.CostEstimate(
            flops=40 * slots * D * BLOCK, bytes_accessed=26 * slots * D * BLOCK, transcendentals=0
        ),
    )(flags, picks, dense, extra, left, right, *state)


def place_of():
    rep = lax.axis_index("rep")
    return rep // 4, (rep // 2) % 2, rep % 2, lax.axis_index("shard")


def rep_of(y, x, c):
    return (y * 2 + x) * 2 + c


def device_at(j):
    shards = lax.axis_size("shard")
    devices = lax.axis_size("rep") * shards
    me = lax.axis_index("rep") * shards + lax.axis_index("shard")
    peer = lax.rem(me + j, devices)
    return peer, (peer // shards, lax.rem(peer, shards))


def meet_all(devices):
    barrier = pltpu.get_barrier_semaphore()

    @pl.loop(1, devices)
    def _(j):
        pl.semaphore_signal(barrier, inc=1, device_id=device_at(j)[1], device_id_type=MESH)

    pl.semaphore_wait(barrier, devices - 1)


def neighbours():
    y, x, c, z = place_of()
    to_x = (rep_of(y, 1 - x, c), z)
    to_y = (rep_of(1 - y, x, c), z)
    to_core = (rep_of(y, x, 1 - c), z)
    to_z = [(rep_of(y, x, c), lax.rem(z + step, 4)) for step in (1, 2, 3)]
    return to_x, to_y, to_core, to_z


def round_copies(step, source, held, sem, arriving):
    y, x, c, z = place_of()
    to_x, to_y, to_core, to_z = neighbours()
    if step == 0:
        copies = []
        for number in (1, 2, 3):
            at_z = lax.rem(z + 4 - number, 4) if arriving else z
            copies.append((source, held.at[y, x, c, at_z], to_z[number - 1]))
    else:
        at_x = 1 - x if arriving and step == 1 else x
        at_y = 1 - y if arriving and step == 2 else y
        at_c = 1 - c if arriving and step == 3 else c
        block = (held.at[y, at_x, c], held.at[at_y, :, c], held.at[:, :, at_c])[step - 1]
        copies = [(block, block, (to_x, to_y, to_core)[step - 1])]
    return [
        pltpu.make_async_remote_copy(
            src_ref=start,
            dst_ref=dest,
            send_sem=sem.at[0, step, number],
            recv_sem=sem.at[1, step, number],
            device_id=target,
            device_id_type=MESH,
        )
        for number, (start, dest, target) in enumerate(copies)
    ]


def gather_kernel(widths, bases, *refs):
    count = len(widths)
    places, share, spread, extra, info, low_slots = refs[:6]
    outs = refs[6 : count + 6]
    every_info, cond_out, modul_out = refs[count + 6 : count + 9]
    pieces = refs[count + 9 : 2 * count + 9]
    time_two, parts, own_sem, send_sem, recv_sem, time_sem, modul_sem, info_sem = refs[
        2 * count + 9 :
    ]
    devices, images = modul_out.shape[:2]
    slots = low_slots.shape[0]
    y, x, c, z = place_of()
    to_x, to_y, to_core, to_z = neighbours()
    me = rep_of(y, x, c) * 4 + z
    meet_all(devices)

    def remote(k, number, source, dest, target):
        return pltpu.make_async_remote_copy(
            src_ref=source,
            dst_ref=dest,
            send_sem=send_sem.at[k, number],
            recv_sem=recv_sem.at[k, number],
            device_id=target,
            device_id_type=MESH,
        )

    def own_copy(k):
        return pltpu.make_async_copy(pieces[k], outs[k].at[c, y, x, z], own_sem.at[k])

    def line_copies(k, arriving):
        copies = []
        for step in (1, 2, 3):
            at_z = lax.rem(z + 4 - step, 4) if arriving else z
            copies.append(
                remote(k, step - 1, pieces[k], outs[k].at[c, y, x, at_z], to_z[step - 1])
            )
        return copies

    def first_copies(k, arriving):
        half = widths[k] // 2
        left, right = pl.ds(0, half), pl.ds(half, half)
        at_x = 1 - x if arriving else x
        at_y = 1 - y if arriving else y
        a_block = outs[k].at[c, y, at_x, :, :, left]
        b_block = outs[k].at[c, at_y, x, :, :, right]
        return [remote(k, 3, a_block, a_block, to_x), remote(k, 4, b_block, b_block, to_y)]

    def second_copies(k, arriving):
        half = widths[k] // 2
        left, right = pl.ds(0, half), pl.ds(half, half)
        at_x = 1 - x if arriving else x
        at_y = 1 - y if arriving else y
        a_block = outs[k].at[c, at_y, :, :, :, left]
        b_block = outs[k].at[c, :, at_x, :, :, right]
        return [remote(k, 5, a_block, a_block, to_y), remote(k, 6, b_block, b_block, to_x)]

    def core_copies(k, arriving):
        block = outs[k].at[1 - c if arriving else c]
        return [remote(k, 7, block, block, to_core)]

    def start(copies):
        for copy in copies:
            copy.start()

    def arrived(copies):
        for copy in copies:
            copy.wait_recv()

    def modul_copy(j, arriving):
        peer, where = device_at(devices - j if arriving else j)
        return pltpu.make_async_remote_copy(
            src_ref=parts.at[pl.ds(peer * images, images)],
            dst_ref=modul_out.at[peer if arriving else me],
            send_sem=modul_sem.at[0, j],
            recv_sem=modul_sem.at[1, j],
            device_id=where,
            device_id_type=MESH,
        )

    def info_copies(step, arriving):
        return round_copies(step, info, every_info, info_sem, arriving)

    def info_rows(first):
        rows = [every_info[:, :, :, :, :, first + j, :] for j in range(D // BLOCK)]
        return jnp.concatenate([row.reshape(devices * images, BLOCK) for row in rows], -1)

    def image_products():
        copy = pltpu.make_async_copy(outs[0], time_two, time_sem)
        copy.start()
        arrived(info_copies(3, True))
        for step in range(4):
            for sent in info_copies(step, False):
                sent.wait_send()
        copy.wait()
        weight = time_two[...].astype(jnp.float32).reshape(D, D).astype(jnp.bfloat16)
        cond = jnp.dot(
            info_rows(0).astype(jnp.bfloat16), weight, preferred_element_type=jnp.float32
        )
        cond = cond + info_rows(8)
        cond_out[...] = cond
        act = (cond * jax.nn.sigmoid(cond)).astype(jnp.bfloat16)
        for s in range(slots):
            parts[:, s, :] = jnp.dot(act, low_slots[s], preferred_element_type=jnp.float32)
        for i in range(images):
            modul_out[me, i] = parts[me * images + i]

        @pl.loop(1, devices)
        def _(j):
            modul_copy(j, False).start()

    start(info_copies(0, False))
    every_info[y, x, c, z] = info[...]
    def send_piece(k):
        for n in range(widths[k] // BLOCK):
            unit = bases[k] + n
            value = spread[places[0, unit]].astype(jnp.float32) * share[0, unit]
            value = value + extra[places[1, unit]].astype(jnp.float32) * share[1, unit]
            pieces[k][:, n * BLOCK : (n + 1) * BLOCK] = value.astype(jnp.bfloat16)
        start(line_copies(k, False))
        own_copy(k).start()

    send_piece(0)
    for t in range(count + 2):
        if t + 1 < count:
            send_piece(t + 1)
        if t < count:
            own_copy(t).wait()
            arrived(line_copies(t, True))
            start(first_copies(t, False))
        if 0 <= t - 1 < count:
            arrived(first_copies(t - 1, True))
            start(second_copies(t - 1, False))
        if 0 <= t - 2 < count:
            arrived(second_copies(t - 2, True))
            start(core_copies(t - 2, False))
        if t < 3:
            arrived(info_copies(t, True))
            start(info_copies(t + 1, False))
        if t == 3:
            arrived(core_copies(0, True))
            image_products()
    for k in range(1, count):
        arrived(core_copies(k, True))

    @pl.loop(1, devices)
    def _(j):
        modul_copy(j, True).wait_recv()
        modul_copy(j, False).wait_send()

    for k in range(count):
        for copies in (line_copies, first_copies, second_copies, core_copies):
            for copy in copies(k, False):
                copy.wait_send()


def scatter_kernel(widths, bases, slots, *refs):
    count = len(widths)
    lefts, rights = refs[:count], refs[count : 2 * count]
    modul, pick, low_slots, edge, factor = refs[2 * count : 2 * count + 5]
    units, chosen, shared = refs[2 * count + 5 : 2 * count + 8]
    scratch = refs[2 * count + 8 :]
    own, first_in, second_in, line_in = (scratch[i * count : (i + 1) * count] for i in range(4))
    (
        left_in, left_turned, right_in, away, every_modul, parts, landed,
        load_sem, send_sem, recv_sem, modul_sem, part_sem, sum_sem,
    ) = scratch[4 * count :]
    devices, images = 32, shared.shape[4]
    y, x, c, z = place_of()
    to_x, to_y, to_core, to_z = neighbours()
    me = rep_of(y, x, c) * 4 + z
    rows = D // 32
    half_rows = D // 2
    meet_all(devices)

    def exchange(source, dest, sem, j, arriving):
        peer, where = device_at(devices - j if arriving else j)
        return pltpu.make_async_remote_copy(
            src_ref=source(peer, me),
            dst_ref=dest(peer if arriving else me),
            send_sem=sem.at[0, j],
            recv_sem=sem.at[1, j],
            device_id=where,
            device_id_type=MESH,
        )

    def modul_copies(step, arriving):
        return round_copies(step, modul, every_modul, modul_sem, arriving)

    def sum_copies(step, arriving):
        return round_copies(step, shared.at[y, x, c, z], shared, sum_sem, arriving)

    def part_copy(j, arriving):
        return exchange(
            lambda peer, mine: parts.at[pl.ds(peer * images, images)],
            lambda owner: landed.at[owner],
            part_sem, j, arriving,
        )

    def all_start(copy):
        @pl.loop(1, devices)
        def _(j):
            copy(j, False).start()

    def all_arrived(copy):
        @pl.loop(1, devices)
        def _(j):
            copy(j, True).wait_recv()

    def all_sent(copy):
        @pl.loop(1, devices)
        def _(j):
            copy(j, False).wait_send()

    def image_parts():
        arrived(modul_copies(3, True))

        @pl.loop(0, devices // 4)
        def _(i):
            for n in range(4):
                for m in range(images):
                    block = every_modul[i // 4, (i // 2) % 2, i % 2, n, m]
                    chosen[(i * 4 + n) * images + m] = jnp.dot(
                        pick[...], block, preferred_element_type=jnp.float32
                    )

        total = jnp.zeros((devices * images, D), jnp.float32)
        for s in range(slots):
            total = total + lax.dot_general(
                chosen[:, s, :].astype(jnp.bfloat16),
                low_slots[s],
                (((1,), (1,)), ((), ())),
                preferred_element_type=jnp.float32,
            )
        parts[...] = edge[...]
        for j in range(D // BLOCK):
            parts[:, j, :] = total[:, j * BLOCK : (j + 1) * BLOCK]
        all_start(part_copy)
        for i in range(images):
            landed[me, i] = parts[me * images + i]

    def image_sums():
        all_arrived(part_copy)
        shared[y, x, c, z] = jnp.sum(landed[...], 0) * factor[...]
        start(sum_copies(0, False))

    def remote(k, number, source, dest, target):
        return pltpu.make_async_remote_copy(
            src_ref=source,
            dst_ref=dest,
            send_sem=send_sem.at[k, number],
            recv_sem=recv_sem.at[k, number],
            device_id=target,
            device_id_type=MESH,
        )

    def load_left(k):
        return pltpu.make_async_copy(lefts[k], left_in.at[k % 2], load_sem.at[0, k % 2])

    def load_right(k):
        place = right_in.at[k % 3, :, pl.ds(0, widths[k])]
        return pltpu.make_async_copy(rights[k], place, load_sem.at[1, k % 3])

    def core_copies(k):
        source = away.at[k % 3, :, :, :, :, pl.ds(0, widths[k])]
        return [remote(k, 0, source, own[k], to_core)]

    def first_copies(k):
        half = widths[k] // 2
        return [
            remote(k, 1, own[k].at[:, 1 - x, :, :, pl.ds(0, half)], first_in[k].at[0], to_x),
            remote(k, 2, own[k].at[1 - y, :, :, :, pl.ds(half, half)], first_in[k].at[1], to_y),
        ]

    def second_copies(k):
        half = widths[k] // 2
        return [
            remote(k, 3, own[k].at[1 - y, x, :, :, pl.ds(0, half)], second_in[k].at[0], to_y),
            remote(k, 4, own[k].at[y, 1 - x, :, :, pl.ds(half, half)], second_in[k].at[1], to_x),
        ]

    def line_copies(k):
        return [
            remote(
                k,
                4 + step,
                own[k].at[y, x, lax.rem(z + step, 4)],
                line_in[k].at[step - 1],
                to_z[step - 1],
            )
            for step in (1, 2, 3)
        ]

    def start(copies):
        for copy in copies:
            copy.start()

    def arrived(copies):
        for copy in copies:
            copy.wait_recv()

    def products(k, half, store):
        slot = k % 3
        tile = D

        @pl.loop(0, widths[k] // tile)
        def _(n):
            columns = pl.ds(pl.multiple_of(n * tile, tile), tile)
            left = left_turned[slot, pl.ds(pl.multiple_of(half * half_rows, half_rows), half_rows)]
            result = jnp.dot(left, right_in[slot, :, columns], preferred_element_type=jnp.float32)
            for i in range(16):
                at = (i // 8, (i // 4) % 2, i % 4, slice(None), columns)
                store(at, result[i * rows : (i + 1) * rows])

    def away_products(k):
        load_left(k).wait()
        load_right(k).wait()
        left_turned[k % 3] = left_in[k % 2].T
        if k + 2 < count:
            load_left(k + 2).start()
        if k >= 3:
            for copy in core_copies(k - 3):
                copy.wait_send()

        def store(at, value):
            away[(k % 3,) + at] = value.astype(jnp.bfloat16)

        products(k, 1 - c, store)
        start(core_copies(k))

    def own_products(k):
        def store(at, value):
            own[k][at] = (value + own[k][at].astype(jnp.float32)).astype(jnp.bfloat16)

        products(k, c, store)

    def first_sum(k):
        half = widths[k] // 2

        @pl.loop(0, 8)
        def _(i):
            two, at_z = i // 4, i % 4
            a_at = (two, x, at_z, slice(None), pl.ds(0, half))
            b_at = (y, two, at_z, slice(None), pl.ds(half, half))
            own[k][a_at] = own[k][a_at] + first_in[k][0, two, at_z]
            own[k][b_at] = own[k][b_at] + first_in[k][1, two, at_z]

    def second_sum(k):
        half = widths[k] // 2

        @pl.loop(0, 4)
        def _(at_z):
            a_at = (y, x, at_z, slice(None), pl.ds(0, half))
            b_at = (y, x, at_z, slice(None), pl.ds(half, half))
            own[k][a_at] = own[k][a_at] + second_in[k][0, at_z]
            own[k][b_at] = own[k][b_at] + second_in[k][1, at_z]

    start(modul_copies(0, False))
    every_modul[y, x, c, z] = modul[...]
    for k in range(min(3, count)):
        load_right(k).start()
        if k < 2:
            load_left(k).start()
    away_products(0)
    for t in range(count + 3):
        if t + 1 < count:
            away_products(t + 1)
        if t < count:
            arrived(core_copies(t))
            own_products(t)
            start(first_copies(t))
            if t + 3 < count:
                load_right(t + 3).start()
        if 0 <= t - 1 < count:
            arrived(first_copies(t - 1))
            first_sum(t - 1)
            start(second_copies(t - 1))
        if 0 <= t - 2 < count:
            arrived(second_copies(t - 2))
            second_sum(t - 2)
            start(line_copies(t - 2))
        if 0 <= t - 3 < count:
            k = t - 3
            arrived(line_copies(k))
            total = own[k][y, x, z].astype(jnp.float32)
            for step in (1, 2, 3):
                total = total + line_in[k][step - 1].astype(jnp.float32)
            for n in range(widths[k] // BLOCK):
                part = total[:, n * BLOCK : (n + 1) * BLOCK]
                units[bases[k] + n] = part.astype(jnp.bfloat16)
        if t < 3:
            arrived(modul_copies(t, True))
            start(modul_copies(t + 1, False))
        if t == 3:
            image_parts()
        if t == 6:
            image_sums()
        if 7 <= t < 10:
            arrived(sum_copies(t - 7, True))
            start(sum_copies(t - 6, False))
    arrived(sum_copies(3, True))
    all_sent(part_copy)
    for step in range(4):
        for copy in modul_copies(step, False) + sum_copies(step, False):
            copy.wait_send()
    for k in range(count):
        for copies in (core_copies, first_copies, second_copies, line_copies):
            if copies is core_copies and k + 3 < count:
                continue
            for copy in copies(k):
                copy.wait_send()


class RingPlan:
    def split_rows(self, values):
        slots = values.shape[0]
        split = values.reshape(slots, 2, 2, 2, 4, D // 32, BLOCK)
        return split.transpose(2, 3, 1, 4, 0, 5, 6).reshape(32, slots, D // 32, BLOCK)

    def join_rows(self, values):
        starts = []
        for device in range(32):
            y, x, c, z = device // 16, device // 8 % 2, device // 4 % 2, device % 4
            starts.append(((((c * 2 + y) * 2 + x) * 4) + z) * (D // 32))
        return values, starts

    def gather(self, places, share, spread, extra, info, low_slots):
        names = unit_groups()
        turn = [len(names) - 1] + sorted(range(len(names) - 1), key=lambda n: (n % 4 == 1, n))
        bases = tuple(names[n][0] for n in turn)
        widths = tuple(names[n][1] * BLOCK for n in turn)
        count, rows = len(turn), D // 32
        all_images = 32 * info.shape[0]
        slots = low_slots.shape[0]
        room = -(-slots // 8) * 8
        size = sum(4 * D * width for width in widths)
        whole_shape = [(2, 2, 2, 4, rows, width) for width in widths]
        *whole, every_info, cond, modul = pl.pallas_call(
            lambda *refs: gather_kernel(widths, bases, *refs),
            out_shape=[
                jax.ShapeDtypeStruct(shape, jnp.bfloat16) for shape in whole_shape
            ]
            + [
                jax.ShapeDtypeStruct((2, 2, 2, 4) + info.shape, jnp.float32),
                jax.ShapeDtypeStruct((all_images, D), jnp.float32),
                jax.ShapeDtypeStruct((32, all_images // 32, room, BLOCK), jnp.float32),
            ],
            in_specs=[pl.BlockSpec(memory_space=pltpu.SMEM)] * 2
            + [pl.BlockSpec(memory_space=pltpu.VMEM)] * 4,
            out_specs=[pl.BlockSpec(memory_space=pl.ANY)] * count
            + [pl.BlockSpec(memory_space=pltpu.VMEM)] * 3,
            scratch_shapes=[pltpu.VMEM((rows, width), jnp.bfloat16) for width in widths]
            + [
                pltpu.VMEM(whole_shape[0], jnp.bfloat16),
                pltpu.VMEM((all_images, room, BLOCK), jnp.float32),
                pltpu.SemaphoreType.DMA((count,)),
                pltpu.SemaphoreType.DMA((count, 8)),
                pltpu.SemaphoreType.DMA((count, 8)),
                pltpu.SemaphoreType.DMA,
                pltpu.SemaphoreType.DMA((2, 32)),
                pltpu.SemaphoreType.DMA((2, 4, 3)),
            ],
            compiler_params=pltpu.CompilerParams(
                collective_id=0, has_side_effects=True, vmem_limit_bytes=GATHER_VMEM
            ),
            cost_estimate=pl.CostEstimate(flops=0, bytes_accessed=size, transcendentals=0),
        )(places, share, spread, extra, info, low_slots)
        whole = [part.reshape(D, -1) for part in whole]
        modul = jnp.swapaxes(modul[:, :, :slots], 0, 1).reshape(-1, 32 * slots, BLOCK)
        ordered = [whole[turn.index(n)] for n in range(count)]
        every_info = every_info.reshape((all_images,) + info.shape[1:])
        return ordered[:-1], ordered[-1], every_info, cond, modul

    def scatter(self, layer_grads, modul, pick, low_slots, edge, factor):
        turn = [(l, n) for l in range(LAYERS) for n in (0, 2, 3)]
        turn = [(LAYERS - 1, 1)] + turn + [(l, 1) for l in range(LAYERS - 1)]
        grads = [layer_grads[l][n] for l, n in turn]
        names = unit_groups()
        bases = tuple(names[4 * l + n][0] for l, n in turn)
        lefts = [left.reshape(-1, D) for left, _ in grads]
        rights = [right.reshape(left.shape[0], -1) for (_, right), left in zip(grads, lefts)]
        widths = tuple(right.shape[1] for right in rights)
        count, rows, tokens = len(grads), D // 32, lefts[0].shape[0]
        widest = max(widths)
        images, slots = modul.shape[0], low_slots.shape[0]
        size = sum(4 * D * width for width in widths)
        scratch = [pltpu.VMEM((2, 2, 4, rows, width), jnp.bfloat16) for width in widths]
        scratch += [pltpu.VMEM((2, 2, 4, rows, width // 2), jnp.bfloat16) for width in widths]
        scratch += [pltpu.VMEM((2, 4, rows, width // 2), jnp.bfloat16) for width in widths]
        scratch += [pltpu.VMEM((3, rows, width), jnp.bfloat16) for width in widths]
        units, chosen, shared = pl.pallas_call(
            lambda *refs: scatter_kernel(widths, bases, slots, *refs),
            out_shape=[
                jax.ShapeDtypeStruct((sum(widths) // BLOCK, rows, BLOCK), jnp.bfloat16),
                jax.ShapeDtypeStruct((32 * images, pick.shape[0], BLOCK), jnp.float32),
                jax.ShapeDtypeStruct((2, 2, 2, 4) + factor.shape, jnp.float32),
            ],
            in_specs=[pl.BlockSpec(memory_space=pl.ANY)] * (2 * count)
            + [pl.BlockSpec(memory_space=pltpu.VMEM)] * 5,
            out_specs=[pl.BlockSpec(memory_space=pltpu.VMEM)] * 3,
            scratch_shapes=scratch
            + [
                pltpu.VMEM((2, tokens, D), jnp.bfloat16),
                pltpu.VMEM((3, D, tokens), jnp.bfloat16),
                pltpu.VMEM((3, tokens, widest), jnp.bfloat16),
                pltpu.VMEM((3, 2, 2, 4, rows, widest), jnp.bfloat16),
                pltpu.VMEM((2, 2, 2, 4) + modul.shape, jnp.bfloat16),
                pltpu.VMEM(edge.shape, jnp.float32),
                pltpu.VMEM((32,) + factor.shape, jnp.float32),
                pltpu.SemaphoreType.DMA((2, 3)),
                pltpu.SemaphoreType.DMA((count, 8)),
                pltpu.SemaphoreType.DMA((count, 8)),
                pltpu.SemaphoreType.DMA((2, 4, 3)),
                pltpu.SemaphoreType.DMA((2, 32)),
                pltpu.SemaphoreType.DMA((2, 4, 3)),
            ],
            compiler_params=pltpu.CompilerParams(
                collective_id=1, has_side_effects=True, vmem_limit_bytes=SCATTER_VMEM
            ),
            cost_estimate=pl.CostEstimate(flops=0, bytes_accessed=size, transcendentals=0),
        )(*lefts, *rights, modul, pick, low_slots, edge, factor)
        return units, chosen[:, :slots].astype(jnp.bfloat16), shared


class PlainPlan:
    def split_rows(self, values):
        slots, devices = values.shape[0], lax.axis_size("rep") * lax.axis_size("shard")
        return jnp.swapaxes(values.reshape(slots, devices, -1, BLOCK), 0, 1)

    def join_rows(self, values):
        return jnp.swapaxes(values, 0, 1).reshape(1, -1, D, BLOCK), [0]

    def gather(self, places, share, spread, extra, info, low_slots):
        units = jnp.take(spread, places[0], axis=0, mode="clip") * share[0, :, None, None]
        units = units + jnp.take(extra, places[1], axis=0, mode="clip") * share[1, :, None, None]
        units = units.astype(jnp.bfloat16)
        whole = []
        for first, number in unit_groups():
            piece = jnp.swapaxes(units[first : first + number], 0, 1)
            piece = piece.reshape(-1, number * BLOCK)
            whole.append(lax.all_gather(piece, AXES, axis=0, tiled=True))
        every_info = lax.all_gather(info, AXES, axis=0, tiled=True)
        blocks = D // BLOCK
        time_act = every_info[:, :blocks].reshape(-1, D).astype(jnp.bfloat16)
        cond = jnp.dot(time_act, whole[-1], preferred_element_type=jnp.float32)
        cond = cond + every_info[:, 8 : 8 + blocks].reshape(-1, D)
        modul = dot_low("gd,sdc->gsc", jax.nn.silu(cond).astype(jnp.bfloat16), low_slots)
        modul = lax.all_to_all(modul, AXES, split_axis=0, concat_axis=1, tiled=True)
        return whole[:-1], whole[-1], every_info, cond, modul

    def scatter(self, layer_grads, modul, pick, low_slots, edge, factor):
        units = []
        for pair in (pair for grads in layer_grads for pair in grads):
            own = lax.psum_scatter(row_product(*pair), AXES, scatter_dimension=0, tiled=True)
            units.append(jnp.swapaxes(own.reshape(own.shape[0], -1, BLOCK), 0, 1))
        slots = low_slots.shape[0]
        every = lax.all_gather(modul, AXES, axis=0, tiled=True)
        chosen = dot_low("su,guc->gsc", pick, every)[:, :slots].astype(jnp.bfloat16)
        part = dot_low("gsc,sdc->gd", chosen, low_slots).reshape(-1, D // BLOCK, BLOCK)
        parts = edge.at[:, : D // BLOCK].set(part)
        own = lax.psum_scatter(parts, AXES, scatter_dimension=0, tiled=True) * factor
        shared = lax.all_gather(own, AXES, axis=0, tiled=False)
        return jnp.concatenate(units, 0), chosen, shared


def unit_lists():
    dense = np.concatenate(
        [np.arange(l * LAYER_UNITS + ADA_UNITS, (l + 1) * LAYER_UNITS) for l in range(LAYERS)]
    )
    time_units = np.arange(TAIL_FIRST, TAIL_FIRST + TIME_UNITS)
    image_units = np.concatenate(
        [np.arange(l * LAYER_UNITS, l * LAYER_UNITS + ADA_UNITS) for l in range(LAYERS)]
        + [np.arange(TAIL_FIRST + TIME_UNITS, UNITS)]
    )
    return dense, time_units, image_units


def on_device(
    latents,
    noise,
    labels,
    t_index,
    owner,
    master,
    first_moment,
    second_moment,
    small,
    small_first,
    small_second,
):
    count = lax.axis_size("rep") * lax.axis_size("shard")
    me = lax.axis_index(AXES)
    slot_dev = master.shape[1]
    slot_total = count * slot_dev
    rows = D // count
    images = latents.shape[0]
    dense_units, time_units, image_units = unit_lists()

    unit_of_slot = (
        jnp.full((slot_total,), -1, jnp.int32).at[owner].set(jnp.arange(UNITS, dtype=jnp.int32))
    )
    my_unit = lax.dynamic_slice_in_dim(unit_of_slot, me * slot_dev, slot_dev)
    low_slots = jnp.swapaxes(master.astype(jnp.bfloat16), 0, 1)

    plan = RingPlan() if (lax.axis_size("rep"), lax.axis_size("shard")) == (8, 4) else PlainPlan()
    moved = np.concatenate([dense_units, time_units])
    in_layers = (unit_of_slot >= 0) & (unit_of_slot < TAIL_FIRST)
    needed = in_layers & (unit_of_slot % LAYER_UNITS >= ADA_UNITS)
    slot_place = unit_of_slot // LAYER_UNITS * DENSE_UNITS + unit_of_slot % LAYER_UNITS
    slot_place = jnp.where(needed, slot_place - ADA_UNITS, 0)
    needed = needed | (unit_of_slot >= TAIL_FIRST) & (unit_of_slot < TAIL_FIRST + TIME_UNITS)
    needed = needed.astype(jnp.int32).reshape(count, slot_dev)
    total_needed = jnp.sum(needed, 1, keepdims=True)
    before = jnp.cumsum(needed, 1)
    turn = jnp.arange(slot_dev, dtype=jnp.int32)[None]
    rank = jnp.where(needed > 0, before - 1, total_needed + turn - before)
    first_slots = max(1, 2 * slot_dev // 3)
    last_slots = slot_dev - first_slots
    overflow = jnp.max(total_needed) > first_slots
    by_rank = (rank[:, :, None] == turn[:, None]).astype(jnp.int32)
    my_rank = lax.dynamic_index_in_dim(rank, me, 0, False)
    my_order = jnp.sum(lax.dynamic_index_in_dim(by_rank, me, 0, False) * turn.T, 0)

    def exchange(blocks):
        return lax.all_to_all(blocks, AXES, split_axis=0, concat_axis=0, tiled=True)

    def exchange_last(blocks_of, values, places_of):
        return lax.cond(
            overflow,
            lambda *given: exchange(blocks_of(*given)),
            lambda *given: jnp.zeros((count, last_slots, rows, BLOCK), jnp.bfloat16),
            values,
            places_of,
        )

    def slot_blocks(values, places_of):
        return plan.split_rows(jnp.take(values, places_of, axis=0, mode="clip"))

    spread = exchange(slot_blocks(low_slots, my_order[:first_slots])).reshape(-1, rows, BLOCK)
    extra = exchange_last(slot_blocks, low_slots, my_order[first_slots:])
    extra = extra.reshape(-1, rows, BLOCK)
    moved_rank = rank.reshape(-1)[owner[moved]]
    moved_device = owner[moved] // slot_dev
    in_first = moved_rank < first_slots
    places = jnp.stack(
        [
            moved_device * first_slots + jnp.minimum(moved_rank, first_slots - 1),
            moved_device * last_slots + jnp.maximum(moved_rank - first_slots, 0),
        ]
    )
    share = jnp.stack([in_first, ~in_first]).astype(jnp.float32)

    x_start = latents.astype(jnp.float32).reshape(-1, PATCHES, CHANNELS)
    noise_f = noise.astype(jnp.float32).reshape(-1, PATCHES, CHANNELS)
    times = (t_index.astype(jnp.float32) + 0.5) / TSTEPS
    noisy = (1.0 - times)[:, None, None] * x_start + times[:, None, None] * noise_f
    target = noise_f - x_start
    loss_weight = 1.0 + 3.0 * times
    small_low = small.astype(jnp.bfloat16)
    patch_w = small_low[:CHANNELS]
    time_w = small_low[CHANNELS : CHANNELS + FREQ]
    table = small[CHANNELS + FREQ : CHANNELS + FREQ + CLASSES]
    head_w = small_low[CHANNELS + FREQ + CLASSES :]
    noisy_low = noisy.astype(jnp.bfloat16)
    hidden = dot_low("gpc,cd->gpd", noisy_low, patch_w) + positions()

    blocks = D // BLOCK
    freq_own = frequencies(times).astype(jnp.bfloat16)
    time_own = jnp.dot(freq_own, time_w, preferred_element_type=jnp.float32)
    act_own = jax.nn.silu(time_own).astype(jnp.bfloat16).astype(jnp.float32)
    label_own = jnp.take(table, labels, axis=0)
    numbers = jnp.stack([t_index, labels], 1).astype(jnp.float32)
    info = jnp.concatenate(
        [
            act_own.reshape(images, blocks, BLOCK),
            jnp.pad(numbers, ((0, 0), (0, BLOCK - 2)))[:, None],
            jnp.zeros((images, 7 - blocks, BLOCK), jnp.float32),
            label_own.reshape(images, blocks, BLOCK),
            jnp.zeros((images, 8 - blocks, BLOCK), jnp.float32),
        ],
        1,
    )
    whole, time_two, every_info, cond_all, slot_modul = plan.gather(
        places, share, spread, extra, info, low_slots
    )
    all_images = cond_all.shape[0]
    every_time = (every_info[:, blocks, 0] + 0.5) / TSTEPS
    every_label = every_info[:, blocks, 1].astype(jnp.int32)
    weight_total = jnp.sum(1.0 + 3.0 * every_time) * PATCHES
    freq_low = frequencies(every_time).astype(jnp.bfloat16)
    time_pre = jnp.dot(freq_low, time_w, preferred_element_type=jnp.float32)
    time_act = every_info[:, :blocks].reshape(all_images, D).astype(jnp.bfloat16)
    weights_all = [tuple(whole[4 * l : 4 * l + 4]) for l in range(LAYERS)]
    cond = lax.dynamic_slice_in_dim(cond_all, me * images, images)
    cond_act = jax.nn.silu(cond_all).astype(jnp.bfloat16)
    modul_all = jnp.take(slot_modul, owner[image_units], axis=1, mode="clip").reshape(images, -1)

    saved_all = []
    for l in range(LAYERS):
        hidden, saved = layer_forward(
            hidden, modul_all[:, l * 6 * D : (l + 1) * 6 * D], weights_all[l]
        )
        saved_all.append(saved)
    shift_f, scale_f = jnp.split(modul_all[:, LAYERS * 6 * D :], 2, -1)
    normed_f = norm_rows(hidden)
    final_in = modulate(normed_f, shift_f, scale_f).astype(jnp.bfloat16)
    predict = dot_low("gpd,cd->gpc", final_in, head_w)
    error = predict - target
    loss_part = jnp.sum(loss_weight[:, None, None] * error * error) / CHANNELS
    grad_pred = (loss_weight[:, None, None] * 2.0 * error / CHANNELS).astype(jnp.bfloat16)
    grad_head = dot_low("gpc,gpd->cd", grad_pred, final_in)
    grad_final_in = dot_low("gpc,cd->gpd", grad_pred, head_w)
    grad_modul_f = jnp.concatenate(
        [jnp.sum(grad_final_in, 1), jnp.sum(grad_final_in * normed_f, 1)], -1
    ).astype(jnp.bfloat16)
    grad_hidden = local_back(norm_rows, hidden, grad_final_in * (1.0 + scale_f[:, None, :]))
    layer_grads = [None] * LAYERS
    grad_moduls = [None] * LAYERS
    for l in reversed(range(LAYERS)):
        grad_hidden, grad_moduls[l], layer_grads[l] = layer_backward(
            grad_hidden, weights_all[l], saved_all[l]
        )
    grad_embed = grad_hidden.astype(jnp.bfloat16)
    grad_patch = dot_low("gpc,gpd->cd", noisy_low, grad_embed)

    image_place = np.full((UNITS + 1,), -1, np.int32)
    image_place[image_units] = np.arange(len(image_units))
    my_place = jnp.asarray(image_place)[my_unit]
    room_slots, room_units = -(-slot_dev // 16) * 16, -(-len(image_units) // 16) * 16
    pick = jnp.pad(my_place, (0, room_slots - slot_dev), constant_values=-1)[:, None]
    pick = (pick == jnp.arange(room_units, dtype=jnp.int32)).astype(jnp.bfloat16)
    modul_grad = jnp.concatenate(grad_moduls + [grad_modul_f], -1).reshape(images, -1, BLOCK)
    modul_grad = jnp.pad(modul_grad, ((0, 0), (0, room_units - len(image_units)), (0, 0)))
    edge = jnp.concatenate([grad_patch, grad_head], 0)
    edge_room = max(all_images, 4 * CHANNELS)
    edge = jnp.concatenate([edge, jnp.broadcast_to(loss_part, (2 * CHANNELS, D))], 0)
    edge = jnp.pad(edge, ((0, edge_room - 4 * CHANNELS), (0, 0)))[:all_images]
    edge = jnp.pad(edge.reshape(all_images, blocks, BLOCK), ((0, 0), (8, 8 - blocks), (0, 0)))
    factor = local_back(jax.nn.silu, cond, jnp.ones_like(cond)).reshape(images, blocks, BLOCK)
    factor = jnp.pad(factor, ((0, 0), (0, 16 - blocks), (0, 0)), constant_values=1.0)
    unit_grads, slot_grad_out, shared = plan.scatter(
        layer_grads, modul_grad, pick, low_slots, edge, factor
    )
    shared = shared.reshape(all_images, 16, BLOCK)
    grad_cond = shared[:, :blocks].reshape(all_images, D)
    edge = shared[:, 8 : 8 + blocks].reshape(all_images, D)
    grad_patch, grad_head = edge[:CHANNELS], edge[CHANNELS : 2 * CHANNELS]
    loss_sum = edge[2 * CHANNELS, 0]
    grad_time_out = grad_cond.astype(jnp.bfloat16)
    grad_time_act = dot_low("ge,de->gd", grad_time_out, time_two)
    grad_time_pre = local_back(jax.nn.silu, time_pre, grad_time_act).astype(jnp.bfloat16)
    grad_time_w = dot_low("gf,gd->fd", freq_low, grad_time_pre)
    grad_table = jnp.zeros((CLASSES, D), jnp.float32).at[every_label].add(grad_cond)
    small_grad = jnp.concatenate([grad_patch, grad_time_w, grad_table, grad_head], 0)

    my_time = jnp.clip(my_unit - TAIL_FIRST, 0, TIME_UNITS - 1)
    is_time = (my_unit >= TAIL_FIRST) & (my_unit < TAIL_FIRST + TIME_UNITS)
    time_cols = jnp.take(grad_time_out.reshape(all_images, TIME_UNITS, BLOCK), my_time, axis=1)
    packed = jnp.sum(by_rank * slot_place.reshape(count, slot_dev, 1), 1)

    def unit_blocks(values, places_of):
        picked = jnp.take(values, places_of.reshape(-1), axis=0, mode="clip")
        return picked.reshape(count, -1, rows, BLOCK)

    dense_grad, starts = plan.join_rows(exchange(unit_blocks(unit_grads, packed[:, :first_slots])))
    extra_grad = exchange_last(unit_blocks, unit_grads, packed[:, first_slots:])
    extra_grad, starts = plan.join_rows(extra_grad)
    is_dense = (my_unit >= 0) & (my_place < 0) & ~is_time
    right = jnp.where(is_time[None, :, None], time_cols, slot_grad_out)
    left = jnp.where(is_time[:, None, None], time_act.T[None], cond_act.T[None])
    in_first = my_rank < first_slots
    flags = [rate_factor * unit_scale(jnp.maximum(my_unit, 0)), my_unit >= 0]
    flags += [is_dense & in_first, is_dense & ~in_first, ~is_dense]
    picks = [jnp.minimum(my_rank, first_slots - 1), jnp.maximum(my_rank - first_slots, 0)]
    flags = jnp.stack([flag.astype(jnp.float32) for flag in flags], 1)
    new_slots = adam_slots(
        dense_grad,
        extra_grad,
        starts,
        flags,
        jnp.stack(picks, 1),
        left,
        jnp.swapaxes(right, 0, 1),
        *[jnp.swapaxes(values, 0, 1) for values in (master, first_moment, second_moment)],
    )
    new_master, new_first, new_second = [jnp.swapaxes(values, 0, 1) for values in new_slots]
    small_rate = rate_factor * table_scale(jnp.arange(small.shape[0], dtype=jnp.int32))[:, None]
    new_small, new_small_first, new_small_second = adam_update(
        small, small_first, small_second, small_grad, small_rate
    )
    return (
        loss_sum,
        weight_total,
        new_master,
        new_first,
        new_second,
        new_small,
        new_small_first,
        new_small_second,
    )


def solution(mesh):
    return jax.shard_map(
        on_device,
        mesh=mesh,
        in_specs=(
            P(("rep", "shard"), None),
            P(("rep", "shard"), None),
            P(("rep", "shard")),
            P(("rep", "shard")),
            P(),
            P(None, ("rep", "shard"), None),
            P(None, ("rep", "shard"), None),
            P(None, ("rep", "shard"), None),
            P(),
            P(),
            P(),
        ),
        out_specs=(
            P(),
            P(),
            P(None, ("rep", "shard"), None),
            P(None, ("rep", "shard"), None),
            P(None, ("rep", "shard"), None),
            P(),
            P(),
            P(),
        ),
        check_vma=False,
    )
```
